32 devices in a mesh: batch: 16 (over z, x, core), head: 2 (over y).
Axes of the slice: x: 2, y: 2, z: 4, core: 2. Of those that a mesh axis runs over, the one named last changes fastest.
Arguments:
- inputs: bfloat16 [16384, 768], P(('batch', 'head')), may hold values from -6 to 6
- cotangent: bfloat16 [16384, 768], P(('batch', 'head')), may hold values from -6 to 6
- segment_ids: int32 [16384], P('batch'), may hold values from 0 to 3, as said below
- lengths: int32 [32], P('batch'), may hold values from 256 to 512, as said below
- w_qkv: bfloat16 [768, 3, 768], P(None, None, 'head'), may hold values from -0.3125 to 0.3125
- bias_query: bfloat16 [768], P('head'), may hold values from -3 to 3
- bias_value: bfloat16 [768], P('head'), may hold values from -3 to 3
- w_out: bfloat16 [768, 768], replicated, may hold values from -1.25 to 1.25
- bias_out: bfloat16 [768], replicated, may hold values from -3 to 3
- gain_one: bfloat16 [768], replicated, may hold values from 0.25 to 1.75
- shift_one: bfloat16 [768], replicated, may hold values from -3 to 3
- w_up: bfloat16 [768, 3072], replicated, may hold values from -0.21875 to 0.21875
- bias_up: bfloat16 [3072], replicated, may hold values from -3 to 3
- w_down: bfloat16 [3072, 768], replicated, may hold values from -0.15625 to 0.15625
- bias_down: bfloat16 [768], replicated, may hold values from -3 to 3
- gain_two: bfloat16 [768], replicated, may hold values from 0.25 to 1.75
- shift_two: bfloat16 [768], replicated, may hold values from -3 to 3
Outputs:
- output: bfloat16 [16384, 768], P(('batch', 'head'))
- input_grad: bfloat16 [16384, 768], P(('batch', 'head'))
- grad_w_qkv: float32 [768, 3, 768], P('batch', None, 'head')
- grad_bias_query: float32 [768], P(('batch', 'head'))
- grad_bias_value: float32 [768], P(('batch', 'head'))
- grad_w_out: float32 [768, 768], P(('batch', 'head'))
- grad_bias_out: float32 [768], P(('batch', 'head'))
- grad_gain_one: float32 [768], P(('batch', 'head'))
- grad_shift_one: float32 [768], P(('batch', 'head'))
- grad_w_up: float32 [768, 3072], P(('batch', 'head'))
- grad_bias_up: float32 [3072], P(('batch', 'head'))
- grad_w_down: float32 [3072, 768], P(('batch', 'head'))
- grad_bias_down: float32 [768], P(('batch', 'head'))
- grad_gain_two: float32 [768], P(('batch', 'head'))
- grad_shift_two: float32 [768], P(('batch', 'head'))
The draws below stay inside these ranges and needn't reach their ends.
Inputs may be any that keep to these rules, and one draw needn't show every extreme that they name: The live tokens of a packed row are its first lengths positions; the others are padding. `segment_ids`: numbered from 0 in each packed row and never falling along it; positions at or past a row's length carry the number of its last live token.
All inputs are finite; a program needn't handle non-finite values.
Results may differ from the reference program's by a relative error of at most 0.018.
Values may be sent and summed in bfloat16 or wider, within the bound.
No kernel may reach another device: no remote copies, remote signals or barrier semaphores. Data moves between devices by JAX's collectives and lax.ppermute only.
A program may use at most 192 MiB of HBM per device.

```python
import math
import jax
import jax.numpy as jnp
from jax import lax

D = 768
HEADS = 12
HEAD_DIM = 64
FF = 3072
SEQ_LEN = 512
SEQS = 32
TOKENS = 16384


def packed_lengths(key):
    drawn = jax.random.randint(key, (SEQS,), SEQ_LEN // 2, SEQ_LEN + 1)
    drawn = drawn.at[0].set(SEQ_LEN).at[SEQS - 1].set(SEQ_LEN // 2)
    return drawn.astype(jnp.int32)


def draw_lengths(key, part):
    return packed_lengths(key)


def draw_segment_ids(key, part):
    drawn = packed_lengths(key)
    key = jax.random.fold_in(key, 2)
    starts = jax.random.randint(key, (SEQS, SEQ_LEN), 0, 96) == 0
    position = jnp.arange(SEQ_LEN, dtype=jnp.int32)
    stride = max(SEQ_LEN // 8, 1)
    forced = (position % stride == 0) & (position < 4 * stride)
    last_row = jnp.arange(SEQS, dtype=jnp.int32) == SEQS - 1
    live = position[None, :] < drawn[:, None]
    flags = starts & live | (position[None, :] == 0) | forced[None, :] & last_row[:, None]
    numbers = jnp.cumsum(flags.astype(jnp.int32), axis=1) - 1
    return jnp.minimum(numbers, 3).reshape(-1).astype(jnp.int32)


def shard_levels(own_key, extent, split, smallest, largest):
    factor_of, own = 1.0, jax.random.fold_in(own_key, 6)
    for axis_at, blocks in split:
        draws = jnp.exp(jax.random.uniform(jax.random.fold_in(own, axis_at), (blocks,), jnp.float32, smallest / len(split), largest / len(split)))
        factor_of = factor_of * jnp.repeat(draws, extent[axis_at] // blocks).reshape([-1 if axis == axis_at else 1 for axis in range(len(extent))])
    return factor_of


def centred(stream_key, extent, width, most, cuts=(), held_as=jnp.bfloat16):
    entries = jax.random.normal(stream_key, extent, jnp.float32) * width
    if len(cuts) > 0:
        entries = shard_levels(stream_key, extent, cuts, -0.22, 0.18) * entries
    return jnp.clip(entries, min=-most, max=most).astype(held_as)


def setup_inputs(seed: int = 0) -> dict:
    key_of = jax.random.split(jax.random.key(seed), 18)
    inputs = centred(key_of[0], (TOKENS, D), 1.0, 6.0, ((0, 32),))
    cotangent = centred(key_of[1], (TOKENS, D), 1.0, 6.0, ((0, 32),))
    segment_ids = draw_segment_ids(jax.random.fold_in(key_of[17], 71), 0)
    lengths = draw_lengths(jax.random.fold_in(key_of[17], 71), 0)
    w_qkv = centred(key_of[4], (D, 3, D), (D // 2) ** -0.5, 0.3125, ((2, 2),))
    bias_query = centred(key_of[5], (D,), 0.5, 3.0, ((0, 2),))
    bias_value = centred(key_of[6], (D,), 0.5, 3.0, ((0, 2),))
    w_out = centred(key_of[7], (D, D), (D // 32) ** -0.5, 1.25)
    bias_out = centred(key_of[8], (D,), 0.5, 3.0)
    gain_one = jnp.clip(1.0 + 0.15 * jax.random.normal(key_of[9], (D,), jnp.float32), 0.25, 1.75).astype(jnp.bfloat16)
    shift_one = centred(key_of[10], (D,), 0.5, 3.0)
    w_up = centred(key_of[11], (D, FF), D ** -0.5, 0.21875)
    bias_up = centred(key_of[12], (FF,), 0.5, 3.0)
    w_down = centred(key_of[13], (FF, D), (FF // 2) ** -0.5, 0.15625)
    bias_down = centred(key_of[14], (D,), 0.5, 3.0)
    gain_two = jnp.clip(1.0 + 0.15 * jax.random.normal(key_of[15], (D,), jnp.float32), 0.25, 1.75).astype(jnp.bfloat16)
    shift_two = centred(key_of[16], (D,), 0.5, 3.0)
    return dict(inputs=inputs, cotangent=cotangent, segment_ids=segment_ids, lengths=lengths, w_qkv=w_qkv, bias_query=bias_query, bias_value=bias_value, w_out=w_out, bias_out=bias_out, gain_one=gain_one, shift_one=shift_one, w_up=w_up, bias_up=bias_up, w_down=w_down, bias_down=bias_down, gain_two=gain_two, shift_two=shift_two)


@jax.custom_vjp
def low(v):
    return lax.optimization_barrier(v.astype(jnp.bfloat16)).astype(jnp.float32)

@jax.custom_vjp
def low_back(v):
    return v

def low_keep(v):
    return (low(v), None)

def low_pass(kept, grad):
    return (grad,)

def back_keep(v):
    return (v, None)

def back_low(kept, grad):
    return (low(grad),)
low.defvjp(low_keep, low_pass)
low_back.defvjp(back_keep, back_low)

def product(left, right):
    return jnp.dot(left, right, precision=lax.Precision.HIGHEST)

def layer_norm(summed, gain, shift):
    centre = summed - lax.optimization_barrier(jnp.mean(summed, -1, keepdims=True))
    scale_inv = lax.rsqrt(lax.optimization_barrier(jnp.mean(centre * centre, -1, keepdims=True)) + 1e-05)
    return centre * scale_inv * gain + shift

def forward(inputs, params, doc_flat, row_limits):
    w_qkv, bias_query, bias_value, w_out, bias_out, gain_one, shift_one, w_up, bias_up, w_down, bias_down, gain_two, shift_two = params
    seq_count = row_limits.shape[0]
    row_count = inputs.shape[0]
    split_shape = (seq_count, SEQ_LEN, HEADS, HEAD_DIM)
    projected = product(inputs, w_qkv.reshape(D, 3 * D)).reshape(row_count, 3, D)
    queries = low_back(low((projected[:, 0] + bias_query) * 0.125)).reshape(split_shape)
    key_rows = low_back(low(projected[:, 1])).reshape(split_shape)
    value_rows = low_back(low(projected[:, 2] + bias_value)).reshape(split_shape)
    scores = low_back(jnp.einsum('sqhd,skhd->shqk', queries, key_rows, precision=lax.Precision.HIGHEST))
    doc_ids = doc_flat.reshape(seq_count, SEQ_LEN)
    position = jnp.arange(SEQ_LEN, dtype=jnp.int32)
    allowed = (doc_ids[:, :, None] == doc_ids[:, None, :]) & (position[None, None, :] < row_limits[:, None, None])
    scores = jnp.where(allowed[:, None], scores, -1e+30)
    row_max = lax.optimization_barrier(jnp.max(scores, -1, keepdims=True))
    weights = jnp.exp(scores - row_max)
    weights = weights / lax.optimization_barrier(jnp.sum(weights, -1, keepdims=True))
    context = jnp.einsum('shqk,skhd->sqhd', low(weights), value_rows, precision=lax.Precision.HIGHEST)
    context = low_back(low(context.reshape(row_count, D)))
    attended = low_back(product(context, w_out) + bias_out)
    hidden = low(layer_norm(inputs + attended, gain_one, shift_one))
    upward = low_back(product(hidden, w_up) + bias_up)
    active = low(jax.nn.gelu(upward, approximate=False))
    branch = low_back(product(active, w_down) + bias_down)
    return layer_norm(hidden + branch, gain_two, shift_two)

def reference(inputs, cotangent, segment_ids, lengths, w_qkv, bias_query, bias_value, w_out, bias_out, gain_one, shift_one, w_up, bias_up, w_down, bias_down, gain_two, shift_two):
    params = tuple((weight.astype(jnp.float32) for weight in (w_qkv, bias_query, bias_value, w_out, bias_out, gain_one, shift_one, w_up, bias_up, w_down, bias_down, gain_two, shift_two)))
    per_block = math.gcd(SEQS, 8)
    blocks = SEQS // per_block
    block_rows = per_block * SEQ_LEN
    stacked = (inputs.astype(jnp.float32).reshape(blocks, block_rows, D), cotangent.astype(jnp.float32).reshape(blocks, block_rows, D), segment_ids.reshape(blocks, block_rows).astype(jnp.int32), lengths.reshape(blocks, per_block).astype(jnp.int32))

    def step(running, pieces):
        block_in, block_cot, block_ids, block_len = pieces
        result, pullback = jax.vjp(lambda first, second: forward(first, second, block_ids, block_len), block_in, params)
        grad_in, grad_params = pullback(block_cot)
        running = jax.tree.map(lambda earlier, addend: earlier + addend, running, grad_params)
        return (running, (result.astype(jnp.bfloat16), grad_in.astype(jnp.bfloat16)))
    zeros = jax.tree.map(jnp.zeros_like, params)
    totals, (out_blocks, grad_blocks) = lax.scan(step, zeros, stacked)
    scale = 1.0 / SEQS
    return (out_blocks.reshape(TOKENS, D), grad_blocks.reshape(TOKENS, D), totals[0] * scale, totals[1] * scale, totals[2] * scale, totals[3] * scale, totals[4] * scale, totals[5] * scale, totals[6] * scale, totals[7] * scale, totals[8] * scale, totals[9] * scale, totals[10] * scale, totals[11] * scale, totals[12] * scale)
```

```python
import functools

import jax
import jax.numpy as jnp
from jax import lax
from jax.experimental import pallas as pl
from jax.experimental.pallas import tpu as pltpu
from jax.sharding import PartitionSpec as P

HEAD_DIM = 64
LANES = 128
BF = jnp.bfloat16
F32 = jnp.float32
BOTH = ("batch", "head")
VMEM = pl.BlockSpec(memory_space=pltpu.VMEM)
SMEM = pl.BlockSpec(memory_space=pltpu.SMEM)


def nn(left, right):
    return lax.dot_general(left, right, (((1,), (0,)), ((), ())), preferred_element_type=F32)


def nt(left, right):
    return lax.dot_general(left, right, (((1,), (1,)), ((), ())), preferred_element_type=F32)


def call(kernel, outs, *operands, scratch=(), flops=0, moved=0, limit=40):
    return pl.pallas_call(
        kernel,
        in_specs=[SMEM if a.dtype == jnp.int32 else VMEM for a in operands],
        out_specs=[VMEM] * len(outs),
        out_shape=[jax.ShapeDtypeStruct(s, t) for s, t in outs],
        scratch_shapes=list(scratch),
        cost_estimate=pl.CostEstimate(flops=flops, bytes_accessed=moved, transcendentals=0),
        compiler_params=pltpu.CompilerParams(vmem_limit_bytes=limit * 2**20),
    )(*operands)


def project(x_ref, where_ref, weight_refs):
    if len(weight_refs) == 1:
        return nn(x_ref[...], weight_refs[0][...])
    depth = weight_refs[0].shape[0]
    core = where_ref[0]
    mine = pl.multiple_of(core * depth, LANES)
    theirs = pl.multiple_of((1 - core) * depth, LANES)
    return nn(x_ref[:, pl.ds(mine, depth)], weight_refs[0][...]) + nn(
        x_ref[:, pl.ds(theirs, depth)], weight_refs[1][...]
    )


def attend_kernel(parts, where_ref, x_ref, small_ref, mask_ref, *refs):
    weight_refs = refs[:parts]
    qkv_ref, probs_ref, context_ref = refs[parts:]
    width = context_ref.shape[1]
    projected = project(x_ref, where_ref, weight_refs)
    small = small_ref[...].astype(F32)
    qkv_ref[:, :width] = ((projected[:, :width] + small[0:1]) * 0.125).astype(BF)
    qkv_ref[:, width : 2 * width] = projected[:, width : 2 * width].astype(BF)
    qkv_ref[:, 2 * width :] = (projected[:, 2 * width :] + small[1:2]).astype(BF)
    first = lax.broadcasted_iota(jnp.int32, (1, LANES), 1) < HEAD_DIM
    for pair in range(width // LANES):
        at = pair * LANES
        q = qkv_ref[:, at : at + LANES]
        k = qkv_ref[:, width + at : width + at + LANES]
        v = qkv_ref[:, 2 * width + at : 2 * width + at + LANES]
        found = []
        for sub in range(2):
            q_one = jnp.where(first if sub == 0 else ~first, q, jnp.zeros_like(q))
            scores = nt(q_one, k) + mask_ref[...]
            weights = jnp.exp(scores - jnp.max(scores, -1, keepdims=True))
            probs = (weights * (1.0 / jnp.sum(weights, -1, keepdims=True))).astype(BF)
            probs_ref[2 * pair + sub] = probs
            found.append(nn(probs, v))
        context_ref[:, at : at + LANES] = jnp.where(first, found[0], found[1]).astype(BF)


def attend(where, x, small, mask, *weights):
    rows, width = x.shape[0], weights[0].shape[1] // 3
    heads = width // HEAD_DIM
    return call(
        functools.partial(attend_kernel, len(weights)),
        [((rows, 3 * width), BF), ((heads, rows, rows), BF), ((rows, width), BF)],
        where, x, small, mask, *weights,
        flops=2 * rows * x.shape[1] * 3 * width + 16 * heads * rows * rows * LANES,
        moved=8 * 2**20,
    )


def normed(summed):
    centre = summed - jnp.mean(summed, -1, keepdims=True)
    scale_inv = lax.rsqrt(jnp.mean(centre * centre, -1, keepdims=True) + 1e-05)
    return centre * scale_inv, scale_inv


def norm_back(grad, n, scale_inv, gain):
    scaled = grad * gain
    first = jnp.mean(scaled, -1, keepdims=True)
    second = jnp.mean(scaled * n, -1, keepdims=True)
    return scale_inv * (scaled - first - n * second)


def turn_rows(source_ref, turned_ref, rows):
    tokens = source_ref.shape[0]
    blocks = source_ref[...].T.reshape(-1, 2, rows, tokens)
    turned_ref[0] = blocks[:, 0].reshape(-1, tokens)
    turned_ref[1] = blocks[:, 1].reshape(-1, tokens)


BIAS_OUT, GAIN_ONE, SHIFT_ONE, BIAS_DOWN, GAIN_TWO, SHIFT_TWO = range(6)


def ffn_kernel(
    where_ref, x_ref, own_ref, other_ref, w_out_ref, params_ref, w_up_ref, bias_up_ref, w_down_ref,
    cot_ref,
    out_ref, hidden_ref, n_one_ref, r_one_ref, active_ref, slope_ref, grad_two_ref, sums_ref,
    send_ref, keep_ref, branch_ref,
):
    half = own_ref.shape[1]
    head, core = where_ref[1], where_ref[0]
    params = params_ref[...].astype(F32)
    row = lambda i: params[i : i + 1]
    own_at = pl.multiple_of(head * half, LANES)
    other_at = pl.multiple_of((1 - head) * half, LANES)
    attended = nn(own_ref[...], w_out_ref[pl.ds(own_at, half), :]) + nn(
        other_ref[...], w_out_ref[pl.ds(other_at, half), :]
    )
    n_one, r_one = normed(x_ref[...].astype(F32) + attended + row(BIAS_OUT))
    n_one_ref[...] = n_one.astype(n_one_ref.dtype)
    r_one_ref[...] = jnp.broadcast_to(r_one, r_one_ref.shape)
    hidden_ref[...] = (n_one * row(GAIN_ONE) + row(SHIFT_ONE)).astype(BF)
    branch_ref[...] = jnp.broadcast_to(row(BIAS_DOWN), branch_ref.shape)
    chunk = 512

    @pl.loop(0, w_up_ref.shape[1] // chunk)
    def _(i):
        at = pl.ds(pl.multiple_of(i * chunk, chunk), chunk)
        v = nn(hidden_ref[...], w_up_ref[:, at]) + bias_up_ref[:, at].astype(F32)
        phi = 0.5 + 0.5 * lax.erf(v * 0.7071067811865476)
        active = (v * phi).astype(BF)
        active_ref[:, at] = active
        slope_ref[:, at] = (phi + v * (jnp.exp(-0.5 * v * v) * 0.3989422804014327)).astype(BF)
        branch_ref[...] += nn(active, w_down_ref[at, :])

    n_two, r_two = normed(hidden_ref[...].astype(F32) + branch_ref[...])
    out_ref[...] = (n_two * row(GAIN_TWO) + row(SHIFT_TWO)).astype(BF)
    cot = cot_ref[...].astype(F32)
    grad_two = norm_back(cot, n_two, r_two, row(GAIN_TWO))
    grad_two_ref[...] = grad_two
    grad_branch = grad_two.astype(BF)
    sums_ref[0:1] = jnp.sum(cot * n_two, 0, keepdims=True)
    sums_ref[1:2] = jnp.sum(cot, 0, keepdims=True)
    sums_ref[2:3] = jnp.sum(grad_branch.astype(F32), 0, keepdims=True)
    groups, rows = send_ref.shape[0], send_ref.shape[1]
    grad_low = branch_ref
    del grad_low

    @pl.loop(0, groups)
    def _(i):
        at = pl.ds(pl.multiple_of(i * 2 * rows, LANES), 2 * rows)
        block = nn(active_ref[:, at].T, grad_two_ref[...].astype(BF)).astype(BF)
        low, high = block[:rows], block[rows:]
        keep_ref[i] = jnp.where(core == 0, low, high)
        send_ref[i] = jnp.where(core == 0, high, low)


def up_kernel(
    where_ref, hidden_ref, n_one_ref, r_one_ref, slope_ref, grad_two_ref, w_up_ref, w_down_ref,
    w_out_ref, params_ref,
    grad_one_ref, grad_own_ref, grad_other_ref, sums_ref, bias_up_ref, send_ref, keep_ref,
    turned_ref, grad_hidden_ref, grad_context_ref,
):
    half = grad_own_ref.shape[1]
    head, core = where_ref[1], where_ref[0]
    params = params_ref[...].astype(F32)
    row = lambda i: params[i : i + 1]
    groups, rows = send_ref.shape[0], send_ref.shape[1]
    tokens = hidden_ref.shape[0]
    turn_rows(hidden_ref, turned_ref, rows)
    grad_hidden_ref[...] = grad_two_ref[...]
    grad_branch = grad_two_ref[...].astype(BF)
    chunk = 512

    @pl.loop(0, w_up_ref.shape[1] // chunk)
    def _(i):
        at = pl.ds(pl.multiple_of(i * chunk, chunk), chunk)
        grad_active = nt(grad_two_ref[...].astype(BF), w_down_ref[at, :])
        grad_up = (grad_active * slope_ref[:, at].astype(F32)).astype(BF)
        bias_up_ref[:, at] = jnp.sum(grad_up.astype(F32), 0, keepdims=True)
        turned_send = turned_ref[1 - core]
        turned_keep = turned_ref[core]
        send_ref[:, :, at] = nn(turned_send, grad_up).astype(BF).reshape(groups, rows, chunk)
        keep_ref[:, :, at] = nn(turned_keep, grad_up).astype(BF).reshape(groups, rows, chunk)
        grad_hidden_ref[...] += nt(grad_up, w_up_ref[:, at])

    grad_hidden = grad_hidden_ref[...]
    n_one = n_one_ref[...].astype(F32)
    grad_one = norm_back(grad_hidden, n_one, r_one_ref[:, :1], row(GAIN_ONE))
    grad_one_ref[...] = grad_one
    grad_attended = grad_one.astype(BF)
    sums_ref[0:1] = jnp.sum(grad_hidden * n_one, 0, keepdims=True)
    sums_ref[1:2] = jnp.sum(grad_hidden, 0, keepdims=True)
    sums_ref[2:3] = jnp.sum(grad_attended.astype(F32), 0, keepdims=True)
    grad_context_ref[...] = nt(grad_attended, w_out_ref[...]).astype(BF)
    own_at = pl.multiple_of(head * half, LANES)
    other_at = pl.multiple_of((1 - head) * half, LANES)
    grad_own_ref[...] = grad_context_ref[:, pl.ds(own_at, half)]
    grad_other_ref[...] = grad_context_ref[:, pl.ds(other_at, half)]


def back_kernel(
    parts, where_ref, x_ref, qkv_ref, probs_ref, context_ref, grad_ref, *refs
):
    weight_refs = refs[:parts]
    send_ref, keep_ref, grad_x_ref, sums_ref, grads_ref, turned_ref = refs[parts:]
    core = where_ref[0]
    tokens, width = context_ref.shape
    groups, rows = send_ref.shape[0], send_ref.shape[1]
    first = lax.broadcasted_iota(jnp.int32, (1, LANES), 1) < HEAD_DIM
    for pair in range(width // LANES):
        at = pair * LANES
        q = qkv_ref[:, at : at + LANES]
        k = qkv_ref[:, width + at : width + at + LANES]
        v = qkv_ref[:, 2 * width + at : 2 * width + at + LANES]
        grad = grad_ref[:, at : at + LANES]
        q_turned, k_turned, grad_turned = q.T, k.T, grad.T
        dot = grad.astype(F32) * context_ref[:, at : at + LANES].astype(F32)
        for sub in range(2):
            here = first if sub == 0 else ~first
            lines = slice(sub * HEAD_DIM, (sub + 1) * HEAD_DIM)
            probs = probs_ref[2 * pair + sub]
            grad_one = jnp.where(here, grad, jnp.zeros_like(grad))
            inner = jnp.sum(jnp.where(here, dot, 0.0), -1, keepdims=True)
            grad_scores = (probs.astype(F32) * (nt(grad_one, v) - inner)).astype(BF)
            grad_q = nt(k_turned[lines], grad_scores).astype(BF)
            grad_k = nn(q_turned[lines], grad_scores).astype(BF)
            grad_v = nn(grad_turned[lines], probs).astype(BF)
            base = at + sub * HEAD_DIM
            grads_ref[base : base + HEAD_DIM] = grad_q * 0.125
            grads_ref[width + base : width + base + HEAD_DIM] = grad_k
            grads_ref[2 * width + base : 2 * width + base + HEAD_DIM] = grad_v
    grads = grads_ref[...]
    total = jnp.sum(grads.astype(F32), -1, keepdims=True)
    sums_ref[...] = jnp.broadcast_to(total, sums_ref.shape)
    turn_rows(x_ref, turned_ref, rows)
    turned_send = turned_ref[1 - core]
    send_ref[...] = nt(turned_send, grads).astype(BF).reshape(send_ref.shape)
    turned_keep = turned_ref[core]
    keep_ref[...] = nt(turned_keep, grads).astype(BF).reshape(keep_ref.shape)
    plain = grads.T
    if parts == 1:
        grad_x_ref[...] = nt(plain, weight_refs[0][...]).astype(grad_x_ref.dtype)
    else:
        depth = weight_refs[0].shape[0]
        mine = pl.multiple_of(core * depth, LANES)
        theirs = pl.multiple_of((1 - core) * depth, LANES)
        grad_x_ref[:, pl.ds(mine, depth)] = nt(plain, weight_refs[0][...]).astype(grad_x_ref.dtype)
        grad_x_ref[:, pl.ds(theirs, depth)] = nt(plain, weight_refs[1][...]).astype(grad_x_ref.dtype)


def attend_back(where, x, qkv, probs, context, grad, weights, groups):
    tokens, width = context.shape
    depth = x.shape[1]
    rows = depth // (2 * groups)
    return call(
        functools.partial(back_kernel, len(weights)),
        [
            ((groups, rows, 3 * width), BF),
            ((groups, rows, 3 * width), BF),
            ((tokens, depth), BF),
            ((3 * width, LANES), F32),
        ],
        where, x, qkv, probs, context, grad, *weights,
        scratch=[pltpu.VMEM((3 * width, tokens), BF), pltpu.VMEM((2, groups * rows, tokens), BF)],
        flops=8 * 10**9,
        moved=10 * 2**20,
    )


class Exchange:
    def __init__(self, batch):
        bits = batch.bit_length() - 1
        self.batch = batch
        stages, bit = [], 1
        if (bits - 1) % 2:
            stages.append((1,))
            bit = 2
        while bit < bits:
            stages.append((bit, bit + 1))
            bit += 2
        self.stages = stages
        self.place = lax.axis_index("batch")
        self.head = lax.axis_index("head")

    def swap(self, value, axis, flip):
        count = lax.axis_size(axis)
        return lax.ppermute(value, axis, [(i, i ^ flip) for i in range(count)])


def pick(value, index, axis):
    return lax.dynamic_index_in_dim(value, index, axis, keepdims=False)


def reduce_axis(value_pairs, index, size, axis, flip_of, swap):
    received = []
    for other in range(1, size):
        parts = [pick(v, index ^ other, axis).astype(F32) for v in value_pairs]
        summed = functools.reduce(jnp.add, parts).astype(BF)
        received.append(swap(summed, other))
    own = [pick(v, index, axis).astype(F32) for v in value_pairs]
    return [functools.reduce(jnp.add, own).astype(BF)] + received if size > 1 else own


def on_device(
    inputs, cotangent, segment_ids, lengths, w_qkv, bias_query, bias_value, w_out, bias_out, gain_one,
    shift_one, w_up, bias_up, w_down, bias_down, gain_two, shift_two,
):
    width = w_out.shape[0]
    half = w_qkv.shape[2]
    ff = w_up.shape[1]
    tokens = inputs.shape[0]
    batch = lax.axis_size("batch")
    heads = lax.axis_size("head")
    place, head = lax.axis_index("batch"), lax.axis_index("head")
    core = place % 2
    scale = 1.0 / (lengths.shape[0] * batch)
    where = jnp.stack([core, head]).astype(jnp.int32)

    def swap_batch(value, flip):
        return lax.ppermute(value, "batch", [(i, i ^ flip) for i in range(batch)])

    def swap_head(value):
        return lax.ppermute(value, "head", [(0, 1), (1, 0)])

    w_own = w_qkv.reshape(width, 3 * half)
    depth = width // 2
    w_mine = swap_head(lax.dynamic_slice_in_dim(w_own, core * depth, depth, 0))
    w_theirs = swap_batch(w_mine, 1)
    small_own = jnp.stack([bias_query, bias_value])
    small_other = swap_head(small_own)
    doc_ids = lax.dynamic_slice_in_dim(segment_ids, head * tokens, tokens, 0)
    length = lax.dynamic_index_in_dim(lengths, head, 0, keepdims=False)
    position = jnp.arange(tokens, dtype=jnp.int32)
    allowed = (doc_ids[:, None] == doc_ids[None, :]) & (position[None, :] < length)
    mask = jnp.where(allowed, 0.0, -1e30).astype(F32)
    params = jnp.stack([bias_out, gain_one, shift_one, bias_down, gain_two, shift_two])

    qkv_own, probs_own, context_own = attend(where, inputs, small_own, mask, w_own)
    qkv_other, probs_other, context_other = attend(
        where, inputs, small_other, mask, w_mine, w_theirs
    )

    groups = batch // 2
    ffn_rows, up_rows = ff // batch, width // batch
    out, hidden, n_one, r_one, active, slope, grad_two, sums_two, down_send, down_keep = call(
        ffn_kernel,
        [
            ((tokens, width), BF),
            ((tokens, width), BF),
            ((tokens, width), F32),
            ((tokens, LANES), F32),
            ((tokens, ff), BF),
            ((tokens, ff), BF),
            ((tokens, width), F32),
            ((8, width), F32),
            ((groups, ffn_rows, width), BF),
            ((groups, ffn_rows, width), BF),
        ],
        where, inputs, context_own, context_other, w_out, params, w_up, bias_up[None], w_down, cotangent,
        scratch=[pltpu.VMEM((tokens, width), F32)],
        flops=16 * 10**9, moved=30 * 2**20,
    )
    down_got = swap_batch(down_send, 1)
    grad_one, grad_own, grad_other, sums_one, sum_bias_up, up_send, up_keep = call(
        up_kernel,
        [
            ((tokens, width), F32),
            ((tokens, half), BF),
            ((tokens, half), BF),
            ((8, width), F32),
            ((1, ff), F32),
            ((groups, up_rows, ff), BF),
            ((groups, up_rows, ff), BF),
        ],
        where, hidden, n_one, r_one, slope, grad_two, w_up, w_down, w_out, params,
        scratch=[
            pltpu.VMEM((2, groups * up_rows, tokens), BF),
            pltpu.VMEM((tokens, width), F32),
            pltpu.VMEM((tokens, width), BF),
        ],
        flops=16 * 10**9, moved=30 * 2**20,
    )
    up_got = swap_batch(up_send, 1)
    q_send, q_keep, grad_x_own, sums_own = attend_back(
        where, inputs, qkv_own, probs_own, context_own, grad_own, (w_own,), groups
    )
    own_got = swap_batch(q_send, 1)
    p_send, p_keep, grad_x_other, sums_other = attend_back(
        where, inputs, qkv_other, probs_other, context_other, grad_other, (w_mine, w_theirs), groups
    )
    other_got = swap_batch(p_send, 1)
    input_grad = (grad_one + grad_x_own.astype(F32) + grad_x_other.astype(F32)).astype(BF)

    context = jnp.concatenate([context_own, context_other], 1)
    context = jnp.where(head == 0, context, jnp.concatenate([context_other, context_own], 1))
    grad_w_out = lax.dot_general(
        context, grad_one.astype(BF), (((0,), (0,)), ((), ())), preferred_element_type=F32
    )

    def both(own, other):
        return jnp.where(head == 0, jnp.concatenate([own, other]), jnp.concatenate([other, own]))

    bias_columns = [
        both(sums_own[:half, 0], sums_other[:half, 0]),
        both(sums_own[2 * half :, 0], sums_other[2 * half :, 0]),
    ]
    rows = [sums_one[2], sums_one[0], sums_one[1], sums_two[2], sums_two[0], sums_two[1]]
    spread = sum_bias_up.reshape(batch * heads, ff // width, width // (batch * heads))
    columns = jnp.stack(bias_columns + rows, 1)
    columns = jnp.concatenate([columns, spread.swapaxes(1, 2).reshape(width, ff // width)], 1)
    columns = jnp.pad(columns, ((0, 0), (0, LANES - columns.shape[1])))
    mixed = jnp.concatenate([grad_w_out, columns], 1).astype(BF)
    mixed = mixed.reshape(groups, 2, up_rows, width + LANES)
    mixed_send, mixed_keep = pick(mixed, 1 - core, 1), pick(mixed, core, 1)
    mixed_got = swap_batch(mixed_send, 1)

    stage_sizes, left = [], groups
    bit = 1
    bits = batch.bit_length() - 1
    plan = []
    if (bits - 1) % 2:
        plan.append((1, 2))
        bit = 2
    while bit < bits:
        plan.append((bit, 4))
        bit += 2

    def add(values, index, axis):
        return functools.reduce(
            jnp.add, [pick(v, index, axis).astype(F32) for v in values]
        )

    def stage_batch(values, bit, size):
        values = [v.reshape(v.shape[0] // size, size, *v.shape[1:]) for v in values]
        index = (place >> bit) % size
        got = [
            swap_batch(add(values, index ^ other, 1).astype(BF), other << bit) for other in range(1, size)
        ]
        return [add(values, index, 1).astype(BF)] + got

    def stage_head(values):
        got = swap_head(add(values, 1 - head, 1).astype(BF))
        return [add(values, head, 1).astype(BF), got]

    def finish(values):
        return functools.reduce(jnp.add, [v.astype(F32) for v in values])[0] * scale

    def chain(values, order):
        for name in order:
            values = stage_head(values) if name == "head" else stage_batch(values, *name)
        return finish(values)

    def rows_of(value):
        return value.reshape(groups, heads, value.shape[1] // heads, value.shape[2])

    head_first = ["head"] + plan
    head_second = plan[:1] + ["head"] + plan[1:]
    sum_down = chain([rows_of(down_keep), rows_of(down_got)], head_first)
    sum_up = chain([rows_of(up_keep), rows_of(up_got)], head_second)
    qkv_got = swap_head((p_keep.astype(F32) + other_got.astype(F32)).astype(BF))
    values = [(q_keep.astype(F32) + own_got.astype(F32)).astype(BF), qkv_got]
    for name in plan:
        values = stage_batch(values, *name)
    sum_qkv = finish(values).reshape(up_rows, 3, half)
    sum_mixed = chain([rows_of(mixed_keep), rows_of(mixed_got)], head_second)
    sum_w_out = sum_mixed[:, :width]
    small = sum_mixed[:, width:]
    sum_bias_up = small[:, 8 : 8 + ff // width].T.reshape(-1)
    return (
        out, input_grad, sum_qkv, small[:, 0], small[:, 1], sum_w_out, small[:, 2], small[:, 3], small[:, 4],
        sum_up, sum_bias_up, sum_down, small[:, 5], small[:, 6], small[:, 7],
    )


def solution(mesh):
    rows = P(BOTH, None)
    placed = (rows, rows, P("batch"), P("batch"), P(None, None, "head"), P("head"), P("head")) + (P(),) * 10
    flat = P(BOTH)
    return jax.shard_map(
        on_device,
        mesh=mesh,
        in_specs=placed,
        out_specs=(
            rows, rows, P("batch", None, "head"), flat, flat, rows, flat, flat, flat, rows, flat, rows, flat,
            flat, flat,
        ),
        check_vma=False,
    )
```

```python
import functools

import jax
import jax.numpy as jnp
from jax import lax
from jax.experimental import pallas as pl
from jax.experimental.pallas import tpu as pltpu
from jax.sharding import PartitionSpec as P

HEAD_DIM = 64
LANES = 128
BF = jnp.bfloat16
F32 = jnp.float32
BOTH = ("batch", "head")
VMEM = pl.BlockSpec(memory_space=pltpu.VMEM)
ANY = pl.BlockSpec(memory_space=pl.ANY)
SMEM = pl.BlockSpec(memory_space=pltpu.SMEM)


def nn(left, right):
    return lax.dot_general(left, right, (((1,), (0,)), ((), ())), preferred_element_type=F32)


def nt(left, right):
    return lax.dot_general(left, right, (((1,), (1,)), ((), ())), preferred_element_type=F32)


class Far:
    def __init__(self, value):
        self.value = value


def call(kernel, outs, *operands, scratch=(), flops=0, moved=0, limit=16, far_outs=()):
    specs = [ANY if isinstance(a, Far) else SMEM if a.dtype == jnp.int32 else VMEM for a in operands]
    operands = [a.value if isinstance(a, Far) else a for a in operands]
    return pl.pallas_call(
        kernel,
        in_specs=specs,
        out_specs=[ANY if i in far_outs else VMEM for i in range(len(outs))],
        out_shape=[jax.ShapeDtypeStruct(s, t) for s, t in outs],
        scratch_shapes=list(scratch),
        cost_estimate=pl.CostEstimate(flops=20 * flops, bytes_accessed=moved, transcendentals=0),
        compiler_params=pltpu.CompilerParams(vmem_limit_bytes=limit * 2**20),
    )(*operands)


def attend_kernel(
    where_ref, x_ref, small_ref, mask_ref, mine_ref, theirs_ref, qkv_ref, probs_ref, context_ref,
    held_ref, sems,
):
    width = context_ref.shape[1]
    depth = mine_ref.shape[1]
    mine = pl.ds(pl.multiple_of(where_ref[0] * depth, LANES), depth)
    theirs = pl.ds(pl.multiple_of((1 - where_ref[0]) * depth, LANES), depth)
    projected = nt(x_ref[:, mine], mine_ref[...]) + nt(x_ref[:, theirs], theirs_ref[...])
    small = small_ref[...].astype(F32)
    qkv_ref[:, :width] = ((projected[:, :width] + small[0:1]) * 0.125).astype(BF)
    qkv_ref[:, width : 2 * width] = projected[:, width : 2 * width].astype(BF)
    qkv_ref[:, 2 * width :] = (projected[:, 2 * width :] + small[1:2]).astype(BF)
    first = lax.broadcasted_iota(jnp.int32, (1, LANES), 1) < HEAD_DIM

    def leave(number, slot):
        return pltpu.make_async_copy(held_ref.at[slot], probs_ref.at[number], sems.at[slot])

    @pl.loop(0, width // LANES)
    def _(pair):
        lanes = [pl.ds(pl.multiple_of(part * width + pair * LANES, LANES), LANES) for part in range(3)]
        q, k, v = [qkv_ref[:, at] for at in lanes]
        found = []
        for sub in range(2):
            q_one = jnp.where(first if sub == 0 else ~first, q, jnp.zeros_like(q))
            scores = nt(q_one, k) + mask_ref[...]
            weights = jnp.exp(scores - jnp.max(scores, -1, keepdims=True))
            probs = (weights * (1.0 / jnp.sum(weights, -1, keepdims=True))).astype(BF)

            @pl.when(pair > 0)
            def _():
                leave(2 * pair - 2 + sub, sub).wait()

            held_ref[sub] = probs
            leave(2 * pair + sub, sub).start()
            found.append(nn(probs, v))
        context_ref[:, lanes[0]] = jnp.where(first, found[0], found[1]).astype(BF)

    for sub in range(2):
        leave(probs_ref.shape[0] - 2 + sub, sub).wait()


def attend(where, x, small, mask, *weights):
    rows, width = x.shape[0], weights[0].shape[0] // 3
    heads = width // HEAD_DIM
    return call(
        attend_kernel,
        [((rows, 3 * width), BF), ((heads, rows, rows), BF), ((rows, width), BF)],
        where, x, small, mask, *weights,
        far_outs=(1,),
        scratch=[pltpu.VMEM((2, rows, rows), BF), pltpu.SemaphoreType.DMA((2,))],
        flops=2 * rows * x.shape[1] * 3 * width + 16 * heads * rows * rows * LANES,
        moved=8 * 2**20,
    )


def normed(summed):
    centre = summed - jnp.mean(summed, -1, keepdims=True)
    scale_inv = lax.rsqrt(jnp.mean(centre * centre, -1, keepdims=True) + 1e-05)
    return centre * scale_inv, scale_inv


def norm_back(grad, n, scale_inv, gain):
    scaled = grad * gain
    first = jnp.mean(scaled, -1, keepdims=True)
    second = jnp.mean(scaled * n, -1, keepdims=True)
    return scale_inv * (scaled - first - n * second)


def turn_rows(source_ref, turned_ref, rows):
    tokens = source_ref.shape[0]
    blocks = source_ref[...].T.reshape(-1, 2, rows, tokens)
    turned_ref[0] = blocks[:, 0].reshape(-1, tokens)
    turned_ref[1] = blocks[:, 1].reshape(-1, tokens)


BIAS_OUT, GAIN_ONE, SHIFT_ONE, BIAS_DOWN, GAIN_TWO, SHIFT_TWO = range(6)


CHUNK = 512
LINES = 16


def blocks(count):
    return [slice(at, at + LINES) for at in range(0, count, LINES)]


def fold(value):
    return jnp.sum(value.reshape(-1, 8, value.shape[-1]), 0)


def total(folded):
    return jnp.sum(folded, 0, keepdims=True)


def ffn_kernel(
    where_ref, x_ref, own_ref, other_ref, w_out_ref, params_ref, w_up_ref, bias_up_ref, w_down_ref,
    cot_ref,
    out_ref, hidden_ref, n_one_ref, r_one_ref, active_ref, slope_ref, grad_two_ref, sums_ref,
    first_ref, second_ref, branch_ref, up_ref, down_ref, sems,
):
    half = own_ref.shape[1]
    tokens, width = x_ref.shape
    head = where_ref[1]
    count = w_up_ref.shape[1] // CHUNK
    span = lambda i: pl.ds(pl.multiple_of(i * CHUNK, CHUNK), CHUNK)

    def fetch_up(i):
        return pltpu.make_async_copy(w_up_ref.at[:, span(i)], up_ref.at[:, span(i)], sems.at[0, i])

    def fetch_down(i):
        return pltpu.make_async_copy(w_down_ref.at[span(i), :], down_ref.at[span(i), :], sems.at[1, i])

    for i in range(count):
        fetch_up(i).start()
        fetch_down(i).start()
    params = params_ref[...].astype(F32)
    row = lambda i: params[i : i + 1]
    own_at = pl.multiple_of(head * half, LANES)
    other_at = pl.multiple_of((1 - head) * half, LANES)
    branch_ref[...] = nn(own_ref[...], w_out_ref[pl.ds(own_at, half), :]) + nn(
        other_ref[...], w_out_ref[pl.ds(other_at, half), :]
    )

    for at in blocks(tokens):
        n, r = normed(x_ref[at, :].astype(F32) + branch_ref[at, :] + row(BIAS_OUT))
        n_one_ref[at, :] = n
        r_one_ref[at, :] = jnp.broadcast_to(r, (LINES, LANES))
        hidden_ref[at, :] = (n * row(GAIN_ONE) + row(SHIFT_ONE)).astype(BF)

    def upward(ref, at):
        ref[...] = nn(hidden_ref[...], up_ref[:, at])

    def gelu(ref, at):
        bias = bias_up_ref[:, at].astype(F32)
        for start in range(0, tokens, LINES):
            lines = slice(start, start + LINES)
            v = ref[lines, :] + bias
            phi = 0.5 + 0.5 * lax.erf(v * 0.7071067811865476)
            active_ref[lines, at] = (v * phi).astype(BF)
            density = jnp.exp(-0.5 * v * v) * 0.3989422804014327
            slope_ref[lines, at] = (phi + v * density).astype(BF)

    def downward(at):
        branch_ref[...] += nn(active_ref[:, at], down_ref[at, :])

    branch_ref[...] = jnp.zeros_like(branch_ref)
    fetch_up(0).wait()
    upward(first_ref, span(0))

    @pl.loop(0, count // 2)
    def _(i):
        fetch_up(2 * i + 1).wait()
        fetch_down(2 * i).wait()
        fetch_down(2 * i + 1).wait()

        @pl.when(2 * i + 2 < count)
        def _():
            fetch_up(2 * i + 2).wait()

        upward(second_ref, span(2 * i + 1))
        gelu(first_ref, span(2 * i))
        downward(span(2 * i))
        upward(first_ref, span(jnp.minimum(2 * i + 2, count - 1)))
        gelu(second_ref, span(2 * i + 1))
        downward(span(2 * i + 1))

    sums = [0.0, 0.0, 0.0]
    for at in blocks(tokens):
        n, r = normed(hidden_ref[at, :].astype(F32) + branch_ref[at, :] + row(BIAS_DOWN))
        out_ref[at, :] = (n * row(GAIN_TWO) + row(SHIFT_TWO)).astype(BF)
        cot = cot_ref[at, :].astype(F32)
        grad = norm_back(cot, n, r, row(GAIN_TWO))
        grad_two_ref[at, :] = grad
        terms = (cot * n, cot, grad.astype(BF).astype(F32))
        sums = [earlier + fold(term) for earlier, term in zip(sums, terms)]
    for i, folded in enumerate(sums):
        sums_ref[i : i + 1] = total(folded)


def down_kernel(where_ref, active_ref, grad_two_ref, send_ref, keep_ref):
    core = where_ref[0]
    groups, rows = send_ref.shape[0], send_ref.shape[1]
    grad_branch = grad_two_ref[...].astype(BF)
    for i in range(groups):
        block = nn(active_ref[:, i * 2 * rows : (i + 1) * 2 * rows].T, grad_branch).astype(BF)
        low, high = block[:rows], block[rows:]
        keep_ref[i] = jnp.where(core == 0, low, high)
        send_ref[i] = jnp.where(core == 0, high, low)


def slope_kernel(
    slope_ref, grad_two_ref, w_down_ref, grad_up_ref, bias_up_ref, branch_ref, down_ref, sems
):
    count = w_down_ref.shape[0] // CHUNK
    span = lambda i: pl.ds(pl.multiple_of(i * CHUNK, CHUNK), CHUNK)

    def fetch(i):
        return pltpu.make_async_copy(w_down_ref.at[span(i), :], down_ref.at[span(i), :], sems.at[i])

    for i in range(count):
        fetch(i).start()
    branch_ref[...] = grad_two_ref[...].astype(BF)

    @pl.loop(0, count)
    def _(i):
        fetch(i).wait()
        grad_active = nt(branch_ref[...], down_ref[span(i), :])
        grad_up = (grad_active * slope_ref[:, span(i)].astype(F32)).astype(BF)
        grad_up_ref[:, span(i)] = grad_up
        bias_up_ref[:, span(i)] = jnp.sum(grad_up.astype(F32), 0, keepdims=True)


def up_kernel(
    where_ref, hidden_ref, n_one_ref, r_one_ref, grad_up_ref, grad_two_ref, w_up_ref, w_out_ref, params_ref,
    own_ref, other_ref,
    grad_one_ref, grad_own_ref, grad_other_ref, sums_ref, send_ref, keep_ref,
    both_ref, turned_ref, grad_hidden_ref, grad_context_ref, up_ref, sem,
):
    half = grad_own_ref.shape[1]
    head, core = where_ref[1], where_ref[0]
    params = params_ref[...].astype(F32)
    row = lambda i: params[i : i + 1]
    groups, rows = send_ref.shape[0], send_ref.shape[1]
    tokens = hidden_ref.shape[0]
    fetch = pltpu.make_async_copy(w_up_ref, up_ref, sem)
    fetch.start()
    turn_rows(hidden_ref, turned_ref, rows)

    @pl.loop(0, w_up_ref.shape[1] // CHUNK)
    def _(i):
        at = pl.ds(pl.multiple_of(i * CHUNK, CHUNK), CHUNK)
        grad_up = grad_up_ref[:, at]
        send_ref[:, :, at] = nn(turned_ref[1 - core], grad_up).astype(BF).reshape(groups, rows, CHUNK)
        keep_ref[:, :, at] = nn(turned_ref[core], grad_up).astype(BF).reshape(groups, rows, CHUNK)

    fetch.wait()
    grad_hidden_ref[...] = nt(grad_up_ref[...], up_ref[...])
    sums = [0.0, 0.0, 0.0]
    for at in blocks(tokens):
        grad_hidden = grad_hidden_ref[at, :] + grad_two_ref[at, :]
        n_one = n_one_ref[at, :]
        grad_one = norm_back(grad_hidden, n_one, r_one_ref[at, :1], row(GAIN_ONE))
        grad_one_ref[at, :] = grad_one
        terms = (grad_hidden * n_one, grad_hidden, grad_one.astype(BF).astype(F32))
        sums = [earlier + fold(term) for earlier, term in zip(sums, terms)]
    for i, folded in enumerate(sums):
        sums_ref[i : i + 1] = total(folded)
    grad_attended = grad_one_ref[...].astype(BF)
    grad_context_ref[...] = nt(grad_attended, w_out_ref[...]).astype(BF)
    own_at = pl.multiple_of(head * half, LANES)
    other_at = pl.multiple_of((1 - head) * half, LANES)
    both_ref[:, pl.ds(own_at, half)] = own_ref[...]
    both_ref[:, pl.ds(other_at, half)] = other_ref[...]
    turn_rows(both_ref, turned_ref, rows)
    ff = w_up_ref.shape[1]
    send_ref[:, :, ff:] = nn(turned_ref[1 - core], grad_attended).astype(BF).reshape(groups, rows, -1)
    keep_ref[:, :, ff:] = nn(turned_ref[core], grad_attended).astype(BF).reshape(groups, rows, -1)
    grad_own_ref[...] = grad_context_ref[:, pl.ds(own_at, half)]
    grad_other_ref[...] = grad_context_ref[:, pl.ds(other_at, half)]


def back_kernel(
    last, where_ref, x_ref, qkv_ref, probs_ref, context_ref, grad_ref, mine_ref, theirs_ref, partial_ref, *refs
):
    if last:
        (sums_own_ref, sums_one_ref, sums_two_ref, bias_up_ref, send_ref, keep_ref, grad_x_ref, sums_ref) = refs[:8]
    else:
        send_ref, keep_ref, grad_x_ref, sums_ref = refs[:4]
    held_ref, grads_ref, turned_ref, sems = refs[-4:]
    core, head = where_ref[0], where_ref[1]
    tokens, width = context_ref.shape
    groups, rows = send_ref.shape[0], send_ref.shape[1]
    pairs = width // LANES
    first = lax.broadcasted_iota(jnp.int32, (1, LANES), 1) < HEAD_DIM

    def fetch(number, slot):
        return pltpu.make_async_copy(probs_ref.at[number], held_ref.at[slot], sems.at[slot])

    for sub in range(2):
        fetch(sub, sub).start()

    @pl.loop(0, pairs)
    def _(pair):
        lanes = [pl.ds(pl.multiple_of(part * width + pair * LANES, LANES), LANES) for part in range(3)]
        q, k, v = [qkv_ref[:, at] for at in lanes]
        grad = grad_ref[:, lanes[0]]
        q_turned, k_turned, grad_turned = q.T, k.T, grad.T
        dot = grad.astype(F32) * context_ref[:, lanes[0]].astype(F32)
        for sub in range(2):
            here = first if sub == 0 else ~first
            lines = slice(sub * HEAD_DIM, (sub + 1) * HEAD_DIM)
            fetch(2 * pair + sub, sub).wait()
            probs = held_ref[sub]
            grad_one = jnp.where(here, grad, jnp.zeros_like(grad))
            inner = jnp.sum(jnp.where(here, dot, 0.0), -1, keepdims=True)
            grad_scores = (probs.astype(F32) * (nt(grad_one, v) - inner)).astype(BF)
            grad_q = nt(k_turned[lines], grad_scores).astype(BF)
            grad_k = nn(q_turned[lines], grad_scores).astype(BF)
            grad_v = nn(grad_turned[lines], probs).astype(BF)
            for part, value in enumerate((grad_q * 0.125, grad_k, grad_v)):
                start = pl.multiple_of(part * width + pair * LANES + sub * HEAD_DIM, HEAD_DIM)
                grads_ref[pl.ds(start, HEAD_DIM)] = value

            @pl.when(pair + 1 < pairs)
            def _():
                fetch(2 * pair + 2 + sub, sub).start()

    grads = grads_ref[...]
    turn_rows(x_ref, turned_ref, rows)
    send_ref[...] = nt(turned_ref[1 - core], grads).astype(BF).reshape(send_ref.shape)
    keep_ref[...] = nt(turned_ref[core], grads).astype(BF).reshape(keep_ref.shape)
    plain = grads.T
    depth = mine_ref.shape[1]
    mine = pl.ds(pl.multiple_of(core * depth, LANES), depth)
    theirs = pl.ds(pl.multiple_of((1 - core) * depth, LANES), depth)
    grad_x_ref[:, mine] = (partial_ref[:, mine] + nn(plain, mine_ref[...])).astype(grad_x_ref.dtype)
    grad_x_ref[:, theirs] = (partial_ref[:, theirs] + nn(plain, theirs_ref[...])).astype(grad_x_ref.dtype)
    sums = total(fold(plain.astype(F32)))
    if last:
        own_at = pl.ds(pl.multiple_of(head * width, LANES), width)
        other_at = pl.ds(pl.multiple_of((1 - head) * width, LANES), width)
        sums_ref[...] = jnp.zeros_like(sums_ref)
        for line, part in ((0, 0), (1, 2)):
            columns = slice(part * width, (part + 1) * width)
            sums_ref[line : line + 1, own_at] = sums_own_ref[0:1, columns]
            sums_ref[line : line + 1, other_at] = sums[:, columns]
        sums_ref[2:5] = sums_one_ref[0:3]
        sums_ref[5:8] = sums_two_ref[0:3]
        for line in range(bias_up_ref.shape[1] // (2 * width)):
            columns = slice(line * 2 * width, (line + 1) * 2 * width)
            sums_ref[8 + line : 9 + line] = bias_up_ref[:, columns]
    else:
        sums_ref[...] = jnp.broadcast_to(sums, sums_ref.shape)


def attend_back(where, x, qkv, probs, context, grad, weights, partial, groups, extra=()):
    tokens, width = context.shape
    depth = x.shape[1]
    rows = depth // (2 * groups)
    last = len(extra) > 0
    return call(
        functools.partial(back_kernel, last),
        [
            ((groups, rows, 3 * width), BF),
            ((groups, rows, 3 * width), BF),
            ((tokens, depth), BF if last else F32),
            ((16, depth) if last else (8, 3 * width), F32),
        ],
        where, x, qkv, Far(probs), context, grad, *weights, partial, *extra,
        scratch=[
            pltpu.VMEM((2, tokens, tokens), BF),
            pltpu.VMEM((3 * width, tokens), BF),
            pltpu.VMEM((2, groups * rows, tokens), BF),
            pltpu.SemaphoreType.DMA((2,)),
        ],
        flops=8 * 10**9,
        moved=10 * 2**20,
    )


def each(count, body):
    if count == 1:
        body(0)
    else:
        pl.loop(0, count)(body)


def open_kernel(cut, split, where_ref, *refs):
    terms, outs = refs[: 4 if split else 2], refs[4 if split else 2 :]
    head_send, head_own, low_own, *low_sends = outs
    low, head = where_ref[2], where_ref[1]
    size = len(low_sends) + 1

    def block(i, bits, half, columns):
        if split:
            return terms[2 * half][i, bits, :, columns] + terms[2 * half + 1][i, bits, :, columns]
        return terms[0][i, bits, half, :, columns] + terms[1][i, bits, half, :, columns]

    def body(i):
        for bits in range(size):
            head_own[i, bits] = block(i, bits, 0 if split else head, slice(0, cut))
            head_send[i, bits] = block(i, bits, 1 if split else 1 - head, slice(0, cut))
        for flip, out in enumerate([low_own, *low_sends]):
            for half in range(2):
                out[i, half] = block(i, low ^ flip, half, slice(cut, None))

    each(head_own.shape[0], body)


def turn_kernel(split, size, where_ref, *refs):
    first, second, outs = refs[:2], refs[2 : 2 + size], refs[2 + size :]
    first_outs, (second_own, second_send) = outs[:size], outs[size:]
    low, head = where_ref[2], where_ref[1]
    own, other = (0, 1) if split else (head, 1 - head)

    def add(values, *at):
        return functools.reduce(jnp.add, [v[at] for v in values])

    def body(i):
        for flip, out in enumerate(first_outs):
            out[i] = add(first, i, low ^ flip)
        second_own[i] = add(second, i, own)
        second_send[i] = add(second, i, other)

    each(second_own.shape[0], body)


def last_kernel(counts, stage, where_ref, *refs):
    parts, at = [], 0
    for count in counts:
        parts.append(refs[at : at + count])
        at += count
    outs = refs[at:]
    index = where_ref[3 + stage]
    size = len(outs)

    def body(i):
        for flip, out in enumerate(outs):
            start = 0
            for part in parts:
                columns = slice(start, start + part[0].shape[2])
                start = columns.stop
                values = [v[i * size + (index ^ flip)].astype(F32) for v in part]
                out[i, :, columns] = functools.reduce(jnp.add, values).astype(BF)

    each(outs[0].shape[0], body)


def close_kernel(scale, *refs):
    refs[-1][...] = functools.reduce(jnp.add, [v[0].astype(F32) for v in refs[:-1]]) * scale


def after(value, *others):
    return lax.optimization_barrier((value, *others))[0]


def pick(value, index, axis):
    return lax.dynamic_index_in_dim(value, index, axis, keepdims=False)


def on_device(
    inputs, cotangent, segment_ids, lengths, w_qkv, bias_query, bias_value, w_out, bias_out, gain_one,
    shift_one, w_up, bias_up, w_down, bias_down, gain_two, shift_two,
):
    width = w_out.shape[0]
    half = w_qkv.shape[2]
    ff = w_up.shape[1]
    tokens = inputs.shape[0]
    batch = lax.axis_size("batch")
    heads = lax.axis_size("head")
    place, head = lax.axis_index("batch"), lax.axis_index("head")
    core = place % 2
    scale = 1.0 / (lengths.shape[0] * batch)

    plan, bit, bits = [], 1, batch.bit_length() - 1
    if (bits - 1) % 2:
        plan.append((1, 2))
        bit = 2
    while bit < bits:
        plan.append((bit, 4))
        bit += 2
    where = jnp.stack([core, head] + [(place >> at) % many for at, many in plan]).astype(jnp.int32)

    def swap_batch(value, flip):
        return lax.ppermute(value, "batch", [(i, i ^ flip) for i in range(batch)])

    def swap_head(value):
        return lax.ppermute(value, "head", [(0, 1), (1, 0)])

    depth = width // 2

    def columns(at):
        part = lax.dynamic_slice_in_dim(w_qkv, at * depth, depth, 0)
        return part.transpose(1, 2, 0).reshape(3 * half, depth)

    own_mine = columns(core)
    w_mine = swap_head(own_mine)
    own_theirs = columns(1 - core)
    small_own = jnp.stack([bias_query, bias_value])
    small_other = swap_head(small_own)
    doc_ids = lax.dynamic_slice_in_dim(segment_ids, head * tokens, tokens, 0)
    length = lax.dynamic_index_in_dim(lengths, head, 0, keepdims=False)
    position = jnp.arange(tokens, dtype=jnp.int32)
    allowed = (doc_ids[:, None] == doc_ids[None, :]) & (position[None, :] < length)
    mask = jnp.where(allowed, 0.0, -1e30).astype(F32)
    params = jnp.stack([bias_out, gain_one, shift_one, bias_down, gain_two, shift_two])

    qkv_own, probs_own, context_own = attend(where, inputs, small_own, mask, own_mine, own_theirs)
    w_mine = after(w_mine, context_own)
    w_theirs = swap_batch(w_mine, 1)
    qkv_other, probs_other, context_other = attend(
        where, inputs, small_other, mask, w_mine, w_theirs
    )

    groups = batch // 2
    ffn_rows, up_rows = ff // batch, width // batch
    out, hidden, n_one, r_one, active, slope, grad_two, sums_two = call(
        ffn_kernel,
        [
            ((tokens, width), BF),
            ((tokens, width), BF),
            ((tokens, width), F32),
            ((tokens, LANES), F32),
            ((tokens, ff), BF),
            ((tokens, ff), BF),
            ((tokens, width), F32),
            ((8, width), F32),
        ],
        where, inputs, context_own, context_other, w_out, params, Far(w_up), bias_up[None], Far(w_down), cotangent,
        scratch=[
            pltpu.VMEM((tokens, CHUNK), F32), pltpu.VMEM((tokens, CHUNK), F32), pltpu.VMEM((tokens, width), F32),
            pltpu.VMEM(w_up.shape, BF), pltpu.VMEM(w_down.shape, BF), pltpu.SemaphoreType.DMA((2, ff // CHUNK)),
        ],
        flops=10 * 10**9, moved=30 * 2**20, limit=28,
    )
    down_send, down_keep = call(
        down_kernel,
        [((groups, ffn_rows, width), BF), ((groups, ffn_rows, width), BF)],
        where, active, grad_two,
        flops=3 * 10**9, moved=10 * 2**20, limit=16,
    )
    low, rest = plan[0], plan[1:]
    size = low[1]
    low_groups = groups // size

    def open_sum(values, cut):
        split = len(values) == 4
        rows = values[0].shape[1] // (1 if split else heads)
        columns = values[0].shape[2]
        lead = (low_groups, size) if split else (low_groups, size, heads)
        values = [v.reshape(*lead, rows, columns) for v in values]
        by_head, by_low = (low_groups, size, rows, cut), (low_groups, heads, rows, columns - cut)
        head_send, head_own, low_own, *low_sends = call(
            functools.partial(open_kernel, cut, split), [(by_head, BF)] * 2 + [(by_low, BF)] * size, where, *values
        )
        got = [swap_batch(v, flip << low[0]) for flip, v in enumerate(low_sends, 1)]
        return head_send, [head_own, swap_head(head_send)], [low_own, *got]

    def turn_sum(first, second, split=False):
        rows = first[0].shape[2]
        cut, more = first[0].shape[3], second[0].shape[3]
        outs = call(
            functools.partial(turn_kernel, split, size),
            [((low_groups, rows, cut), BF)] * size + [((low_groups, rows, more), BF)] * 2,
            where, *first, *second,
        )
        got = [swap_batch(v, flip << low[0]) for flip, v in enumerate(outs[1:size], 1)]
        return outs[0], [outs[0], *got], [outs[size], swap_head(outs[size + 1])]

    def last_sum(*parts):
        for stage, (bit, many) in enumerate(rest):
            rows, columns = parts[0][0].shape[1], sum(part[0].shape[2] for part in parts)
            left = parts[0][0].shape[0] // many
            outs = call(
                functools.partial(last_kernel, [len(part) for part in parts], stage),
                [((left, rows, columns), BF)] * many,
                where, *[v for part in parts for v in part],
            )
            parts = [[outs[0]] + [swap_batch(v, flip << bit) for flip, v in enumerate(outs[1:], 1)]]
        return outs[0], parts[0]

    def close_sum(values):
        return call(functools.partial(close_kernel, scale), [(values[0].shape[1:], F32)], *values)[0]

    def late(values, *before):
        return [values[0]] + [after(v, *before) for v in values[1:]]

    down = [down_keep, swap_batch(down_send, 1)]
    grad_up, sum_bias_up = call(
        slope_kernel,
        [((tokens, ff), BF), ((1, ff), F32)],
        slope, grad_two, Far(w_down),
        scratch=[
            pltpu.VMEM((tokens, width), BF), pltpu.VMEM(w_down.shape, BF), pltpu.SemaphoreType.DMA((ff // CHUNK,)),
        ],
        flops=5 * 10**9, moved=10 * 2**20,
    )
    down[1] = after(down[1], sum_bias_up)
    sent, down, down_low = open_sum(down, width // 2)
    grad_one, grad_own, grad_other, sums_one, up_send, up_keep = call(
        up_kernel,
        [
            ((tokens, width), F32),
            ((tokens, half), BF),
            ((tokens, half), BF),
            ((8, width), F32),
            ((groups, up_rows, ff + width), BF),
            ((groups, up_rows, ff + width), BF),
        ],
        where, hidden, n_one, r_one, after(grad_up, sent), grad_two, Far(w_up), w_out, params, context_own, context_other,
        scratch=[
            pltpu.VMEM((tokens, width), BF),
            pltpu.VMEM((2, groups * up_rows, tokens), BF),
            pltpu.VMEM((tokens, width), F32),
            pltpu.VMEM((tokens, width), BF),
            pltpu.VMEM(w_up.shape, BF),
            pltpu.SemaphoreType.DMA,
        ],
        limit=24,
        flops=11 * 10**9, moved=30 * 2**20,
    )
    up = [up_keep, swap_batch(up_send, 1)]
    sent, down, down_low = turn_sum(late(down, grad_one), down_low)
    q_send, q_keep, partial, sums_own = attend_back(
        where, inputs, qkv_own, probs_own, context_own, after(grad_own, sent), (own_mine, own_theirs), grad_one, groups
    )
    q_got = swap_batch(q_send, 1)
    sent, up, up_low = open_sum(late(up, sums_own), (ff + width) // 2)
    sent, down = last_sum(late(down, sent), down_low)
    p_send, p_keep, input_grad, sums = attend_back(
        where, inputs, qkv_other, probs_other, context_other, after(grad_other, sent), (w_mine, w_theirs), partial,
        groups, (sums_own, sums_one, sums_two, sum_bias_up),
    )
    sum_down = close_sum(late(down, sums))
    sent, up, up_low = turn_sum(late(up, sum_down), up_low)
    p_got = swap_batch(after(p_send, sent), 1)
    sums_got = swap_batch(after(sums, sent), 1)
    cut = 3 * half // 2 // LANES * LANES
    sent, qkv, qkv_low = open_sum([q_keep, after(q_got, sent), p_keep, p_got], cut)
    sums = sums + after(sums_got, sent)
    sums_got = swap_head(sums)
    sent, up = last_sum(late(up, sums), up_low)
    sums = sums + after(sums_got, sent)
    sent, qkv, qkv_low = turn_sum(late(qkv, sums), qkv_low, True)
    for bit, many in plan:
        sums_got = late([sums] + [swap_batch(sums, flip << bit) for flip in range(1, many)], sent)
        sums = functools.reduce(jnp.add, sums_got)
        if bit == low[0]:
            sum_up = close_sum(late(up, sums))
            sent, qkv = last_sum(late(qkv, sum_up), qkv_low)
    sum_qkv = close_sum(late(qkv, sums)).reshape(up_rows, 3, half)
    sums = sums * scale
    device = place * heads + head
    own = width // (batch * heads)
    small = lax.dynamic_slice(sums, (0, device * own), (8, own))
    spread = lax.dynamic_slice_in_dim(sums[8 : 8 + ff // width].reshape(-1), device * ff // (batch * heads), ff // (batch * heads))
    small = [small[i] for i in range(8)]
    return (
        out, input_grad, sum_qkv, small[0], small[1], sum_up[:, ff:], small[4], small[2], small[3],
        sum_up[:, :ff], spread, sum_down, small[7], small[5], small[6],
    )


def solution(mesh):
    rows = P(BOTH, None)
    placed = (rows, rows, P("batch"), P("batch"), P(None, None, "head"), P("head"), P("head")) + (P(),) * 10
    flat = P(BOTH)
    return jax.shard_map(
        on_device,
        mesh=mesh,
        in_specs=placed,
        out_specs=(
            rows, rows, P("batch", None, "head"), flat, flat, rows, flat, flat, flat, rows, flat, rows, flat,
            flat, flat,
        ),
        check_vma=False,
    )
```

```python
import functools

import jax
import jax.numpy as jnp
from jax import lax
from jax.experimental import pallas as pl
from jax.experimental.pallas import tpu as pltpu
from jax.sharding import PartitionSpec as P

HEAD_DIM = 64
LANES = 128
BF = jnp.bfloat16
F32 = jnp.float32
BOTH = ("batch", "head")
VMEM = pl.BlockSpec(memory_space=pltpu.VMEM)
ANY = pl.BlockSpec(memory_space=pltpu.HBM)
SMEM = pl.BlockSpec(memory_space=pltpu.SMEM)


def nn(left, right):
    return lax.dot_general(left, right, (((1,), (0,)), ((), ())), preferred_element_type=F32)


def nt(left, right):
    return lax.dot_general(left, right, (((1,), (1,)), ((), ())), preferred_element_type=F32)


class Near:
    def __init__(self, value):
        self.value = value


class Far:
    def __init__(self, value):
        self.value = value


def call(kernel, outs, *operands, scratch=(), flops=0, moved=0, limit=16):
    specs = [
        ANY if isinstance(a, Far) else VMEM if isinstance(a, Near) or a.dtype != jnp.int32 else SMEM for a in operands
    ]
    operands = [a.value if isinstance(a, (Far, Near)) else a for a in operands]
    return pl.pallas_call(
        kernel,
        in_specs=specs,
        out_specs=[VMEM] * len(outs),
        out_shape=[jax.ShapeDtypeStruct(s, t) for s, t in outs],
        scratch_shapes=list(scratch),
        cost_estimate=pl.CostEstimate(flops=flops, bytes_accessed=moved, transcendentals=0),
        compiler_params=pltpu.CompilerParams(vmem_limit_bytes=limit * 2**20),
    )(*operands)


def tn(left, right):
    return lax.dot_general(left, right, (((0,), (0,)), ((), ())), preferred_element_type=F32)


def head_lines(width, part, number):
    return pl.ds(pl.multiple_of(part * width + number * HEAD_DIM, HEAD_DIM), HEAD_DIM)


def in_turn(count, first_ref, second_ref, begin, finish):
    begin(first_ref, 0)

    @pl.loop(0, count // 2)
    def _(i):
        begin(second_ref, 2 * i + 1)
        finish(first_ref, 2 * i)
        begin(first_ref, jnp.minimum(2 * i + 2, count - 1))
        finish(second_ref, 2 * i + 1)


def attend_kernel(given, where_ref, x_ref, bias_ref, mine_ref, theirs_ref, *refs):
    if given:
        mask_ref, qkv_ref, stats_ref, context_ref, first_ref, second_ref = refs
    else:
        ids_ref, length_ref, mask_ref, qkv_ref, stats_ref, context_ref, first_ref, second_ref = refs
        mine_ids = ids_ref[pl.ds(where_ref[1], 1), :]
        columns = jnp.broadcast_to(mine_ids, (LANES, mine_ids.shape[1])).T
        position = lax.broadcasted_iota(jnp.int32, columns.shape, 0)
        live = position < length_ref[where_ref[1]]
        for at in range(0, mask_ref.shape[1], LANES):
            allowed = (columns == mine_ids[:, at : at + LANES]) & live
            mask_ref[:, at : at + LANES] = jnp.where(allowed, 0.0, -1e30)
    width, tokens = context_ref.shape
    depth = mine_ref.shape[1]
    mine = pl.ds(pl.multiple_of(where_ref[0] * depth, LANES), depth)
    theirs = pl.ds(pl.multiple_of((1 - where_ref[0]) * depth, LANES), depth)
    for part in range(3):
        projected = nn(x_ref[:, mine], mine_ref[part]) + nn(x_ref[:, theirs], theirs_ref[part])
        if part == 0:
            projected = (projected + bias_ref[0:1, :].astype(F32)) * 0.125
        if part == 2:
            projected = projected + bias_ref[1:2, :].astype(F32)
        qkv_ref[part * width : (part + 1) * width, :] = projected.astype(BF).T

    def begin(ref, i):
        ref[...] = tn(qkv_ref[head_lines(width, 1, i), :], qkv_ref[head_lines(width, 0, i), :])

    def finish(ref, i):
        held = []
        for at in range(0, tokens, LANES):
            columns = slice(at, at + LANES)
            scores = ref[:, columns] + mask_ref[:, columns]
            largest = jnp.max(scores, 0, keepdims=True)
            weights = jnp.exp(scores - largest)
            stats_ref[i, 0:1, columns] = largest
            stats_ref[i, 1:2, columns] = 1.0 / jnp.sum(weights, 0, keepdims=True)
            held.append(weights.astype(BF))
        context = nn(qkv_ref[head_lines(width, 2, i), :], jnp.concatenate(held, 1))
        context_ref[head_lines(width, 0, i), :] = (context * stats_ref[i, 1:2, :]).astype(BF)

    in_turn(width // HEAD_DIM, first_ref, second_ref, begin, finish)


def attend(where, x, bias, mine, theirs, *rest):
    tokens, width = x.shape[0], mine.shape[2]
    given = len(rest) == 1
    return call(
        functools.partial(attend_kernel, given),
        ([] if given else [((tokens, tokens), F32)])
        + [((3 * width, tokens), BF), ((width // HEAD_DIM, 8, tokens), F32), ((width, tokens), BF)],
        where, x, bias, mine, theirs, *(rest if given else [Near(rest[0]), rest[1]]),
        scratch=[pltpu.VMEM((tokens, tokens), F32), pltpu.VMEM((tokens, tokens), F32)],
        flops=10**11,
        moved=8 * 2**20,
        limit=8,
    )


def normed(summed):
    centre = summed - jnp.mean(summed, -1, keepdims=True)
    scale_inv = lax.rsqrt(jnp.mean(centre * centre, -1, keepdims=True) + 1e-05)
    return centre * scale_inv, scale_inv


def norm_back(grad, n, scale_inv, gain):
    scaled = grad * gain
    first = jnp.mean(scaled, -1, keepdims=True)
    second = jnp.mean(scaled * n, -1, keepdims=True)
    return scale_inv * (scaled - first - n * second)


def turn_rows(lines, turned_ref, rows):
    tokens = lines.shape[1]
    blocks = lines.reshape(-1, 2, rows, tokens)
    turned_ref[0] = blocks[:, 0].reshape(-1, tokens)
    turned_ref[1] = blocks[:, 1].reshape(-1, tokens)


BIAS_OUT, GAIN_ONE, SHIFT_ONE, BIAS_DOWN, GAIN_TWO, SHIFT_TWO = range(6)


CHUNK = 512
LINES = 16


def blocks(count):
    return [slice(at, at + LINES) for at in range(0, count, LINES)]


def fold(value):
    return jnp.sum(value.reshape(-1, 8, value.shape[-1]), 0)


def total(folded):
    return jnp.sum(folded, 0, keepdims=True)


def ffn_kernel(
    where_ref, x_ref, own_ref, other_ref, w_out_ref, params_ref, w_up_ref, bias_up_ref, w_down_ref,
    cot_ref,
    out_ref, hidden_ref, n_one_ref, r_one_ref, active_ref, slope_ref, grad_two_ref, sums_ref,
    first_ref, second_ref, branch_ref, up_ref, down_ref, sems,
):
    half = own_ref.shape[0]
    tokens, width = x_ref.shape
    head = where_ref[1]
    count = w_up_ref.shape[1] // CHUNK
    span = lambda i: pl.ds(pl.multiple_of(i * CHUNK, CHUNK), CHUNK)

    def fetch_up(i):
        return pltpu.make_async_copy(w_up_ref.at[:, span(i)], up_ref.at[:, span(i)], sems.at[0, i])

    def fetch_down(i):
        return pltpu.make_async_copy(w_down_ref.at[span(i), :], down_ref.at[span(i), :], sems.at[1, i])

    for i in range(count):
        fetch_up(i).start()
        fetch_down(i).start()
    params = params_ref[...].astype(F32)
    row = lambda i: params[i : i + 1]
    own_at = pl.multiple_of(head * half, LANES)
    other_at = pl.multiple_of((1 - head) * half, LANES)
    branch_ref[...] = tn(own_ref[...], w_out_ref[pl.ds(own_at, half), :]) + tn(
        other_ref[...], w_out_ref[pl.ds(other_at, half), :]
    )

    for at in blocks(tokens):
        n, r = normed(x_ref[at, :].astype(F32) + branch_ref[at, :] + row(BIAS_OUT))
        n_one_ref[at, :] = n
        r_one_ref[at, :] = jnp.broadcast_to(r, (LINES, LANES))
        hidden_ref[at, :] = (n * row(GAIN_ONE) + row(SHIFT_ONE)).astype(BF)

    def upward(ref, at):
        ref[...] = nn(hidden_ref[...], up_ref[:, at])

    def gelu(ref, at):
        bias = bias_up_ref[:, at].astype(F32)
        for start in range(0, tokens, LINES):
            lines = slice(start, start + LINES)
            v = ref[lines, :] + bias
            phi = 0.5 + 0.5 * lax.erf(v * 0.7071067811865476)
            active_ref[lines, at] = (v * phi).astype(BF)
            density = jnp.exp(-0.5 * v * v) * 0.3989422804014327
            slope_ref[lines, at] = (phi + v * density).astype(BF)

    def downward(at):
        branch_ref[...] += nn(active_ref[:, at], down_ref[at, :])

    branch_ref[...] = jnp.zeros_like(branch_ref)
    fetch_up(0).wait()
    upward(first_ref, span(0))

    @pl.loop(0, count // 2)
    def _(i):
        fetch_up(2 * i + 1).wait()
        fetch_down(2 * i).wait()
        fetch_down(2 * i + 1).wait()

        @pl.when(2 * i + 2 < count)
        def _():
            fetch_up(2 * i + 2).wait()

        upward(second_ref, span(2 * i + 1))
        gelu(first_ref, span(2 * i))
        downward(span(2 * i))
        upward(first_ref, span(jnp.minimum(2 * i + 2, count - 1)))
        gelu(second_ref, span(2 * i + 1))
        downward(span(2 * i + 1))

    sums = [0.0, 0.0, 0.0]
    for at in blocks(tokens):
        n, r = normed(hidden_ref[at, :].astype(F32) + branch_ref[at, :] + row(BIAS_DOWN))
        out_ref[at, :] = (n * row(GAIN_TWO) + row(SHIFT_TWO)).astype(BF)
        cot = cot_ref[at, :].astype(F32)
        grad = norm_back(cot, n, r, row(GAIN_TWO))
        grad_two_ref[at, :] = grad
        terms = (cot * n, cot, grad.astype(BF).astype(F32))
        sums = [earlier + fold(term) for earlier, term in zip(sums, terms)]
    for i, folded in enumerate(sums):
        sums_ref[i : i + 1] = total(folded)


def down_kernel(where_ref, active_ref, grad_two_ref, send_ref, keep_ref):
    core = where_ref[0]
    groups, rows = send_ref.shape[0], send_ref.shape[1]
    grad_branch = grad_two_ref[...].astype(BF)
    for i in range(groups):
        block = nn(active_ref[:, i * 2 * rows : (i + 1) * 2 * rows].T, grad_branch).astype(BF)
        low, high = block[:rows], block[rows:]
        keep_ref[i] = jnp.where(core == 0, low, high)
        send_ref[i] = jnp.where(core == 0, high, low)


def slope_kernel(
    slope_ref, grad_two_ref, w_down_ref, grad_up_ref, bias_up_ref, branch_ref, down_ref, sems
):
    count = w_down_ref.shape[0] // CHUNK
    span = lambda i: pl.ds(pl.multiple_of(i * CHUNK, CHUNK), CHUNK)

    def fetch(i):
        return pltpu.make_async_copy(w_down_ref.at[span(i), :], down_ref.at[span(i), :], sems.at[i])

    for i in range(count):
        fetch(i).start()
    branch_ref[...] = grad_two_ref[...].astype(BF)

    @pl.loop(0, count)
    def _(i):
        fetch(i).wait()
        grad_active = nt(branch_ref[...], down_ref[span(i), :])
        grad_up = (grad_active * slope_ref[:, span(i)].astype(F32)).astype(BF)
        grad_up_ref[:, span(i)] = grad_up
        bias_up_ref[:, span(i)] = jnp.sum(grad_up.astype(F32), 0, keepdims=True)


def up_kernel(
    where_ref, hidden_ref, n_one_ref, r_one_ref, grad_up_ref, grad_two_ref, w_up_ref, w_out_ref, params_ref,
    own_ref, other_ref,
    grad_one_ref, grad_own_ref, grad_other_ref, sums_ref, send_ref, keep_ref,
    both_ref, turned_ref, grad_hidden_ref, grad_context_ref, up_ref, sem,
):
    half = grad_own_ref.shape[0]
    head, core = where_ref[1], where_ref[0]
    params = params_ref[...].astype(F32)
    row = lambda i: params[i : i + 1]
    groups, rows = send_ref.shape[0], send_ref.shape[1]
    tokens = hidden_ref.shape[0]
    fetch = pltpu.make_async_copy(w_up_ref, up_ref, sem)
    fetch.start()
    turn_rows(hidden_ref[...].T, turned_ref, rows)

    @pl.loop(0, w_up_ref.shape[1] // CHUNK)
    def _(i):
        at = pl.ds(pl.multiple_of(i * CHUNK, CHUNK), CHUNK)
        grad_up = grad_up_ref[:, at]
        send_ref[:, :, at] = nn(turned_ref[1 - core], grad_up).astype(BF).reshape(groups, rows, CHUNK)
        keep_ref[:, :, at] = nn(turned_ref[core], grad_up).astype(BF).reshape(groups, rows, CHUNK)

    fetch.wait()
    grad_hidden_ref[...] = nt(grad_up_ref[...], up_ref[...])
    sums = [0.0, 0.0, 0.0]
    for at in blocks(tokens):
        grad_hidden = grad_hidden_ref[at, :] + grad_two_ref[at, :]
        n_one = n_one_ref[at, :]
        grad_one = norm_back(grad_hidden, n_one, r_one_ref[at, :1], row(GAIN_ONE))
        grad_one_ref[at, :] = grad_one
        terms = (grad_hidden * n_one, grad_hidden, grad_one.astype(BF).astype(F32))
        sums = [earlier + fold(term) for earlier, term in zip(sums, terms)]
    for i, folded in enumerate(sums):
        sums_ref[i : i + 1] = total(folded)
    grad_attended = grad_one_ref[...].astype(BF)
    grad_context_ref[...] = nt(w_out_ref[...], grad_attended).astype(BF)
    own_at = pl.multiple_of(head * half, LANES)
    other_at = pl.multiple_of((1 - head) * half, LANES)
    both_ref[pl.ds(own_at, half), :] = own_ref[...]
    both_ref[pl.ds(other_at, half), :] = other_ref[...]
    turn_rows(both_ref[...], turned_ref, rows)
    ff = w_up_ref.shape[1]
    send_ref[:, :, ff:] = nn(turned_ref[1 - core], grad_attended).astype(BF).reshape(groups, rows, -1)
    keep_ref[:, :, ff:] = nn(turned_ref[core], grad_attended).astype(BF).reshape(groups, rows, -1)
    grad_own_ref[...] = grad_context_ref[pl.ds(own_at, half), :]
    grad_other_ref[...] = grad_context_ref[pl.ds(other_at, half), :]


def back_kernel(
    before, last, where_ref, x_ref, mask_ref, qkv_own_ref, qkv_other_ref, stats_own_ref, stats_other_ref,
    context_own_ref, context_other_ref, grad_own_ref, grad_other_ref, mine_own_ref, mine_other_ref, theirs_own_ref,
    theirs_other_ref, partial_ref, *refs
):
    if last:
        sums_before_ref, sums_one_ref, sums_two_ref, bias_up_ref, *refs = refs
        send_ref, keep_ref, grad_x_ref, ext_send_ref, ext_keep_ref = refs[:5]
        first_ref, second_ref, grads_ref, turned_ref, table_ref, ext_ref = refs[5:]
    else:
        send_ref, keep_ref, grad_x_ref, sums_ref, first_ref, second_ref, grads_ref, turned_ref = refs
    core, head = where_ref[0], where_ref[1]
    width, tokens = context_own_ref.shape
    groups, rows, columns = send_ref.shape[1:]
    wide = columns // 3
    count = wide // HEAD_DIM
    halves = (
        (qkv_own_ref, stats_own_ref, context_own_ref, grad_own_ref),
        (qkv_other_ref, stats_other_ref, context_other_ref, grad_other_ref),
    )

    def scaled(half, i):
        return (halves[half][3][head_lines(width, 0, i), :].astype(F32) * halves[half][1][i, 1:2, :]).astype(BF)

    def begin(ref, half, i):
        q, k, v = [halves[half][0][head_lines(width, part, i), :] for part in range(3)]
        ref[0] = tn(k, q)
        ref[1] = tn(v, scaled(half, i))

    def finish(ref, half, i, to):
        q, k, v = [halves[half][0][head_lines(width, part, i), :] for part in range(3)]
        grad = scaled(half, i)
        context = halves[half][2][head_lines(width, 0, i), :]
        inner = jnp.sum(grad.astype(F32) * context.astype(F32), 0, keepdims=True)
        held, moved = [], []
        for at in range(0, tokens, LANES):
            span = slice(at, at + LANES)
            weights = jnp.exp(ref[0, :, span] + mask_ref[:, span] - halves[half][1][i, 0:1, span])
            held.append(weights.astype(BF))
            moved.append((weights * (ref[1, :, span] - inner[:, span])).astype(BF))
        weights, grad_scores = jnp.concatenate(held, 1), jnp.concatenate(moved, 1)
        grads_ref[half, head_lines(wide, 0, to), :] = nn(k, grad_scores).astype(BF) * 0.125
        grads_ref[half, head_lines(wide, 1, to), :] = nt(q, grad_scores).astype(BF)
        grads_ref[half, head_lines(wide, 2, to), :] = nt(grad, weights).astype(BF)

    begin(first_ref, 0, before)

    @pl.loop(0, count)
    def _(i):
        begin(second_ref, 1, before + i)
        finish(first_ref, 0, before + i, i)
        begin(first_ref, 0, before + jnp.minimum(i + 1, count - 1))
        finish(second_ref, 1, before + i, i)

    turn_rows(x_ref[...].T, turned_ref, rows)
    for half in range(2):
        for out_ref, lines in ((send_ref, 1 - core), (keep_ref, core)):
            out_ref[half] = nt(turned_ref[lines], grads_ref[half]).astype(BF).reshape(groups, rows, columns)
    plain = [grads_ref[half].T for half in range(2)]
    depth = mine_own_ref.shape[1]
    start = before * HEAD_DIM
    for at, weights_refs in ((core, (mine_own_ref, mine_other_ref)), (1 - core, (theirs_own_ref, theirs_other_ref))):
        lanes = pl.ds(pl.multiple_of(at * depth, LANES), depth)
        terms = [
            nt(plain[half][:, part * wide : (part + 1) * wide], weights_refs[half][part, :, start : start + wide])
            for half in range(2)
            for part in range(3)
        ]
        grad_x_ref[:, lanes] = (partial_ref[:, lanes] + sum(terms)).astype(grad_x_ref.dtype)
    sums = [total(fold(value.astype(F32))) for value in plain]
    if not last:
        for half in range(2):
            sums_ref[half] = jnp.broadcast_to(sums[half], sums_ref.shape[1:])
        return
    table_ref[...] = jnp.zeros_like(table_ref)
    for line, part in ((0, 0), (1, 2)):
        for half, at in ((0, head), (1, 1 - head)):
            here = at * width
            span = slice(part * start, (part + 1) * start)
            table_ref[line : line + 1, pl.ds(pl.multiple_of(here, LANES), start)] = sums_before_ref[half, 0:1, span]
            span = slice(part * wide, (part + 1) * wide)
            table_ref[line : line + 1, pl.ds(pl.multiple_of(here + start, LANES), wide)] = sums[half][:, span]
    table_ref[2:5] = sums_one_ref[0:3]
    table_ref[5:8] = sums_two_ref[0:3]
    own = rows // 2
    table = table_ref[...].T.reshape(groups, 2, 2, own, LANES)
    ff = bias_up_ref.shape[1]
    spread = jnp.broadcast_to(bias_up_ref[...], (LANES, ff)).T.reshape(groups, 2, 2, ff // (4 * groups * rows), rows, LANES)
    lane = lax.broadcasted_iota(jnp.int32, (groups, rows, LANES), 2)
    for to_core in range(2):
        for to_head in range(2):
            block = jnp.concatenate([table[:, to_core, to_head], jnp.zeros((groups, rows - own, LANES), F32)], 1)
            for piece in range(spread.shape[3]):
                block = jnp.where(lane == 8 + piece, spread[:, to_core, to_head, piece], block)
            ext_ref[to_core, to_head] = block.astype(BF)
    for half, at in ((0, head), (1, 1 - head)):
        ext_send_ref[half] = ext_ref[1 - core, at]
        ext_keep_ref[half] = ext_ref[core, at]


def attend_back(where, x, mask, own, other, grads, weights, partial, groups, before, count, extra=()):
    width, tokens = own[2].shape
    depth = x.shape[1]
    rows = depth // (2 * groups)
    wide = count * HEAD_DIM
    last = len(extra) > 0
    kept = [v for pair in zip(own, other) for v in pair]
    block = ((2, groups, rows, 3 * wide), BF)
    outs = [block, block, ((tokens, depth), BF if last else F32)]
    outs += [((2, groups, rows, LANES), BF)] * 2 if last else [((2, 8, 3 * wide), F32)]
    scratch = [
        pltpu.VMEM((2, tokens, tokens), F32),
        pltpu.VMEM((2, tokens, tokens), F32),
        pltpu.VMEM((2, 3 * wide, tokens), BF),
        pltpu.VMEM((2, groups * rows, tokens), BF),
    ]
    if last:
        scratch += [pltpu.VMEM((LANES, depth), F32), pltpu.VMEM((2, 2, groups, rows, LANES), BF)]
    return call(
        functools.partial(back_kernel, before, last),
        outs,
        where, x, mask, *kept, *grads, *weights, partial, *extra,
        scratch=scratch,
        flops=2 * 10**11,
        moved=10 * 2**20,
        limit=16,
    )


def each(count, body):
    if count == 1:
        body(0)
    else:
        pl.loop(0, count)(body)


def open_kernel(cut, split, where_ref, *refs):
    count = split or 2
    terms, outs = refs[:count], refs[count:]
    head_send, head_own, low_own, *low_sends = outs
    low, head = where_ref[2], where_ref[1]
    size = len(low_sends) + 1

    def block(i, bits, half, columns):
        if split:
            return terms[0][half, i, bits, :, columns] + terms[1][half, i, bits, :, columns]
        return terms[0][i, bits, half, :, columns] + terms[1][i, bits, half, :, columns]

    def body(i):
        for bits in range(size):
            head_own[i, bits] = block(i, bits, 0 if split else head, slice(0, cut))
            head_send[i, bits] = block(i, bits, 1 if split else 1 - head, slice(0, cut))
        for flip, out in enumerate([low_own, *low_sends]):
            for half in range(2):
                if split != 4:
                    out[i, half] = block(i, low ^ flip, half, slice(cut, None))
                    continue
                wide = terms[0].shape[4] - cut
                out[i, half, :, :wide] = block(i, low ^ flip, half, slice(cut, None))
                out[i, half, :, wide:] = terms[2][half, i, low ^ flip] + terms[3][half, i, low ^ flip]

    each(head_own.shape[0], body)


def turn_kernel(split, size, where_ref, *refs):
    first, second, outs = refs[:2], refs[2 : 2 + size], refs[2 + size :]
    first_outs, (second_own, second_send) = outs[:size], outs[size:]
    low, head = where_ref[2], where_ref[1]
    own, other = (0, 1) if split else (head, 1 - head)

    def add(values, *at):
        return functools.reduce(jnp.add, [v[at] for v in values])

    def body(i):
        for flip, out in enumerate(first_outs):
            out[i] = add(first, i, low ^ flip)
        second_own[i] = add(second, i, own)
        second_send[i] = add(second, i, other)

    each(second_own.shape[0], body)


def last_kernel(counts, stage, where_ref, *refs):
    parts, at = [], 0
    for count in counts:
        parts.append(refs[at : at + count])
        at += count
    outs = refs[at:]
    index = where_ref[3 + stage]
    size = len(outs)

    def body(i):
        for flip, out in enumerate(outs):
            start = 0
            for part in parts:
                columns = slice(start, start + part[0].shape[2])
                start = columns.stop
                values = [v[i * size + (index ^ flip)].astype(F32) for v in part]
                out[i, :, columns] = functools.reduce(jnp.add, values).astype(BF)

    each(outs[0].shape[0], body)


def close_kernel(scale, *refs):
    refs[-1][...] = functools.reduce(jnp.add, [v[0].astype(F32) for v in refs[:-1]]) * scale


def pause_kernel(token_ref, out_ref):
    out_ref[...] = token_ref[...]


def pause(*others):
    token = after(jnp.zeros((8, LANES), F32), *others)
    return call(pause_kernel, [((8, LANES), F32)], token, flops=10**13, limit=2)[0]


def after(value, *others):
    return lax.optimization_barrier((value, *others))[0]


def pick(value, index, axis):
    return lax.dynamic_index_in_dim(value, index, axis, keepdims=False)


def on_device(
    inputs, cotangent, segment_ids, lengths, w_qkv, bias_query, bias_value, w_out, bias_out, gain_one,
    shift_one, w_up, bias_up, w_down, bias_down, gain_two, shift_two,
):
    width = w_out.shape[0]
    half = w_qkv.shape[2]
    ff = w_up.shape[1]
    tokens = inputs.shape[0]
    batch = lax.axis_size("batch")
    heads = lax.axis_size("head")
    place, head = lax.axis_index("batch"), lax.axis_index("head")
    core = place % 2
    scale = 1.0 / (lengths.shape[0] * batch)

    plan, bit, bits = [], 1, batch.bit_length() - 1
    if (bits - 1) % 2:
        plan.append((1, 2))
        bit = 2
    while bit < bits:
        plan.append((bit, 4))
        bit += 2
    where = jnp.stack([core, head] + [(place >> at) % many for at, many in plan]).astype(jnp.int32)

    def swap_batch(value, flip):
        return lax.ppermute(value, "batch", [(i, i ^ flip) for i in range(batch)])

    def swap_head(value):
        return lax.ppermute(value, "head", [(0, 1), (1, 0)])

    depth = width // 2

    def columns(at):
        part = lax.dynamic_slice_in_dim(w_qkv, at * depth, depth, 0)
        return part.transpose(1, 0, 2)

    own_mine = columns(core)
    w_mine = swap_head(own_mine)
    small_own = jnp.stack([bias_query, bias_value])
    small_other = swap_head(after(small_own, own_mine))
    params = jnp.stack([bias_out, gain_one, shift_one, bias_down, gain_two, shift_two])
    ids = segment_ids.reshape(heads, tokens)
    bias_up = bias_up[None]
    prepared = (inputs, where, columns(1 - core), small_own, params, ids, bias_up)
    inputs, where, own_theirs, small_own, params, ids, bias_up = lax.optimization_barrier(prepared)

    mask, *kept_own = attend(where, inputs, small_own, own_mine, own_theirs, ids, lengths)
    context_own = kept_own[2]
    w_mine = after(w_mine, context_own, small_other)
    w_theirs = swap_batch(w_mine, 1)
    kept_other = attend(where, inputs, small_other, w_mine, w_theirs, mask)
    context_other = kept_other[2]

    groups = batch // 2
    ffn_rows, up_rows = ff // batch, width // batch
    out, hidden, n_one, r_one, active, slope, grad_two, sums_two = call(
        ffn_kernel,
        [
            ((tokens, width), BF),
            ((tokens, width), BF),
            ((tokens, width), F32),
            ((tokens, LANES), F32),
            ((tokens, ff), BF),
            ((tokens, ff), BF),
            ((tokens, width), F32),
            ((8, width), F32),
        ],
        where, inputs, context_own, context_other, w_out, params, Far(w_up), bias_up, Far(w_down), cotangent,
        scratch=[
            pltpu.VMEM((tokens, CHUNK), F32), pltpu.VMEM((tokens, CHUNK), F32), pltpu.VMEM((tokens, width), F32),
            pltpu.VMEM(w_up.shape, BF), pltpu.VMEM(w_down.shape, BF), pltpu.SemaphoreType.DMA((2, ff // CHUNK)),
        ],
        flops=2 * 10**11, moved=30 * 2**20, limit=22,
    )
    down_send, down_keep = call(
        down_kernel,
        [((groups, ffn_rows, width), BF), ((groups, ffn_rows, width), BF)],
        where, active, grad_two,
        flops=6 * 10**10, moved=10 * 2**20, limit=12,
    )
    low, rest = plan[0], plan[1:]
    size = low[1]
    low_groups = groups // size

    def open_sum(values, cut, split=False, weigh=0):
        rows, columns = values[0].shape[-2] // (1 if split else heads), values[0].shape[-1]
        lead = (heads, low_groups, size) if split else (low_groups, size, heads)
        more = sum(v.shape[-1] for v in values[2::2])
        values = [v.reshape(*lead, rows, v.shape[-1]) for v in values]
        columns += more
        by_head, by_low = (low_groups, size, rows, cut), (low_groups, heads, rows, columns - cut)
        head_send, head_own, low_own, *low_sends = call(
            functools.partial(open_kernel, cut, len(values) if split else 0), [(by_head, BF)] * 2 + [(by_low, BF)] * size, where, *values,
            flops=weigh,
        )
        got = [swap_batch(v, flip << low[0]) for flip, v in enumerate(low_sends, 1)]
        return head_send, [head_own, swap_head(head_send)], [low_own, *got]

    def turn_sum(first, second, split=False, weigh=0):
        rows = first[0].shape[2]
        cut, more = first[0].shape[3], second[0].shape[3]
        outs = call(
            functools.partial(turn_kernel, split, size),
            [((low_groups, rows, cut), BF)] * size + [((low_groups, rows, more), BF)] * 2,
            where, *first, *second,
            flops=weigh,
        )
        got = [swap_batch(v, flip << low[0]) for flip, v in enumerate(outs[1:size], 1)]
        return outs[0], [outs[0], *got], [outs[size], swap_head(outs[size + 1])]

    def last_sum(*parts, weigh=0):
        for stage, (bit, many) in enumerate(rest):
            rows, columns = parts[0][0].shape[1], sum(part[0].shape[2] for part in parts)
            left = parts[0][0].shape[0] // many
            outs = call(
                functools.partial(last_kernel, [len(part) for part in parts], stage),
                [((left, rows, columns), BF)] * many,
                where, *[v for part in parts for v in part],
                flops=weigh,
            )
            parts = [[outs[0]] + [swap_batch(v, flip << bit) for flip, v in enumerate(outs[1:], 1)]]
        return outs[0], parts[0]

    def close_sum(values, weigh=0):
        return call(functools.partial(close_kernel, scale), [(values[0].shape[1:], F32)], *values, flops=weigh)[0]

    def late(values, *before):
        return [values[0]] + [after(v, *before) for v in values[1:]]

    down = [down_keep, swap_batch(down_send, 1)]
    grad_up, sum_bias_up = call(
        slope_kernel,
        [((tokens, ff), BF), ((1, ff), F32)],
        slope, grad_two, Far(w_down),
        scratch=[
            pltpu.VMEM((tokens, width), BF), pltpu.VMEM(w_down.shape, BF), pltpu.SemaphoreType.DMA((ff // CHUNK,)),
        ],
        flops=10**11, moved=10 * 2**20, limit=14,
    )
    down[1] = after(down[1], sum_bias_up)
    sent, down, down_low = open_sum(down, width // 2)
    grad_one, grad_own, grad_other, sums_one, up_send, up_keep = call(
        up_kernel,
        [
            ((tokens, width), F32),
            ((half, tokens), BF),
            ((half, tokens), BF),
            ((8, width), F32),
            ((groups, up_rows, ff + width), BF),
            ((groups, up_rows, ff + width), BF),
        ],
        where, hidden, n_one, r_one, after(grad_up, sent), grad_two, Far(w_up), w_out, params, context_own, context_other,
        scratch=[
            pltpu.VMEM((width, tokens), BF),
            pltpu.VMEM((2, groups * up_rows, tokens), BF),
            pltpu.VMEM((tokens, width), F32),
            pltpu.VMEM((width, tokens), BF),
            pltpu.VMEM(w_up.shape, BF),
            pltpu.SemaphoreType.DMA,
        ],
        limit=18,
        flops=2 * 10**11, moved=30 * 2**20,
    )
    up = [up_keep, swap_batch(up_send, 1)]
    sent, down, down_low = turn_sum(late(down, grad_one), down_low, weigh=10**12)
    sent, up, up_low = open_sum(late(up, sent), (ff + width) // 2)
    end = half // HEAD_DIM - 2
    weights = (own_mine, w_mine, own_theirs, w_theirs)
    qa_send, qa_keep, partial, sums = attend_back(
        where, inputs, mask, kept_own, kept_other, (after(grad_own, sent), grad_other), weights, grad_one, groups, 0, end
    )
    qa_got = swap_batch(qa_send, 1)
    sent, down = last_sum(late(down, sums), down_low)
    sent, up, up_low = turn_sum(late(up, sent), up_low)
    qb_send, qb_keep, input_grad, ext_send, ext_keep = attend_back(
        where, inputs, mask, kept_own, kept_other, (after(grad_own, sent), grad_other), weights, partial, groups, end, 2,
        (sums, sums_one, sums_two, sum_bias_up),
    )
    qb_got, ext_got = swap_batch(qb_send, 1), swap_batch(ext_send, 1)
    sum_down = close_sum(late(down, input_grad))
    cut_a, cut_b = 3 * end * HEAD_DIM // 2, 2 * LANES
    sent, qa, qa_low = open_sum([qa_keep, after(qa_got, sum_down)], cut_a, True)
    sent, up = last_sum(late(up, sent), up_low, weigh=10**12)
    sent, qb, qb_low = open_sum([qb_keep, after(qb_got, sent), ext_keep, after(ext_got, sent)], cut_b, True)
    sent, qa, qa_low = turn_sum(late(qa, sent), qa_low, True, weigh=10**12)
    sent, qb, qb_low = turn_sum(late(qb, sent), qb_low, True)
    sum_up = close_sum(late(up, sent), weigh=10**12)
    sent, qkv = last_sum(late(qa, sum_up), qa_low, qb, qb_low)
    sum_qkv = close_sum(qkv)
    wide_a, wide_b = end * HEAD_DIM, 2 * HEAD_DIM
    small = sum_qkv[:, 3 * half :]
    sum_qkv = jnp.concatenate(
        [sum_qkv[:, : 3 * wide_a].reshape(up_rows, 3, wide_a), sum_qkv[:, 3 * wide_a : 3 * half].reshape(up_rows, 3, wide_b)],
        2,
    )
    own = up_rows // heads
    pieces = ff // (width * heads)
    spread = small[:, 8 : 8 + pieces].T.reshape(-1)
    small = [small[:own, i] for i in range(8)]
    return (
        out, input_grad, sum_qkv, small[0], small[1], sum_up[:, ff:], small[4], small[2], small[3],
        sum_up[:, :ff], spread, sum_down, small[7], small[5], small[6],
    )


def solution(mesh):
    rows = P(BOTH, None)
    placed = (rows, rows, P("batch"), P("batch"), P(None, None, "head"), P("head"), P("head")) + (P(),) * 10
    flat = P(BOTH)
    return jax.shard_map(
        on_device,
        mesh=mesh,
        in_specs=placed,
        out_specs=(
            rows, rows, P("batch", None, "head"), flat, flat, rows, flat, flat, flat, rows, flat, rows, flat,
            flat, flat,
        ),
        check_vma=False,
    )
```

```python
import functools

import jax
import jax.numpy as jnp
from jax import lax
from jax.experimental import pallas as pl
from jax.experimental.pallas import tpu as pltpu
from jax.sharding import PartitionSpec as P

HEAD_DIM = 64
LANES = 128
BF = jnp.bfloat16
F32 = jnp.float32
BOTH = ("batch", "head")
VMEM = pl.BlockSpec(memory_space=pltpu.VMEM)
ANY = pl.BlockSpec(memory_space=pltpu.HBM)
SMEM = pl.BlockSpec(memory_space=pltpu.SMEM)


def nn(left, right):
    return lax.dot_general(left, right, (((1,), (0,)), ((), ())), preferred_element_type=F32)


def nt(left, right):
    return lax.dot_general(left, right, (((1,), (1,)), ((), ())), preferred_element_type=F32)


class Near:
    def __init__(self, value):
        self.value = value


class Far:
    def __init__(self, value):
        self.value = value


def call(kernel, outs, *operands, scratch=(), flops=0, moved=0, limit=16):
    specs = [
        ANY if isinstance(a, Far) else VMEM if isinstance(a, Near) or a.dtype != jnp.int32 else SMEM for a in operands
    ]
    operands = [a.value if isinstance(a, (Far, Near)) else a for a in operands]
    return pl.pallas_call(
        kernel,
        in_specs=specs,
        out_specs=[VMEM] * len(outs),
        out_shape=[jax.ShapeDtypeStruct(s, t) for s, t in outs],
        scratch_shapes=list(scratch),
        cost_estimate=pl.CostEstimate(flops=flops, bytes_accessed=moved, transcendentals=0),
        compiler_params=pltpu.CompilerParams(vmem_limit_bytes=limit * 2**20),
    )(*operands)


def tn(left, right):
    return lax.dot_general(left, right, (((0,), (0,)), ((), ())), preferred_element_type=F32)


def head_lines(width, part, number):
    return pl.ds(pl.multiple_of(part * width + number * HEAD_DIM, HEAD_DIM), HEAD_DIM)


def in_turn(count, first_ref, second_ref, begin, finish):
    begin(first_ref, 0)

    @pl.loop(0, count // 2)
    def _(i):
        begin(second_ref, 2 * i + 1)
        finish(first_ref, 2 * i)
        begin(first_ref, jnp.minimum(2 * i + 2, count - 1))
        finish(second_ref, 2 * i + 1)


def attend_kernel(given, where_ref, x_ref, bias_ref, mine_ref, theirs_ref, *refs):
    if given:
        mask_ref, qkv_ref, stats_ref, context_ref, first_ref, second_ref = refs
    else:
        ids_ref, length_ref, mask_ref, qkv_ref, stats_ref, context_ref, first_ref, second_ref = refs
        mine_ids = ids_ref[pl.ds(where_ref[1], 1), :]
        columns = jnp.broadcast_to(mine_ids, (LANES, mine_ids.shape[1])).T
        position = lax.broadcasted_iota(jnp.int32, columns.shape, 0)
        live = position < length_ref[where_ref[1]]
        for at in range(0, mask_ref.shape[1], LANES):
            allowed = (columns == mine_ids[:, at : at + LANES]) & live
            mask_ref[:, at : at + LANES] = jnp.where(allowed, 0.0, -1e30)
    width, tokens = context_ref.shape
    depth = mine_ref.shape[1]
    mine = pl.ds(pl.multiple_of(where_ref[0] * depth, LANES), depth)
    theirs = pl.ds(pl.multiple_of((1 - where_ref[0]) * depth, LANES), depth)
    for part in range(3):
        projected = nn(x_ref[:, mine], mine_ref[part]) + nn(x_ref[:, theirs], theirs_ref[part])
        if part == 0:
            projected = (projected + bias_ref[0:1, :].astype(F32)) * 0.125
        if part == 2:
            projected = projected + bias_ref[1:2, :].astype(F32)
        qkv_ref[part * width : (part + 1) * width, :] = projected.astype(BF).T

    def begin(ref, i):
        ref[...] = tn(qkv_ref[head_lines(width, 1, i), :], qkv_ref[head_lines(width, 0, i), :])

    def finish(ref, i):
        held = []
        for at in range(0, tokens, LANES):
            columns = slice(at, at + LANES)
            scores = ref[:, columns] + mask_ref[:, columns]
            largest = jnp.max(scores, 0, keepdims=True)
            weights = jnp.exp(scores - largest)
            stats_ref[i, 0:1, columns] = largest
            stats_ref[i, 1:2, columns] = 1.0 / jnp.sum(weights, 0, keepdims=True)
            held.append(weights.astype(BF))
        context = nn(qkv_ref[head_lines(width, 2, i), :], jnp.concatenate(held, 1))
        context_ref[head_lines(width, 0, i), :] = (context * stats_ref[i, 1:2, :]).astype(BF)

    in_turn(width // HEAD_DIM, first_ref, second_ref, begin, finish)


def attend(where, x, bias, mine, theirs, *rest):
    tokens, width = x.shape[0], mine.shape[2]
    given = len(rest) == 1
    return call(
        functools.partial(attend_kernel, given),
        ([] if given else [((tokens, tokens), F32)])
        + [((3 * width, tokens), BF), ((width // HEAD_DIM, 8, tokens), F32), ((width, tokens), BF)],
        where, x, bias, mine, theirs, *(rest if given else [Near(rest[0]), rest[1]]),
        scratch=[pltpu.VMEM((tokens, tokens), F32), pltpu.VMEM((tokens, tokens), F32)],
        flops=10**11 // 3,
        moved=8 * 2**20,
        limit=8,
    )


def normed(summed):
    centre = summed - jnp.mean(summed, -1, keepdims=True)
    scale_inv = lax.rsqrt(jnp.mean(centre * centre, -1, keepdims=True) + 1e-05)
    return centre * scale_inv, scale_inv


def norm_back(grad, n, scale_inv, gain):
    scaled = grad * gain
    first = jnp.mean(scaled, -1, keepdims=True)
    second = jnp.mean(scaled * n, -1, keepdims=True)
    return scale_inv * (scaled - first - n * second)


def turn_rows(lines, turned_ref, rows):
    tokens = lines.shape[1]
    blocks = lines.reshape(-1, 2, rows, tokens)
    turned_ref[0] = blocks[:, 0].reshape(-1, tokens)
    turned_ref[1] = blocks[:, 1].reshape(-1, tokens)


BIAS_OUT, GAIN_ONE, SHIFT_ONE, BIAS_DOWN, GAIN_TWO, SHIFT_TWO = range(6)


CHUNK = 512
LINES = 16


def blocks(count):
    return [slice(at, at + LINES) for at in range(0, count, LINES)]


def fold(value):
    return jnp.sum(value.reshape(-1, 8, value.shape[-1]), 0)


def total(folded):
    return jnp.sum(folded, 0, keepdims=True)


def ffn_kernel(
    where_ref, x_ref, own_ref, other_ref, w_out_ref, params_ref, w_up_ref, bias_up_ref, w_down_ref,
    cot_ref,
    out_ref, hidden_ref, n_one_ref, r_one_ref, active_ref, slope_ref, grad_two_ref, sums_ref,
    first_ref, second_ref, branch_ref, up_ref, down_ref, sems,
):
    half = own_ref.shape[0]
    tokens, width = x_ref.shape
    head = where_ref[1]
    count = w_up_ref.shape[1] // CHUNK
    span = lambda i: pl.ds(pl.multiple_of(i * CHUNK, CHUNK), CHUNK)

    def fetch_up(i):
        return pltpu.make_async_copy(w_up_ref.at[:, span(i)], up_ref.at[:, span(i)], sems.at[0, i])

    def fetch_down(i):
        return pltpu.make_async_copy(w_down_ref.at[span(i), :], down_ref.at[span(i), :], sems.at[1, i])

    for i in range(count):
        fetch_up(i).start()
        fetch_down(i).start()
    params = params_ref[...].astype(F32)
    row = lambda i: params[i : i + 1]
    own_at = pl.multiple_of(head * half, LANES)
    other_at = pl.multiple_of((1 - head) * half, LANES)
    branch_ref[...] = tn(own_ref[...], w_out_ref[pl.ds(own_at, half), :]) + tn(
        other_ref[...], w_out_ref[pl.ds(other_at, half), :]
    )

    for at in blocks(tokens):
        n, r = normed(x_ref[at, :].astype(F32) + branch_ref[at, :] + row(BIAS_OUT))
        n_one_ref[at, :] = n
        r_one_ref[at, :] = jnp.broadcast_to(r, (LINES, LANES))
        hidden_ref[at, :] = (n * row(GAIN_ONE) + row(SHIFT_ONE)).astype(BF)

    def upward(ref, at):
        ref[...] = nn(hidden_ref[...], up_ref[:, at])

    def gelu(ref, at):
        bias = bias_up_ref[:, at].astype(F32)
        for start in range(0, tokens, LINES):
            lines = slice(start, start + LINES)
            v = ref[lines, :] + bias
            phi = 0.5 + 0.5 * lax.erf(v * 0.7071067811865476)
            active_ref[lines, at] = (v * phi).astype(BF)
            density = jnp.exp(-0.5 * v * v) * 0.3989422804014327
            slope_ref[lines, at] = (phi + v * density).astype(BF)

    def downward(at):
        branch_ref[...] += nn(active_ref[:, at], down_ref[at, :])

    branch_ref[...] = jnp.zeros_like(branch_ref)
    fetch_up(0).wait()
    upward(first_ref, span(0))

    @pl.loop(0, count // 2)
    def _(i):
        fetch_up(2 * i + 1).wait()
        fetch_down(2 * i).wait()
        fetch_down(2 * i + 1).wait()

        @pl.when(2 * i + 2 < count)
        def _():
            fetch_up(2 * i + 2).wait()

        upward(second_ref, span(2 * i + 1))
        gelu(first_ref, span(2 * i))
        downward(span(2 * i))
        upward(first_ref, span(jnp.minimum(2 * i + 2, count - 1)))
        gelu(second_ref, span(2 * i + 1))
        downward(span(2 * i + 1))

    sums = [0.0, 0.0, 0.0]
    for at in blocks(tokens):
        n, r = normed(hidden_ref[at, :].astype(F32) + branch_ref[at, :] + row(BIAS_DOWN))
        out_ref[at, :] = (n * row(GAIN_TWO) + row(SHIFT_TWO)).astype(BF)
        cot = cot_ref[at, :].astype(F32)
        grad = norm_back(cot, n, r, row(GAIN_TWO))
        grad_two_ref[at, :] = grad
        terms = (cot * n, cot, grad.astype(BF).astype(F32))
        sums = [earlier + fold(term) for earlier, term in zip(sums, terms)]
    for i, folded in enumerate(sums):
        sums_ref[i : i + 1] = total(folded)


def down_kernel(where_ref, active_ref, grad_two_ref, send_ref, keep_ref):
    core = where_ref[0]
    groups, rows = send_ref.shape[0], send_ref.shape[1]
    grad_branch = grad_two_ref[...].astype(BF)
    for i in range(groups):
        block = nn(active_ref[:, i * 2 * rows : (i + 1) * 2 * rows].T, grad_branch).astype(BF)
        low, high = block[:rows], block[rows:]
        keep_ref[i] = jnp.where(core == 0, low, high)
        send_ref[i] = jnp.where(core == 0, high, low)


def slope_kernel(
    slope_ref, grad_two_ref, w_down_ref, grad_up_ref, bias_up_ref, branch_ref, down_ref, sems
):
    count = w_down_ref.shape[0] // CHUNK
    span = lambda i: pl.ds(pl.multiple_of(i * CHUNK, CHUNK), CHUNK)

    def fetch(i):
        return pltpu.make_async_copy(w_down_ref.at[span(i), :], down_ref.at[span(i), :], sems.at[i])

    for i in range(count):
        fetch(i).start()
    branch_ref[...] = grad_two_ref[...].astype(BF)

    @pl.loop(0, count)
    def _(i):
        fetch(i).wait()
        grad_active = nt(branch_ref[...], down_ref[span(i), :])
        grad_up = (grad_active * slope_ref[:, span(i)].astype(F32)).astype(BF)
        grad_up_ref[:, span(i)] = grad_up
        bias_up_ref[:, span(i)] = jnp.sum(grad_up.astype(F32), 0, keepdims=True)


def up_kernel(
    where_ref, hidden_ref, n_one_ref, r_one_ref, grad_up_ref, grad_two_ref, w_up_ref, w_out_ref, params_ref,
    own_ref, other_ref,
    grad_one_ref, grad_own_ref, grad_other_ref, sums_ref, send_ref, keep_ref,
    both_ref, turned_ref, grad_hidden_ref, grad_context_ref, up_ref, sem,
):
    half = grad_own_ref.shape[0]
    head, core = where_ref[1], where_ref[0]
    params = params_ref[...].astype(F32)
    row = lambda i: params[i : i + 1]
    groups, rows = send_ref.shape[0], send_ref.shape[1]
    tokens = hidden_ref.shape[0]
    fetch = pltpu.make_async_copy(w_up_ref, up_ref, sem)
    fetch.start()
    turn_rows(hidden_ref[...].T, turned_ref, rows)

    @pl.loop(0, w_up_ref.shape[1] // CHUNK)
    def _(i):
        at = pl.ds(pl.multiple_of(i * CHUNK, CHUNK), CHUNK)
        grad_up = grad_up_ref[:, at]
        send_ref[:, :, at] = nn(turned_ref[1 - core], grad_up).astype(BF).reshape(groups, rows, CHUNK)
        keep_ref[:, :, at] = nn(turned_ref[core], grad_up).astype(BF).reshape(groups, rows, CHUNK)

    fetch.wait()
    grad_hidden_ref[...] = nt(grad_up_ref[...], up_ref[...])
    sums = [0.0, 0.0, 0.0]
    for at in blocks(tokens):
        grad_hidden = grad_hidden_ref[at, :] + grad_two_ref[at, :]
        n_one = n_one_ref[at, :]
        grad_one = norm_back(grad_hidden, n_one, r_one_ref[at, :1], row(GAIN_ONE))
        grad_one_ref[at, :] = grad_one
        terms = (grad_hidden * n_one, grad_hidden, grad_one.astype(BF).astype(F32))
        sums = [earlier + fold(term) for earlier, term in zip(sums, terms)]
    for i, folded in enumerate(sums):
        sums_ref[i : i + 1] = total(folded)
    grad_attended = grad_one_ref[...].astype(BF)
    grad_context_ref[...] = nt(w_out_ref[...], grad_attended).astype(BF)
    own_at = pl.multiple_of(head * half, LANES)
    other_at = pl.multiple_of((1 - head) * half, LANES)
    both_ref[pl.ds(own_at, half), :] = own_ref[...]
    both_ref[pl.ds(other_at, half), :] = other_ref[...]
    turn_rows(both_ref[...], turned_ref, rows)
    ff = w_up_ref.shape[1]
    send_ref[:, :, ff:] = nn(turned_ref[1 - core], grad_attended).astype(BF).reshape(groups, rows, -1)
    keep_ref[:, :, ff:] = nn(turned_ref[core], grad_attended).astype(BF).reshape(groups, rows, -1)
    grad_own_ref[...] = grad_context_ref[pl.ds(own_at, half), :]
    grad_other_ref[...] = grad_context_ref[pl.ds(other_at, half), :]


def back_kernel(
    before, last, where_ref, x_ref, mask_ref, qkv_own_ref, qkv_other_ref, stats_own_ref, stats_other_ref,
    context_own_ref, context_other_ref, grad_own_ref, grad_other_ref, mine_own_ref, mine_other_ref, theirs_own_ref,
    theirs_other_ref, partial_ref, *refs
):
    if last:
        sums_before_ref, sums_one_ref, sums_two_ref, bias_up_ref, *refs = refs
        send_ref, keep_ref, grad_x_ref, ext_send_ref, ext_keep_ref = refs[:5]
        first_ref, second_ref, grads_ref, turned_ref, table_ref, ext_ref = refs[5:]
    else:
        send_ref, keep_ref, grad_x_ref, sums_ref, first_ref, second_ref, grads_ref, turned_ref = refs
    core, head = where_ref[0], where_ref[1]
    width, tokens = context_own_ref.shape
    groups, rows, columns = send_ref.shape[1:]
    wide = columns // 3
    count = wide // HEAD_DIM
    halves = (
        (qkv_own_ref, stats_own_ref, context_own_ref, grad_own_ref),
        (qkv_other_ref, stats_other_ref, context_other_ref, grad_other_ref),
    )

    def scaled(half, i):
        return (halves[half][3][head_lines(width, 0, i), :].astype(F32) * halves[half][1][i, 1:2, :]).astype(BF)

    def begin(ref, half, i):
        q, k, v = [halves[half][0][head_lines(width, part, i), :] for part in range(3)]
        ref[0] = tn(k, q)
        ref[1] = tn(v, scaled(half, i))

    def finish(ref, half, i, to):
        q, k, v = [halves[half][0][head_lines(width, part, i), :] for part in range(3)]
        grad = scaled(half, i)
        context = halves[half][2][head_lines(width, 0, i), :]
        inner = jnp.sum(grad.astype(F32) * context.astype(F32), 0, keepdims=True)
        held, moved = [], []
        for at in range(0, tokens, LANES):
            span = slice(at, at + LANES)
            weights = jnp.exp(ref[0, :, span] + mask_ref[:, span] - halves[half][1][i, 0:1, span])
            held.append(weights.astype(BF))
            moved.append((weights * (ref[1, :, span] - inner[:, span])).astype(BF))
        weights, grad_scores = jnp.concatenate(held, 1), jnp.concatenate(moved, 1)
        grads_ref[half, head_lines(wide, 0, to), :] = nn(k, grad_scores).astype(BF) * 0.125
        grads_ref[half, head_lines(wide, 1, to), :] = nt(q, grad_scores).astype(BF)
        grads_ref[half, head_lines(wide, 2, to), :] = nt(grad, weights).astype(BF)

    begin(first_ref, 0, before)

    @pl.loop(0, count)
    def _(i):
        begin(second_ref, 1, before + i)
        finish(first_ref, 0, before + i, i)
        begin(first_ref, 0, before + jnp.minimum(i + 1, count - 1))
        finish(second_ref, 1, before + i, i)

    turn_rows(x_ref[...].T, turned_ref, rows)
    for half in range(2):
        for out_ref, lines in ((send_ref, 1 - core), (keep_ref, core)):
            out_ref[half] = nt(turned_ref[lines], grads_ref[half]).astype(BF).reshape(groups, rows, columns)
    plain = [grads_ref[half].T for half in range(2)]
    depth = mine_own_ref.shape[1]
    start = before * HEAD_DIM
    for at, weights_refs in ((core, (mine_own_ref, mine_other_ref)), (1 - core, (theirs_own_ref, theirs_other_ref))):
        lanes = pl.ds(pl.multiple_of(at * depth, LANES), depth)
        terms = [
            nt(plain[half][:, part * wide : (part + 1) * wide], weights_refs[half][part, :, start : start + wide])
            for half in range(2)
            for part in range(3)
        ]
        grad_x_ref[:, lanes] = (partial_ref[:, lanes] + sum(terms)).astype(grad_x_ref.dtype)
    sums = [total(fold(value.astype(F32))) for value in plain]
    if not last:
        for half in range(2):
            sums_ref[half] = jnp.broadcast_to(sums[half], sums_ref.shape[1:])
        return
    table_ref[...] = jnp.zeros_like(table_ref)
    for line, part in ((0, 0), (1, 2)):
        for half, at in ((0, head), (1, 1 - head)):
            here = at * width
            span = slice(part * start, (part + 1) * start)
            table_ref[line : line + 1, pl.ds(pl.multiple_of(here, LANES), start)] = sums_before_ref[half, 0:1, span]
            span = slice(part * wide, (part + 1) * wide)
            table_ref[line : line + 1, pl.ds(pl.multiple_of(here + start, LANES), wide)] = sums[half][:, span]
    table_ref[2:5] = sums_one_ref[0:3]
    table_ref[5:8] = sums_two_ref[0:3]
    own = rows // 2
    table = table_ref[...].T.reshape(groups, 2, 2, own, LANES)
    ff = bias_up_ref.shape[1]
    spread = jnp.broadcast_to(bias_up_ref[...], (LANES, ff)).T.reshape(groups, 2, 2, ff // (4 * groups * rows), rows, LANES)
    lane = lax.broadcasted_iota(jnp.int32, (groups, rows, LANES), 2)
    for to_core in range(2):
        for to_head in range(2):
            block = jnp.concatenate([table[:, to_core, to_head], jnp.zeros((groups, rows - own, LANES), F32)], 1)
            for piece in range(spread.shape[3]):
                block = jnp.where(lane == 8 + piece, spread[:, to_core, to_head, piece], block)
            ext_ref[to_core, to_head] = block.astype(BF)
    for half, at in ((0, head), (1, 1 - head)):
        ext_send_ref[half] = ext_ref[1 - core, at]
        ext_keep_ref[half] = ext_ref[core, at]


def attend_back(where, x, mask, own, other, grads, weights, partial, groups, before, count, extra=()):
    width, tokens = own[2].shape
    depth = x.shape[1]
    rows = depth // (2 * groups)
    wide = count * HEAD_DIM
    last = len(extra) > 0
    kept = [v for pair in zip(own, other) for v in pair]
    block = ((2, groups, rows, 3 * wide), BF)
    outs = [block, block, ((tokens, depth), BF if last else F32)]
    outs += [((2, groups, rows, LANES), BF)] * 2 if last else [((2, 8, 3 * wide), F32)]
    scratch = [
        pltpu.VMEM((2, tokens, tokens), F32),
        pltpu.VMEM((2, tokens, tokens), F32),
        pltpu.VMEM((2, 3 * wide, tokens), BF),
        pltpu.VMEM((2, groups * rows, tokens), BF),
    ]
    if last:
        scratch += [pltpu.VMEM((LANES, depth), F32), pltpu.VMEM((2, 2, groups, rows, LANES), BF)]
    return call(
        functools.partial(back_kernel, before, last),
        outs,
        where, x, mask, *kept, *grads, *weights, partial, *extra,
        scratch=scratch,
        flops=2 * 10**11 // 3,
        moved=10 * 2**20,
        limit=16,
    )


def each(count, body):
    if count == 1:
        body(0)
    else:
        pl.loop(0, count)(body)


def open_kernel(cut, split, where_ref, *refs):
    count = split or 2
    terms, outs = refs[:count], refs[count:]
    head_send, head_own, low_own, *low_sends = outs
    low, head = where_ref[2], where_ref[1]
    size = len(low_sends) + 1

    def block(i, bits, half, columns):
        if split:
            return terms[0][half, i, bits, :, columns] + terms[1][half, i, bits, :, columns]
        return terms[0][i, bits, half, :, columns] + terms[1][i, bits, half, :, columns]

    def body(i):
        for bits in range(size):
            head_own[i, bits] = block(i, bits, 0 if split else head, slice(0, cut))
            head_send[i, bits] = block(i, bits, 1 if split else 1 - head, slice(0, cut))
        for flip, out in enumerate([low_own, *low_sends]):
            for half in range(2):
                if split != 4:
                    out[i, half] = block(i, low ^ flip, half, slice(cut, None))
                    continue
                wide = terms[0].shape[4] - cut
                out[i, half, :, :wide] = block(i, low ^ flip, half, slice(cut, None))
                out[i, half, :, wide:] = terms[2][half, i, low ^ flip] + terms[3][half, i, low ^ flip]

    each(head_own.shape[0], body)


def turn_kernel(split, size, where_ref, *refs):
    first, second, outs = refs[:2], refs[2 : 2 + size], refs[2 + size :]
    first_outs, (second_own, second_send) = outs[:size], outs[size:]
    low, head = where_ref[2], where_ref[1]
    own, other = (0, 1) if split else (head, 1 - head)

    def add(values, *at):
        return functools.reduce(jnp.add, [v[at] for v in values])

    def body(i):
        for flip, out in enumerate(first_outs):
            out[i] = add(first, i, low ^ flip)
        second_own[i] = add(second, i, own)
        second_send[i] = add(second, i, other)

    each(second_own.shape[0], body)


def last_kernel(counts, stage, where_ref, *refs):
    parts, at = [], 0
    for count in counts:
        parts.append(refs[at : at + count])
        at += count
    outs = refs[at:]
    index = where_ref[3 + stage]
    size = len(outs)

    def body(i):
        for flip, out in enumerate(outs):
            start = 0
            for part in parts:
                columns = slice(start, start + part[0].shape[2])
                start = columns.stop
                values = [v[i * size + (index ^ flip)].astype(F32) for v in part]
                out[i, :, columns] = functools.reduce(jnp.add, values).astype(BF)

    each(outs[0].shape[0], body)


def close_kernel(scale, *refs):
    refs[-1][...] = functools.reduce(jnp.add, [v[0].astype(F32) for v in refs[:-1]]) * scale


def pause_kernel(token_ref, out_ref):
    out_ref[...] = token_ref[...]


def pause(*others):
    token = after(jnp.zeros((8, LANES), F32), *others)
    return call(pause_kernel, [((8, LANES), F32)], token, flops=10**13, limit=2)[0]


def after(value, *others):
    return lax.optimization_barrier((value, *others))[0]


def pick(value, index, axis):
    return lax.dynamic_index_in_dim(value, index, axis, keepdims=False)


def on_device(
    inputs, cotangent, segment_ids, lengths, w_qkv, bias_query, bias_value, w_out, bias_out, gain_one,
    shift_one, w_up, bias_up, w_down, bias_down, gain_two, shift_two,
):
    width = w_out.shape[0]
    half = w_qkv.shape[2]
    ff = w_up.shape[1]
    tokens = inputs.shape[0]
    batch = lax.axis_size("batch")
    heads = lax.axis_size("head")
    place, head = lax.axis_index("batch"), lax.axis_index("head")
    core = place % 2
    scale = 1.0 / (lengths.shape[0] * batch)

    plan, bit, bits = [], 1, batch.bit_length() - 1
    if (bits - 1) % 2:
        plan.append((1, 2))
        bit = 2
    while bit < bits:
        plan.append((bit, 4))
        bit += 2
    where = jnp.stack([core, head] + [(place >> at) % many for at, many in plan]).astype(jnp.int32)

    def swap_batch(value, flip):
        return lax.ppermute(value, "batch", [(i, i ^ flip) for i in range(batch)])

    def swap_head(value):
        return lax.ppermute(value, "head", [(0, 1), (1, 0)])

    depth = width // 2

    def columns(at):
        part = lax.dynamic_slice_in_dim(w_qkv, at * depth, depth, 0)
        return part.transpose(1, 0, 2)

    own_mine = columns(core)
    w_mine = swap_head(own_mine)
    small_own = jnp.stack([bias_query, bias_value])
    small_other = swap_head(after(small_own, own_mine))
    params = jnp.stack([bias_out, gain_one, shift_one, bias_down, gain_two, shift_two])
    ids = segment_ids.reshape(heads, tokens)
    bias_up = bias_up[None]
    prepared = (inputs, where, columns(1 - core), small_own, params, ids, bias_up)
    inputs, where, own_theirs, small_own, params, ids, bias_up = lax.optimization_barrier(prepared)

    mask, *kept_own = attend(where, inputs, small_own, own_mine, own_theirs, ids, lengths)
    context_own = kept_own[2]
    w_mine = after(w_mine, context_own, small_other)
    w_theirs = swap_batch(w_mine, 1)
    kept_other = attend(where, inputs, small_other, w_mine, w_theirs, mask)
    context_other = kept_other[2]

    groups = batch // 2
    ffn_rows, up_rows = ff // batch, width // batch
    out, hidden, n_one, r_one, active, slope, grad_two, sums_two = call(
        ffn_kernel,
        [
            ((tokens, width), BF),
            ((tokens, width), BF),
            ((tokens, width), F32),
            ((tokens, LANES), F32),
            ((tokens, ff), BF),
            ((tokens, ff), BF),
            ((tokens, width), F32),
            ((8, width), F32),
        ],
        where, inputs, context_own, context_other, w_out, params, Far(w_up), bias_up, Far(w_down), cotangent,
        scratch=[
            pltpu.VMEM((tokens, CHUNK), F32), pltpu.VMEM((tokens, CHUNK), F32), pltpu.VMEM((tokens, width), F32),
            pltpu.VMEM(w_up.shape, BF), pltpu.VMEM(w_down.shape, BF), pltpu.SemaphoreType.DMA((2, ff // CHUNK)),
        ],
        flops=2 * 10**11 // 3, moved=30 * 2**20, limit=22,
    )
    down_send, down_keep = call(
        down_kernel,
        [((groups, ffn_rows, width), BF), ((groups, ffn_rows, width), BF)],
        where, active, grad_two,
        flops=6 * 10**10 // 3, moved=10 * 2**20, limit=12,
    )
    low, rest = plan[0], plan[1:]
    size = low[1]
    low_groups = groups // size

    def open_sum(values, cut, split=False, weigh=0):
        rows, columns = values[0].shape[-2] // (1 if split else heads), values[0].shape[-1]
        lead = (heads, low_groups, size) if split else (low_groups, size, heads)
        more = sum(v.shape[-1] for v in values[2::2])
        values = [v.reshape(*lead, rows, v.shape[-1]) for v in values]
        columns += more
        by_head, by_low = (low_groups, size, rows, cut), (low_groups, heads, rows, columns - cut)
        head_send, head_own, low_own, *low_sends = call(
            functools.partial(open_kernel, cut, len(values) if split else 0), [(by_head, BF)] * 2 + [(by_low, BF)] * size, where, *values,
            flops=weigh,
        )
        got = [swap_batch(v, flip << low[0]) for flip, v in enumerate(low_sends, 1)]
        return head_send, [head_own, swap_head(head_send)], [low_own, *got]

    def turn_sum(first, second, split=False, weigh=0):
        rows = first[0].shape[2]
        cut, more = first[0].shape[3], second[0].shape[3]
        outs = call(
            functools.partial(turn_kernel, split, size),
            [((low_groups, rows, cut), BF)] * size + [((low_groups, rows, more), BF)] * 2,
            where, *first, *second,
            flops=weigh,
        )
        got = [swap_batch(v, flip << low[0]) for flip, v in enumerate(outs[1:size], 1)]
        return outs[0], [outs[0], *got], [outs[size], swap_head(outs[size + 1])]

    def last_sum(*parts, weigh=0):
        for stage, (bit, many) in enumerate(rest):
            rows, columns = parts[0][0].shape[1], sum(part[0].shape[2] for part in parts)
            left = parts[0][0].shape[0] // many
            outs = call(
                functools.partial(last_kernel, [len(part) for part in parts], stage),
                [((left, rows, columns), BF)] * many,
                where, *[v for part in parts for v in part],
                flops=weigh,
            )
            parts = [[outs[0]] + [swap_batch(v, flip << bit) for flip, v in enumerate(outs[1:], 1)]]
        return outs[0], parts[0]

    def close_sum(values, weigh=0):
        return call(functools.partial(close_kernel, scale), [(values[0].shape[1:], F32)], *values, flops=weigh)[0]

    def late(values, *before):
        return [values[0]] + [after(v, *before) for v in values[1:]]

    down = [down_keep, swap_batch(down_send, 1)]
    grad_up, sum_bias_up = call(
        slope_kernel,
        [((tokens, ff), BF), ((1, ff), F32)],
        slope, grad_two, Far(w_down),
        scratch=[
            pltpu.VMEM((tokens, width), BF), pltpu.VMEM(w_down.shape, BF), pltpu.SemaphoreType.DMA((ff // CHUNK,)),
        ],
        flops=10**11 // 3, moved=10 * 2**20, limit=14,
    )
    down[1] = after(down[1], sum_bias_up)
    sent, down, down_low = open_sum(down, width // 2)
    grad_one, grad_own, grad_other, sums_one, up_send, up_keep = call(
        up_kernel,
        [
            ((tokens, width), F32),
            ((half, tokens), BF),
            ((half, tokens), BF),
            ((8, width), F32),
            ((groups, up_rows, ff + width), BF),
            ((groups, up_rows, ff + width), BF),
        ],
        where, hidden, n_one, r_one, after(grad_up, sent), grad_two, Far(w_up), w_out, params, context_own, context_other,
        scratch=[
            pltpu.VMEM((width, tokens), BF),
            pltpu.VMEM((2, groups * up_rows, tokens), BF),
            pltpu.VMEM((tokens, width), F32),
            pltpu.VMEM((width, tokens), BF),
            pltpu.VMEM(w_up.shape, BF),
            pltpu.SemaphoreType.DMA,
        ],
        limit=18,
        flops=2 * 10**11 // 3, moved=30 * 2**20,
    )
    up = [up_keep, swap_batch(up_send, 1)]
    sent, down, down_low = turn_sum(late(down, grad_one), down_low, weigh=10**12 // (10 * 3))
    sent, up, up_low = open_sum(late(up, sent), (ff + width) // 2)
    end = half // HEAD_DIM - 2
    weights = (own_mine, w_mine, own_theirs, w_theirs)
    qa_send, qa_keep, partial, sums = attend_back(
        where, inputs, mask, kept_own, kept_other, (after(grad_own, sent), grad_other), weights, grad_one, groups, 0, end
    )
    qa_got = swap_batch(qa_send, 1)
    sent, down = last_sum(late(down, sums), down_low)
    sent, up, up_low = turn_sum(late(up, sent), up_low)
    qb_send, qb_keep, input_grad, ext_send, ext_keep = attend_back(
        where, inputs, mask, kept_own, kept_other, (after(grad_own, sent), grad_other), weights, partial, groups, end, 2,
        (sums, sums_one, sums_two, sum_bias_up),
    )
    qb_got, ext_got = swap_batch(qb_send, 1), swap_batch(ext_send, 1)
    sum_down = close_sum(late(down, input_grad))
    cut_a, cut_b = 3 * end * HEAD_DIM // 2, 2 * LANES
    sent, qa, qa_low = open_sum([qa_keep, after(qa_got, sum_down)], cut_a, True)
    sent, up = last_sum(late(up, sent), up_low, weigh=10**12 // (10 * 3))
    sent, qb, qb_low = open_sum([qb_keep, after(qb_got, sent), ext_keep, after(ext_got, sent)], cut_b, True)
    sent, qa, qa_low = turn_sum(late(qa, sent), qa_low, True, weigh=10**12 // (10 * 3))
    sent, qb, qb_low = turn_sum(late(qb, sent), qb_low, True)
    sum_up = close_sum(late(up, sent), weigh=10**12 // (10 * 3))
    sent, qkv = last_sum(late(qa, sum_up), qa_low, qb, qb_low)
    sum_qkv = close_sum(qkv)
    wide_a, wide_b = end * HEAD_DIM, 2 * HEAD_DIM
    small = sum_qkv[:, 3 * half :]
    sum_qkv = jnp.concatenate(
        [sum_qkv[:, : 3 * wide_a].reshape(up_rows, 3, wide_a), sum_qkv[:, 3 * wide_a : 3 * half].reshape(up_rows, 3, wide_b)],
        2,
    )
    own = up_rows // heads
    pieces = ff // (width * heads)
    spread = small[:, 8 : 8 + pieces].T.reshape(-1)
    small = [small[:own, i] for i in range(8)]
    return (
        out, input_grad, sum_qkv, small[0], small[1], sum_up[:, ff:], small[4], small[2], small[3],
        sum_up[:, :ff], spread, sum_down, small[7], small[5], small[6],
    )


def solution(mesh):
    rows = P(BOTH, None)
    placed = (rows, rows, P("batch"), P("batch"), P(None, None, "head"), P("head"), P("head")) + (P(),) * 10
    flat = P(BOTH)
    return jax.shard_map(
        on_device,
        mesh=mesh,
        in_specs=placed,
        out_specs=(
            rows, rows, P("batch", None, "head"), flat, flat, rows, flat, flat, flat, rows, flat, rows, flat,
            flat, flat,
        ),
        check_vma=False,
    )
```

```python
import functools

import jax
import jax.numpy as jnp
from jax import lax
from jax.experimental import pallas as pl
from jax.experimental.pallas import tpu as pltpu
from jax.sharding import PartitionSpec as P

HEAD_DIM = 64
LANES = 128
BF = jnp.bfloat16
F32 = jnp.float32
BOTH = ("batch", "head")
VMEM = pl.BlockSpec(memory_space=pltpu.VMEM)
ANY = pl.BlockSpec(memory_space=pltpu.HBM)
SMEM = pl.BlockSpec(memory_space=pltpu.SMEM)


def nn(left, right):
    return lax.dot_general(left, right, (((1,), (0,)), ((), ())), preferred_element_type=F32)


def nt(left, right):
    return lax.dot_general(left, right, (((1,), (1,)), ((), ())), preferred_element_type=F32)


class Near:
    def __init__(self, value):
        self.value = value


class Far:
    def __init__(self, value):
        self.value = value


def call(kernel, outs, *operands, scratch=(), flops=0, moved=0, limit=16):
    specs = [
        ANY if isinstance(a, Far) else VMEM if isinstance(a, Near) or a.dtype != jnp.int32 else SMEM for a in operands
    ]
    operands = [a.value if isinstance(a, (Far, Near)) else a for a in operands]
    return pl.pallas_call(
        kernel,
        in_specs=specs,
        out_specs=[VMEM] * len(outs),
        out_shape=[jax.ShapeDtypeStruct(s, t) for s, t in outs],
        scratch_shapes=list(scratch),
        cost_estimate=pl.CostEstimate(flops=flops, bytes_accessed=moved, transcendentals=0),
        compiler_params=pltpu.CompilerParams(vmem_limit_bytes=limit * 2**20),
    )(*operands)


def tn(left, right):
    return lax.dot_general(left, right, (((0,), (0,)), ((), ())), preferred_element_type=F32)


def head_lines(width, part, number):
    return pl.ds(pl.multiple_of(part * width + number * HEAD_DIM, HEAD_DIM), HEAD_DIM)


def in_turn(count, first_ref, second_ref, begin, finish):
    begin(first_ref, 0)

    @pl.loop(0, count // 2)
    def _(i):
        begin(second_ref, 2 * i + 1)
        finish(first_ref, 2 * i)
        begin(first_ref, jnp.minimum(2 * i + 2, count - 1))
        finish(second_ref, 2 * i + 1)


def attend_kernel(given, where_ref, x_ref, bias_ref, mine_ref, theirs_ref, *refs):
    if given:
        mask_ref, qkv_ref, stats_ref, context_ref, first_ref, second_ref = refs
    else:
        ids_ref, length_ref, mask_ref, qkv_ref, stats_ref, context_ref, first_ref, second_ref = refs
        mine_ids = ids_ref[pl.ds(where_ref[1], 1), :]
        columns = jnp.broadcast_to(mine_ids, (LANES, mine_ids.shape[1])).T
        position = lax.broadcasted_iota(jnp.int32, columns.shape, 0)
        live = position < length_ref[where_ref[1]]
        for at in range(0, mask_ref.shape[1], LANES):
            allowed = (columns == mine_ids[:, at : at + LANES]) & live
            mask_ref[:, at : at + LANES] = jnp.where(allowed, 0.0, -1e30)
    width, tokens = context_ref.shape
    depth = mine_ref.shape[1]
    mine = pl.ds(pl.multiple_of(where_ref[0] * depth, LANES), depth)
    theirs = pl.ds(pl.multiple_of((1 - where_ref[0]) * depth, LANES), depth)
    for part in range(3):
        projected = nn(x_ref[:, mine], mine_ref[part]) + nn(x_ref[:, theirs], theirs_ref[part])
        if part == 0:
            projected = (projected + bias_ref[0:1, :].astype(F32)) * 0.125
        if part == 2:
            projected = projected + bias_ref[1:2, :].astype(F32)
        qkv_ref[part * width : (part + 1) * width, :] = projected.astype(BF).T

    def begin(ref, i):
        ref[...] = tn(qkv_ref[head_lines(width, 1, i), :], qkv_ref[head_lines(width, 0, i), :])

    def finish(ref, i):
        held = []
        for at in range(0, tokens, LANES):
            columns = slice(at, at + LANES)
            scores = ref[:, columns] + mask_ref[:, columns]
            largest = jnp.max(scores, 0, keepdims=True)
            weights = jnp.exp(scores - largest)
            stats_ref[i, 0:1, columns] = largest
            stats_ref[i, 1:2, columns] = 1.0 / jnp.sum(weights, 0, keepdims=True)
            held.append(weights.astype(BF))
        context = nn(qkv_ref[head_lines(width, 2, i), :], jnp.concatenate(held, 1))
        context_ref[head_lines(width, 0, i), :] = (context * stats_ref[i, 1:2, :]).astype(BF)

    in_turn(width // HEAD_DIM, first_ref, second_ref, begin, finish)


def attend(where, x, bias, mine, theirs, *rest):
    tokens, width = x.shape[0], mine.shape[2]
    given = len(rest) == 1
    return call(
        functools.partial(attend_kernel, given),
        ([] if given else [((tokens, tokens), F32)])
        + [((3 * width, tokens), BF), ((width // HEAD_DIM, 8, tokens), F32), ((width, tokens), BF)],
        where, x, bias, mine, theirs, *(rest if given else [Near(rest[0]), rest[1]]),
        scratch=[pltpu.VMEM((tokens, tokens), F32), pltpu.VMEM((tokens, tokens), F32)],
        flops=10**11 // 3,
        moved=8 * 2**20,
        limit=8,
    )


def normed(summed):
    centre = summed - jnp.mean(summed, -1, keepdims=True)
    scale_inv = lax.rsqrt(jnp.mean(centre * centre, -1, keepdims=True) + 1e-05)
    return centre * scale_inv, scale_inv


def norm_back(grad, n, scale_inv, gain):
    scaled = grad * gain
    first = jnp.mean(scaled, -1, keepdims=True)
    second = jnp.mean(scaled * n, -1, keepdims=True)
    return scale_inv * (scaled - first - n * second)


def turn_rows(lines, turned_ref, rows):
    tokens = lines.shape[1]
    blocks = lines.reshape(-1, 2, rows, tokens)
    turned_ref[0] = blocks[:, 0].reshape(-1, tokens)
    turned_ref[1] = blocks[:, 1].reshape(-1, tokens)


BIAS_OUT, GAIN_ONE, SHIFT_ONE, BIAS_DOWN, GAIN_TWO, SHIFT_TWO = range(6)


CHUNK = 512
LINES = 16


def blocks(count):
    return [slice(at, at + LINES) for at in range(0, count, LINES)]


def fold(value):
    return jnp.sum(value.reshape(-1, 8, value.shape[-1]), 0)


def total(folded):
    return jnp.sum(folded, 0, keepdims=True)


def ffn_kernel(
    where_ref, x_ref, own_ref, other_ref, w_out_ref, params_ref, w_up_ref, bias_up_ref, w_down_ref,
    cot_ref,
    out_ref, hidden_ref, n_one_ref, r_one_ref, active_ref, slope_ref, grad_two_ref, sums_ref,
    first_ref, second_ref, branch_ref,
):
    half = own_ref.shape[0]
    tokens, width = x_ref.shape
    head = where_ref[1]
    count = w_up_ref.shape[1] // CHUNK
    span = lambda i: pl.ds(pl.multiple_of(i * CHUNK, CHUNK), CHUNK)

    params = params_ref[...].astype(F32)
    row = lambda i: params[i : i + 1]
    own_at = pl.multiple_of(head * half, LANES)
    other_at = pl.multiple_of((1 - head) * half, LANES)
    branch_ref[...] = tn(own_ref[...], w_out_ref[pl.ds(own_at, half), :]) + tn(
        other_ref[...], w_out_ref[pl.ds(other_at, half), :]
    )

    for at in blocks(tokens):
        n, r = normed(x_ref[at, :].astype(F32) + branch_ref[at, :] + row(BIAS_OUT))
        n_one_ref[at, :] = n
        r_one_ref[at, :] = jnp.broadcast_to(r, (LINES, LANES))
        hidden_ref[at, :] = (n * row(GAIN_ONE) + row(SHIFT_ONE)).astype(BF)

    def upward(ref, at):
        ref[...] = nn(hidden_ref[...], w_up_ref[:, at])

    def gelu(ref, at):
        bias = bias_up_ref[:, at].astype(F32)
        for start in range(0, tokens, LINES):
            lines = slice(start, start + LINES)
            v = ref[lines, :] + bias
            phi = 0.5 + 0.5 * lax.erf(v * 0.7071067811865476)
            active_ref[lines, at] = (v * phi).astype(BF)
            density = jnp.exp(-0.5 * v * v) * 0.3989422804014327
            slope_ref[lines, at] = (phi + v * density).astype(BF)

    def downward(at):
        branch_ref[...] += nn(active_ref[:, at], w_down_ref[at, :])

    branch_ref[...] = jnp.zeros_like(branch_ref)
    upward(first_ref, span(0))

    @pl.loop(0, count // 2)
    def _(i):
        upward(second_ref, span(2 * i + 1))
        gelu(first_ref, span(2 * i))
        downward(span(2 * i))
        upward(first_ref, span(jnp.minimum(2 * i + 2, count - 1)))
        gelu(second_ref, span(2 * i + 1))
        downward(span(2 * i + 1))

    sums = [0.0, 0.0, 0.0]
    for at in blocks(tokens):
        n, r = normed(hidden_ref[at, :].astype(F32) + branch_ref[at, :] + row(BIAS_DOWN))
        out_ref[at, :] = (n * row(GAIN_TWO) + row(SHIFT_TWO)).astype(BF)
        cot = cot_ref[at, :].astype(F32)
        grad = norm_back(cot, n, r, row(GAIN_TWO))
        grad_two_ref[at, :] = grad
        terms = (cot * n, cot, grad.astype(BF).astype(F32))
        sums = [earlier + fold(term) for earlier, term in zip(sums, terms)]
    for i, folded in enumerate(sums):
        sums_ref[i : i + 1] = total(folded)


def down_kernel(where_ref, active_ref, grad_two_ref, send_ref, keep_ref):
    core = where_ref[0]
    groups, rows = send_ref.shape[0], send_ref.shape[1]
    grad_branch = grad_two_ref[...].astype(BF)
    for i in range(groups):
        block = nn(active_ref[:, i * 2 * rows : (i + 1) * 2 * rows].T, grad_branch).astype(BF)
        low, high = block[:rows], block[rows:]
        keep_ref[i] = jnp.where(core == 0, low, high)
        send_ref[i] = jnp.where(core == 0, high, low)


def slope_kernel(
    slope_ref, grad_two_ref, w_down_ref, grad_up_ref, bias_up_ref, branch_ref
):
    count = w_down_ref.shape[0] // CHUNK
    span = lambda i: pl.ds(pl.multiple_of(i * CHUNK, CHUNK), CHUNK)

    branch_ref[...] = grad_two_ref[...].astype(BF)

    @pl.loop(0, count)
    def _(i):
        grad_active = nt(branch_ref[...], w_down_ref[span(i), :])
        grad_up = (grad_active * slope_ref[:, span(i)].astype(F32)).astype(BF)
        grad_up_ref[:, span(i)] = grad_up
        bias_up_ref[:, span(i)] = jnp.sum(grad_up.astype(F32), 0, keepdims=True)


def up_kernel(
    where_ref, hidden_ref, n_one_ref, r_one_ref, grad_up_ref, grad_two_ref, w_up_ref, w_out_ref, params_ref,
    own_ref, other_ref,
    grad_one_ref, grad_own_ref, grad_other_ref, sums_ref, send_ref, keep_ref,
    both_ref, turned_ref, grad_hidden_ref, grad_context_ref,
):
    half = grad_own_ref.shape[0]
    head, core = where_ref[1], where_ref[0]
    params = params_ref[...].astype(F32)
    row = lambda i: params[i : i + 1]
    groups, rows = send_ref.shape[0], send_ref.shape[1]
    tokens = hidden_ref.shape[0]
    turn_rows(hidden_ref[...].T, turned_ref, rows)

    @pl.loop(0, w_up_ref.shape[1] // CHUNK)
    def _(i):
        at = pl.ds(pl.multiple_of(i * CHUNK, CHUNK), CHUNK)
        grad_up = grad_up_ref[:, at]
        send_ref[:, :, at] = nn(turned_ref[1 - core], grad_up).astype(BF).reshape(groups, rows, CHUNK)
        keep_ref[:, :, at] = nn(turned_ref[core], grad_up).astype(BF).reshape(groups, rows, CHUNK)

    grad_hidden_ref[...] = nt(grad_up_ref[...], w_up_ref[...])
    sums = [0.0, 0.0, 0.0]
    for at in blocks(tokens):
        grad_hidden = grad_hidden_ref[at, :] + grad_two_ref[at, :]
        n_one = n_one_ref[at, :]
        grad_one = norm_back(grad_hidden, n_one, r_one_ref[at, :1], row(GAIN_ONE))
        grad_one_ref[at, :] = grad_one
        terms = (grad_hidden * n_one, grad_hidden, grad_one.astype(BF).astype(F32))
        sums = [earlier + fold(term) for earlier, term in zip(sums, terms)]
    for i, folded in enumerate(sums):
        sums_ref[i : i + 1] = total(folded)
    grad_attended = grad_one_ref[...].astype(BF)
    grad_context_ref[...] = nt(w_out_ref[...], grad_attended).astype(BF)
    own_at = pl.multiple_of(head * half, LANES)
    other_at = pl.multiple_of((1 - head) * half, LANES)
    both_ref[pl.ds(own_at, half), :] = own_ref[...]
    both_ref[pl.ds(other_at, half), :] = other_ref[...]
    turn_rows(both_ref[...], turned_ref, rows)
    ff = w_up_ref.shape[1]
    send_ref[:, :, ff:] = nn(turned_ref[1 - core], grad_attended).astype(BF).reshape(groups, rows, -1)
    keep_ref[:, :, ff:] = nn(turned_ref[core], grad_attended).astype(BF).reshape(groups, rows, -1)
    grad_own_ref[...] = grad_context_ref[pl.ds(own_at, half), :]
    grad_other_ref[...] = grad_context_ref[pl.ds(other_at, half), :]


def back_kernel(
    before, last, where_ref, x_ref, mask_ref, qkv_own_ref, qkv_other_ref, stats_own_ref, stats_other_ref,
    context_own_ref, context_other_ref, grad_own_ref, grad_other_ref, mine_own_ref, mine_other_ref, theirs_own_ref,
    theirs_other_ref, partial_ref, *refs
):
    if last:
        sums_before_ref, sums_one_ref, sums_two_ref, bias_up_ref, *refs = refs
        send_ref, keep_ref, grad_x_ref, ext_send_ref, ext_keep_ref = refs[:5]
        first_ref, second_ref, grads_ref, turned_ref, table_ref, ext_ref = refs[5:]
    else:
        send_ref, keep_ref, grad_x_ref, sums_ref, first_ref, second_ref, grads_ref, turned_ref = refs
    core, head = where_ref[0], where_ref[1]
    width, tokens = context_own_ref.shape
    groups, rows, columns = send_ref.shape[1:]
    wide = columns // 3
    count = wide // HEAD_DIM
    halves = (
        (qkv_own_ref, stats_own_ref, context_own_ref, grad_own_ref),
        (qkv_other_ref, stats_other_ref, context_other_ref, grad_other_ref),
    )

    def scaled(half, i):
        return (halves[half][3][head_lines(width, 0, i), :].astype(F32) * halves[half][1][i, 1:2, :]).astype(BF)

    def begin(ref, half, i):
        q, k, v = [halves[half][0][head_lines(width, part, i), :] for part in range(3)]
        ref[0] = tn(k, q)
        ref[1] = tn(v, scaled(half, i))

    def finish(ref, half, i, to):
        q, k, v = [halves[half][0][head_lines(width, part, i), :] for part in range(3)]
        grad = scaled(half, i)
        context = halves[half][2][head_lines(width, 0, i), :]
        inner = jnp.sum(grad.astype(F32) * context.astype(F32), 0, keepdims=True)
        held, moved = [], []
        for at in range(0, tokens, LANES):
            span = slice(at, at + LANES)
            weights = jnp.exp(ref[0, :, span] + mask_ref[:, span] - halves[half][1][i, 0:1, span])
            held.append(weights.astype(BF))
            moved.append((weights * (ref[1, :, span] - inner[:, span])).astype(BF))
        weights, grad_scores = jnp.concatenate(held, 1), jnp.concatenate(moved, 1)
        grads_ref[half, head_lines(wide, 0, to), :] = nn(k, grad_scores).astype(BF) * 0.125
        grads_ref[half, head_lines(wide, 1, to), :] = nt(q, grad_scores).astype(BF)
        grads_ref[half, head_lines(wide, 2, to), :] = nt(grad, weights).astype(BF)

    begin(first_ref, 0, before)

    @pl.loop(0, count)
    def _(i):
        begin(second_ref, 1, before + i)
        finish(first_ref, 0, before + i, i)
        begin(first_ref, 0, before + jnp.minimum(i + 1, count - 1))
        finish(second_ref, 1, before + i, i)

    turn_rows(x_ref[...].T, turned_ref, rows)
    for half in range(2):
        for out_ref, lines in ((send_ref, 1 - core), (keep_ref, core)):
            out_ref[half] = nt(turned_ref[lines], grads_ref[half]).astype(BF).reshape(groups, rows, columns)
    plain = [grads_ref[half].T for half in range(2)]
    depth = mine_own_ref.shape[1]
    start = before * HEAD_DIM
    for at, weights_refs in ((core, (mine_own_ref, mine_other_ref)), (1 - core, (theirs_own_ref, theirs_other_ref))):
        lanes = pl.ds(pl.multiple_of(at * depth, LANES), depth)
        terms = [
            nt(plain[half][:, part * wide : (part + 1) * wide], weights_refs[half][part, :, start : start + wide])
            for half in range(2)
            for part in range(3)
        ]
        grad_x_ref[:, lanes] = (partial_ref[:, lanes] + sum(terms)).astype(grad_x_ref.dtype)
    sums = [total(fold(value.astype(F32))) for value in plain]
    if not last:
        for half in range(2):
            sums_ref[half] = jnp.broadcast_to(sums[half], sums_ref.shape[1:])
        return
    table_ref[...] = jnp.zeros_like(table_ref)
    for line, part in ((0, 0), (1, 2)):
        for half, at in ((0, head), (1, 1 - head)):
            here = at * width
            span = slice(part * start, (part + 1) * start)
            table_ref[line : line + 1, pl.ds(pl.multiple_of(here, LANES), start)] = sums_before_ref[half, 0:1, span]
            span = slice(part * wide, (part + 1) * wide)
            table_ref[line : line + 1, pl.ds(pl.multiple_of(here + start, LANES), wide)] = sums[half][:, span]
    table_ref[2:5] = sums_one_ref[0:3]
    table_ref[5:8] = sums_two_ref[0:3]
    own = rows // 2
    table = table_ref[...].T.reshape(groups, 2, 2, own, LANES)
    ff = bias_up_ref.shape[1]
    spread = jnp.broadcast_to(bias_up_ref[...], (LANES, ff)).T.reshape(groups, 2, 2, ff // (4 * groups * rows), rows, LANES)
    lane = lax.broadcasted_iota(jnp.int32, (groups, rows, LANES), 2)
    for to_core in range(2):
        for to_head in range(2):
            block = jnp.concatenate([table[:, to_core, to_head], jnp.zeros((groups, rows - own, LANES), F32)], 1)
            for piece in range(spread.shape[3]):
                block = jnp.where(lane == 8 + piece, spread[:, to_core, to_head, piece], block)
            ext_ref[to_core, to_head] = block.astype(BF)
    for half, at in ((0, head), (1, 1 - head)):
        ext_send_ref[half] = ext_ref[1 - core, at]
        ext_keep_ref[half] = ext_ref[core, at]


def attend_back(where, x, mask, own, other, grads, weights, partial, groups, before, count, extra=()):
    width, tokens = own[2].shape
    depth = x.shape[1]
    rows = depth // (2 * groups)
    wide = count * HEAD_DIM
    last = len(extra) > 0
    kept = [v for pair in zip(own, other) for v in pair]
    block = ((2, groups, rows, 3 * wide), BF)
    outs = [block, block, ((tokens, depth), BF if last else F32)]
    outs += [((2, groups, rows, LANES), BF)] * 2 if last else [((2, 8, 3 * wide), F32)]
    scratch = [
        pltpu.VMEM((2, tokens, tokens), F32),
        pltpu.VMEM((2, tokens, tokens), F32),
        pltpu.VMEM((2, 3 * wide, tokens), BF),
        pltpu.VMEM((2, groups * rows, tokens), BF),
    ]
    if last:
        scratch += [pltpu.VMEM((LANES, depth), F32), pltpu.VMEM((2, 2, groups, rows, LANES), BF)]
    return call(
        functools.partial(back_kernel, before, last),
        outs,
        where, x, mask, *kept, *grads, *weights, partial, *extra,
        scratch=scratch,
        flops=2 * 10**11 // 3,
        moved=10 * 2**20,
        limit=16,
    )


def each(count, body):
    if count == 1:
        body(0)
    else:
        pl.loop(0, count)(body)


def open_kernel(cut, split, where_ref, *refs):
    count = split or 2
    terms, outs = refs[:count], refs[count:]
    head_send, head_own, low_own, *low_sends = outs
    low, head = where_ref[2], where_ref[1]
    size = len(low_sends) + 1

    def block(i, bits, half, columns):
        if split:
            return terms[0][half, i, bits, :, columns] + terms[1][half, i, bits, :, columns]
        return terms[0][i, bits, half, :, columns] + terms[1][i, bits, half, :, columns]

    def body(i):
        for bits in range(size):
            head_own[i, bits] = block(i, bits, 0 if split else head, slice(0, cut))
            head_send[i, bits] = block(i, bits, 1 if split else 1 - head, slice(0, cut))
        for flip, out in enumerate([low_own, *low_sends]):
            for half in range(2):
                if split != 4:
                    out[i, half] = block(i, low ^ flip, half, slice(cut, None))
                    continue
                wide = terms[0].shape[4] - cut
                out[i, half, :, :wide] = block(i, low ^ flip, half, slice(cut, None))
                out[i, half, :, wide:] = terms[2][half, i, low ^ flip] + terms[3][half, i, low ^ flip]

    each(head_own.shape[0], body)


def turn_kernel(split, size, where_ref, *refs):
    first, second, outs = refs[:2], refs[2 : 2 + size], refs[2 + size :]
    first_outs, (second_own, second_send) = outs[:size], outs[size:]
    low, head = where_ref[2], where_ref[1]
    own, other = (0, 1) if split else (head, 1 - head)

    def add(values, *at):
        return functools.reduce(jnp.add, [v[at] for v in values])

    def body(i):
        for flip, out in enumerate(first_outs):
            out[i] = add(first, i, low ^ flip)
        second_own[i] = add(second, i, own)
        second_send[i] = add(second, i, other)

    each(second_own.shape[0], body)


def last_kernel(counts, stage, where_ref, *refs):
    parts, at = [], 0
    for count in counts:
        parts.append(refs[at : at + count])
        at += count
    outs = refs[at:]
    index = where_ref[3 + stage]
    size = len(outs)

    def body(i):
        for flip, out in enumerate(outs):
            start = 0
            for part in parts:
                columns = slice(start, start + part[0].shape[2])
                start = columns.stop
                values = [v[i * size + (index ^ flip)].astype(F32) for v in part]
                out[i, :, columns] = functools.reduce(jnp.add, values).astype(BF)

    each(outs[0].shape[0], body)


def close_kernel(scale, *refs):
    refs[-1][...] = functools.reduce(jnp.add, [v[0].astype(F32) for v in refs[:-1]]) * scale


def pause_kernel(token_ref, out_ref):
    out_ref[...] = token_ref[...]


def pause(*others):
    token = after(jnp.zeros((8, LANES), F32), *others)
    return call(pause_kernel, [((8, LANES), F32)], token, flops=10**13, limit=2)[0]


def after(value, *others):
    return lax.optimization_barrier((value, *others))[0]


def pick(value, index, axis):
    return lax.dynamic_index_in_dim(value, index, axis, keepdims=False)


def on_device(
    inputs, cotangent, segment_ids, lengths, w_qkv, bias_query, bias_value, w_out, bias_out, gain_one,
    shift_one, w_up, bias_up, w_down, bias_down, gain_two, shift_two,
):
    width = w_out.shape[0]
    half = w_qkv.shape[2]
    ff = w_up.shape[1]
    tokens = inputs.shape[0]
    batch = lax.axis_size("batch")
    heads = lax.axis_size("head")
    place, head = lax.axis_index("batch"), lax.axis_index("head")
    core = place % 2
    scale = 1.0 / (lengths.shape[0] * batch)

    plan, bit, bits = [], 1, batch.bit_length() - 1
    if (bits - 1) % 2:
        plan.append((1, 2))
        bit = 2
    while bit < bits:
        plan.append((bit, 4))
        bit += 2
    where = jnp.stack([core, head] + [(place >> at) % many for at, many in plan]).astype(jnp.int32)

    def swap_batch(value, flip):
        return lax.ppermute(value, "batch", [(i, i ^ flip) for i in range(batch)])

    def swap_head(value):
        return lax.ppermute(value, "head", [(0, 1), (1, 0)])

    depth = width // 2

    def columns(at):
        part = lax.dynamic_slice_in_dim(w_qkv, at * depth, depth, 0)
        return part.transpose(1, 0, 2)

    own_mine = columns(core)
    w_mine = swap_head(own_mine)
    small_own = jnp.stack([bias_query, bias_value])
    small_other = swap_head(after(small_own, own_mine))
    params = jnp.stack([bias_out, gain_one, shift_one, bias_down, gain_two, shift_two])
    ids = segment_ids.reshape(heads, tokens)
    bias_up = bias_up[None]
    prepared = (inputs, where, columns(1 - core), small_own, params, ids, bias_up)
    inputs, where, own_theirs, small_own, params, ids, bias_up = lax.optimization_barrier(prepared)

    mask, *kept_own = attend(where, inputs, small_own, own_mine, own_theirs, ids, lengths)
    context_own = kept_own[2]
    w_mine = after(w_mine, context_own, small_other)
    w_theirs = swap_batch(w_mine, 1)
    kept_other = attend(where, inputs, small_other, w_mine, w_theirs, mask)
    context_other = kept_other[2]

    groups = batch // 2
    ffn_rows, up_rows = ff // batch, width // batch
    out, hidden, n_one, r_one, active, slope, grad_two, sums_two = call(
        ffn_kernel,
        [
            ((tokens, width), BF),
            ((tokens, width), BF),
            ((tokens, width), F32),
            ((tokens, LANES), F32),
            ((tokens, ff), BF),
            ((tokens, ff), BF),
            ((tokens, width), F32),
            ((8, width), F32),
        ],
        where, inputs, context_own, context_other, w_out, params, w_up, bias_up, w_down, cotangent,
        scratch=[
            pltpu.VMEM((tokens, CHUNK), F32), pltpu.VMEM((tokens, CHUNK), F32), pltpu.VMEM((tokens, width), F32),
        ],
        flops=2 * 10**11 // 3, moved=30 * 2**20, limit=14,
    )
    down_send, down_keep = call(
        down_kernel,
        [((groups, ffn_rows, width), BF), ((groups, ffn_rows, width), BF)],
        where, active, grad_two,
        flops=6 * 10**10 // 3, moved=10 * 2**20, limit=12,
    )
    low, rest = plan[0], plan[1:]
    size = low[1]
    low_groups = groups // size

    def open_sum(values, cut, split=False, weigh=0):
        rows, columns = values[0].shape[-2] // (1 if split else heads), values[0].shape[-1]
        lead = (heads, low_groups, size) if split else (low_groups, size, heads)
        more = sum(v.shape[-1] for v in values[2::2])
        values = [v.reshape(*lead, rows, v.shape[-1]) for v in values]
        columns += more
        by_head, by_low = (low_groups, size, rows, cut), (low_groups, heads, rows, columns - cut)
        head_send, head_own, low_own, *low_sends = call(
            functools.partial(open_kernel, cut, len(values) if split else 0), [(by_head, BF)] * 2 + [(by_low, BF)] * size, where, *values,
            flops=weigh,
        )
        got = [swap_batch(v, flip << low[0]) for flip, v in enumerate(low_sends, 1)]
        return head_send, [head_own, swap_head(head_send)], [low_own, *got]

    def turn_sum(first, second, split=False, weigh=0):
        rows = first[0].shape[2]
        cut, more = first[0].shape[3], second[0].shape[3]
        outs = call(
            functools.partial(turn_kernel, split, size),
            [((low_groups, rows, cut), BF)] * size + [((low_groups, rows, more), BF)] * 2,
            where, *first, *second,
            flops=weigh,
        )
        got = [swap_batch(v, flip << low[0]) for flip, v in enumerate(outs[1:size], 1)]
        return outs[0], [outs[0], *got], [outs[size], swap_head(outs[size + 1])]

    def last_sum(*parts, weigh=0):
        for stage, (bit, many) in enumerate(rest):
            rows, columns = parts[0][0].shape[1], sum(part[0].shape[2] for part in parts)
            left = parts[0][0].shape[0] // many
            outs = call(
                functools.partial(last_kernel, [len(part) for part in parts], stage),
                [((left, rows, columns), BF)] * many,
                where, *[v for part in parts for v in part],
                flops=weigh,
            )
            parts = [[outs[0]] + [swap_batch(v, flip << bit) for flip, v in enumerate(outs[1:], 1)]]
        return outs[0], parts[0]

    def close_sum(values, weigh=0):
        return call(functools.partial(close_kernel, scale), [(values[0].shape[1:], F32)], *values, flops=weigh)[0]

    def late(values, *before):
        return [values[0]] + [after(v, *before) for v in values[1:]]

    down = [down_keep, swap_batch(down_send, 1)]
    grad_up, sum_bias_up = call(
        slope_kernel,
        [((tokens, ff), BF), ((1, ff), F32)],
        slope, grad_two, w_down,
        scratch=[
            pltpu.VMEM((tokens, width), BF),
        ],
        flops=10**11 // 3, moved=10 * 2**20, limit=8,
    )
    down[1] = after(down[1], sum_bias_up)
    sent, down, down_low = open_sum(down, width // 2)
    grad_one, grad_own, grad_other, sums_one, up_send, up_keep = call(
        up_kernel,
        [
            ((tokens, width), F32),
            ((half, tokens), BF),
            ((half, tokens), BF),
            ((8, width), F32),
            ((groups, up_rows, ff + width), BF),
            ((groups, up_rows, ff + width), BF),
        ],
        where, hidden, n_one, r_one, after(grad_up, sent), grad_two, w_up, w_out, params, context_own, context_other,
        scratch=[
            pltpu.VMEM((width, tokens), BF),
            pltpu.VMEM((2, groups * up_rows, tokens), BF),
            pltpu.VMEM((tokens, width), F32),
            pltpu.VMEM((width, tokens), BF),
        ],
        limit=13,
        flops=2 * 10**11 // 3, moved=30 * 2**20,
    )
    up = [up_keep, swap_batch(up_send, 1)]
    sent, down, down_low = turn_sum(late(down, grad_one), down_low, weigh=10**12 // (10 * 3))
    sent, up, up_low = open_sum(late(up, sent), (ff + width) // 2)
    end = half // HEAD_DIM - 2
    weights = (own_mine, w_mine, own_theirs, w_theirs)
    qa_send, qa_keep, partial, sums = attend_back(
        where, inputs, mask, kept_own, kept_other, (after(grad_own, sent), grad_other), weights, grad_one, groups, 0, end
    )
    qa_got = swap_batch(qa_send, 1)
    sent, down = last_sum(late(down, sums), down_low)
    sent, up, up_low = turn_sum(late(up, sent), up_low)
    qb_send, qb_keep, input_grad, ext_send, ext_keep = attend_back(
        where, inputs, mask, kept_own, kept_other, (after(grad_own, sent), grad_other), weights, partial, groups, end, 2,
        (sums, sums_one, sums_two, sum_bias_up),
    )
    qb_got, ext_got = swap_batch(qb_send, 1), swap_batch(ext_send, 1)
    sum_down = close_sum(late(down, input_grad))
    cut_a, cut_b = 3 * end * HEAD_DIM // 2, 2 * LANES
    sent, qa, qa_low = open_sum([qa_keep, after(qa_got, sum_down)], cut_a, True)
    sent, up = last_sum(late(up, sent), up_low, weigh=10**12 // (10 * 3))
    sent, qb, qb_low = open_sum([qb_keep, after(qb_got, sent), ext_keep, after(ext_got, sent)], cut_b, True)
    sent, qa, qa_low = turn_sum(late(qa, sent), qa_low, True, weigh=10**12 // (10 * 3))
    sent, qb, qb_low = turn_sum(late(qb, sent), qb_low, True)
    sum_up = close_sum(late(up, sent), weigh=10**12 // (10 * 3))
    sent, qkv = last_sum(late(qa, sum_up), qa_low, qb, qb_low)
    sum_qkv = close_sum(qkv)
    wide_a, wide_b = end * HEAD_DIM, 2 * HEAD_DIM
    small = sum_qkv[:, 3 * half :]
    sum_qkv = jnp.concatenate(
        [sum_qkv[:, : 3 * wide_a].reshape(up_rows, 3, wide_a), sum_qkv[:, 3 * wide_a : 3 * half].reshape(up_rows, 3, wide_b)],
        2,
    )
    own = up_rows // heads
    pieces = ff // (width * heads)
    spread = small[:, 8 : 8 + pieces].T.reshape(-1)
    small = [small[:own, i] for i in range(8)]
    return (
        out, input_grad, sum_qkv, small[0], small[1], sum_up[:, ff:], small[4], small[2], small[3],
        sum_up[:, :ff], spread, sum_down, small[7], small[5], small[6],
    )


def solution(mesh):
    rows = P(BOTH, None)
    placed = (rows, rows, P("batch"), P("batch"), P(None, None, "head"), P("head"), P("head")) + (P(),) * 10
    flat = P(BOTH)
    return jax.shard_map(
        on_device,
        mesh=mesh,
        in_specs=placed,
        out_specs=(
            rows, rows, P("batch", None, "head"), flat, flat, rows, flat, flat, flat, rows, flat, rows, flat,
            flat, flat,
        ),
        check_vma=False,
    )
```

```python
import functools

import jax
import jax.numpy as jnp
from jax import lax
from jax.experimental import pallas as pl
from jax.experimental.pallas import tpu as pltpu
from jax.sharding import PartitionSpec as P

HEAD_DIM = 64
LANES = 128
BF = jnp.bfloat16
F32 = jnp.float32
BOTH = ("batch", "head")
VMEM = pl.BlockSpec(memory_space=pltpu.VMEM)
ANY = pl.BlockSpec(memory_space=pltpu.HBM)
SMEM = pl.BlockSpec(memory_space=pltpu.SMEM)


def nn(left, right):
    return lax.dot_general(left, right, (((1,), (0,)), ((), ())), preferred_element_type=F32)


def nt(left, right):
    return lax.dot_general(left, right, (((1,), (1,)), ((), ())), preferred_element_type=F32)


class Near:
    def __init__(self, value):
        self.value = value


class Far:
    def __init__(self, value):
        self.value = value


def call(kernel, outs, *operands, scratch=(), flops=0, moved=0, limit=16):
    specs = [
        ANY if isinstance(a, Far) else VMEM if isinstance(a, Near) or a.dtype != jnp.int32 else SMEM for a in operands
    ]
    operands = [a.value if isinstance(a, (Far, Near)) else a for a in operands]
    return pl.pallas_call(
        kernel,
        in_specs=specs,
        out_specs=[VMEM] * len(outs),
        out_shape=[jax.ShapeDtypeStruct(s, t) for s, t in outs],
        scratch_shapes=list(scratch),
        cost_estimate=pl.CostEstimate(flops=flops, bytes_accessed=moved, transcendentals=0),
        compiler_params=pltpu.CompilerParams(vmem_limit_bytes=limit * 2**20),
    )(*operands)


def tn(left, right):
    return lax.dot_general(left, right, (((0,), (0,)), ((), ())), preferred_element_type=F32)


def head_lines(width, part, number):
    return pl.ds(pl.multiple_of(part * width + number * HEAD_DIM, HEAD_DIM), HEAD_DIM)


def in_turn(count, first_ref, second_ref, begin, finish):
    begin(first_ref, 0)

    @pl.loop(0, count // 2)
    def _(i):
        begin(second_ref, 2 * i + 1)
        finish(first_ref, 2 * i)
        begin(first_ref, jnp.minimum(2 * i + 2, count - 1))
        finish(second_ref, 2 * i + 1)


def attend_kernel(given, turned_rows, where_ref, x_ref, bias_ref, mine_ref, theirs_ref, *refs):
    if given:
        mask_ref, qkv_ref, stats_ref, context_ref, first_ref, second_ref = refs
    else:
        (ids_ref, length_ref, w_out_ref, params_ref, mask_ref, summed_ref, turned_ref, qkv_ref, stats_ref, context_ref,
         first_ref, second_ref) = refs
        turn_rows(x_ref[...].T, turned_ref, turned_rows)
        mine_ids = ids_ref[pl.ds(where_ref[1], 1), :]
        columns = jnp.broadcast_to(mine_ids, (LANES, mine_ids.shape[1])).T
        position = lax.broadcasted_iota(jnp.int32, columns.shape, 0)
        live = position < length_ref[where_ref[1]]
        for at in range(0, mask_ref.shape[1], LANES):
            allowed = (columns == mine_ids[:, at : at + LANES]) & live
            mask_ref[:, at : at + LANES] = jnp.where(allowed, 0.0, -1e30)
    width, tokens = context_ref.shape
    depth = mine_ref.shape[1]
    mine = pl.ds(pl.multiple_of(where_ref[0] * depth, LANES), depth)
    theirs = pl.ds(pl.multiple_of((1 - where_ref[0]) * depth, LANES), depth)
    for part in range(3):
        projected = nn(x_ref[:, mine], mine_ref[part]) + nn(x_ref[:, theirs], theirs_ref[part])
        if part == 0:
            projected = (projected + bias_ref[0:1, :].astype(F32)) * 0.125
        if part == 2:
            projected = projected + bias_ref[1:2, :].astype(F32)
        qkv_ref[part * width : (part + 1) * width, :] = projected.astype(BF).T

    def begin(ref, i):
        ref[...] = tn(qkv_ref[head_lines(width, 1, i), :], qkv_ref[head_lines(width, 0, i), :])

    def finish(ref, i):
        held = []
        for at in range(0, tokens, LANES):
            columns = slice(at, at + LANES)
            scores = ref[:, columns] + mask_ref[:, columns]
            largest = jnp.max(scores, 0, keepdims=True)
            weights = jnp.exp(scores - largest)
            stats_ref[i, 0:1, columns] = largest
            stats_ref[i, 1:2, columns] = 1.0 / jnp.sum(weights, 0, keepdims=True)
            held.append(weights.astype(BF))
        context = nn(qkv_ref[head_lines(width, 2, i), :], jnp.concatenate(held, 1))
        context_ref[head_lines(width, 0, i), :] = (context * stats_ref[i, 1:2, :]).astype(BF)

    in_turn(width // HEAD_DIM, first_ref, second_ref, begin, finish)
    if not given:
        lines = pl.ds(pl.multiple_of(where_ref[1] * width, LANES), width)
        attended = tn(context_ref[...], w_out_ref[lines, :])
        summed_ref[...] = x_ref[...].astype(F32) + attended + params_ref[BIAS_OUT : BIAS_OUT + 1].astype(F32)


def attend(where, x, bias, mine, theirs, *rest, turned_rows=0):
    tokens, width = x.shape[0], mine.shape[2]
    given = len(rest) == 1
    return call(
        functools.partial(attend_kernel, given, turned_rows),
        ([] if given else [((tokens, tokens), F32), (x.shape, F32), ((2, x.shape[1] // 2, tokens), BF)])
        + [((3 * width, tokens), BF), ((width // HEAD_DIM, 8, tokens), F32), ((width, tokens), BF)],
        where, x, bias, mine, theirs, *(rest if given else [Near(rest[0]), *rest[1:]]),
        scratch=[pltpu.VMEM((tokens, tokens), F32), pltpu.VMEM((tokens, tokens), F32)],
        flops=10**11 // 3,
        moved=8 * 2**20,
        limit=8 if given else 12,
    )


def normed(summed):
    centre = summed - jnp.mean(summed, -1, keepdims=True)
    scale_inv = lax.rsqrt(jnp.mean(centre * centre, -1, keepdims=True) + 1e-05)
    return centre * scale_inv, scale_inv


def norm_back(grad, n, scale_inv, gain):
    scaled = grad * gain
    first = jnp.mean(scaled, -1, keepdims=True)
    second = jnp.mean(scaled * n, -1, keepdims=True)
    return scale_inv * (scaled - first - n * second)


def turn_rows(lines, turned_ref, rows):
    tokens = lines.shape[1]
    blocks = lines.reshape(-1, 2, rows, tokens)
    turned_ref[0] = blocks[:, 0].reshape(-1, tokens)
    turned_ref[1] = blocks[:, 1].reshape(-1, tokens)


BIAS_OUT, GAIN_ONE, SHIFT_ONE, BIAS_DOWN, GAIN_TWO, SHIFT_TWO = range(6)


CHUNK = 512
WEIGH = 10**12 // 30
LINES = 16


def blocks(count):
    return [slice(at, at + LINES) for at in range(0, count, LINES)]


def fold(value):
    return jnp.sum(value.reshape(-1, 8, value.shape[-1]), 0)


def total(folded):
    return jnp.sum(folded, 0, keepdims=True)


def ffn_kernel(
    where_ref, summed_ref, other_ref, w_out_ref, params_ref, w_up_ref, bias_up_ref, w_down_ref, cot_ref,
    out_ref, hidden_ref, n_one_ref, r_one_ref, active_ref, slope_ref, grad_two_ref, sums_ref,
    first_ref, second_ref, branch_ref,
):
    half = other_ref.shape[0]
    tokens, width = summed_ref.shape
    head = where_ref[1]
    count = w_up_ref.shape[1] // CHUNK
    span = lambda i: pl.ds(pl.multiple_of(i * CHUNK, CHUNK), CHUNK)

    params = params_ref[...].astype(F32)
    row = lambda i: params[i : i + 1]
    other_at = pl.multiple_of((1 - head) * half, LANES)
    branch_ref[...] = tn(other_ref[...], w_out_ref[pl.ds(other_at, half), :])

    for at in blocks(tokens):
        n, r = normed(summed_ref[at, :] + branch_ref[at, :])
        n_one_ref[at, :] = n
        r_one_ref[at, :] = jnp.broadcast_to(r, (LINES, LANES))
        hidden_ref[at, :] = (n * row(GAIN_ONE) + row(SHIFT_ONE)).astype(BF)

    def upward(ref, at):
        ref[...] = nn(hidden_ref[...], w_up_ref[:, at])

    def gelu(ref, at):
        bias = bias_up_ref[:, at].astype(F32)
        for start in range(0, tokens, LINES):
            lines = slice(start, start + LINES)
            v = ref[lines, :] + bias
            phi = 0.5 + 0.5 * lax.erf(v * 0.7071067811865476)
            active_ref[lines, at] = (v * phi).astype(BF)
            density = jnp.exp(-0.5 * v * v) * 0.3989422804014327
            slope_ref[lines, at] = (phi + v * density).astype(BF)

    def downward(at):
        branch_ref[...] += nn(active_ref[:, at], w_down_ref[at, :])

    branch_ref[...] = jnp.zeros_like(branch_ref)
    upward(first_ref, span(0))

    @pl.loop(0, count // 2)
    def _(i):
        upward(second_ref, span(2 * i + 1))
        gelu(first_ref, span(2 * i))
        downward(span(2 * i))
        upward(first_ref, span(jnp.minimum(2 * i + 2, count - 1)))
        gelu(second_ref, span(2 * i + 1))
        downward(span(2 * i + 1))

    sums = [0.0, 0.0, 0.0]
    for at in blocks(tokens):
        n, r = normed(hidden_ref[at, :].astype(F32) + branch_ref[at, :] + row(BIAS_DOWN))
        out_ref[at, :] = (n * row(GAIN_TWO) + row(SHIFT_TWO)).astype(BF)
        cot = cot_ref[at, :].astype(F32)
        grad = norm_back(cot, n, r, row(GAIN_TWO))
        grad_two_ref[at, :] = grad
        terms = (cot * n, cot, grad.astype(BF).astype(F32))
        sums = [earlier + fold(term) for earlier, term in zip(sums, terms)]
    for i, folded in enumerate(sums):
        sums_ref[i : i + 1] = total(folded)


def down_kernel(where_ref, active_ref, grad_two_ref, send_ref, keep_ref):
    core = where_ref[0]
    groups, rows = send_ref.shape[0], send_ref.shape[1]
    grad_branch = grad_two_ref[...].astype(BF)
    for i in range(groups):
        block = nn(active_ref[:, i * 2 * rows : (i + 1) * 2 * rows].T, grad_branch).astype(BF)
        low, high = block[:rows], block[rows:]
        keep_ref[i] = jnp.where(core == 0, low, high)
        send_ref[i] = jnp.where(core == 0, high, low)


def slope_kernel(
    slope_ref, grad_two_ref, w_down_ref, grad_up_ref, bias_up_ref, branch_ref
):
    count = w_down_ref.shape[0] // CHUNK
    span = lambda i: pl.ds(pl.multiple_of(i * CHUNK, CHUNK), CHUNK)

    branch_ref[...] = grad_two_ref[...].astype(BF)

    @pl.loop(0, count)
    def _(i):
        grad_active = nt(branch_ref[...], w_down_ref[span(i), :])
        grad_up = (grad_active * slope_ref[:, span(i)].astype(F32)).astype(BF)
        grad_up_ref[:, span(i)] = grad_up
        bias_up_ref[:, span(i)] = jnp.sum(grad_up.astype(F32), 0, keepdims=True)


def up_kernel(
    where_ref, hidden_ref, n_one_ref, r_one_ref, grad_up_ref, grad_two_ref, w_up_ref, w_out_ref, params_ref,
    own_ref, other_ref,
    grad_one_ref, grad_own_ref, grad_other_ref, sums_ref, send_ref, keep_ref,
    both_ref, turned_ref, grad_hidden_ref, grad_context_ref,
):
    half = grad_own_ref.shape[0]
    head, core = where_ref[1], where_ref[0]
    params = params_ref[...].astype(F32)
    row = lambda i: params[i : i + 1]
    groups, rows = send_ref.shape[0], send_ref.shape[1]
    tokens = hidden_ref.shape[0]
    turn_rows(hidden_ref[...].T, turned_ref, rows)

    @pl.loop(0, w_up_ref.shape[1] // CHUNK)
    def _(i):
        at = pl.ds(pl.multiple_of(i * CHUNK, CHUNK), CHUNK)
        grad_up = grad_up_ref[:, at]
        send_ref[:, :, at] = nn(turned_ref[1 - core], grad_up).astype(BF).reshape(groups, rows, CHUNK)
        keep_ref[:, :, at] = nn(turned_ref[core], grad_up).astype(BF).reshape(groups, rows, CHUNK)

    grad_hidden_ref[...] = nt(grad_up_ref[...], w_up_ref[...])
    sums = [0.0, 0.0, 0.0]
    for at in blocks(tokens):
        grad_hidden = grad_hidden_ref[at, :] + grad_two_ref[at, :]
        n_one = n_one_ref[at, :]
        grad_one = norm_back(grad_hidden, n_one, r_one_ref[at, :1], row(GAIN_ONE))
        grad_one_ref[at, :] = grad_one
        terms = (grad_hidden * n_one, grad_hidden, grad_one.astype(BF).astype(F32))
        sums = [earlier + fold(term) for earlier, term in zip(sums, terms)]
    for i, folded in enumerate(sums):
        sums_ref[i : i + 1] = total(folded)
    grad_attended = grad_one_ref[...].astype(BF)
    grad_context_ref[...] = nt(w_out_ref[...], grad_attended).astype(BF)
    own_at = pl.multiple_of(head * half, LANES)
    other_at = pl.multiple_of((1 - head) * half, LANES)
    both_ref[pl.ds(own_at, half), :] = own_ref[...]
    both_ref[pl.ds(other_at, half), :] = other_ref[...]
    turn_rows(both_ref[...], turned_ref, rows)
    ff = w_up_ref.shape[1]
    send_ref[:, :, ff:] = nn(turned_ref[1 - core], grad_attended).astype(BF).reshape(groups, rows, -1)
    keep_ref[:, :, ff:] = nn(turned_ref[core], grad_attended).astype(BF).reshape(groups, rows, -1)
    grad_own_ref[...] = grad_context_ref[pl.ds(own_at, half), :]
    grad_other_ref[...] = grad_context_ref[pl.ds(other_at, half), :]


def back_kernel(
    before, last, where_ref, turned_ref, mask_ref, qkv_own_ref, qkv_other_ref, stats_own_ref, stats_other_ref,
    context_own_ref, context_other_ref, grad_own_ref, grad_other_ref, mine_own_ref, mine_other_ref, theirs_own_ref,
    theirs_other_ref, partial_ref, *refs
):
    if last:
        sums_before_ref, sums_one_ref, sums_two_ref, bias_up_ref, *refs = refs
        send_ref, keep_ref, grad_x_ref, ext_send_ref, ext_keep_ref = refs[:5]
        first_ref, second_ref, grads_ref, table_ref, ext_ref = refs[5:]
    else:
        send_ref, keep_ref, grad_x_ref, sums_ref, first_ref, second_ref, grads_ref = refs
    core, head = where_ref[0], where_ref[1]
    width, tokens = context_own_ref.shape
    groups, rows, columns = send_ref.shape[1:]
    wide = columns // 3
    count = wide // HEAD_DIM
    halves = (
        (qkv_own_ref, stats_own_ref, context_own_ref, grad_own_ref),
        (qkv_other_ref, stats_other_ref, context_other_ref, grad_other_ref),
    )

    def scaled(half, i):
        return (halves[half][3][head_lines(width, 0, i), :].astype(F32) * halves[half][1][i, 1:2, :]).astype(BF)

    def begin(ref, half, i):
        q, k, v = [halves[half][0][head_lines(width, part, i), :] for part in range(3)]
        ref[0] = tn(k, q)
        ref[1] = tn(v, scaled(half, i))

    def finish(ref, half, i, to):
        q, k, v = [halves[half][0][head_lines(width, part, i), :] for part in range(3)]
        grad = scaled(half, i)
        context = halves[half][2][head_lines(width, 0, i), :]
        inner = jnp.sum(grad.astype(F32) * context.astype(F32), 0, keepdims=True)
        held, moved = [], []
        for at in range(0, tokens, LANES):
            span = slice(at, at + LANES)
            weights = jnp.exp(ref[0, :, span] + mask_ref[:, span] - halves[half][1][i, 0:1, span])
            held.append(weights.astype(BF))
            moved.append((weights * (ref[1, :, span] - inner[:, span])).astype(BF))
        weights, grad_scores = jnp.concatenate(held, 1), jnp.concatenate(moved, 1)
        grads_ref[half, head_lines(wide, 0, to), :] = nn(k, grad_scores).astype(BF) * 0.125
        grads_ref[half, head_lines(wide, 1, to), :] = nt(q, grad_scores).astype(BF)
        grads_ref[half, head_lines(wide, 2, to), :] = nt(grad, weights).astype(BF)

    begin(first_ref, 0, before)

    @pl.loop(0, count)
    def _(i):
        begin(second_ref, 1, before + i)
        finish(first_ref, 0, before + i, i)
        begin(first_ref, 0, before + jnp.minimum(i + 1, count - 1))
        finish(second_ref, 1, before + i, i)

    for half in range(2):
        for out_ref, lines in ((send_ref, 1 - core), (keep_ref, core)):
            out_ref[half] = nt(turned_ref[lines], grads_ref[half]).astype(BF).reshape(groups, rows, columns)
    plain = [grads_ref[half].T for half in range(2)]
    depth = mine_own_ref.shape[1]
    start = before * HEAD_DIM
    for at, weights_refs in ((core, (mine_own_ref, mine_other_ref)), (1 - core, (theirs_own_ref, theirs_other_ref))):
        lanes = pl.ds(pl.multiple_of(at * depth, LANES), depth)
        terms = [
            nt(plain[half][:, part * wide : (part + 1) * wide], weights_refs[half][part, :, start : start + wide])
            for half in range(2)
            for part in range(3)
        ]
        grad_x_ref[:, lanes] = (partial_ref[:, lanes] + sum(terms)).astype(grad_x_ref.dtype)
    sums = [total(fold(value.astype(F32))) for value in plain]
    if not last:
        for half in range(2):
            sums_ref[half] = jnp.broadcast_to(sums[half], sums_ref.shape[1:])
        return
    table_ref[...] = jnp.zeros_like(table_ref)
    for line, part in ((0, 0), (1, 2)):
        for half, at in ((0, head), (1, 1 - head)):
            here = at * width
            span = slice(part * start, (part + 1) * start)
            table_ref[line : line + 1, pl.ds(pl.multiple_of(here, LANES), start)] = sums_before_ref[half, 0:1, span]
            span = slice(part * wide, (part + 1) * wide)
            table_ref[line : line + 1, pl.ds(pl.multiple_of(here + start, LANES), wide)] = sums[half][:, span]
    table_ref[2:5] = sums_one_ref[0:3]
    table_ref[5:8] = sums_two_ref[0:3]
    own = rows // 2
    table = table_ref[...].T.reshape(groups, 2, 2, own, LANES)
    ff = bias_up_ref.shape[1]
    spread = jnp.broadcast_to(bias_up_ref[...], (LANES, ff)).T.reshape(groups, 2, 2, ff // (4 * groups * rows), rows, LANES)
    lane = lax.broadcasted_iota(jnp.int32, (groups, rows, LANES), 2)
    for to_core in range(2):
        for to_head in range(2):
            block = jnp.concatenate([table[:, to_core, to_head], jnp.zeros((groups, rows - own, LANES), F32)], 1)
            for piece in range(spread.shape[3]):
                block = jnp.where(lane == 8 + piece, spread[:, to_core, to_head, piece], block)
            ext_ref[to_core, to_head] = block.astype(BF)
    for half, at in ((0, head), (1, 1 - head)):
        ext_send_ref[half] = ext_ref[1 - core, at]
        ext_keep_ref[half] = ext_ref[core, at]


def attend_back(where, turned, mask, own, other, grads, weights, partial, groups, before, count, extra=()):
    width, tokens = own[2].shape
    depth = 2 * turned.shape[1]
    rows = depth // (2 * groups)
    wide = count * HEAD_DIM
    last = len(extra) > 0
    kept = [v for pair in zip(own, other) for v in pair]
    block = ((2, groups, rows, 3 * wide), BF)
    outs = [block, block, ((tokens, depth), BF if last else F32)]
    outs += [((2, groups, rows, LANES), BF)] * 2 if last else [((2, 8, 3 * wide), F32)]
    scratch = [
        pltpu.VMEM((2, tokens, tokens), F32),
        pltpu.VMEM((2, tokens, tokens), F32),
        pltpu.VMEM((2, 3 * wide, tokens), BF),
    ]
    if last:
        scratch += [pltpu.VMEM((LANES, depth), F32), pltpu.VMEM((2, 2, groups, rows, LANES), BF)]
    return call(
        functools.partial(back_kernel, before, last),
        outs,
        where, turned, mask, *kept, *grads, *weights, partial, *extra,
        scratch=scratch,
        flops=2 * 10**11 // 3,
        moved=10 * 2**20,
        limit=16,
    )


def each(count, body):
    if count == 1:
        body(0)
    else:
        pl.loop(0, count)(body)


def open_kernel(cut, split, where_ref, *refs):
    count = split or 2
    terms, outs = refs[:count], refs[count:]
    head_send, head_own, low_own, *low_sends = outs
    low, head = where_ref[2], where_ref[1]
    size = len(low_sends) + 1

    def block(i, bits, half, columns):
        if split:
            return terms[0][half, i, bits, :, columns] + terms[1][half, i, bits, :, columns]
        return terms[0][i, bits, half, :, columns] + terms[1][i, bits, half, :, columns]

    def body(i):
        for bits in range(size):
            head_own[i, bits] = block(i, bits, 0 if split else head, slice(0, cut))
            head_send[i, bits] = block(i, bits, 1 if split else 1 - head, slice(0, cut))
        for flip, out in enumerate([low_own, *low_sends]):
            for half in range(2):
                if split != 4:
                    out[i, half] = block(i, low ^ flip, half, slice(cut, None))
                    continue
                wide = terms[0].shape[4] - cut
                out[i, half, :, :wide] = block(i, low ^ flip, half, slice(cut, None))
                out[i, half, :, wide:] = terms[2][half, i, low ^ flip] + terms[3][half, i, low ^ flip]

    each(head_own.shape[0], body)


def turn_kernel(split, size, where_ref, *refs):
    first, second, outs = refs[:2], refs[2 : 2 + size], refs[2 + size :]
    first_outs, (second_own, second_send) = outs[:size], outs[size:]
    low, head = where_ref[2], where_ref[1]
    own, other = (0, 1) if split else (head, 1 - head)

    def add(values, *at):
        return functools.reduce(jnp.add, [v[at] for v in values])

    def body(i):
        for flip, out in enumerate(first_outs):
            out[i] = add(first, i, low ^ flip)
        second_own[i] = add(second, i, own)
        second_send[i] = add(second, i, other)

    each(second_own.shape[0], body)


def last_kernel(counts, stage, where_ref, *refs):
    parts, at = [], 0
    for count in counts:
        parts.append(refs[at : at + count])
        at += count
    outs = refs[at:]
    index = where_ref[stage]
    size = len(outs)

    def body(i):
        for flip, out in enumerate(outs):
            start = 0
            for part in parts:
                columns = slice(start, start + part[0].shape[2])
                start = columns.stop
                values = [v[i * size + (index ^ flip)].astype(F32) for v in part]
                out[i, :, columns] = functools.reduce(jnp.add, values).astype(BF)

    each(outs[0].shape[0], body)


def close_last_kernel(scale, wide_a, wide_b, *refs):
    terms, (out_ref, small_ref, spread_ref) = refs[:-3], refs[-3:]
    summed = functools.reduce(jnp.add, [v[0].astype(F32) for v in terms]) * scale
    rows, start = summed.shape[0], 3 * wide_a
    for part in range(3):
        out_ref[:, part, :wide_a] = summed[:, part * wide_a : (part + 1) * wide_a]
        out_ref[:, part, wide_a:] = summed[:, start + part * wide_b : start + (part + 1) * wide_b]
    lines = summed[:, 3 * (wide_a + wide_b) :].T
    small_ref[...] = lines[:8, : small_ref.shape[1]]
    for piece in range(spread_ref.shape[1] // rows):
        spread_ref[:, piece * rows : (piece + 1) * rows] = lines[8 + piece : 9 + piece, :rows]


def close_kernel(scale, *refs):
    refs[-1][...] = functools.reduce(jnp.add, [v[0].astype(F32) for v in refs[:-1]]) * scale


def pause_kernel(token_ref, out_ref):
    out_ref[...] = token_ref[...]


def pause(*others):
    token = after(jnp.zeros((8, LANES), F32), *others)
    return call(pause_kernel, [((8, LANES), F32)], token, flops=10**13, limit=2)[0]


def after(value, *others):
    return lax.optimization_barrier((value, *others))[0]


def pick(value, index, axis):
    return lax.dynamic_index_in_dim(value, index, axis, keepdims=False)


def on_device(
    inputs, cotangent, segment_ids, lengths, w_qkv, bias_query, bias_value, w_out, bias_out, gain_one,
    shift_one, w_up, bias_up, w_down, bias_down, gain_two, shift_two,
):
    width = w_out.shape[0]
    half = w_qkv.shape[2]
    ff = w_up.shape[1]
    tokens = inputs.shape[0]
    batch = lax.axis_size("batch")
    heads = lax.axis_size("head")
    place, head = lax.axis_index("batch"), lax.axis_index("head")
    core = place % 2
    scale = 1.0 / (lengths.shape[0] * batch)

    plan, bit, bits = [], 1, batch.bit_length() - 1
    if (bits - 1) % 2:
        plan.append((1, 2))
        bit = 2
    while bit < bits:
        plan.append((bit, 4))
        bit += 2
    halving = [(at, 2) for at in range(plan[0][0] + plan[0][1] // 2, bits)]
    where = jnp.stack([core, head] + [(place >> at) % many for at, many in plan + halving]).astype(jnp.int32)

    def swap_batch(value, flip):
        return lax.ppermute(value, "batch", [(i, i ^ flip) for i in range(batch)])

    def swap_head(value):
        return lax.ppermute(value, "head", [(0, 1), (1, 0)])

    depth = width // 2

    def columns(source, at):
        part = lax.dynamic_slice_in_dim(source, at * depth, depth, 0)
        return part.transpose(1, 0, 2)

    own_mine = columns(w_qkv, core)
    w_mine = swap_head(own_mine)
    small_own = jnp.stack([bias_query, bias_value])
    small_other = swap_head(after(small_own, own_mine))
    params = jnp.stack([bias_out, gain_one, shift_one, bias_down, gain_two, shift_two])
    ids = segment_ids.reshape(heads, tokens)
    bias_up = bias_up[None]
    prepared = (inputs, where, columns(after(w_qkv, own_mine), 1 - core), small_own, params, ids, bias_up)
    inputs, where, own_theirs, small_own, params, ids, bias_up = lax.optimization_barrier(prepared)

    mask, summed, turned, *kept_own = attend(
        where, inputs, small_own, own_mine, own_theirs, ids, lengths, w_out, params, turned_rows=width // batch
    )
    context_own = kept_own[2]
    w_mine = after(w_mine, context_own, small_other)
    w_theirs = swap_batch(w_mine, 1)
    kept_other = attend(where, inputs, small_other, w_mine, w_theirs, mask)
    context_other = kept_other[2]

    groups = batch // 2
    ffn_rows, up_rows = ff // batch, width // batch
    out, hidden, n_one, r_one, active, slope, grad_two, sums_two = call(
        ffn_kernel,
        [
            ((tokens, width), BF),
            ((tokens, width), BF),
            ((tokens, width), F32),
            ((tokens, LANES), F32),
            ((tokens, ff), BF),
            ((tokens, ff), BF),
            ((tokens, width), F32),
            ((8, width), F32),
        ],
        where, summed, context_other, w_out, params, w_up, bias_up, w_down, cotangent,
        scratch=[
            pltpu.VMEM((tokens, CHUNK), F32), pltpu.VMEM((tokens, CHUNK), F32), pltpu.VMEM((tokens, width), F32),
        ],
        flops=2 * 10**11 // 3, moved=30 * 2**20, limit=14,
    )
    down_send, down_keep = call(
        down_kernel,
        [((groups, ffn_rows, width), BF), ((groups, ffn_rows, width), BF)],
        where, active, grad_two,
        flops=6 * 10**10 // 3, moved=10 * 2**20, limit=12,
    )
    low, rest = plan[0], plan[1:]
    size = low[1]
    low_groups = groups // size

    def open_sum(values, cut, split=False, weigh=0):
        rows, columns = values[0].shape[-2] // (1 if split else heads), values[0].shape[-1]
        lead = (heads, low_groups, size) if split else (low_groups, size, heads)
        more = sum(v.shape[-1] for v in values[2::2])
        values = [v.reshape(*lead, rows, v.shape[-1]) for v in values]
        columns += more
        by_head, by_low = (low_groups, size, rows, cut), (low_groups, heads, rows, columns - cut)
        head_send, head_own, low_own, *low_sends = call(
            functools.partial(open_kernel, cut, len(values) if split else 0), [(by_head, BF)] * 2 + [(by_low, BF)] * size, where, *values,
            flops=weigh,
        )
        got = [swap_batch(v, flip << low[0]) for flip, v in enumerate(low_sends, 1)]
        return head_send, [head_own, swap_head(head_send)], [low_own, *got]

    def turn_sum(first, second, split=False, weigh=0):
        rows = first[0].shape[2]
        cut, more = first[0].shape[3], second[0].shape[3]
        outs = call(
            functools.partial(turn_kernel, split, size),
            [((low_groups, rows, cut), BF)] * size + [((low_groups, rows, more), BF)] * 2,
            where, *first, *second,
            flops=weigh,
        )
        got = [swap_batch(v, flip << low[0]) for flip, v in enumerate(outs[1:size], 1)]
        return outs[0], [outs[0], *got], [outs[size], swap_head(outs[size + 1])]

    def last_sum(*parts, stages=None, weigh=0):
        for bit, many in stages or rest:
            stage = 2 + (plan + halving).index((bit, many))
            rows, columns = parts[0][0].shape[1], sum(part[0].shape[2] for part in parts)
            left = parts[0][0].shape[0] // many
            outs = call(
                functools.partial(last_kernel, [len(part) for part in parts], stage),
                [((left, rows, columns), BF)] * many,
                where, *[v for part in parts for v in part],
                flops=weigh,
            )
            parts = [[outs[0]] + [swap_batch(v, flip << bit) for flip, v in enumerate(outs[1:], 1)]]
        return outs[0], parts[0]

    def close_sum(values, weigh=0):
        return call(functools.partial(close_kernel, scale), [(values[0].shape[1:], F32)], *values, flops=weigh)[0]

    def late(values, *before):
        return [values[0]] + [after(v, *before) for v in values[1:]]

    down = [down_keep, swap_batch(down_send, 1)]
    grad_up, sum_bias_up = call(
        slope_kernel,
        [((tokens, ff), BF), ((1, ff), F32)],
        slope, grad_two, w_down,
        scratch=[
            pltpu.VMEM((tokens, width), BF),
        ],
        flops=10**11 // 3, moved=10 * 2**20, limit=8,
    )
    down[1] = after(down[1], sum_bias_up)
    sent, down, down_low = open_sum(down, width // 2)
    grad_one, grad_own, grad_other, sums_one, up_send, up_keep = call(
        up_kernel,
        [
            ((tokens, width), F32),
            ((half, tokens), BF),
            ((half, tokens), BF),
            ((8, width), F32),
            ((groups, up_rows, ff + width), BF),
            ((groups, up_rows, ff + width), BF),
        ],
        where, hidden, n_one, r_one, after(grad_up, sent), grad_two, w_up, w_out, params, context_own, context_other,
        scratch=[
            pltpu.VMEM((width, tokens), BF),
            pltpu.VMEM((2, groups * up_rows, tokens), BF),
            pltpu.VMEM((tokens, width), F32),
            pltpu.VMEM((width, tokens), BF),
        ],
        limit=13,
        flops=2 * 10**11 // 3, moved=30 * 2**20,
    )
    up = [up_keep, swap_batch(up_send, 1)]
    sent, down, down_low = turn_sum(late(down, grad_one), down_low, weigh=WEIGH)
    sent, up, up_low = open_sum(late(up, sent), (ff + width) // 2)
    end = half // HEAD_DIM - 2
    weights = (own_mine, w_mine, own_theirs, w_theirs)
    qa_send, qa_keep, partial, sums = attend_back(
        where, turned, mask, kept_own, kept_other, (after(grad_own, sent), grad_other), weights, grad_one, groups, 0, end
    )
    qa_got = swap_batch(qa_send, 1)
    sent, down = last_sum(late(down, sums), down_low)
    sent, up, up_low = turn_sum(late(up, sent), up_low)
    qb_send, qb_keep, input_grad, ext_send, ext_keep = attend_back(
        where, turned, mask, kept_own, kept_other, (after(grad_own, sent), grad_other), weights, partial, groups, end, 2,
        (sums, sums_one, sums_two, sum_bias_up),
    )
    qb_got, ext_got = swap_batch(qb_send, 1), swap_batch(ext_send, 1)
    sum_down = close_sum(late(down, input_grad))
    cut_a, cut_b = 3 * end * HEAD_DIM // 2, 2 * LANES
    sent, qa, qa_low = open_sum([qa_keep, after(qa_got, sum_down)], cut_a, True)
    sent, up = last_sum(late(up, sent), up_low, stages=halving[:1], weigh=WEIGH)
    sent, qb, qb_low = open_sum([qb_keep, after(qb_got, sent), ext_keep, after(ext_got, sent)], cut_b, True)
    sent, qa, qa_low = turn_sum(late(qa, sent), qa_low, True, weigh=WEIGH)
    sent, up = last_sum(late(up, sent), stages=halving[1:])
    sent, qb, qb_low = turn_sum(late(qb, sent), qb_low, True, weigh=WEIGH)
    sent, qkv = last_sum(late(qa, sent), qa_low, qb, qb_low)
    sum_up = close_sum(late(up, sent))
    own, pieces = up_rows // heads, ff // (heads * width)
    sum_qkv, small, spread = call(
        functools.partial(close_last_kernel, scale, end * HEAD_DIM, 2 * HEAD_DIM),
        [((up_rows, 3, half), F32), ((8, own), F32), ((1, pieces * up_rows), F32)],
        *qkv,
    )
    small = [small[i] for i in range(8)]
    spread = spread[0]
    return (
        out, input_grad, sum_qkv, small[0], small[1], sum_up[:, ff:], small[4], small[2], small[3],
        sum_up[:, :ff], spread, sum_down, small[7], small[5], small[6],
    )


def solution(mesh):
    rows = P(BOTH, None)
    placed = (rows, rows, P("batch"), P("batch"), P(None, None, "head"), P("head"), P("head")) + (P(),) * 10
    flat = P(BOTH)
    return jax.shard_map(
        on_device,
        mesh=mesh,
        in_specs=placed,
        out_specs=(
            rows, rows, P("batch", None, "head"), flat, flat, rows, flat, flat, flat, rows, flat, rows, flat,
            flat, flat,
        ),
        check_vma=False,
    )
```

```python
import functools

import jax
import jax.numpy as jnp
from jax import lax
from jax.experimental import pallas as pl
from jax.experimental.pallas import tpu as pltpu
from jax.sharding import PartitionSpec as P

HEAD_DIM = 64
LANES = 128
BF = jnp.bfloat16
F32 = jnp.float32
BOTH = ("batch", "head")
VMEM = pl.BlockSpec(memory_space=pltpu.VMEM)
ANY = pl.BlockSpec(memory_space=pltpu.HBM)
SMEM = pl.BlockSpec(memory_space=pltpu.SMEM)


def nn(left, right):
    return lax.dot_general(left, right, (((1,), (0,)), ((), ())), preferred_element_type=F32)


def nt(left, right):
    return lax.dot_general(left, right, (((1,), (1,)), ((), ())), preferred_element_type=F32)


class Near:
    def __init__(self, value):
        self.value = value


class Far:
    def __init__(self, value):
        self.value = value


def call(kernel, outs, *operands, scratch=(), flops=0, moved=0, limit=16):
    specs = [
        ANY if isinstance(a, Far) else VMEM if isinstance(a, Near) or a.dtype != jnp.int32 else SMEM for a in operands
    ]
    operands = [a.value if isinstance(a, (Far, Near)) else a for a in operands]
    return pl.pallas_call(
        kernel,
        in_specs=specs,
        out_specs=[VMEM] * len(outs),
        out_shape=[jax.ShapeDtypeStruct(s, t) for s, t in outs],
        scratch_shapes=list(scratch),
        cost_estimate=pl.CostEstimate(flops=flops, bytes_accessed=moved, transcendentals=0),
        compiler_params=pltpu.CompilerParams(vmem_limit_bytes=limit * 2**20),
    )(*operands)


def tn(left, right):
    return lax.dot_general(left, right, (((0,), (0,)), ((), ())), preferred_element_type=F32)


def head_lines(width, part, number):
    return pl.ds(pl.multiple_of(part * width + number * HEAD_DIM, HEAD_DIM), HEAD_DIM)


def in_turn(count, first_ref, second_ref, begin, finish):
    begin(first_ref, 0)

    @pl.loop(0, count // 2)
    def _(i):
        begin(second_ref, 2 * i + 1)
        finish(first_ref, 2 * i)
        begin(first_ref, jnp.minimum(2 * i + 2, count - 1))
        finish(second_ref, 2 * i + 1)


def attend_kernel(given, turned_rows, where_ref, x_ref, bias_ref, mine_ref, theirs_ref, *refs):
    if given:
        mask_ref, qkv_ref, stats_ref, context_ref, first_ref, second_ref = refs
    else:
        (ids_ref, length_ref, w_out_ref, params_ref, mask_ref, summed_ref, turned_ref, qkv_ref, stats_ref, context_ref,
         first_ref, second_ref) = refs
        turn_rows(x_ref[...].T, turned_ref, turned_rows)
        mine_ids = ids_ref[pl.ds(where_ref[1], 1), :]
        columns = jnp.broadcast_to(mine_ids, (LANES, mine_ids.shape[1])).T
        position = lax.broadcasted_iota(jnp.int32, columns.shape, 0)
        live = position < length_ref[where_ref[1]]
        for at in range(0, mask_ref.shape[1], LANES):
            allowed = (columns == mine_ids[:, at : at + LANES]) & live
            mask_ref[:, at : at + LANES] = jnp.where(allowed, 0.0, -1e30)
    width, tokens = context_ref.shape
    depth = mine_ref.shape[1]
    mine = pl.ds(pl.multiple_of(where_ref[0] * depth, LANES), depth)
    theirs = pl.ds(pl.multiple_of((1 - where_ref[0]) * depth, LANES), depth)
    for part in range(3):
        projected = nn(x_ref[:, mine], mine_ref[part]) + nn(x_ref[:, theirs], theirs_ref[part])
        if part == 0:
            projected = (projected + bias_ref[0:1, :].astype(F32)) * 0.125
        if part == 2:
            projected = projected + bias_ref[1:2, :].astype(F32)
        qkv_ref[part * width : (part + 1) * width, :] = projected.astype(BF).T

    def begin(ref, i):
        ref[...] = tn(qkv_ref[head_lines(width, 1, i), :], qkv_ref[head_lines(width, 0, i), :])

    def finish(ref, i):
        held = []
        for at in range(0, tokens, LANES):
            columns = slice(at, at + LANES)
            scores = ref[:, columns] + mask_ref[:, columns]
            largest = jnp.max(scores, 0, keepdims=True)
            weights = jnp.exp(scores - largest)
            stats_ref[i, 0:1, columns] = largest
            stats_ref[i, 1:2, columns] = 1.0 / jnp.sum(weights, 0, keepdims=True)
            held.append(weights.astype(BF))
        context = nn(qkv_ref[head_lines(width, 2, i), :], jnp.concatenate(held, 1))
        context_ref[head_lines(width, 0, i), :] = (context * stats_ref[i, 1:2, :]).astype(BF)

    in_turn(width // HEAD_DIM, first_ref, second_ref, begin, finish)
    if not given:
        lines = pl.ds(pl.multiple_of(where_ref[1] * width, LANES), width)
        attended = tn(context_ref[...], w_out_ref[lines, :])
        summed_ref[...] = x_ref[...].astype(F32) + attended + params_ref[BIAS_OUT : BIAS_OUT + 1].astype(F32)


def attend(where, x, bias, mine, theirs, *rest, turned_rows=0):
    tokens, width = x.shape[0], mine.shape[2]
    given = len(rest) == 1
    return call(
        functools.partial(attend_kernel, given, turned_rows),
        ([] if given else [((tokens, tokens), F32), (x.shape, F32), ((2, x.shape[1] // 2, tokens), BF)])
        + [((3 * width, tokens), BF), ((width // HEAD_DIM, 8, tokens), F32), ((width, tokens), BF)],
        where, x, bias, mine, theirs, *(rest if given else [Near(rest[0]), *rest[1:]]),
        scratch=[pltpu.VMEM((tokens, tokens), F32), pltpu.VMEM((tokens, tokens), F32)],
        flops=10**11 // 3,
        moved=8 * 2**20,
        limit=8 if given else 12,
    )


def normed(summed):
    centre = summed - jnp.mean(summed, -1, keepdims=True)
    scale_inv = lax.rsqrt(jnp.mean(centre * centre, -1, keepdims=True) + 1e-05)
    return centre * scale_inv, scale_inv


def norm_back(grad, n, scale_inv, gain):
    scaled = grad * gain
    first = jnp.mean(scaled, -1, keepdims=True)
    second = jnp.mean(scaled * n, -1, keepdims=True)
    return scale_inv * (scaled - first - n * second)


def turn_rows(lines, turned_ref, rows):
    tokens = lines.shape[1]
    blocks = lines.reshape(-1, 2, rows, tokens)
    turned_ref[0] = blocks[:, 0].reshape(-1, tokens)
    turned_ref[1] = blocks[:, 1].reshape(-1, tokens)


BIAS_OUT, GAIN_ONE, SHIFT_ONE, BIAS_DOWN, GAIN_TWO, SHIFT_TWO = range(6)


CHUNK = 512
WEIGH = 10**12 // 30
LINES = 16


def blocks(count):
    return [slice(at, at + LINES) for at in range(0, count, LINES)]


def fold(value):
    return jnp.sum(value.reshape(-1, 8, value.shape[-1]), 0)


def total(folded):
    return jnp.sum(folded, 0, keepdims=True)


def ffn_kernel(
    where_ref, summed_ref, other_ref, w_out_ref, params_ref, w_up_ref, bias_up_ref, w_down_ref, cot_ref,
    out_ref, hidden_ref, n_one_ref, r_one_ref, active_ref, slope_ref, grad_two_ref, sums_ref,
    first_ref, second_ref, branch_ref,
):
    half = other_ref.shape[0]
    tokens, width = summed_ref.shape
    head = where_ref[1]
    count = w_up_ref.shape[1] // CHUNK
    span = lambda i: pl.ds(pl.multiple_of(i * CHUNK, CHUNK), CHUNK)

    params = params_ref[...].astype(F32)
    row = lambda i: params[i : i + 1]
    other_at = pl.multiple_of((1 - head) * half, LANES)
    branch_ref[...] = tn(other_ref[...], w_out_ref[pl.ds(other_at, half), :])

    for at in blocks(tokens):
        n, r = normed(summed_ref[at, :] + branch_ref[at, :])
        n_one_ref[at, :] = n
        r_one_ref[at, :] = jnp.broadcast_to(r, (LINES, LANES))
        hidden_ref[at, :] = (n * row(GAIN_ONE) + row(SHIFT_ONE)).astype(BF)

    def upward(ref, at):
        ref[...] = nn(hidden_ref[...], w_up_ref[:, at])

    def gelu(ref, at):
        bias = bias_up_ref[:, at].astype(F32)
        for start in range(0, tokens, LINES):
            lines = slice(start, start + LINES)
            v = ref[lines, :] + bias
            phi = 0.5 + 0.5 * lax.erf(v * 0.7071067811865476)
            active_ref[lines, at] = (v * phi).astype(BF)
            density = jnp.exp(-0.5 * v * v) * 0.3989422804014327
            slope_ref[lines, at] = (phi + v * density).astype(BF)

    def downward(at):
        branch_ref[...] += nn(active_ref[:, at], w_down_ref[at, :])

    branch_ref[...] = jnp.zeros_like(branch_ref)
    upward(first_ref, span(0))

    @pl.loop(0, count // 2)
    def _(i):
        upward(second_ref, span(2 * i + 1))
        gelu(first_ref, span(2 * i))
        downward(span(2 * i))
        upward(first_ref, span(jnp.minimum(2 * i + 2, count - 1)))
        gelu(second_ref, span(2 * i + 1))
        downward(span(2 * i + 1))

    sums = [0.0, 0.0, 0.0]
    for at in blocks(tokens):
        n, r = normed(hidden_ref[at, :].astype(F32) + branch_ref[at, :] + row(BIAS_DOWN))
        out_ref[at, :] = (n * row(GAIN_TWO) + row(SHIFT_TWO)).astype(BF)
        cot = cot_ref[at, :].astype(F32)
        grad = norm_back(cot, n, r, row(GAIN_TWO))
        grad_two_ref[at, :] = grad
        terms = (cot * n, cot, grad.astype(BF).astype(F32))
        sums = [earlier + fold(term) for earlier, term in zip(sums, terms)]
    for i, folded in enumerate(sums):
        sums_ref[i : i + 1] = total(folded)


def down_kernel(where_ref, active_ref, grad_two_ref, send_ref, keep_ref):
    core = where_ref[0]
    groups, rows = send_ref.shape[0], send_ref.shape[1]
    grad_branch = grad_two_ref[...].astype(BF)
    for i in range(groups):
        block = nn(active_ref[:, i * 2 * rows : (i + 1) * 2 * rows].T, grad_branch).astype(BF)
        low, high = block[:rows], block[rows:]
        keep_ref[i] = jnp.where(core == 0, low, high)
        send_ref[i] = jnp.where(core == 0, high, low)


def slope_kernel(
    slope_ref, grad_two_ref, w_down_ref, grad_up_ref, bias_up_ref, branch_ref
):
    count = w_down_ref.shape[0] // CHUNK
    span = lambda i: pl.ds(pl.multiple_of(i * CHUNK, CHUNK), CHUNK)

    branch_ref[...] = grad_two_ref[...].astype(BF)

    @pl.loop(0, count)
    def _(i):
        grad_active = nt(branch_ref[...], w_down_ref[span(i), :])
        grad_up = (grad_active * slope_ref[:, span(i)].astype(F32)).astype(BF)
        grad_up_ref[:, span(i)] = grad_up
        bias_up_ref[:, span(i)] = jnp.sum(grad_up.astype(F32), 0, keepdims=True)


def up_kernel(
    where_ref, hidden_ref, n_one_ref, r_one_ref, grad_up_ref, grad_two_ref, w_up_ref, w_out_ref, params_ref,
    own_ref, other_ref,
    grad_one_ref, grad_own_ref, grad_other_ref, sums_ref, send_ref, keep_ref,
    both_ref, turned_ref, grad_hidden_ref, grad_context_ref,
):
    half = grad_own_ref.shape[0]
    head, core = where_ref[1], where_ref[0]
    params = params_ref[...].astype(F32)
    row = lambda i: params[i : i + 1]
    groups, rows = send_ref.shape[0], send_ref.shape[1]
    tokens = hidden_ref.shape[0]
    turn_rows(hidden_ref[...].T, turned_ref, rows)

    @pl.loop(0, w_up_ref.shape[1] // CHUNK)
    def _(i):
        at = pl.ds(pl.multiple_of(i * CHUNK, CHUNK), CHUNK)
        grad_up = grad_up_ref[:, at]
        send_ref[:, :, at] = nn(turned_ref[1 - core], grad_up).astype(BF).reshape(groups, rows, CHUNK)
        keep_ref[:, :, at] = nn(turned_ref[core], grad_up).astype(BF).reshape(groups, rows, CHUNK)

    grad_hidden_ref[...] = nt(grad_up_ref[...], w_up_ref[...])
    sums = [0.0, 0.0, 0.0]
    for at in blocks(tokens):
        grad_hidden = grad_hidden_ref[at, :] + grad_two_ref[at, :]
        n_one = n_one_ref[at, :]
        grad_one = norm_back(grad_hidden, n_one, r_one_ref[at, :1], row(GAIN_ONE))
        grad_one_ref[at, :] = grad_one
        terms = (grad_hidden * n_one, grad_hidden, grad_one.astype(BF).astype(F32))
        sums = [earlier + fold(term) for earlier, term in zip(sums, terms)]
    for i, folded in enumerate(sums):
        sums_ref[i : i + 1] = total(folded)
    grad_attended = grad_one_ref[...].astype(BF)
    grad_context_ref[...] = nt(w_out_ref[...], grad_attended).astype(BF)
    own_at = pl.multiple_of(head * half, LANES)
    other_at = pl.multiple_of((1 - head) * half, LANES)
    both_ref[pl.ds(own_at, half), :] = own_ref[...]
    both_ref[pl.ds(other_at, half), :] = other_ref[...]
    turn_rows(both_ref[...], turned_ref, rows)
    ff = w_up_ref.shape[1]
    send_ref[:, :, ff:] = nn(turned_ref[1 - core], grad_attended).astype(BF).reshape(groups, rows, -1)
    keep_ref[:, :, ff:] = nn(turned_ref[core], grad_attended).astype(BF).reshape(groups, rows, -1)
    grad_own_ref[...] = grad_context_ref[pl.ds(own_at, half), :]
    grad_other_ref[...] = grad_context_ref[pl.ds(other_at, half), :]


def back_kernel(
    where_ref, turned_ref, mask_ref, qkv_own_ref, qkv_other_ref, stats_own_ref, stats_other_ref, context_own_ref,
    context_other_ref, grad_own_ref, grad_other_ref,
    send_ref, keep_ref, grads_ref, sums_ref,
    first_ref, second_ref,
):
    core = where_ref[0]
    width, tokens = context_own_ref.shape
    count = width // HEAD_DIM
    halves = (
        (qkv_own_ref, stats_own_ref, context_own_ref, grad_own_ref),
        (qkv_other_ref, stats_other_ref, context_other_ref, grad_other_ref),
    )

    def scaled(half, i):
        return (halves[half][3][head_lines(width, 0, i), :].astype(F32) * halves[half][1][i, 1:2, :]).astype(BF)

    def begin(ref, half, i):
        q, k, v = [halves[half][0][head_lines(width, part, i), :] for part in range(3)]
        ref[0] = tn(k, q)
        ref[1] = tn(v, scaled(half, i))

    def finish(ref, half, i):
        q, k, v = [halves[half][0][head_lines(width, part, i), :] for part in range(3)]
        grad = scaled(half, i)
        context = halves[half][2][head_lines(width, 0, i), :]
        inner = jnp.sum(grad.astype(F32) * context.astype(F32), 0, keepdims=True)
        held, moved = [], []
        for at in range(0, tokens, LANES):
            span = slice(at, at + LANES)
            weights = jnp.exp(ref[0, :, span] + mask_ref[:, span] - halves[half][1][i, 0:1, span])
            held.append(weights.astype(BF))
            moved.append((weights * (ref[1, :, span] - inner[:, span])).astype(BF))
        weights, grad_scores = jnp.concatenate(held, 1), jnp.concatenate(moved, 1)
        grads_ref[half, head_lines(width, 0, i), :] = nn(k, grad_scores).astype(BF) * 0.125
        grads_ref[half, head_lines(width, 1, i), :] = nt(q, grad_scores).astype(BF)
        grads_ref[half, head_lines(width, 2, i), :] = nt(grad, weights).astype(BF)

    begin(first_ref, 0, 0)

    @pl.loop(0, count)
    def _(i):
        begin(second_ref, 1, i)
        finish(first_ref, 0, i)
        begin(first_ref, 0, jnp.minimum(i + 1, count - 1))
        finish(second_ref, 1, i)

    weigh_heads(core, turned_ref, grads_ref, send_ref, keep_ref, 0, send_ref.shape[3])
    ones = jnp.ones((LANES, tokens), BF)
    for half in range(2):
        sums_ref[half] = nt(grads_ref[half], ones)


def weigh_heads(core, turned_ref, grads_ref, send_ref, keep_ref, start, columns):
    groups, rows = send_ref.shape[1:3]
    width, wide = grads_ref.shape[1] // 3, columns // 3
    for half in range(2):
        for out_ref, lines in ((send_ref, 1 - core), (keep_ref, core)):
            for part in range(3):
                at = part * width + start
                found = nt(turned_ref[lines], grads_ref[half, at : at + wide, :]).astype(BF)
                out_ref[half, :, :, part * wide : (part + 1) * wide] = found.reshape(groups, rows, wide)


def end_kernel(
    where_ref, turned_ref, grads_ref, sums_ref, sums_one_ref, sums_two_ref, bias_up_ref,
    send_ref, keep_ref,
    table_ref, flipped_ref, ext_ref,
):
    core, head = where_ref[0], where_ref[1]
    groups, rows, columns = send_ref.shape[1:]
    columns -= LANES
    width = grads_ref.shape[1] // 3
    weigh_heads(core, turned_ref, grads_ref, send_ref, keep_ref, width - columns // 3, columns)
    table_ref[...] = jnp.zeros_like(table_ref)
    table_ref[2:5] = sums_one_ref[0:3]
    table_ref[5:8] = sums_two_ref[0:3]
    flipped_ref[...] = table_ref[...].T
    lane = lax.broadcasted_iota(jnp.int32, (1, LANES), 1)
    for half, at in ((0, head), (1, 1 - head)):
        lines = pl.ds(pl.multiple_of(at * width, LANES), width)
        query, value = sums_ref[half, :width], sums_ref[half, 2 * width :]
        flipped_ref[lines] = jnp.where(lane == 0, query, jnp.where(lane == 1, value, flipped_ref[lines]))
    own = rows // 2
    table = flipped_ref[...].reshape(groups, 2, 2, own, LANES)
    ff = bias_up_ref.shape[1]
    spread = jnp.broadcast_to(bias_up_ref[...], (LANES, ff)).T.reshape(groups, 2, 2, ff // (4 * groups * rows), rows, LANES)
    lane = lax.broadcasted_iota(jnp.int32, (groups, rows, LANES), 2)
    for to_core in range(2):
        for to_head in range(2):
            block = jnp.concatenate([table[:, to_core, to_head], jnp.zeros((groups, rows - own, LANES), F32)], 1)
            for piece in range(spread.shape[3]):
                block = jnp.where(lane == 8 + piece, spread[:, to_core, to_head, piece], block)
            ext_ref[to_core, to_head] = block.astype(BF)
    for half, at in ((0, head), (1, 1 - head)):
        send_ref[half, :, :, columns:] = ext_ref[1 - core, at]
        keep_ref[half, :, :, columns:] = ext_ref[core, at]


def attend_back(where, turned, mask, own, other, grads, groups, count):
    width, tokens = own[2].shape
    rows = turned.shape[1] // groups
    kept = [v for pair in zip(own, other) for v in pair]
    block = ((2, groups, rows, 3 * count * HEAD_DIM), BF)
    return call(
        back_kernel,
        [block, block, ((2, 3 * width, tokens), BF), ((2, 3 * width, LANES), F32)],
        where, turned, mask, *kept, *grads,
        scratch=[pltpu.VMEM((2, tokens, tokens), F32), pltpu.VMEM((2, tokens, tokens), F32)],
        flops=2 * 10**11 // 3,
        moved=10 * 2**20,
        limit=14,
    )


def attend_end(where, turned, grads, groups, count, *sums):
    depth = 2 * turned.shape[1]
    rows = turned.shape[1] // groups
    block = ((2, groups, rows, 3 * count * HEAD_DIM + LANES), BF)
    return call(
        end_kernel,
        [block, block],
        where, turned, grads, *sums,
        scratch=[
            pltpu.VMEM((LANES, depth), F32), pltpu.VMEM((depth, LANES), F32),
            pltpu.VMEM((2, 2, groups, rows, LANES), BF),
        ],
        flops=2 * 10**11 // 3,
        moved=10 * 2**20,
        limit=8,
    )


def input_kernel(
    where_ref, grads_ref, mine_own_ref, mine_other_ref, theirs_own_ref, theirs_other_ref, grad_one_ref, out_ref
):
    depth, width = mine_own_ref.shape[1:]
    core = where_ref[0]
    plain = [grads_ref[half].T for half in range(2)]
    for at, weights_refs in ((core, (mine_own_ref, mine_other_ref)), (1 - core, (theirs_own_ref, theirs_other_ref))):
        lanes = pl.ds(pl.multiple_of(at * depth, LANES), depth)
        terms = [
            nt(plain[half][:, part * width : (part + 1) * width], weights_refs[half][part])
            for half in range(2)
            for part in range(3)
        ]
        out_ref[:, lanes] = (grad_one_ref[:, lanes] + sum(terms)).astype(BF)


def each(count, body):
    if count == 1:
        body(0)
    else:
        pl.loop(0, count)(body)


def open_kernel(cut, split, where_ref, *refs):
    count = split or 2
    terms, outs = refs[:count], refs[count:]
    head_send, head_own, low_own, *low_sends = outs
    low, head = where_ref[2], where_ref[1]
    size = len(low_sends) + 1

    def block(i, bits, half, columns):
        if split:
            return terms[0][half, i, bits, :, columns] + terms[1][half, i, bits, :, columns]
        return terms[0][i, bits, half, :, columns] + terms[1][i, bits, half, :, columns]

    def body(i):
        for bits in range(size):
            head_own[i, bits] = block(i, bits, 0 if split else head, slice(0, cut))
            head_send[i, bits] = block(i, bits, 1 if split else 1 - head, slice(0, cut))
        for flip, out in enumerate([low_own, *low_sends]):
            for half in range(2):
                if split != 4:
                    out[i, half] = block(i, low ^ flip, half, slice(cut, None))
                    continue
                wide = terms[0].shape[4] - cut
                out[i, half, :, :wide] = block(i, low ^ flip, half, slice(cut, None))
                out[i, half, :, wide:] = terms[2][half, i, low ^ flip] + terms[3][half, i, low ^ flip]

    each(head_own.shape[0], body)


def turn_kernel(split, size, where_ref, *refs):
    first, second, outs = refs[:2], refs[2 : 2 + size], refs[2 + size :]
    first_outs, (second_own, second_send) = outs[:size], outs[size:]
    low, head = where_ref[2], where_ref[1]
    own, other = (0, 1) if split else (head, 1 - head)

    def add(values, *at):
        return functools.reduce(jnp.add, [v[at] for v in values])

    def body(i):
        for flip, out in enumerate(first_outs):
            out[i] = add(first, i, low ^ flip)
        second_own[i] = add(second, i, own)
        second_send[i] = add(second, i, other)

    each(second_own.shape[0], body)


def last_kernel(counts, stage, where_ref, *refs):
    parts, at = [], 0
    for count in counts:
        parts.append(refs[at : at + count])
        at += count
    outs = refs[at:]
    index = where_ref[stage]
    size = len(outs)

    def body(i):
        for flip, out in enumerate(outs):
            start = 0
            for part in parts:
                columns = slice(start, start + part[0].shape[2])
                start = columns.stop
                values = [v[i * size + (index ^ flip)].astype(F32) for v in part]
                out[i, :, columns] = functools.reduce(jnp.add, values).astype(BF)

    each(outs[0].shape[0], body)


def part_kernel(cut, where_ref, *refs):
    terms, (first_own, first_send, second_own, second_send) = refs[:-4], refs[-4:]
    low, head = where_ref[2], where_ref[1]
    for out, index, columns in (
        (first_own, low, slice(0, cut)), (first_send, 1 - low, slice(0, cut)),
        (second_own, head, slice(cut, None)), (second_send, 1 - head, slice(cut, None)),
    ):
        out[...] = functools.reduce(jnp.add, [v[0, index, :, columns] for v in terms])


def close_parts_kernel(scale, *refs):
    out = refs[-1]
    cut = refs[0].shape[1]
    for columns, pair in ((slice(0, cut), refs[0:2]), (slice(cut, None), refs[2:4])):
        out[:, columns] = (pair[0][...].astype(F32) + pair[1][...].astype(F32)) * scale


def close_last_kernel(scale, wide_a, wide_b, *refs):
    terms, (out_ref, small_ref, spread_ref) = refs[:-3], refs[-3:]
    summed = functools.reduce(jnp.add, [v[0].astype(F32) for v in terms]) * scale
    rows, start = summed.shape[0], 3 * wide_a
    for part in range(3):
        out_ref[:, part, :wide_a] = summed[:, part * wide_a : (part + 1) * wide_a]
        out_ref[:, part, wide_a:] = summed[:, start + part * wide_b : start + (part + 1) * wide_b]
    lines = summed[:, 3 * (wide_a + wide_b) :].T
    small_ref[...] = lines[:8, : small_ref.shape[1]]
    for piece in range(spread_ref.shape[1] // rows):
        spread_ref[:, piece * rows : (piece + 1) * rows] = lines[8 + piece : 9 + piece, :rows]


def close_kernel(scale, *refs):
    refs[-1][...] = functools.reduce(jnp.add, [v[0].astype(F32) for v in refs[:-1]]) * scale


def pause_kernel(token_ref, out_ref):
    out_ref[...] = token_ref[...]


def pause(*others):
    token = after(jnp.zeros((8, LANES), F32), *others)
    return call(pause_kernel, [((8, LANES), F32)], token, flops=10**13, limit=2)[0]


def after(value, *others):
    return lax.optimization_barrier((value, *others))[0]


def pick(value, index, axis):
    return lax.dynamic_index_in_dim(value, index, axis, keepdims=False)


def on_device(
    inputs, cotangent, segment_ids, lengths, w_qkv, bias_query, bias_value, w_out, bias_out, gain_one,
    shift_one, w_up, bias_up, w_down, bias_down, gain_two, shift_two,
):
    width = w_out.shape[0]
    half = w_qkv.shape[2]
    ff = w_up.shape[1]
    tokens = inputs.shape[0]
    batch = lax.axis_size("batch")
    heads = lax.axis_size("head")
    place, head = lax.axis_index("batch"), lax.axis_index("head")
    core = place % 2
    scale = 1.0 / (lengths.shape[0] * batch)

    plan, bit, bits = [], 1, batch.bit_length() - 1
    if (bits - 1) % 2:
        plan.append((1, 2))
        bit = 2
    while bit < bits:
        plan.append((bit, 4))
        bit += 2
    halving = [(at, 2) for at in range(plan[0][0] + plan[0][1] // 2, bits)]
    where = jnp.stack([core, head] + [(place >> at) % many for at, many in plan + halving]).astype(jnp.int32)

    def swap_batch(value, flip):
        return lax.ppermute(value, "batch", [(i, i ^ flip) for i in range(batch)])

    def swap_head(value):
        return lax.ppermute(value, "head", [(0, 1), (1, 0)])

    depth = width // 2

    def columns(source, at):
        part = lax.dynamic_slice_in_dim(source, at * depth, depth, 0)
        return part.transpose(1, 0, 2)

    own_mine = columns(w_qkv, core)
    w_mine = swap_head(own_mine)
    small_own = jnp.stack([bias_query, bias_value])
    small_other = swap_head(after(small_own, own_mine))
    params = jnp.stack([bias_out, gain_one, shift_one, bias_down, gain_two, shift_two])
    ids = segment_ids.reshape(heads, tokens)
    bias_up = bias_up[None]
    prepared = (inputs, where, columns(after(w_qkv, own_mine), 1 - core), small_own, params, ids, bias_up)
    inputs, where, own_theirs, small_own, params, ids, bias_up = lax.optimization_barrier(prepared)

    mask, summed, turned, *kept_own = attend(
        where, inputs, small_own, own_mine, own_theirs, ids, lengths, w_out, params, turned_rows=width // batch
    )
    context_own = kept_own[2]
    w_mine = after(w_mine, context_own, small_other)
    w_theirs = swap_batch(w_mine, 1)
    kept_other = attend(where, inputs, small_other, w_mine, w_theirs, mask)
    context_other = kept_other[2]

    groups = batch // 2
    ffn_rows, up_rows = ff // batch, width // batch
    out, hidden, n_one, r_one, active, slope, grad_two, sums_two = call(
        ffn_kernel,
        [
            ((tokens, width), BF),
            ((tokens, width), BF),
            ((tokens, width), F32),
            ((tokens, LANES), F32),
            ((tokens, ff), BF),
            ((tokens, ff), BF),
            ((tokens, width), F32),
            ((8, width), F32),
        ],
        where, summed, context_other, w_out, params, w_up, bias_up, w_down, cotangent,
        scratch=[
            pltpu.VMEM((tokens, CHUNK), F32), pltpu.VMEM((tokens, CHUNK), F32), pltpu.VMEM((tokens, width), F32),
        ],
        flops=2 * 10**11 // 3, moved=30 * 2**20, limit=14,
    )
    down_send, down_keep = call(
        down_kernel,
        [((groups, ffn_rows, width), BF), ((groups, ffn_rows, width), BF)],
        where, active, grad_two,
        flops=6 * 10**10 // 3, moved=10 * 2**20, limit=12,
    )
    low, rest = plan[0], plan[1:]
    size = low[1]
    low_groups = groups // size

    def open_sum(values, cut, split=False, weigh=0):
        rows, columns = values[0].shape[-2] // (1 if split else heads), values[0].shape[-1]
        lead = (heads, low_groups, size) if split else (low_groups, size, heads)
        more = sum(v.shape[-1] for v in values[2::2])
        values = [v.reshape(*lead, rows, v.shape[-1]) for v in values]
        columns += more
        by_head, by_low = (low_groups, size, rows, cut), (low_groups, heads, rows, columns - cut)
        head_send, head_own, low_own, *low_sends = call(
            functools.partial(open_kernel, cut, len(values) if split else 0), [(by_head, BF)] * 2 + [(by_low, BF)] * size, where, *values,
            flops=weigh,
        )
        got = [swap_batch(v, flip << low[0]) for flip, v in enumerate(low_sends, 1)]
        return head_send, [head_own, swap_head(head_send)], [low_own, *got]

    def turn_sum(first, second, split=False, weigh=0):
        rows = first[0].shape[2]
        cut, more = first[0].shape[3], second[0].shape[3]
        outs = call(
            functools.partial(turn_kernel, split, size),
            [((low_groups, rows, cut), BF)] * size + [((low_groups, rows, more), BF)] * 2,
            where, *first, *second,
            flops=weigh,
        )
        got = [swap_batch(v, flip << low[0]) for flip, v in enumerate(outs[1:size], 1)]
        return outs[0], [outs[0], *got], [outs[size], swap_head(outs[size + 1])]

    def last_sum(*parts, stages=None, weigh=0):
        for bit, many in stages or rest:
            stage = 2 + (plan + halving).index((bit, many))
            rows, columns = parts[0][0].shape[1], sum(part[0].shape[2] for part in parts)
            left = parts[0][0].shape[0] // many
            outs = call(
                functools.partial(last_kernel, [len(part) for part in parts], stage),
                [((left, rows, columns), BF)] * many,
                where, *[v for part in parts for v in part],
                flops=weigh,
            )
            parts = [[outs[0]] + [swap_batch(v, flip << bit) for flip, v in enumerate(outs[1:], 1)]]
        return outs[0], parts[0]

    def close_sum(values, weigh=0):
        return call(functools.partial(close_kernel, scale), [(values[0].shape[1:], F32)], *values, flops=weigh)[0]

    def late(values, *before):
        return [values[0]] + [after(v, *before) for v in values[1:]]

    down = [down_keep, swap_batch(down_send, 1)]
    grad_up, sum_bias_up = call(
        slope_kernel,
        [((tokens, ff), BF), ((1, ff), F32)],
        slope, grad_two, w_down,
        scratch=[
            pltpu.VMEM((tokens, width), BF),
        ],
        flops=10**11 // 3, moved=10 * 2**20, limit=8,
    )
    down[1] = after(down[1], sum_bias_up)
    sent, down, down_low = open_sum(down, width // 2)
    grad_one, grad_own, grad_other, sums_one, up_send, up_keep = call(
        up_kernel,
        [
            ((tokens, width), F32),
            ((half, tokens), BF),
            ((half, tokens), BF),
            ((8, width), F32),
            ((groups, up_rows, ff + width), BF),
            ((groups, up_rows, ff + width), BF),
        ],
        where, hidden, n_one, r_one, after(grad_up, sent), grad_two, w_up, w_out, params, context_own, context_other,
        scratch=[
            pltpu.VMEM((width, tokens), BF),
            pltpu.VMEM((2, groups * up_rows, tokens), BF),
            pltpu.VMEM((tokens, width), F32),
            pltpu.VMEM((width, tokens), BF),
        ],
        limit=13,
        flops=2 * 10**11 // 3, moved=30 * 2**20,
    )
    up = [up_keep, swap_batch(up_send, 1)]
    early = size == heads and len(halving) == 2
    if early:
        flat = lambda v: v.reshape(low_groups, -1, v.shape[3])
        down_cut, down_rows = down[0].shape[3], down[0].shape[2]
        sent, down = last_sum(
            [flat(v) for v in late(down, grad_one)], [flat(v) for v in down_low], stages=halving[:1], weigh=WEIGH
        )
    else:
        sent, down, down_low = turn_sum(late(down, grad_one), down_low, weigh=WEIGH)
    sent, up, up_low = open_sum(late(up, sent), (ff + width) // 2)
    end = half // HEAD_DIM - 2
    weights = (own_mine, w_mine, own_theirs, w_theirs)
    qa_send, qa_keep, grads, sums = attend_back(
        where, turned, mask, kept_own, kept_other, (after(grad_own, sent), grad_other), groups, end
    )
    qa_got = swap_batch(qa_send, 1)
    if early:
        sent, down = last_sum(late(down, sums), stages=halving[1:])
    else:
        sent, down = last_sum(late(down, sums), down_low)
    sent, up, up_low = turn_sum(late(up, sent), up_low)
    qb_send, qb_keep = attend_end(
        where, turned, after(grads, sent), groups, 2, sums, sums_one, sums_two, sum_bias_up
    )
    input_grad = call(
        input_kernel,
        [((tokens, width), BF)],
        where, grads, *weights, grad_one,
        flops=10**10, moved=10 * 2**20, limit=10,
    )[0]
    qb_got = swap_batch(qb_send, 1)
    cut_a, cut_b = 3 * end * HEAD_DIM // 2, 2 * LANES
    sent, qa, qa_low = open_sum([qa_keep, after(qa_got, qb_keep)], cut_a, True)
    sent, up = last_sum(late(up, sent), up_low, stages=halving[:1], weigh=WEIGH)
    if early:
        by_low, by_head = (down_rows, down_cut), (down_rows, down[0].shape[2] - down_cut)
        outs = call(
            functools.partial(part_kernel, down_cut), [(by_low, BF)] * 2 + [(by_head, BF)] * 2,
            where, *[v.reshape(1, 2, down_rows, -1) for v in late(down, sent)],
        )
        down = [outs[0], swap_batch(outs[1], 1 << low[0]), outs[2], swap_head(outs[3])]
        sent = outs[1]
    sent, qb, qb_low = open_sum([qb_keep, after(qb_got, sent)], cut_b, True)
    sent, qa, qa_low = turn_sum(late(qa, sent), qa_low, True, weigh=WEIGH)
    if early:
        down = late(down, sent)
        sum_down = call(
            functools.partial(close_parts_kernel, scale), [((down_rows, down_cut + down[2].shape[1]), F32)], *down
        )[0]
    else:
        sum_down = close_sum(late(down, sent))
    sent, up = last_sum(late(up, sum_down), stages=halving[1:])
    sent, qb, qb_low = turn_sum(late(qb, sent), qb_low, True, weigh=WEIGH)
    sent, qkv = last_sum(late(qa, sent), qa_low, qb, qb_low)
    sum_up = close_sum(late(up, sent))
    own, pieces = up_rows // heads, ff // (heads * width)
    sum_qkv, small, spread = call(
        functools.partial(close_last_kernel, scale, end * HEAD_DIM, 2 * HEAD_DIM),
        [((up_rows, 3, half), F32), ((8, own), F32), ((1, pieces * up_rows), F32)],
        *qkv,
    )
    small = [small[i] for i in range(8)]
    spread = spread[0]
    return (
        out, input_grad, sum_qkv, small[0], small[1], sum_up[:, ff:], small[4], small[2], small[3],
        sum_up[:, :ff], spread, sum_down, small[7], small[5], small[6],
    )


def solution(mesh):
    rows = P(BOTH, None)
    placed = (rows, rows, P("batch"), P("batch"), P(None, None, "head"), P("head"), P("head")) + (P(),) * 10
    flat = P(BOTH)
    return jax.shard_map(
        on_device,
        mesh=mesh,
        in_specs=placed,
        out_specs=(
            rows, rows, P("batch", None, "head"), flat, flat, rows, flat, flat, flat, rows, flat, rows, flat,
            flat, flat,
        ),
        check_vma=False,
    )
```

```python
import functools

import jax
import jax.numpy as jnp
from jax import lax
from jax.experimental import pallas as pl
from jax.experimental.pallas import tpu as pltpu
from jax.sharding import PartitionSpec as P

HEAD_DIM = 64
LANES = 128
BF = jnp.bfloat16
F32 = jnp.float32
BOTH = ("batch", "head")
VMEM = pl.BlockSpec(memory_space=pltpu.VMEM)
ANY = pl.BlockSpec(memory_space=pltpu.HBM)
SMEM = pl.BlockSpec(memory_space=pltpu.SMEM)


def nn(left, right):
    return lax.dot_general(left, right, (((1,), (0,)), ((), ())), preferred_element_type=F32)


def nt(left, right):
    return lax.dot_general(left, right, (((1,), (1,)), ((), ())), preferred_element_type=F32)


class Near:
    def __init__(self, value):
        self.value = value


class Far:
    def __init__(self, value):
        self.value = value


def call(kernel, outs, *operands, scratch=(), flops=0, moved=0, limit=16):
    specs = [
        ANY if isinstance(a, Far) else VMEM if isinstance(a, Near) or a.dtype != jnp.int32 else SMEM for a in operands
    ]
    operands = [a.value if isinstance(a, (Far, Near)) else a for a in operands]
    return pl.pallas_call(
        kernel,
        in_specs=specs,
        out_specs=[VMEM] * len(outs),
        out_shape=[jax.ShapeDtypeStruct(s, t) for s, t in outs],
        scratch_shapes=list(scratch),
        cost_estimate=pl.CostEstimate(flops=flops, bytes_accessed=moved, transcendentals=0),
        compiler_params=pltpu.CompilerParams(vmem_limit_bytes=limit * 2**20),
    )(*operands)


def tn(left, right):
    return lax.dot_general(left, right, (((0,), (0,)), ((), ())), preferred_element_type=F32)


def head_lines(width, part, number):
    return pl.ds(pl.multiple_of(part * width + number * HEAD_DIM, HEAD_DIM), HEAD_DIM)


def in_turn(count, first_ref, second_ref, begin, finish):
    begin(first_ref, 0)

    @pl.loop(0, count // 2)
    def _(i):
        begin(second_ref, 2 * i + 1)
        finish(first_ref, 2 * i)
        begin(first_ref, jnp.minimum(2 * i + 2, count - 1))
        finish(second_ref, 2 * i + 1)


def attend_kernel(given, turned_rows, where_ref, x_ref, bias_ref, mine_ref, theirs_ref, *refs):
    if given:
        mask_ref, qkv_ref, stats_ref, context_ref, first_ref, second_ref = refs
    else:
        (ids_ref, length_ref, w_out_ref, params_ref, mask_ref, summed_ref, turned_ref, qkv_ref, stats_ref, context_ref,
         first_ref, second_ref) = refs
        turn_rows(x_ref[...].T, turned_ref, turned_rows)
        mine_ids = ids_ref[pl.ds(where_ref[1], 1), :]
        columns = jnp.broadcast_to(mine_ids, (LANES, mine_ids.shape[1])).T
        position = lax.broadcasted_iota(jnp.int32, columns.shape, 0)
        live = position < length_ref[where_ref[1]]
        for at in range(0, mask_ref.shape[1], LANES):
            allowed = (columns == mine_ids[:, at : at + LANES]) & live
            mask_ref[:, at : at + LANES] = jnp.where(allowed, 0.0, -1e30)
    width, tokens = context_ref.shape
    depth = mine_ref.shape[1]
    mine = pl.ds(pl.multiple_of(where_ref[0] * depth, LANES), depth)
    theirs = pl.ds(pl.multiple_of((1 - where_ref[0]) * depth, LANES), depth)
    for part in range(3):
        projected = nn(x_ref[:, mine], mine_ref[part]) + nn(x_ref[:, theirs], theirs_ref[part])
        if part == 0:
            projected = (projected + bias_ref[0:1, :].astype(F32)) * 0.125
        if part == 2:
            projected = projected + bias_ref[1:2, :].astype(F32)
        qkv_ref[part * width : (part + 1) * width, :] = projected.astype(BF).T

    def begin(ref, i):
        ref[...] = tn(qkv_ref[head_lines(width, 1, i), :], qkv_ref[head_lines(width, 0, i), :])

    def finish(ref, i):
        held = []
        for at in range(0, tokens, LANES):
            columns = slice(at, at + LANES)
            scores = ref[:, columns] + mask_ref[:, columns]
            largest = jnp.max(scores, 0, keepdims=True)
            weights = jnp.exp(scores - largest)
            stats_ref[i, 0:1, columns] = largest
            stats_ref[i, 1:2, columns] = 1.0 / jnp.sum(weights, 0, keepdims=True)
            held.append(weights.astype(BF))
        context = nn(qkv_ref[head_lines(width, 2, i), :], jnp.concatenate(held, 1))
        context_ref[head_lines(width, 0, i), :] = (context * stats_ref[i, 1:2, :]).astype(BF)

    in_turn(width // HEAD_DIM, first_ref, second_ref, begin, finish)
    if not given:
        lines = pl.ds(pl.multiple_of(where_ref[1] * width, LANES), width)
        attended = tn(context_ref[...], w_out_ref[lines, :])
        summed_ref[...] = x_ref[...].astype(F32) + attended + params_ref[BIAS_OUT : BIAS_OUT + 1].astype(F32)


def attend(where, x, bias, mine, theirs, *rest, turned_rows=0):
    tokens, width = x.shape[0], mine.shape[2]
    given = len(rest) == 1
    return call(
        functools.partial(attend_kernel, given, turned_rows),
        ([] if given else [((tokens, tokens), F32), (x.shape, F32), ((2, x.shape[1] // 2, tokens), BF)])
        + [((3 * width, tokens), BF), ((width // HEAD_DIM, 8, tokens), F32), ((width, tokens), BF)],
        where, x, bias, mine, theirs, *(rest if given else [Near(rest[0]), *rest[1:]]),
        scratch=[pltpu.VMEM((tokens, tokens), F32), pltpu.VMEM((tokens, tokens), F32)],
        flops=10**11 // 3,
        moved=8 * 2**20,
        limit=8 if given else 12,
    )


def normed(summed):
    centre = summed - jnp.mean(summed, -1, keepdims=True)
    scale_inv = lax.rsqrt(jnp.mean(centre * centre, -1, keepdims=True) + 1e-05)
    return centre * scale_inv, scale_inv


def norm_back(grad, n, scale_inv, gain):
    scaled = grad * gain
    first = jnp.mean(scaled, -1, keepdims=True)
    second = jnp.mean(scaled * n, -1, keepdims=True)
    return scale_inv * (scaled - first - n * second)


def turn_rows(lines, turned_ref, rows):
    tokens = lines.shape[1]
    blocks = lines.reshape(-1, 2, rows, tokens)
    turned_ref[0] = blocks[:, 0].reshape(-1, tokens)
    turned_ref[1] = blocks[:, 1].reshape(-1, tokens)


BIAS_OUT, GAIN_ONE, SHIFT_ONE, BIAS_DOWN, GAIN_TWO, SHIFT_TWO = range(6)


CHUNK = 512
WEIGH = 10**12 // 30
LINES = 16


def blocks(count):
    return [slice(at, at + LINES) for at in range(0, count, LINES)]


def fold(value):
    return jnp.sum(value.reshape(-1, 8, value.shape[-1]), 0)


def total(folded):
    return jnp.sum(folded, 0, keepdims=True)


def ffn_kernel(
    where_ref, summed_ref, other_ref, w_out_ref, params_ref, w_up_ref, bias_up_ref, w_down_ref, cot_ref,
    out_ref, hidden_ref, n_one_ref, r_one_ref, active_ref, slope_ref, grad_two_ref, sums_ref,
    first_ref, second_ref, branch_ref,
):
    half = other_ref.shape[0]
    tokens, width = summed_ref.shape
    head = where_ref[1]
    count = w_up_ref.shape[1] // CHUNK
    span = lambda i: pl.ds(pl.multiple_of(i * CHUNK, CHUNK), CHUNK)

    params = params_ref[...].astype(F32)
    row = lambda i: params[i : i + 1]
    other_at = pl.multiple_of((1 - head) * half, LANES)
    branch_ref[...] = tn(other_ref[...], w_out_ref[pl.ds(other_at, half), :])

    for at in blocks(tokens):
        n, r = normed(summed_ref[at, :] + branch_ref[at, :])
        n_one_ref[at, :] = n
        r_one_ref[at, :] = jnp.broadcast_to(r, (LINES, LANES))
        hidden_ref[at, :] = (n * row(GAIN_ONE) + row(SHIFT_ONE)).astype(BF)

    def upward(ref, at):
        ref[...] = nn(hidden_ref[...], w_up_ref[:, at])

    def gelu(ref, at):
        bias = bias_up_ref[:, at].astype(F32)
        for start in range(0, tokens, LINES):
            lines = slice(start, start + LINES)
            v = ref[lines, :] + bias
            phi = 0.5 + 0.5 * lax.erf(v * 0.7071067811865476)
            active_ref[lines, at] = (v * phi).astype(BF)
            density = jnp.exp(-0.5 * v * v) * 0.3989422804014327
            slope_ref[lines, at] = (phi + v * density).astype(BF)

    def downward(at):
        branch_ref[...] += nn(active_ref[:, at], w_down_ref[at, :])

    branch_ref[...] = jnp.zeros_like(branch_ref)
    upward(first_ref, span(0))

    @pl.loop(0, count // 2)
    def _(i):
        upward(second_ref, span(2 * i + 1))
        gelu(first_ref, span(2 * i))
        downward(span(2 * i))
        upward(first_ref, span(jnp.minimum(2 * i + 2, count - 1)))
        gelu(second_ref, span(2 * i + 1))
        downward(span(2 * i + 1))

    sums = [0.0, 0.0, 0.0]
    for at in blocks(tokens):
        n, r = normed(hidden_ref[at, :].astype(F32) + branch_ref[at, :] + row(BIAS_DOWN))
        out_ref[at, :] = (n * row(GAIN_TWO) + row(SHIFT_TWO)).astype(BF)
        cot = cot_ref[at, :].astype(F32)
        grad = norm_back(cot, n, r, row(GAIN_TWO))
        grad_two_ref[at, :] = grad
        terms = (cot * n, cot, grad.astype(BF).astype(F32))
        sums = [earlier + fold(term) for earlier, term in zip(sums, terms)]
    for i, folded in enumerate(sums):
        sums_ref[i : i + 1] = total(folded)


def down_kernel(where_ref, active_ref, grad_two_ref, send_ref, keep_ref):
    core = where_ref[0]
    groups, rows = send_ref.shape[0], send_ref.shape[1]
    grad_branch = grad_two_ref[...].astype(BF)
    for i in range(groups):
        block = nn(active_ref[:, i * 2 * rows : (i + 1) * 2 * rows].T, grad_branch).astype(BF)
        low, high = block[:rows], block[rows:]
        keep_ref[i] = jnp.where(core == 0, low, high)
        send_ref[i] = jnp.where(core == 0, high, low)


def slope_kernel(
    slope_ref, grad_two_ref, w_down_ref, grad_up_ref, bias_up_ref, branch_ref
):
    count = w_down_ref.shape[0] // CHUNK
    span = lambda i: pl.ds(pl.multiple_of(i * CHUNK, CHUNK), CHUNK)

    branch_ref[...] = grad_two_ref[...].astype(BF)

    @pl.loop(0, count)
    def _(i):
        grad_active = nt(branch_ref[...], w_down_ref[span(i), :])
        grad_up = (grad_active * slope_ref[:, span(i)].astype(F32)).astype(BF)
        grad_up_ref[:, span(i)] = grad_up
        bias_up_ref[:, span(i)] = jnp.sum(grad_up.astype(F32), 0, keepdims=True)


def up_kernel(
    where_ref, hidden_ref, n_one_ref, r_one_ref, grad_up_ref, grad_two_ref, w_up_ref, w_out_ref, params_ref,
    own_ref, other_ref,
    grad_one_ref, grad_own_ref, grad_other_ref, sums_ref, send_ref, keep_ref,
    both_ref, turned_ref, grad_hidden_ref, grad_context_ref,
):
    half = grad_own_ref.shape[0]
    head, core = where_ref[1], where_ref[0]
    params = params_ref[...].astype(F32)
    row = lambda i: params[i : i + 1]
    groups, rows = send_ref.shape[0], send_ref.shape[1]
    tokens = hidden_ref.shape[0]
    turn_rows(hidden_ref[...].T, turned_ref, rows)

    @pl.loop(0, w_up_ref.shape[1] // CHUNK)
    def _(i):
        at = pl.ds(pl.multiple_of(i * CHUNK, CHUNK), CHUNK)
        grad_up = grad_up_ref[:, at]
        send_ref[:, :, at] = nn(turned_ref[1 - core], grad_up).astype(BF).reshape(groups, rows, CHUNK)
        keep_ref[:, :, at] = nn(turned_ref[core], grad_up).astype(BF).reshape(groups, rows, CHUNK)

    grad_hidden_ref[...] = nt(grad_up_ref[...], w_up_ref[...])
    sums = [0.0, 0.0, 0.0]
    for at in blocks(tokens):
        grad_hidden = grad_hidden_ref[at, :] + grad_two_ref[at, :]
        n_one = n_one_ref[at, :]
        grad_one = norm_back(grad_hidden, n_one, r_one_ref[at, :1], row(GAIN_ONE))
        grad_one_ref[at, :] = grad_one
        terms = (grad_hidden * n_one, grad_hidden, grad_one.astype(BF).astype(F32))
        sums = [earlier + fold(term) for earlier, term in zip(sums, terms)]
    for i, folded in enumerate(sums):
        sums_ref[i : i + 1] = total(folded)
    grad_attended = grad_one_ref[...].astype(BF)
    grad_context_ref[...] = nt(w_out_ref[...], grad_attended).astype(BF)
    own_at = pl.multiple_of(head * half, LANES)
    other_at = pl.multiple_of((1 - head) * half, LANES)
    both_ref[pl.ds(own_at, half), :] = own_ref[...]
    both_ref[pl.ds(other_at, half), :] = other_ref[...]
    turn_rows(both_ref[...], turned_ref, rows)
    ff = w_up_ref.shape[1]
    send_ref[:, :, ff:] = nn(turned_ref[1 - core], grad_attended).astype(BF).reshape(groups, rows, -1)
    keep_ref[:, :, ff:] = nn(turned_ref[core], grad_attended).astype(BF).reshape(groups, rows, -1)
    grad_own_ref[...] = grad_context_ref[pl.ds(own_at, half), :]
    grad_other_ref[...] = grad_context_ref[pl.ds(other_at, half), :]


def back_kernel(
    where_ref, turned_ref, mask_ref, qkv_own_ref, qkv_other_ref, stats_own_ref, stats_other_ref, context_own_ref,
    context_other_ref, grad_own_ref, grad_other_ref,
    send_ref, keep_ref, grads_ref, sums_ref,
    first_ref, second_ref,
):
    core = where_ref[0]
    width, tokens = context_own_ref.shape
    count = width // HEAD_DIM
    halves = (
        (qkv_own_ref, stats_own_ref, context_own_ref, grad_own_ref),
        (qkv_other_ref, stats_other_ref, context_other_ref, grad_other_ref),
    )

    def scaled(half, i):
        return (halves[half][3][head_lines(width, 0, i), :].astype(F32) * halves[half][1][i, 1:2, :]).astype(BF)

    def begin(ref, half, i):
        q, k, v = [halves[half][0][head_lines(width, part, i), :] for part in range(3)]
        ref[0] = tn(k, q)
        ref[1] = tn(v, scaled(half, i))

    def finish(ref, half, i):
        q, k, v = [halves[half][0][head_lines(width, part, i), :] for part in range(3)]
        grad = scaled(half, i)
        context = halves[half][2][head_lines(width, 0, i), :]
        inner = jnp.sum(grad.astype(F32) * context.astype(F32), 0, keepdims=True)
        held, moved = [], []
        for at in range(0, tokens, LANES):
            span = slice(at, at + LANES)
            weights = jnp.exp(ref[0, :, span] + mask_ref[:, span] - halves[half][1][i, 0:1, span])
            held.append(weights.astype(BF))
            moved.append((weights * (ref[1, :, span] - inner[:, span])).astype(BF))
        weights, grad_scores = jnp.concatenate(held, 1), jnp.concatenate(moved, 1)
        grads_ref[half, head_lines(width, 0, i), :] = nn(k, grad_scores).astype(BF) * 0.125
        grads_ref[half, head_lines(width, 1, i), :] = nt(q, grad_scores).astype(BF)
        grads_ref[half, head_lines(width, 2, i), :] = nt(grad, weights).astype(BF)

    begin(first_ref, 0, 0)

    @pl.loop(0, count)
    def _(i):
        begin(second_ref, 1, i)
        finish(first_ref, 0, i)
        begin(first_ref, 0, jnp.minimum(i + 1, count - 1))
        finish(second_ref, 1, i)

    weigh_heads(core, turned_ref, grads_ref, send_ref, keep_ref, 0, send_ref.shape[3])
    ones = jnp.ones((LANES, tokens), BF)
    for half in range(2):
        sums_ref[half] = nt(grads_ref[half], ones)


def weigh_heads(core, turned_ref, grads_ref, send_ref, keep_ref, start, columns):
    groups, rows = send_ref.shape[1:3]
    width, wide = grads_ref.shape[1] // 3, columns // 3
    for half in range(2):
        for out_ref, lines in ((send_ref, 1 - core), (keep_ref, core)):
            for part in range(3):
                at = part * width + start
                found = nt(turned_ref[lines], grads_ref[half, at : at + wide, :]).astype(BF)
                out_ref[half, :, :, part * wide : (part + 1) * wide] = found.reshape(groups, rows, wide)


def end_kernel(
    where_ref, turned_ref, grads_ref, sums_ref, sums_one_ref, sums_two_ref, bias_up_ref,
    send_ref, keep_ref,
    table_ref, flipped_ref, ext_ref,
):
    core, head = where_ref[0], where_ref[1]
    groups, rows, columns = send_ref.shape[1:]
    columns -= LANES
    width = grads_ref.shape[1] // 3
    weigh_heads(core, turned_ref, grads_ref, send_ref, keep_ref, width - columns // 3, columns)
    table_ref[...] = jnp.zeros_like(table_ref)
    table_ref[2:5] = sums_one_ref[0:3]
    table_ref[5:8] = sums_two_ref[0:3]
    flipped_ref[...] = table_ref[...].T
    lane = lax.broadcasted_iota(jnp.int32, (1, LANES), 1)
    for half, at in ((0, head), (1, 1 - head)):
        lines = pl.ds(pl.multiple_of(at * width, LANES), width)
        query, value = sums_ref[half, :width], sums_ref[half, 2 * width :]
        flipped_ref[lines] = jnp.where(lane == 0, query, jnp.where(lane == 1, value, flipped_ref[lines]))
    own = rows // 2
    table = flipped_ref[...].reshape(groups, 2, 2, own, LANES)
    ff = bias_up_ref.shape[1]
    spread = jnp.broadcast_to(bias_up_ref[...], (LANES, ff)).T.reshape(groups, 2, 2, ff // (4 * groups * rows), rows, LANES)
    lane = lax.broadcasted_iota(jnp.int32, (groups, rows, LANES), 2)
    for to_core in range(2):
        for to_head in range(2):
            block = jnp.concatenate([table[:, to_core, to_head], jnp.zeros((groups, rows - own, LANES), F32)], 1)
            for piece in range(spread.shape[3]):
                block = jnp.where(lane == 8 + piece, spread[:, to_core, to_head, piece], block)
            ext_ref[to_core, to_head] = block.astype(BF)
    for half, at in ((0, head), (1, 1 - head)):
        send_ref[half, :, :, columns:] = ext_ref[1 - core, at]
        keep_ref[half, :, :, columns:] = ext_ref[core, at]


def attend_back(where, turned, mask, own, other, grads, groups, count):
    width, tokens = own[2].shape
    rows = turned.shape[1] // groups
    kept = [v for pair in zip(own, other) for v in pair]
    block = ((2, groups, rows, 3 * count * HEAD_DIM), BF)
    return call(
        back_kernel,
        [block, block, ((2, 3 * width, tokens), BF), ((2, 3 * width, LANES), F32)],
        where, turned, mask, *kept, *grads,
        scratch=[pltpu.VMEM((2, tokens, tokens), F32), pltpu.VMEM((2, tokens, tokens), F32)],
        flops=2 * 10**11 // 3,
        moved=10 * 2**20,
        limit=14,
    )


def attend_end(where, turned, grads, groups, count, *sums):
    depth = 2 * turned.shape[1]
    rows = turned.shape[1] // groups
    block = ((2, groups, rows, 3 * count * HEAD_DIM + LANES), BF)
    return call(
        end_kernel,
        [block, block],
        where, turned, grads, *sums,
        scratch=[
            pltpu.VMEM((LANES, depth), F32), pltpu.VMEM((depth, LANES), F32),
            pltpu.VMEM((2, 2, groups, rows, LANES), BF),
        ],
        flops=2 * 10**11 // 3,
        moved=10 * 2**20,
        limit=8,
    )


def input_kernel(
    where_ref, grads_ref, mine_own_ref, mine_other_ref, theirs_own_ref, theirs_other_ref, grad_one_ref, out_ref
):
    depth, width = mine_own_ref.shape[1:]
    core = where_ref[0]
    plain = [grads_ref[half].T for half in range(2)]
    for at, weights_refs in ((core, (mine_own_ref, mine_other_ref)), (1 - core, (theirs_own_ref, theirs_other_ref))):
        lanes = pl.ds(pl.multiple_of(at * depth, LANES), depth)
        terms = [
            nt(plain[half][:, part * width : (part + 1) * width], weights_refs[half][part])
            for half in range(2)
            for part in range(3)
        ]
        out_ref[:, lanes] = (grad_one_ref[:, lanes] + sum(terms)).astype(BF)


def each(count, body):
    if count == 1:
        body(0)
    else:
        pl.loop(0, count)(body)


def open_kernel(cut, split, where_ref, *refs):
    count = split or 2
    terms, outs = refs[:count], refs[count:]
    head_send, head_own, low_own, *low_sends = outs
    low, head = where_ref[2], where_ref[1]
    size = len(low_sends) + 1

    def block(i, bits, half, columns):
        if split:
            return terms[0][half, i, bits, :, columns] + terms[1][half, i, bits, :, columns]
        return terms[0][i, bits, half, :, columns] + terms[1][i, bits, half, :, columns]

    def body(i):
        for bits in range(size):
            head_own[i, bits] = block(i, bits, 0 if split else head, slice(0, cut))
            head_send[i, bits] = block(i, bits, 1 if split else 1 - head, slice(0, cut))
        for flip, out in enumerate([low_own, *low_sends]):
            for half in range(2):
                if split != 4:
                    out[i, half] = block(i, low ^ flip, half, slice(cut, None))
                    continue
                wide = terms[0].shape[4] - cut
                out[i, half, :, :wide] = block(i, low ^ flip, half, slice(cut, None))
                out[i, half, :, wide:] = terms[2][half, i, low ^ flip] + terms[3][half, i, low ^ flip]

    each(head_own.shape[0], body)


def turn_kernel(split, size, where_ref, *refs):
    first, second, outs = refs[:2], refs[2 : 2 + size], refs[2 + size :]
    first_outs, (second_own, second_send) = outs[:size], outs[size:]
    low, head = where_ref[2], where_ref[1]
    own, other = (0, 1) if split else (head, 1 - head)

    def add(values, *at):
        return functools.reduce(jnp.add, [v[at] for v in values])

    def body(i):
        for flip, out in enumerate(first_outs):
            out[i] = add(first, i, low ^ flip)
        second_own[i] = add(second, i, own)
        second_send[i] = add(second, i, other)

    each(second_own.shape[0], body)


def last_kernel(counts, stage, where_ref, *refs):
    parts, at = [], 0
    for count in counts:
        parts.append(refs[at : at + count])
        at += count
    outs = refs[at:]
    index = where_ref[stage]
    size = len(outs)

    def body(i):
        for flip, out in enumerate(outs):
            start = 0
            for part in parts:
                columns = slice(start, start + part[0].shape[2])
                start = columns.stop
                values = [v[i * size + (index ^ flip)].astype(F32) for v in part]
                out[i, :, columns] = functools.reduce(jnp.add, values).astype(BF)

    each(outs[0].shape[0], body)


def part_kernel(cut, where_ref, *refs):
    terms, (first_own, first_send, second_own, second_send) = refs[:-4], refs[-4:]
    low, head = where_ref[2], where_ref[1]
    for out, index, columns in (
        (first_own, low, slice(0, cut)), (first_send, 1 - low, slice(0, cut)),
        (second_own, head, slice(cut, None)), (second_send, 1 - head, slice(cut, None)),
    ):
        out[...] = functools.reduce(jnp.add, [v[0, index, :, columns] for v in terms])


def close_parts_kernel(scale, *refs):
    out = refs[-1]
    cut = refs[0].shape[1]
    for columns, pair in ((slice(0, cut), refs[0:2]), (slice(cut, None), refs[2:4])):
        out[:, columns] = (pair[0][...].astype(F32) + pair[1][...].astype(F32)) * scale


def close_last_kernel(scale, wide_a, wide_b, *refs):
    terms, (out_ref, small_ref, spread_ref) = refs[:-3], refs[-3:]
    summed = functools.reduce(jnp.add, [v[0].astype(F32) for v in terms]) * scale
    rows, start = summed.shape[0], 3 * wide_a
    for part in range(3):
        out_ref[:, part, :wide_a] = summed[:, part * wide_a : (part + 1) * wide_a]
        out_ref[:, part, wide_a:] = summed[:, start + part * wide_b : start + (part + 1) * wide_b]
    lines = summed[:, 3 * (wide_a + wide_b) :].T
    small_ref[...] = lines[:8, : small_ref.shape[1]]
    for piece in range(spread_ref.shape[1] // rows):
        spread_ref[:, piece * rows : (piece + 1) * rows] = lines[8 + piece : 9 + piece, :rows]


def close_kernel(scale, *refs):
    refs[-1][...] = functools.reduce(jnp.add, [v[0].astype(F32) for v in refs[:-1]]) * scale


def pause_kernel(token_ref, out_ref):
    out_ref[...] = token_ref[...]


def pause(*others):
    token = after(jnp.zeros((8, LANES), F32), *others)
    return call(pause_kernel, [((8, LANES), F32)], token, flops=10**13, limit=2)[0]


def after(value, *others):
    return lax.optimization_barrier((value, *others))[0]


def pick(value, index, axis):
    return lax.dynamic_index_in_dim(value, index, axis, keepdims=False)


def on_device(
    inputs, cotangent, segment_ids, lengths, w_qkv, bias_query, bias_value, w_out, bias_out, gain_one,
    shift_one, w_up, bias_up, w_down, bias_down, gain_two, shift_two,
):
    width = w_out.shape[0]
    half = w_qkv.shape[2]
    ff = w_up.shape[1]
    tokens = inputs.shape[0]
    batch = lax.axis_size("batch")
    heads = lax.axis_size("head")
    place, head = lax.axis_index("batch"), lax.axis_index("head")
    core = place % 2
    scale = 1.0 / (lengths.shape[0] * batch)

    plan, bit, bits = [], 1, batch.bit_length() - 1
    if (bits - 1) % 2:
        plan.append((1, 2))
        bit = 2
    while bit < bits:
        plan.append((bit, 4))
        bit += 2
    halving = [(at, 2) for at in range(plan[0][0] + plan[0][1] // 2, bits)]
    where = jnp.stack([core, head] + [(place >> at) % many for at, many in plan + halving]).astype(jnp.int32)

    def swap_batch(value, flip):
        return lax.ppermute(value, "batch", [(i, i ^ flip) for i in range(batch)])

    def swap_head(value):
        return lax.ppermute(value, "head", [(0, 1), (1, 0)])

    depth = width // 2

    def columns(source, at):
        part = lax.dynamic_slice_in_dim(source, at * depth, depth, 0)
        return part.transpose(1, 0, 2)

    own_mine = columns(w_qkv, core)
    w_mine = swap_head(own_mine)
    small_own = jnp.stack([bias_query, bias_value])
    small_other = swap_head(after(small_own, own_mine))
    params = jnp.stack([bias_out, gain_one, shift_one, bias_down, gain_two, shift_two])
    ids = segment_ids.reshape(heads, tokens)
    bias_up = bias_up[None]
    prepared = (inputs, where, columns(after(w_qkv, own_mine), 1 - core), small_own, params, ids, bias_up)
    inputs, where, own_theirs, small_own, params, ids, bias_up = lax.optimization_barrier(prepared)

    mask, summed, turned, *kept_own = attend(
        where, inputs, small_own, own_mine, own_theirs, ids, lengths, w_out, params, turned_rows=width // batch
    )
    context_own = kept_own[2]
    w_mine = after(w_mine, context_own, small_other)
    w_theirs = swap_batch(w_mine, 1)
    kept_other = attend(where, inputs, small_other, w_mine, w_theirs, mask)
    context_other = kept_other[2]

    groups = batch // 2
    ffn_rows, up_rows = ff // batch, width // batch
    out, hidden, n_one, r_one, active, slope, grad_two, sums_two = call(
        ffn_kernel,
        [
            ((tokens, width), BF),
            ((tokens, width), BF),
            ((tokens, width), F32),
            ((tokens, LANES), F32),
            ((tokens, ff), BF),
            ((tokens, ff), BF),
            ((tokens, width), F32),
            ((8, width), F32),
        ],
        where, summed, context_other, w_out, params, w_up, bias_up, w_down, cotangent,
        scratch=[
            pltpu.VMEM((tokens, CHUNK), F32), pltpu.VMEM((tokens, CHUNK), F32), pltpu.VMEM((tokens, width), F32),
        ],
        flops=2 * 10**11 // 3, moved=30 * 2**20, limit=14,
    )
    down_send, down_keep = call(
        down_kernel,
        [((groups, ffn_rows, width), BF), ((groups, ffn_rows, width), BF)],
        where, active, grad_two,
        flops=6 * 10**10 // 3, moved=10 * 2**20, limit=12,
    )
    low, rest = plan[0], plan[1:]
    size = low[1]
    low_groups = groups // size

    def open_sum(values, cut, split=False, weigh=0):
        rows, columns = values[0].shape[-2] // (1 if split else heads), values[0].shape[-1]
        lead = (heads, low_groups, size) if split else (low_groups, size, heads)
        more = sum(v.shape[-1] for v in values[2::2])
        values = [v.reshape(*lead, rows, v.shape[-1]) for v in values]
        columns += more
        by_head, by_low = (low_groups, size, rows, cut), (low_groups, heads, rows, columns - cut)
        head_send, head_own, low_own, *low_sends = call(
            functools.partial(open_kernel, cut, len(values) if split else 0), [(by_head, BF)] * 2 + [(by_low, BF)] * size, where, *values,
            flops=weigh,
        )
        got = [swap_batch(v, flip << low[0]) for flip, v in enumerate(low_sends, 1)]
        return head_send, [head_own, swap_head(head_send)], [low_own, *got]

    def turn_sum(first, second, split=False, weigh=0):
        rows = first[0].shape[2]
        cut, more = first[0].shape[3], second[0].shape[3]
        outs = call(
            functools.partial(turn_kernel, split, size),
            [((low_groups, rows, cut), BF)] * size + [((low_groups, rows, more), BF)] * 2,
            where, *first, *second,
            flops=weigh,
        )
        got = [swap_batch(v, flip << low[0]) for flip, v in enumerate(outs[1:size], 1)]
        return outs[0], [outs[0], *got], [outs[size], swap_head(outs[size + 1])]

    def last_sum(*parts, stages=None, weigh=0):
        for bit, many in stages or rest:
            stage = 2 + (plan + halving).index((bit, many))
            rows, columns = parts[0][0].shape[1], sum(part[0].shape[2] for part in parts)
            left = parts[0][0].shape[0] // many
            outs = call(
                functools.partial(last_kernel, [len(part) for part in parts], stage),
                [((left, rows, columns), BF)] * many,
                where, *[v for part in parts for v in part],
                flops=weigh,
            )
            parts = [[outs[0]] + [swap_batch(v, flip << bit) for flip, v in enumerate(outs[1:], 1)]]
        return outs[0], parts[0]

    def close_sum(values, weigh=0):
        return call(functools.partial(close_kernel, scale), [(values[0].shape[1:], F32)], *values, flops=weigh)[0]

    def late(values, *before):
        return [values[0]] + [after(v, *before) for v in values[1:]]

    down = [down_keep, swap_batch(down_send, 1)]
    grad_up, sum_bias_up = call(
        slope_kernel,
        [((tokens, ff), BF), ((1, ff), F32)],
        slope, grad_two, w_down,
        scratch=[
            pltpu.VMEM((tokens, width), BF),
        ],
        flops=10**11 // 3, moved=10 * 2**20, limit=8,
    )
    down[1] = after(down[1], sum_bias_up)
    sent, down, down_low = open_sum(down, width // 2)
    grad_one, grad_own, grad_other, sums_one, up_send, up_keep = call(
        up_kernel,
        [
            ((tokens, width), F32),
            ((half, tokens), BF),
            ((half, tokens), BF),
            ((8, width), F32),
            ((groups, up_rows, ff + width), BF),
            ((groups, up_rows, ff + width), BF),
        ],
        where, hidden, n_one, r_one, after(grad_up, sent), grad_two, w_up, w_out, params, context_own, context_other,
        scratch=[
            pltpu.VMEM((width, tokens), BF),
            pltpu.VMEM((2, groups * up_rows, tokens), BF),
            pltpu.VMEM((tokens, width), F32),
            pltpu.VMEM((width, tokens), BF),
        ],
        limit=13,
        flops=2 * 10**11 // 3, moved=30 * 2**20,
    )
    up = [up_keep, swap_batch(up_send, 1)]
    early = size == heads and len(halving) == 2
    if early:
        flat = lambda v: v.reshape(low_groups, -1, v.shape[3])
        down_cut, down_rows = down[0].shape[3], down[0].shape[2]
        sent, down = last_sum(
            [flat(v) for v in late(down, grad_one)], [flat(v) for v in down_low], stages=halving[:1], weigh=WEIGH
        )
    else:
        sent, down, down_low = turn_sum(late(down, grad_one), down_low, weigh=WEIGH)
    sent, up, up_low = open_sum(late(up, sent), (ff + width) // 2)
    end = half // HEAD_DIM - 2
    weights = (own_mine, w_mine, own_theirs, w_theirs)
    qa_send, qa_keep, grads, sums = attend_back(
        where, turned, mask, kept_own, kept_other, (after(grad_own, sent), grad_other), groups, end
    )
    qa_got = swap_batch(qa_send, 1)
    if early:
        sent, down = last_sum(late(down, sums), stages=halving[1:])
    else:
        sent, down = last_sum(late(down, sums), down_low)
    sent, up, up_low = turn_sum(late(up, sent), up_low)
    qb_send, qb_keep = attend_end(
        where, turned, after(grads, sent), groups, 2, sums, sums_one, sums_two, sum_bias_up
    )
    cut_a, cut_b = 3 * end * HEAD_DIM // 2, 2 * LANES
    sent, qa, qa_low = open_sum([qa_keep, after(qa_got, qb_keep)], cut_a, True)
    input_grad = call(
        input_kernel,
        [((tokens, width), BF)],
        where, after(grads, sent), *weights, grad_one,
        flops=WEIGH, moved=10 * 2**20, limit=10,
    )[0]
    if early:
        down[1] = after(down[1], input_grad)
        up[0] = after(up[0], down[1])
    sent, up = last_sum(late(up, input_grad), up_low, stages=halving[:1])
    qb_got = swap_batch(after(qb_send, sent), 1)
    sent, qa, qa_low = turn_sum(late(qa, sent), qa_low, True, weigh=WEIGH)
    sent, qb, qb_low = open_sum([qb_keep, after(qb_got, sent)], cut_b, True)
    sent, up = last_sum(late(up, sent), stages=halving[1:])
    sent, qb, qb_low = turn_sum(late(qb, sent), qb_low, True, weigh=WEIGH)
    sent, qkv = last_sum(late(qa, sent), qa_low, qb, qb_low)
    sum_up = close_sum(late(up, sent))
    if early:
        by_low, by_head = (down_rows, down_cut), (down_rows, down[0].shape[2] - down_cut)
        outs = call(
            functools.partial(part_kernel, down_cut), [(by_low, BF)] * 2 + [(by_head, BF)] * 2,
            where, *[v.reshape(1, 2, down_rows, -1) for v in [after(down[0], sum_up), *down[1:]]],
        )
        down = [outs[0], swap_batch(outs[1], 1 << low[0]), outs[2], swap_head(outs[3])]
        sum_down = call(
            functools.partial(close_parts_kernel, scale), [((down_rows, down_cut + down[2].shape[1]), F32)], *down
        )[0]
    else:
        sum_down = close_sum(late(down, sum_up))
    own, pieces = up_rows // heads, ff // (heads * width)
    sum_qkv, small, spread = call(
        functools.partial(close_last_kernel, scale, end * HEAD_DIM, 2 * HEAD_DIM),
        [((up_rows, 3, half), F32), ((8, own), F32), ((1, pieces * up_rows), F32)],
        *qkv,
    )
    small = [small[i] for i in range(8)]
    spread = spread[0]
    return (
        out, input_grad, sum_qkv, small[0], small[1], sum_up[:, ff:], small[4], small[2], small[3],
        sum_up[:, :ff], spread, sum_down, small[7], small[5], small[6],
    )


def solution(mesh):
    rows = P(BOTH, None)
    placed = (rows, rows, P("batch"), P("batch"), P(None, None, "head"), P("head"), P("head")) + (P(),) * 10
    flat = P(BOTH)
    return jax.shard_map(
        on_device,
        mesh=mesh,
        in_specs=placed,
        out_specs=(
            rows, rows, P("batch", None, "head"), flat, flat, rows, flat, flat, flat, rows, flat, rows, flat,
            flat, flat,
        ),
        check_vma=False,
    )
```

```python
import functools

import jax
import jax.numpy as jnp
from jax import lax
from jax.experimental import pallas as pl
from jax.experimental.pallas import tpu as pltpu
from jax.sharding import PartitionSpec as P

HEAD_DIM = 64
LANES = 128
BF = jnp.bfloat16
F32 = jnp.float32
BOTH = ("batch", "head")
VMEM = pl.BlockSpec(memory_space=pltpu.VMEM)
ANY = pl.BlockSpec(memory_space=pltpu.HBM)
SMEM = pl.BlockSpec(memory_space=pltpu.SMEM)


def nn(left, right):
    return lax.dot_general(left, right, (((1,), (0,)), ((), ())), preferred_element_type=F32)


def nt(left, right):
    return lax.dot_general(left, right, (((1,), (1,)), ((), ())), preferred_element_type=F32)


class Near:
    def __init__(self, value):
        self.value = value


class Far:
    def __init__(self, value):
        self.value = value


def call(kernel, outs, *operands, scratch=(), flops=0, moved=0, limit=16):
    specs = [
        ANY if isinstance(a, Far) else VMEM if isinstance(a, Near) or a.dtype != jnp.int32 else SMEM for a in operands
    ]
    operands = [a.value if isinstance(a, (Far, Near)) else a for a in operands]
    return pl.pallas_call(
        kernel,
        in_specs=specs,
        out_specs=[VMEM] * len(outs),
        out_shape=[jax.ShapeDtypeStruct(s, t) for s, t in outs],
        scratch_shapes=list(scratch),
        cost_estimate=pl.CostEstimate(flops=flops, bytes_accessed=moved, transcendentals=0),
        compiler_params=pltpu.CompilerParams(vmem_limit_bytes=limit * 2**20),
    )(*operands)


def tn(left, right):
    return lax.dot_general(left, right, (((0,), (0,)), ((), ())), preferred_element_type=F32)


def head_lines(width, part, number):
    return pl.ds(pl.multiple_of(part * width + number * HEAD_DIM, HEAD_DIM), HEAD_DIM)


def in_turn(count, first_ref, second_ref, begin, finish):
    begin(first_ref, 0)

    @pl.loop(0, count // 2)
    def _(i):
        begin(second_ref, 2 * i + 1)
        finish(first_ref, 2 * i)
        begin(first_ref, jnp.minimum(2 * i + 2, count - 1))
        finish(second_ref, 2 * i + 1)


def attend_kernel(given, turned_rows, where_ref, x_ref, bias_ref, mine_ref, theirs_ref, *refs):
    if given:
        mask_ref, qkv_ref, stats_ref, context_ref, first_ref, second_ref = refs
    else:
        (ids_ref, length_ref, w_out_ref, mask_ref, summed_ref, turned_ref, qkv_ref, stats_ref, context_ref,
         first_ref, second_ref) = refs
        turn_rows(x_ref[...].T, turned_ref, turned_rows)
        spans = mask_ref.shape[0] // LANES
        mine_ids = jnp.concatenate([ids_ref[pl.ds(where_ref[1] * spans + i, 1), :] for i in range(spans)], 1)
        columns = jnp.broadcast_to(mine_ids, (LANES, mine_ids.shape[1])).T
        position = lax.broadcasted_iota(jnp.int32, columns.shape, 0)
        live = position < length_ref[where_ref[1]]
        for at in range(0, mask_ref.shape[1], LANES):
            allowed = (columns == mine_ids[:, at : at + LANES]) & live
            mask_ref[:, at : at + LANES] = jnp.where(allowed, 0.0, -1e30)
    width, tokens = context_ref.shape
    depth = mine_ref.shape[1]
    mine = pl.ds(pl.multiple_of(where_ref[0] * depth, LANES), depth)
    theirs = pl.ds(pl.multiple_of((1 - where_ref[0]) * depth, LANES), depth)
    for part in range(3):
        projected = nn(x_ref[:, mine], mine_ref[part]) + nn(x_ref[:, theirs], theirs_ref[part])
        if part == 0:
            projected = (projected + bias_ref[0:1, :width].astype(F32)) * 0.125
        if part == 2:
            projected = projected + bias_ref[0:1, width:].astype(F32)
        qkv_ref[part * width : (part + 1) * width, :] = projected.astype(BF).T

    def begin(ref, i):
        ref[...] = tn(qkv_ref[head_lines(width, 1, i), :], qkv_ref[head_lines(width, 0, i), :])

    def finish(ref, i):
        held = []
        for at in range(0, tokens, LANES):
            columns = slice(at, at + LANES)
            scores = ref[:, columns] + mask_ref[:, columns]
            largest = jnp.max(scores, 0, keepdims=True)
            weights = jnp.exp(scores - largest)
            stats_ref[i, 0:1, columns] = largest
            stats_ref[i, 1:2, columns] = 1.0 / jnp.sum(weights, 0, keepdims=True)
            held.append(weights.astype(BF))
        context = nn(qkv_ref[head_lines(width, 2, i), :], jnp.concatenate(held, 1))
        context_ref[head_lines(width, 0, i), :] = (context * stats_ref[i, 1:2, :]).astype(BF)

    in_turn(width // HEAD_DIM, first_ref, second_ref, begin, finish)
    if not given:
        lines = pl.ds(pl.multiple_of(where_ref[1] * width, LANES), width)
        attended = tn(context_ref[...], w_out_ref[lines, :])
        summed_ref[...] = x_ref[...].astype(F32) + attended


def attend(where, x, bias, mine, theirs, *rest, turned_rows=0):
    tokens, width = x.shape[0], mine.shape[2]
    given = len(rest) == 1
    return call(
        functools.partial(attend_kernel, given, turned_rows),
        ([] if given else [((tokens, tokens), F32), (x.shape, F32), ((2, x.shape[1] // 2, tokens), BF)])
        + [((3 * width, tokens), BF), ((width // HEAD_DIM, 8, tokens), F32), ((width, tokens), BF)],
        where, x, bias, mine, theirs, *(rest if given else [Near(rest[0]), *rest[1:]]),
        scratch=[pltpu.VMEM((tokens, tokens), F32), pltpu.VMEM((tokens, tokens), F32)],
        flops=10**11 // 3,
        moved=8 * 2**20,
        limit=8 if given else 12,
    )


def lines_kernel(*refs):
    out_ref = refs[-1]
    width, line = out_ref.shape[1], 0
    for ref in refs[:-1]:
        for at in range(0, ref.shape[0], width):
            out_ref[line : line + 1, :] = ref[pl.ds(at, width)].astype(F32).reshape(1, width)
            line += 1


def pair_kernel(first_ref, second_ref, out_ref):
    half = first_ref.shape[0]
    out_ref[:, :half] = first_ref[...].astype(F32).reshape(1, half)
    out_ref[:, half:] = second_ref[...].astype(F32).reshape(1, half)


def gather_kernel(where_ref, first_ref, second_ref, third_ref, out_ref):
    rows = first_ref.shape[1]
    low = jnp.bitwise_and(where_ref[2], 1)
    out_ref[:, pl.ds(pl.multiple_of(low * rows, rows), rows), :] = first_ref[...]
    out_ref[:, pl.ds(pl.multiple_of((1 - low) * rows, rows), rows), :] = third_ref[...]
    out_ref[:, 2 * rows :, :] = second_ref[...]


def normed(summed):
    centre = summed - jnp.mean(summed, -1, keepdims=True)
    scale_inv = lax.rsqrt(jnp.mean(centre * centre, -1, keepdims=True) + 1e-05)
    return centre * scale_inv, scale_inv


def norm_back(grad, n, scale_inv, gain):
    scaled = grad * gain
    first = jnp.mean(scaled, -1, keepdims=True)
    second = jnp.mean(scaled * n, -1, keepdims=True)
    return scale_inv * (scaled - first - n * second)


def turn_rows(lines, turned_ref, rows):
    tokens = lines.shape[1]
    blocks = lines.reshape(-1, 2, rows, tokens)
    turned_ref[0] = blocks[:, 0].reshape(-1, tokens)
    turned_ref[1] = blocks[:, 1].reshape(-1, tokens)


BIAS_OUT, GAIN_ONE, SHIFT_ONE, BIAS_DOWN, GAIN_TWO, SHIFT_TWO, BIAS_UP = range(7)


CHUNK = 512
WEIGH = 10**12 // 30
LINES = 16


def blocks(count):
    return [slice(at, at + LINES) for at in range(0, count, LINES)]


def fold(value):
    return jnp.sum(value.reshape(-1, 8, value.shape[-1]), 0)


def total(folded):
    return jnp.sum(folded, 0, keepdims=True)


def ffn_kernel(
    where_ref, summed_ref, other_ref, w_out_ref, params_ref, w_up_ref, w_down_ref, cot_ref,
    out_ref, hidden_ref, n_one_ref, r_one_ref, active_ref, slope_ref, grad_two_ref, sums_ref,
    first_ref, second_ref, branch_ref, bias_ref,
):
    half = other_ref.shape[0]
    tokens, width = summed_ref.shape
    head = where_ref[1]
    count = w_up_ref.shape[1] // CHUNK
    span = lambda i: pl.ds(pl.multiple_of(i * CHUNK, CHUNK), CHUNK)

    params = params_ref[...].astype(F32)
    row = lambda i: params[i : i + 1]
    for i in range(bias_ref.shape[1] // width):
        bias_ref[:, i * width : (i + 1) * width] = row(BIAS_UP + i)
    other_at = pl.multiple_of((1 - head) * half, LANES)
    branch_ref[...] = tn(other_ref[...], w_out_ref[pl.ds(other_at, half), :])

    for at in blocks(tokens):
        n, r = normed(summed_ref[at, :] + branch_ref[at, :] + row(BIAS_OUT))
        n_one_ref[at, :] = n
        r_one_ref[at, :] = jnp.broadcast_to(r, (LINES, LANES))
        hidden_ref[at, :] = (n * row(GAIN_ONE) + row(SHIFT_ONE)).astype(BF)

    def upward(ref, at):
        ref[...] = nn(hidden_ref[...], w_up_ref[:, at])

    def gelu(ref, at):
        bias = bias_ref[:, at]
        for start in range(0, tokens, LINES):
            lines = slice(start, start + LINES)
            v = ref[lines, :] + bias
            phi = 0.5 + 0.5 * lax.erf(v * 0.7071067811865476)
            active_ref[lines, at] = (v * phi).astype(BF)
            density = jnp.exp(-0.5 * v * v) * 0.3989422804014327
            slope_ref[lines, at] = (phi + v * density).astype(BF)

    def downward(at):
        branch_ref[...] += nn(active_ref[:, at], w_down_ref[at, :])

    branch_ref[...] = jnp.zeros_like(branch_ref)
    upward(first_ref, span(0))

    @pl.loop(0, count // 2)
    def _(i):
        upward(second_ref, span(2 * i + 1))
        gelu(first_ref, span(2 * i))
        downward(span(2 * i))
        upward(first_ref, span(jnp.minimum(2 * i + 2, count - 1)))
        gelu(second_ref, span(2 * i + 1))
        downward(span(2 * i + 1))

    sums = [0.0, 0.0, 0.0]
    for at in blocks(tokens):
        n, r = normed(hidden_ref[at, :].astype(F32) + branch_ref[at, :] + row(BIAS_DOWN))
        out_ref[at, :] = (n * row(GAIN_TWO) + row(SHIFT_TWO)).astype(BF)
        cot = cot_ref[at, :].astype(F32)
        grad = norm_back(cot, n, r, row(GAIN_TWO))
        grad_two_ref[at, :] = grad
        terms = (cot * n, cot, grad.astype(BF).astype(F32))
        sums = [earlier + fold(term) for earlier, term in zip(sums, terms)]
    for i, folded in enumerate(sums):
        sums_ref[i : i + 1] = total(folded)


def down_kernel(where_ref, active_ref, grad_two_ref, send_ref, keep_ref):
    core = where_ref[0]
    groups, rows = send_ref.shape[0], send_ref.shape[1]
    grad_branch = grad_two_ref[...].astype(BF)
    for i in range(groups):
        block = nn(active_ref[:, i * 2 * rows : (i + 1) * 2 * rows].T, grad_branch).astype(BF)
        low, high = block[:rows], block[rows:]
        keep_ref[i] = jnp.where(core == 0, low, high)
        send_ref[i] = jnp.where(core == 0, high, low)


def slope_kernel(
    slope_ref, grad_two_ref, w_down_ref, grad_up_ref, bias_up_ref, branch_ref
):
    count = w_down_ref.shape[0] // CHUNK
    span = lambda i: pl.ds(pl.multiple_of(i * CHUNK, CHUNK), CHUNK)

    branch_ref[...] = grad_two_ref[...].astype(BF)

    @pl.loop(0, count)
    def _(i):
        grad_active = nt(branch_ref[...], w_down_ref[span(i), :])
        grad_up = (grad_active * slope_ref[:, span(i)].astype(F32)).astype(BF)
        grad_up_ref[:, span(i)] = grad_up
        bias_up_ref[:, span(i)] = jnp.sum(grad_up.astype(F32), 0, keepdims=True)


def up_kernel(
    where_ref, hidden_ref, n_one_ref, r_one_ref, grad_up_ref, grad_two_ref, w_up_ref, w_out_ref, params_ref,
    own_ref, other_ref,
    grad_one_ref, grad_own_ref, grad_other_ref, sums_ref, send_ref, keep_ref,
    both_ref, turned_ref, grad_hidden_ref, grad_context_ref,
):
    half = grad_own_ref.shape[0]
    head, core = where_ref[1], where_ref[0]
    params = params_ref[...].astype(F32)
    row = lambda i: params[i : i + 1]
    groups, rows = send_ref.shape[0], send_ref.shape[1]
    tokens = hidden_ref.shape[0]
    turn_rows(hidden_ref[...].T, turned_ref, rows)

    @pl.loop(0, w_up_ref.shape[1] // CHUNK)
    def _(i):
        at = pl.ds(pl.multiple_of(i * CHUNK, CHUNK), CHUNK)
        grad_up = grad_up_ref[:, at]
        send_ref[:, :, at] = nn(turned_ref[1 - core], grad_up).astype(BF).reshape(groups, rows, CHUNK)
        keep_ref[:, :, at] = nn(turned_ref[core], grad_up).astype(BF).reshape(groups, rows, CHUNK)

    grad_hidden_ref[...] = nt(grad_up_ref[...], w_up_ref[...])
    sums = [0.0, 0.0, 0.0]
    for at in blocks(tokens):
        grad_hidden = grad_hidden_ref[at, :] + grad_two_ref[at, :]
        n_one = n_one_ref[at, :]
        grad_one = norm_back(grad_hidden, n_one, r_one_ref[at, :1], row(GAIN_ONE))
        grad_one_ref[at, :] = grad_one
        terms = (grad_hidden * n_one, grad_hidden, grad_one.astype(BF).astype(F32))
        sums = [earlier + fold(term) for earlier, term in zip(sums, terms)]
    for i, folded in enumerate(sums):
        sums_ref[i : i + 1] = total(folded)
    grad_attended = grad_one_ref[...].astype(BF)
    grad_context_ref[...] = nt(w_out_ref[...], grad_attended).astype(BF)
    own_at = pl.multiple_of(head * half, LANES)
    other_at = pl.multiple_of((1 - head) * half, LANES)
    both_ref[pl.ds(own_at, half), :] = own_ref[...]
    both_ref[pl.ds(other_at, half), :] = other_ref[...]
    turn_rows(both_ref[...], turned_ref, rows)
    ff = w_up_ref.shape[1]
    send_ref[:, :, ff:] = nn(turned_ref[1 - core], grad_attended).astype(BF).reshape(groups, rows, -1)
    keep_ref[:, :, ff:] = nn(turned_ref[core], grad_attended).astype(BF).reshape(groups, rows, -1)
    grad_own_ref[...] = grad_context_ref[pl.ds(own_at, half), :]
    grad_other_ref[...] = grad_context_ref[pl.ds(other_at, half), :]


def back_kernel(
    where_ref, turned_ref, mask_ref, qkv_own_ref, qkv_other_ref, stats_own_ref, stats_other_ref, context_own_ref,
    context_other_ref, grad_own_ref, grad_other_ref,
    send_ref, keep_ref, grads_ref, sums_ref,
    first_ref, second_ref,
):
    core = where_ref[0]
    width, tokens = context_own_ref.shape
    count = width // HEAD_DIM
    halves = (
        (qkv_own_ref, stats_own_ref, context_own_ref, grad_own_ref),
        (qkv_other_ref, stats_other_ref, context_other_ref, grad_other_ref),
    )

    def scaled(half, i):
        return (halves[half][3][head_lines(width, 0, i), :].astype(F32) * halves[half][1][i, 1:2, :]).astype(BF)

    def begin(ref, half, i):
        q, k, v = [halves[half][0][head_lines(width, part, i), :] for part in range(3)]
        ref[0] = tn(k, q)
        ref[1] = tn(v, scaled(half, i))

    def finish(ref, half, i):
        q, k, v = [halves[half][0][head_lines(width, part, i), :] for part in range(3)]
        grad = scaled(half, i)
        context = halves[half][2][head_lines(width, 0, i), :]
        inner = jnp.sum(grad.astype(F32) * context.astype(F32), 0, keepdims=True)
        held, moved = [], []
        for at in range(0, tokens, LANES):
            span = slice(at, at + LANES)
            weights = jnp.exp(ref[0, :, span] + mask_ref[:, span] - halves[half][1][i, 0:1, span])
            held.append(weights.astype(BF))
            moved.append((weights * (ref[1, :, span] - inner[:, span])).astype(BF))
        weights, grad_scores = jnp.concatenate(held, 1), jnp.concatenate(moved, 1)
        grads_ref[half, head_lines(width, 0, i), :] = nn(k, grad_scores).astype(BF) * 0.125
        grads_ref[half, head_lines(width, 1, i), :] = nt(q, grad_scores).astype(BF)
        grads_ref[half, head_lines(width, 2, i), :] = nt(grad, weights).astype(BF)

    begin(first_ref, 0, 0)

    @pl.loop(0, count)
    def _(i):
        begin(second_ref, 1, i)
        finish(first_ref, 0, i)
        begin(first_ref, 0, jnp.minimum(i + 1, count - 1))
        finish(second_ref, 1, i)

    weigh_heads(core, turned_ref, grads_ref, send_ref, keep_ref, 0, send_ref.shape[3])
    ones = jnp.ones((LANES, tokens), BF)
    for half in range(2):
        sums_ref[half] = nt(grads_ref[half], ones)


def weigh_heads(core, turned_ref, grads_ref, send_ref, keep_ref, start, columns):
    groups, rows = send_ref.shape[1:3]
    width, wide = grads_ref.shape[1] // 3, columns // 3
    for half in range(2):
        for out_ref, lines in ((send_ref, 1 - core), (keep_ref, core)):
            for part in range(3):
                at = part * width + start
                found = nt(turned_ref[lines], grads_ref[half, at : at + wide, :]).astype(BF)
                out_ref[half, :, :, part * wide : (part + 1) * wide] = found.reshape(groups, rows, wide)


def end_kernel(
    where_ref, turned_ref, grads_ref, sums_ref, sums_one_ref, sums_two_ref, bias_up_ref,
    send_ref, keep_ref,
    table_ref, flipped_ref, ext_ref,
):
    core, head = where_ref[0], where_ref[1]
    groups, rows, columns = send_ref.shape[1:]
    columns -= LANES
    width = grads_ref.shape[1] // 3
    weigh_heads(core, turned_ref, grads_ref, send_ref, keep_ref, width - columns // 3, columns)
    table_ref[...] = jnp.zeros_like(table_ref)
    table_ref[2:5] = sums_one_ref[0:3]
    table_ref[5:8] = sums_two_ref[0:3]
    flipped_ref[...] = table_ref[...].T
    lane = lax.broadcasted_iota(jnp.int32, (1, LANES), 1)
    for half, at in ((0, head), (1, 1 - head)):
        lines = pl.ds(pl.multiple_of(at * width, LANES), width)
        query, value = sums_ref[half, :width], sums_ref[half, 2 * width :]
        flipped_ref[lines] = jnp.where(lane == 0, query, jnp.where(lane == 1, value, flipped_ref[lines]))
    own = rows // 2
    table = flipped_ref[...].reshape(groups, 2, 2, own, LANES)
    ff = bias_up_ref.shape[1]
    spread = jnp.broadcast_to(bias_up_ref[...], (LANES, ff)).T.reshape(groups, 2, 2, ff // (4 * groups * rows), rows, LANES)
    lane = lax.broadcasted_iota(jnp.int32, (groups, rows, LANES), 2)
    for to_core in range(2):
        for to_head in range(2):
            block = jnp.concatenate([table[:, to_core, to_head], jnp.zeros((groups, rows - own, LANES), F32)], 1)
            for piece in range(spread.shape[3]):
                block = jnp.where(lane == 8 + piece, spread[:, to_core, to_head, piece], block)
            ext_ref[to_core, to_head] = block.astype(BF)
    for half, at in ((0, head), (1, 1 - head)):
        send_ref[half, :, :, columns:] = ext_ref[1 - core, at]
        keep_ref[half, :, :, columns:] = ext_ref[core, at]


def attend_back(where, turned, mask, own, other, grads, groups, count):
    width, tokens = own[2].shape
    rows = turned.shape[1] // groups
    kept = [v for pair in zip(own, other) for v in pair]
    block = ((2, groups, rows, 3 * count * HEAD_DIM), BF)
    return call(
        back_kernel,
        [block, block, ((2, 3 * width, tokens), BF), ((2, 3 * width, LANES), F32)],
        where, turned, mask, *kept, *grads,
        scratch=[pltpu.VMEM((2, tokens, tokens), F32), pltpu.VMEM((2, tokens, tokens), F32)],
        flops=2 * 10**11 // 3,
        moved=10 * 2**20,
        limit=14,
    )


def attend_end(where, turned, grads, groups, count, *sums):
    depth = 2 * turned.shape[1]
    rows = turned.shape[1] // groups
    block = ((2, groups, rows, 3 * count * HEAD_DIM + LANES), BF)
    return call(
        end_kernel,
        [block, block],
        where, turned, grads, *sums,
        scratch=[
            pltpu.VMEM((LANES, depth), F32), pltpu.VMEM((depth, LANES), F32),
            pltpu.VMEM((2, 2, groups, rows, LANES), BF),
        ],
        flops=2 * 10**11 // 3,
        moved=10 * 2**20,
        limit=8,
    )


def input_kernel(
    where_ref, grads_ref, mine_own_ref, mine_other_ref, theirs_own_ref, theirs_other_ref, grad_one_ref, out_ref
):
    depth, width = mine_own_ref.shape[1:]
    core = where_ref[0]
    plain = [grads_ref[half].T for half in range(2)]
    for at, weights_refs in ((core, (mine_own_ref, mine_other_ref)), (1 - core, (theirs_own_ref, theirs_other_ref))):
        lanes = pl.ds(pl.multiple_of(at * depth, LANES), depth)
        terms = [
            nt(plain[half][:, part * width : (part + 1) * width], weights_refs[half][part])
            for half in range(2)
            for part in range(3)
        ]
        out_ref[:, lanes] = (grad_one_ref[:, lanes] + sum(terms)).astype(BF)


def each(count, body):
    if count == 1:
        body(0)
    else:
        pl.loop(0, count)(body)


def open_kernel(cut, split, where_ref, *refs):
    count = split or 2
    terms, outs = refs[:count], refs[count:]
    head_send, head_own, low_own, *low_sends = outs
    low, head = where_ref[2], where_ref[1]
    size = len(low_sends) + 1

    def block(i, bits, half, columns):
        if split:
            return terms[0][half, i, bits, :, columns] + terms[1][half, i, bits, :, columns]
        return terms[0][i, bits, half, :, columns] + terms[1][i, bits, half, :, columns]

    def body(i):
        for bits in range(size):
            head_own[i, bits] = block(i, bits, 0 if split else head, slice(0, cut))
            head_send[i, bits] = block(i, bits, 1 if split else 1 - head, slice(0, cut))
        for flip, out in enumerate([low_own, *low_sends]):
            for half in range(2):
                if split != 4:
                    out[i, half] = block(i, low ^ flip, half, slice(cut, None))
                    continue
                wide = terms[0].shape[4] - cut
                out[i, half, :, :wide] = block(i, low ^ flip, half, slice(cut, None))
                out[i, half, :, wide:] = terms[2][half, i, low ^ flip] + terms[3][half, i, low ^ flip]

    each(head_own.shape[0], body)


def turn_kernel(split, size, where_ref, *refs):
    first, second, outs = refs[:2], refs[2 : 2 + size], refs[2 + size :]
    first_outs, (second_own, second_send) = outs[:size], outs[size:]
    low, head = where_ref[2], where_ref[1]
    own, other = (0, 1) if split else (head, 1 - head)

    def add(values, *at):
        return functools.reduce(jnp.add, [v[at] for v in values])

    def body(i):
        for flip, out in enumerate(first_outs):
            out[i] = add(first, i, low ^ flip)
        second_own[i] = add(second, i, own)
        second_send[i] = add(second, i, other)

    each(second_own.shape[0], body)


def last_kernel(counts, stage, where_ref, *refs):
    parts, at = [], 0
    for count in counts:
        parts.append(refs[at : at + count])
        at += count
    outs = refs[at:]
    index = where_ref[stage]
    size = len(outs)

    def body(i):
        for flip, out in enumerate(outs):
            start = 0
            for part in parts:
                columns = slice(start, start + part[0].shape[2])
                start = columns.stop
                values = [v[i * size + (index ^ flip)].astype(F32) for v in part]
                out[i, :, columns] = functools.reduce(jnp.add, values).astype(BF)

    each(outs[0].shape[0], body)


def part_kernel(cut, where_ref, *refs):
    terms, (first_own, first_send, second_own, second_send) = refs[:-4], refs[-4:]
    low, head = where_ref[2], where_ref[1]
    for out, index, columns in (
        (first_own, low, slice(0, cut)), (first_send, 1 - low, slice(0, cut)),
        (second_own, head, slice(cut, None)), (second_send, 1 - head, slice(cut, None)),
    ):
        out[...] = functools.reduce(jnp.add, [v[0, index, :, columns] for v in terms])


def close_parts_kernel(scale, *refs):
    out = refs[-1]
    cut = refs[0].shape[1]
    for columns, pair in ((slice(0, cut), refs[0:2]), (slice(cut, None), refs[2:4])):
        out[:, columns] = (pair[0][...].astype(F32) + pair[1][...].astype(F32)) * scale


def close_last_kernel(scale, wide_a, wide_b, *refs):
    terms, (out_ref, small_ref, spread_ref) = refs[:-3], refs[-3:]
    summed = functools.reduce(jnp.add, [v[0].astype(F32) for v in terms]) * scale
    rows, start = summed.shape[0], 3 * wide_a
    for part in range(3):
        out_ref[:, part, :wide_a] = summed[:, part * wide_a : (part + 1) * wide_a]
        out_ref[:, part, wide_a:] = summed[:, start + part * wide_b : start + (part + 1) * wide_b]
    lines = summed[:, 3 * (wide_a + wide_b) :].T
    small_ref[...] = lines[:8, : small_ref.shape[1]]
    for piece in range(spread_ref.shape[1] // rows):
        spread_ref[:, piece * rows : (piece + 1) * rows] = lines[8 + piece : 9 + piece, :rows]


def close_kernel(scale, *refs):
    refs[-1][...] = functools.reduce(jnp.add, [v[0].astype(F32) for v in refs[:-1]]) * scale


def pause_kernel(token_ref, out_ref):
    out_ref[...] = token_ref[...]


def pause(*others):
    token = after(jnp.zeros((8, LANES), F32), *others)
    return call(pause_kernel, [((8, LANES), F32)], token, flops=10**13, limit=2)[0]


def after(value, *others):
    return lax.optimization_barrier((value, *others))[0]


def pick(value, index, axis):
    return lax.dynamic_index_in_dim(value, index, axis, keepdims=False)


def on_device(
    inputs, cotangent, segment_ids, lengths, w_qkv, bias_query, bias_value, w_out, bias_out, gain_one,
    shift_one, w_up, bias_up, w_down, bias_down, gain_two, shift_two,
):
    width = w_out.shape[0]
    half = w_qkv.shape[2]
    ff = w_up.shape[1]
    tokens = inputs.shape[0]
    batch = lax.axis_size("batch")
    heads = lax.axis_size("head")
    place, head = lax.axis_index("batch"), lax.axis_index("head")
    core = place % 2
    scale = 1.0 / (lengths.shape[0] * batch)

    plan, bit, bits = [], 1, batch.bit_length() - 1
    if (bits - 1) % 2:
        plan.append((1, 2))
        bit = 2
    while bit < bits:
        plan.append((bit, 4))
        bit += 2
    halving = [(at, 2) for at in range(plan[0][0] + plan[0][1] // 2, bits)]
    where = jnp.stack([core, head] + [(place >> at) % many for at, many in plan + halving]).astype(jnp.int32)

    def swap_batch(value, flip):
        return lax.ppermute(value, "batch", [(i, i ^ flip) for i in range(batch)])

    def swap_head(value):
        return lax.ppermute(value, "head", [(0, 1), (1, 0)])

    depth = width // 2

    def columns(source, at):
        part = lax.dynamic_slice_in_dim(source, at * depth, depth, 0)
        return part.transpose(1, 0, 2)

    third = depth // 3

    def piece(at):
        return lax.dynamic_slice_in_dim(w_qkv, core * depth + at * third, third, 0).transpose(1, 0, 2)

    early_piece = piece((place >> 1) % 2)
    w_first = swap_head(early_piece)
    late_piece = piece(after(jnp.int32(2), early_piece))
    w_second = swap_head(late_piece)
    pair = (after(bias_query, late_piece), bias_value)
    small_own = call(pair_kernel, [((1, width), F32)], *pair, limit=2)[0]
    small_other = swap_head(small_own)
    own_mine = columns(after(w_qkv, late_piece), core)
    w_third = swap_batch(w_first, 2)
    ids = segment_ids.reshape(-1, LANES)
    prepared = (inputs, where, columns(after(w_qkv, own_mine), 1 - core), small_own, ids)
    inputs, where, own_theirs, small_own, ids = lax.optimization_barrier(prepared)

    mask, summed, turned, *kept_own = attend(
        where, inputs, small_own, own_mine, own_theirs, ids, lengths, w_out, turned_rows=width // batch
    )
    context_own = kept_own[2]
    vectors = [bias_out, gain_one, shift_one, bias_down, gain_two, shift_two, bias_up]
    params = call(
        lines_kernel, [((BIAS_UP + ff // width, width), F32)], after(vectors[0], context_own), *vectors[1:], limit=2
    )[0]
    w_first, w_second, w_third = [after(v, context_own, small_other) for v in (w_first, w_second, w_third)]
    w_mine = call(gather_kernel, [(own_mine.shape, BF)], where, w_first, w_second, w_third, limit=6)[0]
    w_theirs = swap_batch(w_mine, 1)
    kept_other = attend(where, inputs, small_other, w_mine, w_theirs, mask)
    context_other = kept_other[2]

    groups = batch // 2
    ffn_rows, up_rows = ff // batch, width // batch
    out, hidden, n_one, r_one, active, slope, grad_two, sums_two = call(
        ffn_kernel,
        [
            ((tokens, width), BF),
            ((tokens, width), BF),
            ((tokens, width), F32),
            ((tokens, LANES), F32),
            ((tokens, ff), BF),
            ((tokens, ff), BF),
            ((tokens, width), F32),
            ((8, width), F32),
        ],
        where, summed, context_other, w_out, params, w_up, w_down, cotangent,
        scratch=[
            pltpu.VMEM((tokens, CHUNK), F32), pltpu.VMEM((tokens, CHUNK), F32), pltpu.VMEM((tokens, width), F32),
            pltpu.VMEM((1, ff), F32),
        ],
        flops=2 * 10**11 // 3, moved=30 * 2**20, limit=14,
    )
    down_send, down_keep = call(
        down_kernel,
        [((groups, ffn_rows, width), BF), ((groups, ffn_rows, width), BF)],
        where, active, grad_two,
        flops=6 * 10**10 // 3, moved=10 * 2**20, limit=12,
    )
    low, rest = plan[0], plan[1:]
    size = low[1]
    low_groups = groups // size

    def open_sum(values, cut, split=False, weigh=0):
        rows, columns = values[0].shape[-2] // (1 if split else heads), values[0].shape[-1]
        lead = (heads, low_groups, size) if split else (low_groups, size, heads)
        more = sum(v.shape[-1] for v in values[2::2])
        values = [v.reshape(*lead, rows, v.shape[-1]) for v in values]
        columns += more
        by_head, by_low = (low_groups, size, rows, cut), (low_groups, heads, rows, columns - cut)
        head_send, head_own, low_own, *low_sends = call(
            functools.partial(open_kernel, cut, len(values) if split else 0), [(by_head, BF)] * 2 + [(by_low, BF)] * size, where, *values,
            flops=weigh,
        )
        got = [swap_batch(v, flip << low[0]) for flip, v in enumerate(low_sends, 1)]
        return head_send, [head_own, swap_head(head_send)], [low_own, *got]

    def turn_sum(first, second, split=False, weigh=0):
        rows = first[0].shape[2]
        cut, more = first[0].shape[3], second[0].shape[3]
        outs = call(
            functools.partial(turn_kernel, split, size),
            [((low_groups, rows, cut), BF)] * size + [((low_groups, rows, more), BF)] * 2,
            where, *first, *second,
            flops=weigh,
        )
        got = [swap_batch(v, flip << low[0]) for flip, v in enumerate(outs[1:size], 1)]
        return outs[0], [outs[0], *got], [outs[size], swap_head(outs[size + 1])]

    def last_sum(*parts, stages=None, weigh=0):
        for bit, many in stages or rest:
            stage = 2 + (plan + halving).index((bit, many))
            rows, columns = parts[0][0].shape[1], sum(part[0].shape[2] for part in parts)
            left = parts[0][0].shape[0] // many
            outs = call(
                functools.partial(last_kernel, [len(part) for part in parts], stage),
                [((left, rows, columns), BF)] * many,
                where, *[v for part in parts for v in part],
                flops=weigh,
            )
            parts = [[outs[0]] + [swap_batch(v, flip << bit) for flip, v in enumerate(outs[1:], 1)]]
        return outs[0], parts[0]

    def close_sum(values, weigh=0):
        return call(functools.partial(close_kernel, scale), [(values[0].shape[1:], F32)], *values, flops=weigh)[0]

    def late(values, *before):
        return [values[0]] + [after(v, *before) for v in values[1:]]

    down = [down_keep, swap_batch(down_send, 1)]
    grad_up, sum_bias_up = call(
        slope_kernel,
        [((tokens, ff), BF), ((1, ff), F32)],
        slope, grad_two, w_down,
        scratch=[
            pltpu.VMEM((tokens, width), BF),
        ],
        flops=10**11 // 3, moved=10 * 2**20, limit=8,
    )
    down[1] = after(down[1], sum_bias_up)
    sent, down, down_low = open_sum(down, width // 2)
    grad_one, grad_own, grad_other, sums_one, up_send, up_keep = call(
        up_kernel,
        [
            ((tokens, width), F32),
            ((half, tokens), BF),
            ((half, tokens), BF),
            ((8, width), F32),
            ((groups, up_rows, ff + width), BF),
            ((groups, up_rows, ff + width), BF),
        ],
        where, hidden, n_one, r_one, after(grad_up, sent), grad_two, w_up, w_out, params, context_own, context_other,
        scratch=[
            pltpu.VMEM((width, tokens), BF),
            pltpu.VMEM((2, groups * up_rows, tokens), BF),
            pltpu.VMEM((tokens, width), F32),
            pltpu.VMEM((width, tokens), BF),
        ],
        limit=13,
        flops=2 * 10**11 // 3, moved=30 * 2**20,
    )
    up = [up_keep, swap_batch(up_send, 1)]
    early = size == heads and len(halving) == 2
    if early:
        flat = lambda v: v.reshape(low_groups, -1, v.shape[3])
        down_cut, down_rows = down[0].shape[3], down[0].shape[2]
        sent, down = last_sum(
            [flat(v) for v in late(down, grad_one)], [flat(v) for v in down_low], stages=halving[:1], weigh=WEIGH
        )
    else:
        sent, down, down_low = turn_sum(late(down, grad_one), down_low, weigh=WEIGH)
    sent, up, up_low = open_sum(late(up, sent), (ff + width) // 2)
    end = half // HEAD_DIM - 2
    weights = (own_mine, w_mine, own_theirs, w_theirs)
    qa_send, qa_keep, grads, sums = attend_back(
        where, turned, mask, kept_own, kept_other, (after(grad_own, sent), grad_other), groups, end
    )
    qa_got = swap_batch(qa_send, 1)
    if early:
        sent, down = last_sum(late(down, sums), stages=halving[1:])
    else:
        sent, down = last_sum(late(down, sums), down_low)
    sent, up, up_low = turn_sum(late(up, sent), up_low)
    qb_send, qb_keep = attend_end(
        where, turned, after(grads, sent), groups, 2, sums, sums_one, sums_two, sum_bias_up
    )
    cut_a, cut_b = 3 * end * HEAD_DIM // 2, 2 * LANES
    sent, qa, qa_low = open_sum([qa_keep, after(qa_got, qb_keep)], cut_a, True)
    input_grad = call(
        input_kernel,
        [((tokens, width), BF)],
        where, after(grads, sent), *weights, grad_one,
        flops=WEIGH, moved=10 * 2**20, limit=10,
    )[0]
    if early:
        down[1] = after(down[1], input_grad)
        up[0] = after(up[0], down[1])
    sent, up = last_sum(late(up, input_grad), up_low, stages=halving[:1])
    qb_got = swap_batch(after(qb_send, sent), 1)
    sent, qa, qa_low = turn_sum(late(qa, sent), qa_low, True, weigh=WEIGH)
    sent, qb, qb_low = open_sum([qb_keep, after(qb_got, sent)], cut_b, True)
    sent, up = last_sum(late(up, sent), stages=halving[1:])
    sent, qb, qb_low = turn_sum(late(qb, sent), qb_low, True, weigh=WEIGH)
    if early:
        by_low, by_head = (down_rows, down_cut), (down_rows, down[0].shape[2] - down_cut)
        outs = call(
            functools.partial(part_kernel, down_cut), [(by_low, BF)] * 2 + [(by_head, BF)] * 2,
            where, *[v.reshape(1, 2, down_rows, -1) for v in [after(down[0], sent), *down[1:]]],
        )
        down = [outs[0], swap_batch(outs[1], 1 << low[0]), outs[2], swap_head(outs[3])]
        sent = outs[1]
    sent, qkv = last_sum(late(qa, sent), qa_low, qb, qb_low)
    sum_up = close_sum(late(up, sent))
    if early:
        down = [down[0], after(down[1], sum_up), down[2], after(down[3], sum_up)]
        sum_down = call(
            functools.partial(close_parts_kernel, scale), [((down_rows, down_cut + down[2].shape[1]), F32)], *down
        )[0]
    else:
        sum_down = close_sum(late(down, sum_up))
    own, pieces = up_rows // heads, ff // (heads * width)
    sum_qkv, small, spread = call(
        functools.partial(close_last_kernel, scale, end * HEAD_DIM, 2 * HEAD_DIM),
        [((up_rows, 3, half), F32), ((8, own), F32), ((1, pieces * up_rows), F32)],
        *qkv,
    )
    small = [small[i] for i in range(8)]
    spread = spread[0]
    return (
        out, input_grad, sum_qkv, small[0], small[1], sum_up[:, ff:], small[4], small[2], small[3],
        sum_up[:, :ff], spread, sum_down, small[7], small[5], small[6],
    )


def solution(mesh):
    rows = P(BOTH, None)
    placed = (rows, rows, P("batch"), P("batch"), P(None, None, "head"), P("head"), P("head")) + (P(),) * 10
    flat = P(BOTH)
    return jax.shard_map(
        on_device,
        mesh=mesh,
        in_specs=placed,
        out_specs=(
            rows, rows, P("batch", None, "head"), flat, flat, rows, flat, flat, flat, rows, flat, rows, flat,
            flat, flat,
        ),
        check_vma=False,
    )
```

```python
import functools

import jax
import jax.numpy as jnp
from jax import lax
from jax.experimental import pallas as pl
from jax.experimental.pallas import tpu as pltpu
from jax.sharding import PartitionSpec as P

HEAD_DIM = 64
LANES = 128
BF = jnp.bfloat16
F32 = jnp.float32
BOTH = ("batch", "head")
VMEM = pl.BlockSpec(memory_space=pltpu.VMEM)
ANY = pl.BlockSpec(memory_space=pltpu.HBM)
SMEM = pl.BlockSpec(memory_space=pltpu.SMEM)


def nn(left, right):
    return lax.dot_general(left, right, (((1,), (0,)), ((), ())), preferred_element_type=F32)


def nt(left, right):
    return lax.dot_general(left, right, (((1,), (1,)), ((), ())), preferred_element_type=F32)


class Near:
    def __init__(self, value):
        self.value = value


class Far:
    def __init__(self, value):
        self.value = value


def call(kernel, outs, *operands, scratch=(), flops=0, moved=0, limit=16):
    specs = [
        ANY if isinstance(a, Far) else VMEM if isinstance(a, Near) or a.dtype != jnp.int32 else SMEM for a in operands
    ]
    operands = [a.value if isinstance(a, (Far, Near)) else a for a in operands]
    return pl.pallas_call(
        kernel,
        in_specs=specs,
        out_specs=[VMEM] * len(outs),
        out_shape=[jax.ShapeDtypeStruct(s, t) for s, t in outs],
        scratch_shapes=list(scratch),
        cost_estimate=pl.CostEstimate(flops=flops, bytes_accessed=moved, transcendentals=0),
        compiler_params=pltpu.CompilerParams(vmem_limit_bytes=limit * 2**20),
    )(*operands)


def tn(left, right):
    return lax.dot_general(left, right, (((0,), (0,)), ((), ())), preferred_element_type=F32)


def head_lines(width, part, number):
    return pl.ds(pl.multiple_of(part * width + number * HEAD_DIM, HEAD_DIM), HEAD_DIM)


def in_turn(count, first_ref, second_ref, begin, finish):
    begin(first_ref, 0)

    @pl.loop(0, count // 2)
    def _(i):
        begin(second_ref, 2 * i + 1)
        finish(first_ref, 2 * i)
        begin(first_ref, jnp.minimum(2 * i + 2, count - 1))
        finish(second_ref, 2 * i + 1)


def attend_kernel(given, turned_rows, where_ref, x_ref, bias_ref, mine_ref, theirs_ref, *refs):
    if given:
        mask_ref, qkv_ref, stats_ref, context_ref, first_ref, second_ref = refs
    else:
        (ids_ref, length_ref, w_out_ref, mask_ref, summed_ref, turned_ref, qkv_ref, stats_ref, context_ref,
         first_ref, second_ref) = refs
        turn_rows(x_ref[...].T, turned_ref, turned_rows)
        spans = mask_ref.shape[0] // LANES
        mine_ids = jnp.concatenate([ids_ref[pl.ds(where_ref[1] * spans + i, 1), :] for i in range(spans)], 1)
        columns = jnp.broadcast_to(mine_ids, (LANES, mine_ids.shape[1])).T
        position = lax.broadcasted_iota(jnp.int32, columns.shape, 0)
        live = position < length_ref[where_ref[1]]
        for at in range(0, mask_ref.shape[1], LANES):
            allowed = (columns == mine_ids[:, at : at + LANES]) & live
            mask_ref[:, at : at + LANES] = jnp.where(allowed, 0.0, -1e30)
    width, tokens = context_ref.shape
    depth = mine_ref.shape[1]
    mine = pl.ds(pl.multiple_of(where_ref[0] * depth, LANES), depth)
    theirs = pl.ds(pl.multiple_of((1 - where_ref[0]) * depth, LANES), depth)
    for part in range(3):
        projected = nn(x_ref[:, mine], mine_ref[part]) + nn(x_ref[:, theirs], theirs_ref[part])
        if part == 0:
            projected = (projected + bias_ref[0:1, :width].astype(F32)) * 0.125
        if part == 2:
            projected = projected + bias_ref[0:1, width:].astype(F32)
        qkv_ref[part * width : (part + 1) * width, :] = projected.astype(BF).T

    def begin(ref, i):
        ref[...] = tn(qkv_ref[head_lines(width, 1, i), :], qkv_ref[head_lines(width, 0, i), :])

    def finish(ref, i):
        held = []
        for at in range(0, tokens, LANES):
            columns = slice(at, at + LANES)
            scores = ref[:, columns] + mask_ref[:, columns]
            largest = jnp.max(scores, 0, keepdims=True)
            weights = jnp.exp(scores - largest)
            stats_ref[i, 0:1, columns] = largest
            stats_ref[i, 1:2, columns] = 1.0 / jnp.sum(weights, 0, keepdims=True)
            held.append(weights.astype(BF))
        context = nn(qkv_ref[head_lines(width, 2, i), :], jnp.concatenate(held, 1))
        context_ref[head_lines(width, 0, i), :] = (context * stats_ref[i, 1:2, :]).astype(BF)

    in_turn(width // HEAD_DIM, first_ref, second_ref, begin, finish)
    if not given:
        lines = pl.ds(pl.multiple_of(where_ref[1] * width, LANES), width)
        attended = tn(context_ref[...], w_out_ref[lines, :])
        summed_ref[...] = x_ref[...].astype(F32) + attended


def attend(where, x, bias, mine, theirs, *rest, turned_rows=0):
    tokens, width = x.shape[0], mine.shape[2]
    given = len(rest) == 1
    return call(
        functools.partial(attend_kernel, given, turned_rows),
        ([] if given else [((tokens, tokens), F32), (x.shape, F32), ((2, x.shape[1] // 2, tokens), BF)])
        + [((3 * width, tokens), BF), ((width // HEAD_DIM, 8, tokens), F32), ((width, tokens), BF)],
        where, x, bias, mine, theirs, *(rest if given else [Near(rest[0]), *rest[1:]]),
        scratch=[pltpu.VMEM((tokens, tokens), F32), pltpu.VMEM((tokens, tokens), F32)],
        flops=10**11 // 3,
        moved=8 * 2**20,
        limit=8 if given else 12,
    )


def lines_kernel(*refs):
    out_ref = refs[-1]
    width, line = out_ref.shape[1], 0
    for ref in refs[:-1]:
        for at in range(0, ref.shape[0], width):
            out_ref[line : line + 1, :] = ref[pl.ds(at, width)].astype(F32).reshape(1, width)
            line += 1


def pair_kernel(first_ref, second_ref, out_ref):
    half = first_ref.shape[0]
    out_ref[:, :half] = first_ref[...].astype(F32).reshape(1, half)
    out_ref[:, half:] = second_ref[...].astype(F32).reshape(1, half)


def gather_kernel(where_ref, first_ref, second_ref, third_ref, out_ref):
    rows = first_ref.shape[1]
    low = jnp.bitwise_and(where_ref[2], 1)
    out_ref[:, pl.ds(pl.multiple_of(low * rows, rows), rows), :] = first_ref[...]
    out_ref[:, pl.ds(pl.multiple_of((1 - low) * rows, rows), rows), :] = third_ref[...]
    out_ref[:, 2 * rows :, :] = second_ref[...]


def normed(summed):
    centre = summed - jnp.mean(summed, -1, keepdims=True)
    scale_inv = lax.rsqrt(jnp.mean(centre * centre, -1, keepdims=True) + 1e-05)
    return centre * scale_inv, scale_inv


def norm_back(grad, n, scale_inv, gain):
    scaled = grad * gain
    first = jnp.mean(scaled, -1, keepdims=True)
    second = jnp.mean(scaled * n, -1, keepdims=True)
    return scale_inv * (scaled - first - n * second)


def turn_rows(lines, turned_ref, rows):
    tokens = lines.shape[1]
    blocks = lines.reshape(-1, 2, rows, tokens)
    turned_ref[0] = blocks[:, 0].reshape(-1, tokens)
    turned_ref[1] = blocks[:, 1].reshape(-1, tokens)


BIAS_OUT, GAIN_ONE, SHIFT_ONE, BIAS_DOWN, GAIN_TWO, SHIFT_TWO, BIAS_UP = range(7)


CHUNK = 512
WEIGH = 10**12 // 30
LINES = 16


def blocks(count):
    return [slice(at, at + LINES) for at in range(0, count, LINES)]


def fold(value):
    return jnp.sum(value.reshape(-1, 8, value.shape[-1]), 0)


def total(folded):
    return jnp.sum(folded, 0, keepdims=True)


def ffn_kernel(
    where_ref, summed_ref, other_ref, w_out_ref, params_ref, w_up_ref, w_down_ref, cot_ref,
    out_ref, hidden_ref, n_one_ref, r_one_ref, active_ref, slope_ref, grad_two_ref, sums_ref,
    first_ref, second_ref, branch_ref, bias_ref,
):
    half = other_ref.shape[0]
    tokens, width = summed_ref.shape
    head = where_ref[1]
    count = w_up_ref.shape[1] // CHUNK
    span = lambda i: pl.ds(pl.multiple_of(i * CHUNK, CHUNK), CHUNK)

    params = params_ref[...].astype(F32)
    row = lambda i: params[i : i + 1]
    for i in range(bias_ref.shape[1] // width):
        bias_ref[:, i * width : (i + 1) * width] = row(BIAS_UP + i)
    other_at = pl.multiple_of((1 - head) * half, LANES)
    branch_ref[...] = tn(other_ref[...], w_out_ref[pl.ds(other_at, half), :])

    for at in blocks(tokens):
        n, r = normed(summed_ref[at, :] + branch_ref[at, :] + row(BIAS_OUT))
        n_one_ref[at, :] = n
        r_one_ref[at, :] = jnp.broadcast_to(r, (LINES, LANES))
        hidden_ref[at, :] = (n * row(GAIN_ONE) + row(SHIFT_ONE)).astype(BF)

    def upward(ref, at):
        ref[...] = nn(hidden_ref[...], w_up_ref[:, at])

    def gelu(ref, at):
        bias = bias_ref[:, at]
        for start in range(0, tokens, LINES):
            lines = slice(start, start + LINES)
            v = ref[lines, :] + bias
            phi = 0.5 + 0.5 * lax.erf(v * 0.7071067811865476)
            active_ref[lines, at] = (v * phi).astype(BF)
            density = jnp.exp(-0.5 * v * v) * 0.3989422804014327
            slope_ref[lines, at] = (phi + v * density).astype(BF)

    def downward(at):
        branch_ref[...] += nn(active_ref[:, at], w_down_ref[at, :])

    branch_ref[...] = jnp.zeros_like(branch_ref)
    upward(first_ref, span(0))

    @pl.loop(0, count // 2)
    def _(i):
        upward(second_ref, span(2 * i + 1))
        gelu(first_ref, span(2 * i))
        downward(span(2 * i))
        upward(first_ref, span(jnp.minimum(2 * i + 2, count - 1)))
        gelu(second_ref, span(2 * i + 1))
        downward(span(2 * i + 1))

    sums = [0.0, 0.0, 0.0]
    for at in blocks(tokens):
        n, r = normed(hidden_ref[at, :].astype(F32) + branch_ref[at, :] + row(BIAS_DOWN))
        out_ref[at, :] = (n * row(GAIN_TWO) + row(SHIFT_TWO)).astype(BF)
        cot = cot_ref[at, :].astype(F32)
        grad = norm_back(cot, n, r, row(GAIN_TWO))
        grad_two_ref[at, :] = grad
        terms = (cot * n, cot, grad.astype(BF).astype(F32))
        sums = [earlier + fold(term) for earlier, term in zip(sums, terms)]
    for i, folded in enumerate(sums):
        sums_ref[i : i + 1] = total(folded)


def down_kernel(where_ref, active_ref, grad_two_ref, send_ref, keep_ref):
    core = where_ref[0]
    groups, rows = send_ref.shape[0], send_ref.shape[1]
    grad_branch = grad_two_ref[...].astype(BF)
    for i in range(groups):
        block = nn(active_ref[:, i * 2 * rows : (i + 1) * 2 * rows].T, grad_branch).astype(BF)
        low, high = block[:rows], block[rows:]
        keep_ref[i] = jnp.where(core == 0, low, high)
        send_ref[i] = jnp.where(core == 0, high, low)


def slope_kernel(
    slope_ref, grad_two_ref, w_down_ref, grad_up_ref, bias_up_ref, branch_ref
):
    count = w_down_ref.shape[0] // CHUNK
    span = lambda i: pl.ds(pl.multiple_of(i * CHUNK, CHUNK), CHUNK)

    branch_ref[...] = grad_two_ref[...].astype(BF)

    @pl.loop(0, count)
    def _(i):
        grad_active = nt(branch_ref[...], w_down_ref[span(i), :])
        grad_up = (grad_active * slope_ref[:, span(i)].astype(F32)).astype(BF)
        grad_up_ref[:, span(i)] = grad_up
        bias_up_ref[:, span(i)] = jnp.sum(grad_up.astype(F32), 0, keepdims=True)


def up_kernel(
    where_ref, hidden_ref, n_one_ref, r_one_ref, grad_up_ref, grad_two_ref, w_up_ref, w_out_ref, params_ref,
    own_ref, other_ref,
    grad_one_ref, grad_own_ref, grad_other_ref, sums_ref, send_ref, keep_ref,
    both_ref, turned_ref, grad_hidden_ref, grad_context_ref,
):
    half = grad_own_ref.shape[0]
    head, core = where_ref[1], where_ref[0]
    params = params_ref[...].astype(F32)
    row = lambda i: params[i : i + 1]
    groups, rows = send_ref.shape[0], send_ref.shape[1]
    tokens = hidden_ref.shape[0]
    turn_rows(hidden_ref[...].T, turned_ref, rows)

    @pl.loop(0, w_up_ref.shape[1] // CHUNK)
    def _(i):
        at = pl.ds(pl.multiple_of(i * CHUNK, CHUNK), CHUNK)
        grad_up = grad_up_ref[:, at]
        send_ref[:, :, at] = nn(turned_ref[1 - core], grad_up).astype(BF).reshape(groups, rows, CHUNK)
        keep_ref[:, :, at] = nn(turned_ref[core], grad_up).astype(BF).reshape(groups, rows, CHUNK)

    grad_hidden_ref[...] = nt(grad_up_ref[...], w_up_ref[...])
    sums = [0.0, 0.0, 0.0]
    for at in blocks(tokens):
        grad_hidden = grad_hidden_ref[at, :] + grad_two_ref[at, :]
        n_one = n_one_ref[at, :]
        grad_one = norm_back(grad_hidden, n_one, r_one_ref[at, :1], row(GAIN_ONE))
        grad_one_ref[at, :] = grad_one
        terms = (grad_hidden * n_one, grad_hidden, grad_one.astype(BF).astype(F32))
        sums = [earlier + fold(term) for earlier, term in zip(sums, terms)]
    for i, folded in enumerate(sums):
        sums_ref[i : i + 1] = total(folded)
    grad_attended = grad_one_ref[...].astype(BF)
    grad_context_ref[...] = nt(w_out_ref[...], grad_attended).astype(BF)
    own_at = pl.multiple_of(head * half, LANES)
    other_at = pl.multiple_of((1 - head) * half, LANES)
    both_ref[pl.ds(own_at, half), :] = own_ref[...]
    both_ref[pl.ds(other_at, half), :] = other_ref[...]
    turn_rows(both_ref[...], turned_ref, rows)
    ff = w_up_ref.shape[1]
    send_ref[:, :, ff:] = nn(turned_ref[1 - core], grad_attended).astype(BF).reshape(groups, rows, -1)
    keep_ref[:, :, ff:] = nn(turned_ref[core], grad_attended).astype(BF).reshape(groups, rows, -1)
    grad_own_ref[...] = grad_context_ref[pl.ds(own_at, half), :]
    grad_other_ref[...] = grad_context_ref[pl.ds(other_at, half), :]


def back_kernel(
    where_ref, turned_ref, mask_ref, qkv_own_ref, qkv_other_ref, stats_own_ref, stats_other_ref, context_own_ref,
    context_other_ref, grad_own_ref, grad_other_ref,
    send_ref, keep_ref, grads_ref, sums_ref,
    first_ref, second_ref,
):
    core = where_ref[0]
    width, tokens = context_own_ref.shape
    count = width // HEAD_DIM
    halves = (
        (qkv_own_ref, stats_own_ref, context_own_ref, grad_own_ref),
        (qkv_other_ref, stats_other_ref, context_other_ref, grad_other_ref),
    )

    def scaled(half, i):
        return (halves[half][3][head_lines(width, 0, i), :].astype(F32) * halves[half][1][i, 1:2, :]).astype(BF)

    def begin(ref, half, i):
        q, k, v = [halves[half][0][head_lines(width, part, i), :] for part in range(3)]
        ref[0] = tn(k, q)
        ref[1] = tn(v, scaled(half, i))

    def finish(ref, half, i):
        q, k, v = [halves[half][0][head_lines(width, part, i), :] for part in range(3)]
        grad = scaled(half, i)
        context = halves[half][2][head_lines(width, 0, i), :]
        inner = jnp.sum(grad.astype(F32) * context.astype(F32), 0, keepdims=True)
        held, moved = [], []
        for at in range(0, tokens, LANES):
            span = slice(at, at + LANES)
            weights = jnp.exp(ref[0, :, span] + mask_ref[:, span] - halves[half][1][i, 0:1, span])
            held.append(weights.astype(BF))
            moved.append((weights * (ref[1, :, span] - inner[:, span])).astype(BF))
        weights, grad_scores = jnp.concatenate(held, 1), jnp.concatenate(moved, 1)
        grads_ref[half, head_lines(width, 0, i), :] = nn(k, grad_scores).astype(BF) * 0.125
        grads_ref[half, head_lines(width, 1, i), :] = nt(q, grad_scores).astype(BF)
        grads_ref[half, head_lines(width, 2, i), :] = nt(grad, weights).astype(BF)

    begin(first_ref, 0, 0)

    @pl.loop(0, count)
    def _(i):
        begin(second_ref, 1, i)
        finish(first_ref, 0, i)
        begin(first_ref, 0, jnp.minimum(i + 1, count - 1))
        finish(second_ref, 1, i)

    weigh_heads(core, turned_ref, grads_ref, send_ref, keep_ref, 0, send_ref.shape[3])
    ones = jnp.ones((LANES, tokens), BF)
    for half in range(2):
        sums_ref[half] = nt(grads_ref[half], ones)


def weigh_heads(core, turned_ref, grads_ref, send_ref, keep_ref, start, columns):
    groups, rows = send_ref.shape[1:3]
    width, wide = grads_ref.shape[1] // 3, columns // 3
    for half in range(2):
        for out_ref, lines in ((send_ref, 1 - core), (keep_ref, core)):
            for part in range(3):
                at = part * width + start
                found = nt(turned_ref[lines], grads_ref[half, at : at + wide, :]).astype(BF)
                out_ref[half, :, :, part * wide : (part + 1) * wide] = found.reshape(groups, rows, wide)


def end_kernel(
    where_ref, turned_ref, grads_ref, sums_ref, sums_one_ref, sums_two_ref, bias_up_ref,
    send_ref, keep_ref,
    table_ref, flipped_ref, ext_ref,
):
    core, head = where_ref[0], where_ref[1]
    groups, rows, columns = send_ref.shape[1:]
    columns -= LANES
    width = grads_ref.shape[1] // 3
    weigh_heads(core, turned_ref, grads_ref, send_ref, keep_ref, width - columns // 3, columns)
    table_ref[...] = jnp.zeros_like(table_ref)
    table_ref[2:5] = sums_one_ref[0:3]
    table_ref[5:8] = sums_two_ref[0:3]
    flipped_ref[...] = table_ref[...].T
    lane = lax.broadcasted_iota(jnp.int32, (1, LANES), 1)
    for half, at in ((0, head), (1, 1 - head)):
        lines = pl.ds(pl.multiple_of(at * width, LANES), width)
        query, value = sums_ref[half, :width], sums_ref[half, 2 * width :]
        flipped_ref[lines] = jnp.where(lane == 0, query, jnp.where(lane == 1, value, flipped_ref[lines]))
    own = rows // 2
    table = flipped_ref[...].reshape(groups, 2, 2, own, LANES)
    ff = bias_up_ref.shape[1]
    spread = jnp.broadcast_to(bias_up_ref[...], (LANES, ff)).T.reshape(groups, 2, 2, ff // (4 * groups * rows), rows, LANES)
    lane = lax.broadcasted_iota(jnp.int32, (groups, rows, LANES), 2)
    for to_core in range(2):
        for to_head in range(2):
            block = jnp.concatenate([table[:, to_core, to_head], jnp.zeros((groups, rows - own, LANES), F32)], 1)
            for piece in range(spread.shape[3]):
                block = jnp.where(lane == 8 + piece, spread[:, to_core, to_head, piece], block)
            ext_ref[to_core, to_head] = block.astype(BF)
    for half, at in ((0, head), (1, 1 - head)):
        send_ref[half, :, :, columns:] = ext_ref[1 - core, at]
        keep_ref[half, :, :, columns:] = ext_ref[core, at]


def attend_back(where, turned, mask, own, other, grads, groups, count):
    width, tokens = own[2].shape
    rows = turned.shape[1] // groups
    kept = [v for pair in zip(own, other) for v in pair]
    block = ((2, groups, rows, 3 * count * HEAD_DIM), BF)
    return call(
        back_kernel,
        [block, block, ((2, 3 * width, tokens), BF), ((2, 3 * width, LANES), F32)],
        where, turned, mask, *kept, *grads,
        scratch=[pltpu.VMEM((2, tokens, tokens), F32), pltpu.VMEM((2, tokens, tokens), F32)],
        flops=2 * 10**11 // 3,
        moved=10 * 2**20,
        limit=14,
    )


def attend_end(where, turned, grads, groups, count, *sums):
    depth = 2 * turned.shape[1]
    rows = turned.shape[1] // groups
    block = ((2, groups, rows, 3 * count * HEAD_DIM + LANES), BF)
    return call(
        end_kernel,
        [block, block],
        where, turned, grads, *sums,
        scratch=[
            pltpu.VMEM((LANES, depth), F32), pltpu.VMEM((depth, LANES), F32),
            pltpu.VMEM((2, 2, groups, rows, LANES), BF),
        ],
        flops=2 * 10**11 // 3,
        moved=10 * 2**20,
        limit=8,
    )


def input_kernel(
    where_ref, grads_ref, mine_own_ref, mine_other_ref, theirs_own_ref, theirs_other_ref, grad_one_ref, out_ref
):
    depth, width = mine_own_ref.shape[1:]
    core = where_ref[0]
    plain = [grads_ref[half].T for half in range(2)]
    for at, weights_refs in ((core, (mine_own_ref, mine_other_ref)), (1 - core, (theirs_own_ref, theirs_other_ref))):
        lanes = pl.ds(pl.multiple_of(at * depth, LANES), depth)
        terms = [
            nt(plain[half][:, part * width : (part + 1) * width], weights_refs[half][part])
            for half in range(2)
            for part in range(3)
        ]
        out_ref[:, lanes] = (grad_one_ref[:, lanes] + sum(terms)).astype(BF)


def each(count, body):
    if count == 1:
        body(0)
    else:
        pl.loop(0, count)(body)


def open_kernel(cut, split, where_ref, *refs):
    count = split or 2
    terms, outs = refs[:count], refs[count:]
    head_send, head_own, low_own, *low_sends = outs
    low, head = where_ref[2], where_ref[1]
    size = len(low_sends) + 1

    def block(i, bits, half, columns):
        if split:
            return terms[0][half, i, bits, :, columns] + terms[1][half, i, bits, :, columns]
        return terms[0][i, bits, half, :, columns] + terms[1][i, bits, half, :, columns]

    def body(i):
        for bits in range(size):
            head_own[i, bits] = block(i, bits, 0 if split else head, slice(0, cut))
            head_send[i, bits] = block(i, bits, 1 if split else 1 - head, slice(0, cut))
        for flip, out in enumerate([low_own, *low_sends]):
            for half in range(2):
                if split != 4:
                    out[i, half] = block(i, low ^ flip, half, slice(cut, None))
                    continue
                wide = terms[0].shape[4] - cut
                out[i, half, :, :wide] = block(i, low ^ flip, half, slice(cut, None))
                out[i, half, :, wide:] = terms[2][half, i, low ^ flip] + terms[3][half, i, low ^ flip]

    each(head_own.shape[0], body)


def turn_kernel(split, size, where_ref, *refs):
    first, second, outs = refs[:2], refs[2 : 2 + size], refs[2 + size :]
    first_outs, (second_own, second_send) = outs[:size], outs[size:]
    low, head = where_ref[2], where_ref[1]
    own, other = (0, 1) if split else (head, 1 - head)

    def add(values, *at):
        return functools.reduce(jnp.add, [v[at] for v in values])

    def body(i):
        for flip, out in enumerate(first_outs):
            out[i] = add(first, i, low ^ flip)
        second_own[i] = add(second, i, own)
        second_send[i] = add(second, i, other)

    each(second_own.shape[0], body)


def last_kernel(counts, stage, where_ref, *refs):
    parts, at = [], 0
    for count in counts:
        parts.append(refs[at : at + count])
        at += count
    outs = refs[at:]
    index = where_ref[stage]
    size = len(outs)

    def body(i):
        for flip, out in enumerate(outs):
            start = 0
            for part in parts:
                columns = slice(start, start + part[0].shape[2])
                start = columns.stop
                values = [v[i * size + (index ^ flip)].astype(F32) for v in part]
                out[i, :, columns] = functools.reduce(jnp.add, values).astype(BF)

    each(outs[0].shape[0], body)


def part_kernel(cut, where_ref, *refs):
    terms, (first_own, first_send, second_own, second_send) = refs[:-4], refs[-4:]
    low, head = where_ref[2], where_ref[1]
    for out, index, columns in (
        (first_own, low, slice(0, cut)), (first_send, 1 - low, slice(0, cut)),
        (second_own, head, slice(cut, None)), (second_send, 1 - head, slice(cut, None)),
    ):
        out[...] = functools.reduce(jnp.add, [v[0, index, :, columns] for v in terms])


def close_parts_kernel(scale, *refs):
    out = refs[-1]
    cut = refs[0].shape[1]
    for columns, pair in ((slice(0, cut), refs[0:2]), (slice(cut, None), refs[2:4])):
        out[:, columns] = (pair[0][...].astype(F32) + pair[1][...].astype(F32)) * scale


def close_last_kernel(scale, wide_a, wide_b, *refs):
    terms, out_ref, small_refs, spread_ref = refs[:-10], refs[-10], refs[-9:-1], refs[-1]
    summed = functools.reduce(jnp.add, [v[0].astype(F32) for v in terms]) * scale
    rows, start = summed.shape[0], 3 * wide_a
    for part in range(3):
        out_ref[:, part, :wide_a] = summed[:, part * wide_a : (part + 1) * wide_a]
        out_ref[:, part, wide_a:] = summed[:, start + part * wide_b : start + (part + 1) * wide_b]
    lines = summed[:, 3 * (wide_a + wide_b) :].T
    for i, ref in enumerate(small_refs):
        ref[...] = lines[i, : ref.shape[0]]
    pieces = spread_ref.shape[0] // rows
    spread_ref[...] = jnp.concatenate([lines[8 + i : 9 + i, :rows] for i in range(pieces)], 1)[0]


def close_both_kernel(scale, wide_a, wide_b, *refs):
    close_parts_kernel(scale, *refs[:4], refs[-1])
    close_last_kernel(scale, wide_a, wide_b, *refs[4:-1])


def close_kernel(scale, *refs):
    refs[-1][...] = functools.reduce(jnp.add, [v[0].astype(F32) for v in refs[:-1]]) * scale


def pause_kernel(token_ref, out_ref):
    out_ref[...] = token_ref[...]


def pause(*others):
    token = after(jnp.zeros((8, LANES), F32), *others)
    return call(pause_kernel, [((8, LANES), F32)], token, flops=10**13, limit=2)[0]


def after(value, *others):
    return lax.optimization_barrier((value, *others))[0]


def pick(value, index, axis):
    return lax.dynamic_index_in_dim(value, index, axis, keepdims=False)


def on_device(
    inputs, cotangent, segment_ids, lengths, w_qkv, bias_query, bias_value, w_out, bias_out, gain_one,
    shift_one, w_up, bias_up, w_down, bias_down, gain_two, shift_two,
):
    width = w_out.shape[0]
    half = w_qkv.shape[2]
    ff = w_up.shape[1]
    tokens = inputs.shape[0]
    batch = lax.axis_size("batch")
    heads = lax.axis_size("head")
    place, head = lax.axis_index("batch"), lax.axis_index("head")
    core = place % 2
    scale = 1.0 / (lengths.shape[0] * batch)

    plan, bit, bits = [], 1, batch.bit_length() - 1
    if (bits - 1) % 2:
        plan.append((1, 2))
        bit = 2
    while bit < bits:
        plan.append((bit, 4))
        bit += 2
    halving = [(at, 2) for at in range(plan[0][0] + plan[0][1] // 2, bits)]
    where = jnp.stack([core, head] + [(place >> at) % many for at, many in plan + halving]).astype(jnp.int32)

    def swap_batch(value, flip):
        return lax.ppermute(value, "batch", [(i, i ^ flip) for i in range(batch)])

    def swap_head(value):
        return lax.ppermute(value, "head", [(0, 1), (1, 0)])

    depth = width // 2

    def columns(source, at):
        part = lax.dynamic_slice_in_dim(source, at * depth, depth, 0)
        return part.transpose(1, 0, 2)

    third = depth // 3

    def piece(at):
        return lax.dynamic_slice_in_dim(w_qkv, core * depth + at * third, third, 0).transpose(1, 0, 2)

    early_piece = piece((place >> 1) % 2)
    w_first = swap_head(early_piece)
    late_piece = piece(after(jnp.int32(2), early_piece))
    w_second = swap_head(late_piece)
    pair = (after(bias_query, late_piece), bias_value)
    small_own = call(pair_kernel, [((1, width), F32)], *pair, limit=2)[0]
    small_other = swap_head(small_own)
    own_mine = columns(after(w_qkv, late_piece), core)
    w_third = swap_batch(w_first, 2)
    ids = segment_ids.reshape(-1, LANES)
    prepared = (inputs, where, columns(after(w_qkv, own_mine), 1 - core), small_own, ids)
    inputs, where, own_theirs, small_own, ids = lax.optimization_barrier(prepared)

    mask, summed, turned, *kept_own = attend(
        where, inputs, small_own, own_mine, own_theirs, ids, lengths, w_out, turned_rows=width // batch
    )
    context_own = kept_own[2]
    vectors = [bias_out, gain_one, shift_one, bias_down, gain_two, shift_two, bias_up]
    params = call(
        lines_kernel, [((BIAS_UP + ff // width, width), F32)], after(vectors[0], context_own), *vectors[1:], limit=2
    )[0]
    w_first, w_second, w_third = [after(v, context_own, small_other) for v in (w_first, w_second, w_third)]
    w_mine = call(gather_kernel, [(own_mine.shape, BF)], where, w_first, w_second, w_third, limit=6)[0]
    w_theirs = swap_batch(w_mine, 1)
    kept_other = attend(where, inputs, small_other, w_mine, w_theirs, mask)
    context_other = kept_other[2]

    groups = batch // 2
    ffn_rows, up_rows = ff // batch, width // batch
    out, hidden, n_one, r_one, active, slope, grad_two, sums_two = call(
        ffn_kernel,
        [
            ((tokens, width), BF),
            ((tokens, width), BF),
            ((tokens, width), F32),
            ((tokens, LANES), F32),
            ((tokens, ff), BF),
            ((tokens, ff), BF),
            ((tokens, width), F32),
            ((8, width), F32),
        ],
        where, summed, context_other, w_out, params, w_up, w_down, cotangent,
        scratch=[
            pltpu.VMEM((tokens, CHUNK), F32), pltpu.VMEM((tokens, CHUNK), F32), pltpu.VMEM((tokens, width), F32),
            pltpu.VMEM((1, ff), F32),
        ],
        flops=2 * 10**11 // 3, moved=30 * 2**20, limit=14,
    )
    down_send, down_keep = call(
        down_kernel,
        [((groups, ffn_rows, width), BF), ((groups, ffn_rows, width), BF)],
        where, active, grad_two,
        flops=6 * 10**10 // 3, moved=10 * 2**20, limit=12,
    )
    low, rest = plan[0], plan[1:]
    size = low[1]
    low_groups = groups // size

    def open_sum(values, cut, split=False, weigh=0):
        rows, columns = values[0].shape[-2] // (1 if split else heads), values[0].shape[-1]
        lead = (heads, low_groups, size) if split else (low_groups, size, heads)
        more = sum(v.shape[-1] for v in values[2::2])
        values = [v.reshape(*lead, rows, v.shape[-1]) for v in values]
        columns += more
        by_head, by_low = (low_groups, size, rows, cut), (low_groups, heads, rows, columns - cut)
        head_send, head_own, low_own, *low_sends = call(
            functools.partial(open_kernel, cut, len(values) if split else 0), [(by_head, BF)] * 2 + [(by_low, BF)] * size, where, *values,
            flops=weigh,
        )
        got = [swap_batch(v, flip << low[0]) for flip, v in enumerate(low_sends, 1)]
        return head_send, [head_own, swap_head(head_send)], [low_own, *got]

    def turn_sum(first, second, split=False, weigh=0):
        rows = first[0].shape[2]
        cut, more = first[0].shape[3], second[0].shape[3]
        outs = call(
            functools.partial(turn_kernel, split, size),
            [((low_groups, rows, cut), BF)] * size + [((low_groups, rows, more), BF)] * 2,
            where, *first, *second,
            flops=weigh,
        )
        got = [swap_batch(v, flip << low[0]) for flip, v in enumerate(outs[1:size], 1)]
        return outs[0], [outs[0], *got], [outs[size], swap_head(outs[size + 1])]

    def last_sum(*parts, stages=None, weigh=0):
        for bit, many in stages or rest:
            stage = 2 + (plan + halving).index((bit, many))
            rows, columns = parts[0][0].shape[1], sum(part[0].shape[2] for part in parts)
            left = parts[0][0].shape[0] // many
            outs = call(
                functools.partial(last_kernel, [len(part) for part in parts], stage),
                [((left, rows, columns), BF)] * many,
                where, *[v for part in parts for v in part],
                flops=weigh,
            )
            parts = [[outs[0]] + [swap_batch(v, flip << bit) for flip, v in enumerate(outs[1:], 1)]]
        return outs[0], parts[0]

    def close_sum(values, weigh=0):
        return call(functools.partial(close_kernel, scale), [(values[0].shape[1:], F32)], *values, flops=weigh)[0]

    def late(values, *before):
        return [values[0]] + [after(v, *before) for v in values[1:]]

    down = [down_keep, swap_batch(down_send, 1)]
    grad_up, sum_bias_up = call(
        slope_kernel,
        [((tokens, ff), BF), ((1, ff), F32)],
        slope, grad_two, w_down,
        scratch=[
            pltpu.VMEM((tokens, width), BF),
        ],
        flops=10**11 // 3, moved=10 * 2**20, limit=8,
    )
    down[1] = after(down[1], sum_bias_up)
    sent, down, down_low = open_sum(down, width // 2)
    grad_one, grad_own, grad_other, sums_one, up_send, up_keep = call(
        up_kernel,
        [
            ((tokens, width), F32),
            ((half, tokens), BF),
            ((half, tokens), BF),
            ((8, width), F32),
            ((groups, up_rows, ff + width), BF),
            ((groups, up_rows, ff + width), BF),
        ],
        where, hidden, n_one, r_one, after(grad_up, sent), grad_two, w_up, w_out, params, context_own, context_other,
        scratch=[
            pltpu.VMEM((width, tokens), BF),
            pltpu.VMEM((2, groups * up_rows, tokens), BF),
            pltpu.VMEM((tokens, width), F32),
            pltpu.VMEM((width, tokens), BF),
        ],
        limit=13,
        flops=2 * 10**11 // 3, moved=30 * 2**20,
    )
    up = [up_keep, swap_batch(up_send, 1)]
    early = size == heads and len(halving) == 2
    if early:
        flat = lambda v: v.reshape(low_groups, -1, v.shape[3])
        down_cut, down_rows = down[0].shape[3], down[0].shape[2]
        sent, down = last_sum(
            [flat(v) for v in late(down, grad_one)], [flat(v) for v in down_low], stages=halving[:1], weigh=WEIGH
        )
    else:
        sent, down, down_low = turn_sum(late(down, grad_one), down_low, weigh=WEIGH)
    sent, up, up_low = open_sum(late(up, sent), (ff + width) // 2)
    end = half // HEAD_DIM - 2
    weights = (own_mine, w_mine, own_theirs, w_theirs)
    qa_send, qa_keep, grads, sums = attend_back(
        where, turned, mask, kept_own, kept_other, (after(grad_own, sent), grad_other), groups, end
    )
    qa_got = swap_batch(qa_send, 1)
    if early:
        sent, down = last_sum(late(down, sums), stages=halving[1:])
    else:
        sent, down = last_sum(late(down, sums), down_low)
    sent, up, up_low = turn_sum(late(up, sent), up_low)
    qb_send, qb_keep = attend_end(
        where, turned, after(grads, sent), groups, 2, sums, sums_one, sums_two, sum_bias_up
    )
    cut_a, cut_b = 3 * end * HEAD_DIM // 2, 2 * LANES
    sent, qa, qa_low = open_sum([qa_keep, after(qa_got, qb_keep)], cut_a, True)
    input_grad = call(
        input_kernel,
        [((tokens, width), BF)],
        where, after(grads, sent), *weights, grad_one,
        flops=WEIGH, moved=10 * 2**20, limit=10,
    )[0]
    if early:
        down[1] = after(down[1], input_grad)
        up[0] = after(up[0], down[1])
    sent, up = last_sum(late(up, input_grad), up_low, stages=halving[:1])
    qb_got = swap_batch(after(qb_send, sent), 1)
    sent, qa, qa_low = turn_sum(late(qa, sent), qa_low, True, weigh=WEIGH)
    sent, qb, qb_low = open_sum([qb_keep, after(qb_got, sent)], cut_b, True)
    sent, up = last_sum(late(up, sent), stages=halving[1:])
    sent, qb, qb_low = turn_sum(late(qb, sent), qb_low, True, weigh=WEIGH)
    if early:
        by_low, by_head = (down_rows, down_cut), (down_rows, down[0].shape[2] - down_cut)
        outs = call(
            functools.partial(part_kernel, down_cut), [(by_low, BF)] * 2 + [(by_head, BF)] * 2,
            where, *[v.reshape(1, 2, down_rows, -1) for v in [after(down[0], sent), *down[1:]]],
        )
        down = [outs[0], swap_batch(outs[1], 1 << low[0]), outs[2], swap_head(outs[3])]
        sent = outs[1]
    sent, qkv = last_sum(late(qa, sent), qa_low, qb, qb_low)
    sum_up = close_sum(late(up, sent))
    own, pieces = up_rows // heads, ff // (heads * width)
    wide = (end * HEAD_DIM, 2 * HEAD_DIM)
    shapes = [((up_rows, 3, half), F32)] + [((own,), F32)] * 8 + [((pieces * up_rows,), F32)]
    if early:
        down = [down[0], after(down[1], sum_up), down[2], after(down[3], sum_up)]
        shapes.append(((down_rows, down_cut + down[2].shape[1]), F32))
        sum_qkv, *small, spread, sum_down = call(
            functools.partial(close_both_kernel, scale, *wide), shapes, *down, *qkv
        )
    else:
        sum_down = close_sum(late(down, sum_up))
        sum_qkv, *small, spread = call(functools.partial(close_last_kernel, scale, *wide), shapes, *qkv)
    return (
        out, input_grad, sum_qkv, small[0], small[1], sum_up[:, ff:], small[4], small[2], small[3],
        sum_up[:, :ff], spread, sum_down, small[7], small[5], small[6],
    )


def solution(mesh):
    rows = P(BOTH, None)
    placed = (rows, rows, P("batch"), P("batch"), P(None, None, "head"), P("head"), P("head")) + (P(),) * 10
    flat = P(BOTH)
    return jax.shard_map(
        on_device,
        mesh=mesh,
        in_specs=placed,
        out_specs=(
            rows, rows, P("batch", None, "head"), flat, flat, rows, flat, flat, flat, rows, flat, rows, flat,
            flat, flat,
        ),
        check_vma=False,
    )
```

```python
import functools

import jax
import jax.numpy as jnp
from jax import lax
from jax.experimental import pallas as pl
from jax.experimental.pallas import tpu as pltpu
from jax.sharding import PartitionSpec as P

HEAD_DIM = 64
LANES = 128
BF = jnp.bfloat16
F32 = jnp.float32
BOTH = ("batch", "head")
VMEM = pl.BlockSpec(memory_space=pltpu.VMEM)
SMEM = pl.BlockSpec(memory_space=pltpu.SMEM)


def nn(left, right):
    return lax.dot_general(left, right, (((1,), (0,)), ((), ())), preferred_element_type=F32)


def nt(left, right):
    return lax.dot_general(left, right, (((1,), (1,)), ((), ())), preferred_element_type=F32)


class Near:
    def __init__(self, value):
        self.value = value


def call(kernel, outs, *operands, scratch=(), flops=0, moved=0, limit=16):
    specs = [VMEM if isinstance(a, Near) or a.dtype != jnp.int32 else SMEM for a in operands]
    operands = [a.value if isinstance(a, Near) else a for a in operands]
    return pl.pallas_call(
        kernel,
        in_specs=specs,
        out_specs=[VMEM] * len(outs),
        out_shape=[jax.ShapeDtypeStruct(s, t) for s, t in outs],
        scratch_shapes=list(scratch),
        cost_estimate=pl.CostEstimate(flops=flops, bytes_accessed=moved, transcendentals=0),
        compiler_params=pltpu.CompilerParams(vmem_limit_bytes=limit * 2**20),
    )(*operands)


def tn(left, right):
    return lax.dot_general(left, right, (((0,), (0,)), ((), ())), preferred_element_type=F32)


def head_lines(width, part, number):
    return pl.ds(pl.multiple_of(part * width + number * HEAD_DIM, HEAD_DIM), HEAD_DIM)


def in_turn(count, first_ref, second_ref, begin, finish):
    begin(first_ref, 0)

    @pl.loop(0, count // 2)
    def _(i):
        begin(second_ref, 2 * i + 1)
        finish(first_ref, 2 * i)
        begin(first_ref, jnp.minimum(2 * i + 2, count - 1))
        finish(second_ref, 2 * i + 1)


def attend_kernel(given, turned_rows, where_ref, x_ref, bias_ref, mine_ref, theirs_ref, *refs):
    if given:
        mask_ref, qkv_ref, stats_ref, context_ref, first_ref, second_ref = refs
    else:
        (ids_ref, length_ref, w_out_ref, mask_ref, summed_ref, turned_ref, qkv_ref, stats_ref, context_ref,
         first_ref, second_ref) = refs
        turn_rows(x_ref[...].T, turned_ref, turned_rows)
        spans = mask_ref.shape[0] // LANES
        mine_ids = jnp.concatenate([ids_ref[pl.ds(where_ref[1] * spans + i, 1), :] for i in range(spans)], 1)
        columns = jnp.broadcast_to(mine_ids, (LANES, mine_ids.shape[1])).T
        position = lax.broadcasted_iota(jnp.int32, columns.shape, 0)
        live = position < length_ref[where_ref[1]]
        for at in range(0, mask_ref.shape[1], LANES):
            allowed = (columns == mine_ids[:, at : at + LANES]) & live
            mask_ref[:, at : at + LANES] = jnp.where(allowed, 0.0, -1e30)
    width, tokens = context_ref.shape
    depth = mine_ref.shape[1]
    mine = pl.ds(pl.multiple_of(where_ref[0] * depth, LANES), depth)
    theirs = pl.ds(pl.multiple_of((1 - where_ref[0]) * depth, LANES), depth)
    for part in range(3):
        projected = nn(x_ref[:, mine], mine_ref[part]) + nn(x_ref[:, theirs], theirs_ref[part])
        if part == 0:
            projected = (projected + bias_ref[0:1, :width].astype(F32)) * 0.125
        if part == 2:
            projected = projected + bias_ref[0:1, width:].astype(F32)
        qkv_ref[part * width : (part + 1) * width, :] = projected.astype(BF).T

    def begin(ref, i):
        ref[...] = tn(qkv_ref[head_lines(width, 1, i), :], qkv_ref[head_lines(width, 0, i), :])

    def finish(ref, i):
        held = []
        for at in range(0, tokens, LANES):
            columns = slice(at, at + LANES)
            scores = ref[:, columns] + mask_ref[:, columns]
            largest = jnp.max(scores, 0, keepdims=True)
            weights = jnp.exp(scores - largest)
            stats_ref[i, 0:1, columns] = largest
            stats_ref[i, 1:2, columns] = 1.0 / jnp.sum(weights, 0, keepdims=True)
            held.append(weights.astype(BF))
        context = nn(qkv_ref[head_lines(width, 2, i), :], jnp.concatenate(held, 1))
        context_ref[head_lines(width, 0, i), :] = (context * stats_ref[i, 1:2, :]).astype(BF)

    in_turn(width // HEAD_DIM, first_ref, second_ref, begin, finish)
    if not given:
        lines = pl.ds(pl.multiple_of(where_ref[1] * width, LANES), width)
        attended = tn(context_ref[...], w_out_ref[lines, :])
        summed_ref[...] = x_ref[...].astype(F32) + attended


def attend(where, x, bias, mine, theirs, *rest, turned_rows=0):
    tokens, width = x.shape[0], mine.shape[2]
    given = len(rest) == 1
    return call(
        functools.partial(attend_kernel, given, turned_rows),
        ([] if given else [((tokens, tokens), F32), (x.shape, F32), ((2, x.shape[1] // 2, tokens), BF)])
        + [((3 * width, tokens), BF), ((width // HEAD_DIM, 8, tokens), F32), ((width, tokens), BF)],
        where, x, bias, mine, theirs, *(rest if given else [Near(rest[0]), *rest[1:]]),
        scratch=[pltpu.VMEM((tokens, tokens), F32), pltpu.VMEM((tokens, tokens), F32)],
        flops=10**11 // 3,
        moved=8 * 2**20,
        limit=8 if given else 12,
    )


def lines_kernel(*refs):
    out_ref = refs[-1]
    width, line = out_ref.shape[1], 0
    for ref in refs[:-1]:
        for at in range(0, ref.shape[0], width):
            out_ref[line : line + 1, :] = ref[pl.ds(at, width)].astype(F32).reshape(1, width)
            line += 1


def pair_kernel(first_ref, second_ref, out_ref):
    half = first_ref.shape[0]
    out_ref[:, :half] = first_ref[...].astype(F32).reshape(1, half)
    out_ref[:, half:] = second_ref[...].astype(F32).reshape(1, half)


def gather_kernel(where_ref, first_ref, second_ref, third_ref, out_ref):
    rows = first_ref.shape[1]
    low = jnp.bitwise_and(where_ref[2], 1)
    out_ref[:, pl.ds(pl.multiple_of(low * rows, rows), rows), :] = first_ref[...]
    out_ref[:, pl.ds(pl.multiple_of((1 - low) * rows, rows), rows), :] = third_ref[...]
    out_ref[:, 2 * rows :, :] = second_ref[...]


def normed(summed):
    centre = summed - jnp.mean(summed, -1, keepdims=True)
    scale_inv = lax.rsqrt(jnp.mean(centre * centre, -1, keepdims=True) + 1e-05)
    return centre * scale_inv, scale_inv


def norm_back(grad, n, scale_inv, gain):
    scaled = grad * gain
    first = jnp.mean(scaled, -1, keepdims=True)
    second = jnp.mean(scaled * n, -1, keepdims=True)
    return scale_inv * (scaled - first - n * second)


def turn_rows(lines, turned_ref, rows):
    tokens = lines.shape[1]
    blocks = lines.reshape(-1, 2, rows, tokens)
    turned_ref[0] = blocks[:, 0].reshape(-1, tokens)
    turned_ref[1] = blocks[:, 1].reshape(-1, tokens)


BIAS_OUT, GAIN_ONE, SHIFT_ONE, BIAS_DOWN, GAIN_TWO, SHIFT_TWO, BIAS_UP = range(7)


CHUNK = 512
WEIGH = 10**12 // 30
LINES = 16


def blocks(count):
    return [slice(at, at + LINES) for at in range(0, count, LINES)]


def fold(value):
    return jnp.sum(value.reshape(-1, 8, value.shape[-1]), 0)


def total(folded):
    return jnp.sum(folded, 0, keepdims=True)


def ffn_kernel(
    where_ref, summed_ref, other_ref, w_out_ref, params_ref, w_up_ref, w_down_ref, cot_ref,
    out_ref, hidden_ref, n_one_ref, r_one_ref, active_ref, slope_ref, grad_two_ref, sums_ref,
    first_ref, second_ref, branch_ref, bias_ref,
):
    half = other_ref.shape[0]
    tokens, width = summed_ref.shape
    head = where_ref[1]
    count = w_up_ref.shape[1] // CHUNK
    span = lambda i: pl.ds(pl.multiple_of(i * CHUNK, CHUNK), CHUNK)

    params = params_ref[...].astype(F32)
    row = lambda i: params[i : i + 1]
    for i in range(bias_ref.shape[1] // width):
        bias_ref[:, i * width : (i + 1) * width] = row(BIAS_UP + i)
    other_at = pl.multiple_of((1 - head) * half, LANES)
    branch_ref[...] = tn(other_ref[...], w_out_ref[pl.ds(other_at, half), :])

    for at in blocks(tokens):
        n, r = normed(summed_ref[at, :] + branch_ref[at, :] + row(BIAS_OUT))
        n_one_ref[at, :] = n
        r_one_ref[at, :] = jnp.broadcast_to(r, (LINES, LANES))
        hidden_ref[at, :] = (n * row(GAIN_ONE) + row(SHIFT_ONE)).astype(BF)

    def upward(ref, at):
        ref[...] = nn(hidden_ref[...], w_up_ref[:, at])

    def gelu(ref, at):
        bias = bias_ref[:, at]
        for start in range(0, tokens, LINES):
            lines = slice(start, start + LINES)
            v = ref[lines, :] + bias
            phi = 0.5 + 0.5 * lax.erf(v * 0.7071067811865476)
            active_ref[lines, at] = (v * phi).astype(BF)
            density = jnp.exp(-0.5 * v * v) * 0.3989422804014327
            slope_ref[lines, at] = (phi + v * density).astype(BF)

    def downward(at):
        branch_ref[...] += nn(active_ref[:, at], w_down_ref[at, :])

    branch_ref[...] = jnp.zeros_like(branch_ref)
    upward(first_ref, span(0))

    @pl.loop(0, count // 2)
    def _(i):
        upward(second_ref, span(2 * i + 1))
        gelu(first_ref, span(2 * i))
        downward(span(2 * i))
        upward(first_ref, span(jnp.minimum(2 * i + 2, count - 1)))
        gelu(second_ref, span(2 * i + 1))
        downward(span(2 * i + 1))

    sums = [0.0, 0.0, 0.0]
    for at in blocks(tokens):
        n, r = normed(hidden_ref[at, :].astype(F32) + branch_ref[at, :] + row(BIAS_DOWN))
        out_ref[at, :] = (n * row(GAIN_TWO) + row(SHIFT_TWO)).astype(BF)
        cot = cot_ref[at, :].astype(F32)
        grad = norm_back(cot, n, r, row(GAIN_TWO))
        grad_two_ref[at, :] = grad
        terms = (cot * n, cot, grad.astype(BF).astype(F32))
        sums = [earlier + fold(term) for earlier, term in zip(sums, terms)]
    for i, folded in enumerate(sums):
        sums_ref[i : i + 1] = total(folded)


def down_kernel(where_ref, active_ref, grad_two_ref, send_ref, keep_ref):
    core = where_ref[0]
    groups, rows = send_ref.shape[0], send_ref.shape[1]
    grad_branch = grad_two_ref[...].astype(BF)
    for i in range(groups):
        block = nn(active_ref[:, i * 2 * rows : (i + 1) * 2 * rows].T, grad_branch).astype(BF)
        low, high = block[:rows], block[rows:]
        keep_ref[i] = jnp.where(core == 0, low, high)
        send_ref[i] = jnp.where(core == 0, high, low)


def slope_kernel(
    slope_ref, grad_two_ref, w_down_ref, grad_up_ref, bias_up_ref, branch_ref
):
    count = w_down_ref.shape[0] // CHUNK
    span = lambda i: pl.ds(pl.multiple_of(i * CHUNK, CHUNK), CHUNK)

    branch_ref[...] = grad_two_ref[...].astype(BF)

    @pl.loop(0, count)
    def _(i):
        grad_active = nt(branch_ref[...], w_down_ref[span(i), :])
        grad_up = (grad_active * slope_ref[:, span(i)].astype(F32)).astype(BF)
        grad_up_ref[:, span(i)] = grad_up
        bias_up_ref[:, span(i)] = jnp.sum(grad_up.astype(F32), 0, keepdims=True)


def up_kernel(
    where_ref, hidden_ref, n_one_ref, r_one_ref, grad_up_ref, grad_two_ref, w_up_ref, w_out_ref, params_ref,
    own_ref, other_ref,
    grad_one_ref, grad_own_ref, grad_other_ref, sums_ref, send_ref, keep_ref,
    both_ref, turned_ref, grad_hidden_ref, grad_context_ref,
):
    half = grad_own_ref.shape[0]
    head, core = where_ref[1], where_ref[0]
    params = params_ref[...].astype(F32)
    row = lambda i: params[i : i + 1]
    groups, rows = send_ref.shape[0], send_ref.shape[1]
    tokens = hidden_ref.shape[0]
    turn_rows(hidden_ref[...].T, turned_ref, rows)

    @pl.loop(0, w_up_ref.shape[1] // CHUNK)
    def _(i):
        at = pl.ds(pl.multiple_of(i * CHUNK, CHUNK), CHUNK)
        grad_up = grad_up_ref[:, at]
        send_ref[:, :, at] = nn(turned_ref[1 - core], grad_up).astype(BF).reshape(groups, rows, CHUNK)
        keep_ref[:, :, at] = nn(turned_ref[core], grad_up).astype(BF).reshape(groups, rows, CHUNK)

    grad_hidden_ref[...] = nt(grad_up_ref[...], w_up_ref[...])
    sums = [0.0, 0.0, 0.0]
    for at in blocks(tokens):
        grad_hidden = grad_hidden_ref[at, :] + grad_two_ref[at, :]
        n_one = n_one_ref[at, :]
        grad_one = norm_back(grad_hidden, n_one, r_one_ref[at, :1], row(GAIN_ONE))
        grad_one_ref[at, :] = grad_one
        terms = (grad_hidden * n_one, grad_hidden, grad_one.astype(BF).astype(F32))
        sums = [earlier + fold(term) for earlier, term in zip(sums, terms)]
    for i, folded in enumerate(sums):
        sums_ref[i : i + 1] = total(folded)
    grad_attended = grad_one_ref[...].astype(BF)
    grad_context_ref[...] = nt(w_out_ref[...], grad_attended).astype(BF)
    own_at = pl.multiple_of(head * half, LANES)
    other_at = pl.multiple_of((1 - head) * half, LANES)
    both_ref[pl.ds(own_at, half), :] = own_ref[...]
    both_ref[pl.ds(other_at, half), :] = other_ref[...]
    turn_rows(both_ref[...], turned_ref, rows)
    ff = w_up_ref.shape[1]
    send_ref[:, :, ff:] = nn(turned_ref[1 - core], grad_attended).astype(BF).reshape(groups, rows, -1)
    keep_ref[:, :, ff:] = nn(turned_ref[core], grad_attended).astype(BF).reshape(groups, rows, -1)
    grad_own_ref[...] = grad_context_ref[pl.ds(own_at, half), :]
    grad_other_ref[...] = grad_context_ref[pl.ds(other_at, half), :]


def back_kernel(
    where_ref, turned_ref, mask_ref, qkv_own_ref, qkv_other_ref, stats_own_ref, stats_other_ref, context_own_ref,
    context_other_ref, grad_own_ref, grad_other_ref,
    send_ref, keep_ref, grads_ref, sums_ref,
    first_ref, second_ref,
):
    core = where_ref[0]
    width, tokens = context_own_ref.shape
    count = width // HEAD_DIM
    halves = (
        (qkv_own_ref, stats_own_ref, context_own_ref, grad_own_ref),
        (qkv_other_ref, stats_other_ref, context_other_ref, grad_other_ref),
    )

    def scaled(half, i):
        return (halves[half][3][head_lines(width, 0, i), :].astype(F32) * halves[half][1][i, 1:2, :]).astype(BF)

    def begin(ref, half, i):
        q, k, v = [halves[half][0][head_lines(width, part, i), :] for part in range(3)]
        ref[0] = tn(k, q)
        ref[1] = tn(v, scaled(half, i))

    def finish(ref, half, i):
        q, k, v = [halves[half][0][head_lines(width, part, i), :] for part in range(3)]
        grad = scaled(half, i)
        context = halves[half][2][head_lines(width, 0, i), :]
        inner = jnp.sum(grad.astype(F32) * context.astype(F32), 0, keepdims=True)
        held, moved = [], []
        for at in range(0, tokens, LANES):
            span = slice(at, at + LANES)
            weights = jnp.exp(ref[0, :, span] + mask_ref[:, span] - halves[half][1][i, 0:1, span])
            held.append(weights.astype(BF))
            moved.append((weights * (ref[1, :, span] - inner[:, span])).astype(BF))
        weights, grad_scores = jnp.concatenate(held, 1), jnp.concatenate(moved, 1)
        grads_ref[half, head_lines(width, 0, i), :] = nn(k, grad_scores).astype(BF) * 0.125
        grads_ref[half, head_lines(width, 1, i), :] = nt(q, grad_scores).astype(BF)
        grads_ref[half, head_lines(width, 2, i), :] = nt(grad, weights).astype(BF)

    begin(first_ref, 0, 0)

    @pl.loop(0, count)
    def _(i):
        begin(second_ref, 1, i)
        finish(first_ref, 0, i)
        begin(first_ref, 0, jnp.minimum(i + 1, count - 1))
        finish(second_ref, 1, i)

    weigh_heads(core, turned_ref, grads_ref, send_ref, keep_ref, 0, send_ref.shape[3])
    ones = jnp.ones((LANES, tokens), BF)
    for half in range(2):
        sums_ref[half] = nt(grads_ref[half], ones)


def weigh_heads(core, turned_ref, grads_ref, send_ref, keep_ref, start, columns):
    groups, rows = send_ref.shape[1:3]
    width, wide = grads_ref.shape[1] // 3, columns // 3
    for half in range(2):
        for out_ref, lines in ((send_ref, 1 - core), (keep_ref, core)):
            for part in range(3):
                at = part * width + start
                found = nt(turned_ref[lines], grads_ref[half, at : at + wide, :]).astype(BF)
                out_ref[half, :, :, part * wide : (part + 1) * wide] = found.reshape(groups, rows, wide)


def end_kernel(
    where_ref, turned_ref, grads_ref, sums_ref, sums_one_ref, sums_two_ref, bias_up_ref,
    send_ref, keep_ref,
    table_ref, flipped_ref, ext_ref,
):
    core, head = where_ref[0], where_ref[1]
    groups, rows, columns = send_ref.shape[1:]
    columns -= LANES
    width = grads_ref.shape[1] // 3
    weigh_heads(core, turned_ref, grads_ref, send_ref, keep_ref, width - columns // 3, columns)
    table_ref[...] = jnp.zeros_like(table_ref)
    table_ref[2:5] = sums_one_ref[0:3]
    table_ref[5:8] = sums_two_ref[0:3]
    flipped_ref[...] = table_ref[...].T
    lane = lax.broadcasted_iota(jnp.int32, (1, LANES), 1)
    for half, at in ((0, head), (1, 1 - head)):
        lines = pl.ds(pl.multiple_of(at * width, LANES), width)
        query, value = sums_ref[half, :width], sums_ref[half, 2 * width :]
        flipped_ref[lines] = jnp.where(lane == 0, query, jnp.where(lane == 1, value, flipped_ref[lines]))
    own = rows // 2
    table = flipped_ref[...].reshape(groups, 2, 2, own, LANES)
    ff = bias_up_ref.shape[1]
    spread = jnp.broadcast_to(bias_up_ref[...], (LANES, ff)).T.reshape(groups, 2, 2, ff // (4 * groups * rows), rows, LANES)
    lane = lax.broadcasted_iota(jnp.int32, (groups, rows, LANES), 2)
    for to_core in range(2):
        for to_head in range(2):
            block = jnp.concatenate([table[:, to_core, to_head], jnp.zeros((groups, rows - own, LANES), F32)], 1)
            for piece in range(spread.shape[3]):
                block = jnp.where(lane == 8 + piece, spread[:, to_core, to_head, piece], block)
            ext_ref[to_core, to_head] = block.astype(BF)
    for half, at in ((0, head), (1, 1 - head)):
        send_ref[half, :, :, columns:] = ext_ref[1 - core, at]
        keep_ref[half, :, :, columns:] = ext_ref[core, at]


def attend_back(where, turned, mask, own, other, grads, groups, count):
    width, tokens = own[2].shape
    rows = turned.shape[1] // groups
    kept = [v for pair in zip(own, other) for v in pair]
    block = ((2, groups, rows, 3 * count * HEAD_DIM), BF)
    return call(
        back_kernel,
        [block, block, ((2, 3 * width, tokens), BF), ((2, 3 * width, LANES), F32)],
        where, turned, mask, *kept, *grads,
        scratch=[pltpu.VMEM((2, tokens, tokens), F32), pltpu.VMEM((2, tokens, tokens), F32)],
        flops=2 * 10**11 // 3,
        moved=10 * 2**20,
        limit=14,
    )


def attend_end(where, turned, grads, groups, count, *sums):
    depth = 2 * turned.shape[1]
    rows = turned.shape[1] // groups
    block = ((2, groups, rows, 3 * count * HEAD_DIM + LANES), BF)
    return call(
        end_kernel,
        [block, block],
        where, turned, grads, *sums,
        scratch=[
            pltpu.VMEM((LANES, depth), F32), pltpu.VMEM((depth, LANES), F32),
            pltpu.VMEM((2, 2, groups, rows, LANES), BF),
        ],
        flops=2 * 10**11 // 3,
        moved=10 * 2**20,
        limit=8,
    )


def input_kernel(
    where_ref, grads_ref, mine_own_ref, mine_other_ref, theirs_own_ref, theirs_other_ref, grad_one_ref, out_ref
):
    depth, width = mine_own_ref.shape[1:]
    core = where_ref[0]
    plain = [grads_ref[half].T for half in range(2)]
    for at, weights_refs in ((core, (mine_own_ref, mine_other_ref)), (1 - core, (theirs_own_ref, theirs_other_ref))):
        lanes = pl.ds(pl.multiple_of(at * depth, LANES), depth)
        terms = [
            nt(plain[half][:, part * width : (part + 1) * width], weights_refs[half][part])
            for half in range(2)
            for part in range(3)
        ]
        out_ref[:, lanes] = (grad_one_ref[:, lanes] + sum(terms)).astype(BF)


def each(count, body):
    if count == 1:
        body(0)
    else:
        pl.loop(0, count)(body)


def open_kernel(cut, split, where_ref, *refs):
    count = split or 2
    terms, outs = refs[:count], refs[count:]
    head_send, head_own, low_own, *low_sends = outs
    low, head = where_ref[2], where_ref[1]
    size = len(low_sends) + 1

    def block(i, bits, half, columns):
        if split:
            return terms[0][half, i, bits, :, columns] + terms[1][half, i, bits, :, columns]
        return terms[0][i, bits, half, :, columns] + terms[1][i, bits, half, :, columns]

    def body(i):
        for bits in range(size):
            head_own[i, bits] = block(i, bits, 0 if split else head, slice(0, cut))
            head_send[i, bits] = block(i, bits, 1 if split else 1 - head, slice(0, cut))
        for flip, out in enumerate([low_own, *low_sends]):
            for half in range(2):
                if split != 4:
                    out[i, half] = block(i, low ^ flip, half, slice(cut, None))
                    continue
                wide = terms[0].shape[4] - cut
                out[i, half, :, :wide] = block(i, low ^ flip, half, slice(cut, None))
                out[i, half, :, wide:] = terms[2][half, i, low ^ flip] + terms[3][half, i, low ^ flip]

    each(head_own.shape[0], body)


def turn_kernel(split, size, where_ref, *refs):
    first, second, outs = refs[:2], refs[2 : 2 + size], refs[2 + size :]
    first_outs, (second_own, second_send) = outs[:size], outs[size:]
    low, head = where_ref[2], where_ref[1]
    own, other = (0, 1) if split else (head, 1 - head)

    def add(values, *at):
        return functools.reduce(jnp.add, [v[at] for v in values])

    def body(i):
        for flip, out in enumerate(first_outs):
            out[i] = add(first, i, low ^ flip)
        second_own[i] = add(second, i, own)
        second_send[i] = add(second, i, other)

    each(second_own.shape[0], body)


def last_kernel(counts, stage, where_ref, *refs):
    parts, at = [], 0
    for count in counts:
        parts.append(refs[at : at + count])
        at += count
    outs = refs[at:]
    index = where_ref[stage]
    size = len(outs)

    def body(i):
        for flip, out in enumerate(outs):
            start = 0
            for part in parts:
                columns = slice(start, start + part[0].shape[2])
                start = columns.stop
                values = [v[i * size + (index ^ flip)].astype(F32) for v in part]
                out[i, :, columns] = functools.reduce(jnp.add, values).astype(BF)

    each(outs[0].shape[0], body)


def part_kernel(cut, where_ref, *refs):
    terms, (first_own, first_send, second_own, second_send) = refs[:-4], refs[-4:]
    low, head = where_ref[2], where_ref[1]
    for out, index, columns in (
        (first_own, low, slice(0, cut)), (first_send, 1 - low, slice(0, cut)),
        (second_own, head, slice(cut, None)), (second_send, 1 - head, slice(cut, None)),
    ):
        out[...] = functools.reduce(jnp.add, [v[0, index, :, columns] for v in terms])


def close_parts_kernel(scale, *refs):
    out = refs[-1]
    cut = refs[0].shape[1]
    for columns, pair in ((slice(0, cut), refs[0:2]), (slice(cut, None), refs[2:4])):
        out[:, columns] = (pair[0][...].astype(F32) + pair[1][...].astype(F32)) * scale


def close_last_kernel(scale, wide_a, wide_b, *refs):
    terms, out_ref, small_refs, spread_ref = refs[:-10], refs[-10], refs[-9:-1], refs[-1]
    summed = functools.reduce(jnp.add, [v[0].astype(F32) for v in terms]) * scale
    rows, start = summed.shape[0], 3 * wide_a
    for part in range(3):
        out_ref[:, part, :wide_a] = summed[:, part * wide_a : (part + 1) * wide_a]
        out_ref[:, part, wide_a:] = summed[:, start + part * wide_b : start + (part + 1) * wide_b]
    lines = summed[:, 3 * (wide_a + wide_b) :].T
    for i, ref in enumerate(small_refs):
        ref[...] = lines[i, : ref.shape[0]]
    pieces = spread_ref.shape[0] // rows
    spread_ref[...] = jnp.concatenate([lines[8 + i : 9 + i, :rows] for i in range(pieces)], 1)[0]


def close_both_kernel(scale, wide_a, wide_b, *refs):
    close_parts_kernel(scale, *refs[:4], refs[-1])
    close_last_kernel(scale, wide_a, wide_b, *refs[4:-1])


def close_kernel(scale, *refs):
    refs[-1][...] = functools.reduce(jnp.add, [v[0].astype(F32) for v in refs[:-1]]) * scale


def after(value, *others):
    return lax.optimization_barrier((value, *others))[0]


def on_device(
    inputs, cotangent, segment_ids, lengths, w_qkv, bias_query, bias_value, w_out, bias_out, gain_one,
    shift_one, w_up, bias_up, w_down, bias_down, gain_two, shift_two,
):
    width = w_out.shape[0]
    half = w_qkv.shape[2]
    ff = w_up.shape[1]
    tokens = inputs.shape[0]
    batch = lax.axis_size("batch")
    heads = lax.axis_size("head")
    place, head = lax.axis_index("batch"), lax.axis_index("head")
    core = place % 2
    scale = 1.0 / (lengths.shape[0] * batch)

    plan, bit, bits = [], 1, batch.bit_length() - 1
    if (bits - 1) % 2:
        plan.append((1, 2))
        bit = 2
    while bit < bits:
        plan.append((bit, 4))
        bit += 2
    halving = [(at, 2) for at in range(plan[0][0] + plan[0][1] // 2, bits)]
    where = jnp.stack([core, head] + [(place >> at) % many for at, many in plan + halving]).astype(jnp.int32)

    def swap_batch(value, flip):
        return lax.ppermute(value, "batch", [(i, i ^ flip) for i in range(batch)])

    def swap_head(value):
        return lax.ppermute(value, "head", [(0, 1), (1, 0)])

    depth = width // 2

    def columns(source, at):
        part = lax.dynamic_slice_in_dim(source, at * depth, depth, 0)
        return part.transpose(1, 0, 2)

    third = depth // 3

    def piece(at):
        return lax.dynamic_slice_in_dim(w_qkv, core * depth + at * third, third, 0).transpose(1, 0, 2)

    early_piece = piece((place >> 1) % 2)
    w_first = swap_head(early_piece)
    late_piece = piece(after(jnp.int32(2), early_piece))
    w_second = swap_head(late_piece)
    pair = (after(bias_query, late_piece), bias_value)
    small_own = call(pair_kernel, [((1, width), F32)], *pair, limit=2)[0]
    small_other = swap_head(small_own)
    own_mine = columns(after(w_qkv, late_piece), core)
    w_third = swap_batch(w_first, 2)
    ids = segment_ids.reshape(-1, LANES)
    prepared = (inputs, where, columns(after(w_qkv, own_mine), 1 - core), small_own, ids)
    inputs, where, own_theirs, small_own, ids = lax.optimization_barrier(prepared)

    mask, summed, turned, *kept_own = attend(
        where, inputs, small_own, own_mine, own_theirs, ids, lengths, w_out, turned_rows=width // batch
    )
    context_own = kept_own[2]
    vectors = [bias_out, gain_one, shift_one, bias_down, gain_two, shift_two, bias_up]
    params = call(
        lines_kernel, [((BIAS_UP + ff // width, width), F32)], after(vectors[0], context_own), *vectors[1:], limit=2
    )[0]
    w_first, w_second, w_third = [after(v, context_own, small_other) for v in (w_first, w_second, w_third)]
    w_mine = call(gather_kernel, [(own_mine.shape, BF)], where, w_first, w_second, w_third, limit=6)[0]
    w_theirs = swap_batch(w_mine, 1)
    kept_other = attend(where, inputs, small_other, w_mine, w_theirs, mask)
    context_other = kept_other[2]

    groups = batch // 2
    ffn_rows, up_rows = ff // batch, width // batch
    out, hidden, n_one, r_one, active, slope, grad_two, sums_two = call(
        ffn_kernel,
        [
            ((tokens, width), BF),
            ((tokens, width), BF),
            ((tokens, width), F32),
            ((tokens, LANES), F32),
            ((tokens, ff), BF),
            ((tokens, ff), BF),
            ((tokens, width), F32),
            ((8, width), F32),
        ],
        where, summed, context_other, w_out, params, w_up, w_down, cotangent,
        scratch=[
            pltpu.VMEM((tokens, CHUNK), F32), pltpu.VMEM((tokens, CHUNK), F32), pltpu.VMEM((tokens, width), F32),
            pltpu.VMEM((1, ff), F32),
        ],
        flops=2 * 10**11 // 3, moved=30 * 2**20, limit=14,
    )
    down_send, down_keep = call(
        down_kernel,
        [((groups, ffn_rows, width), BF), ((groups, ffn_rows, width), BF)],
        where, active, grad_two,
        flops=6 * 10**10 // 3, moved=10 * 2**20, limit=12,
    )
    low, rest = plan[0], plan[1:]
    size = low[1]
    low_groups = groups // size

    def open_sum(values, cut, split=False, weigh=0):
        rows, columns = values[0].shape[-2] // (1 if split else heads), values[0].shape[-1]
        lead = (heads, low_groups, size) if split else (low_groups, size, heads)
        more = sum(v.shape[-1] for v in values[2::2])
        values = [v.reshape(*lead, rows, v.shape[-1]) for v in values]
        columns += more
        by_head, by_low = (low_groups, size, rows, cut), (low_groups, heads, rows, columns - cut)
        head_send, head_own, low_own, *low_sends = call(
            functools.partial(open_kernel, cut, len(values) if split else 0), [(by_head, BF)] * 2 + [(by_low, BF)] * size, where, *values,
            flops=weigh,
        )
        got = [swap_batch(v, flip << low[0]) for flip, v in enumerate(low_sends, 1)]
        return head_send, [head_own, swap_head(head_send)], [low_own, *got]

    def turn_sum(first, second, split=False, weigh=0):
        rows = first[0].shape[2]
        cut, more = first[0].shape[3], second[0].shape[3]
        outs = call(
            functools.partial(turn_kernel, split, size),
            [((low_groups, rows, cut), BF)] * size + [((low_groups, rows, more), BF)] * 2,
            where, *first, *second,
            flops=weigh,
        )
        got = [swap_batch(v, flip << low[0]) for flip, v in enumerate(outs[1:size], 1)]
        return outs[0], [outs[0], *got], [outs[size], swap_head(outs[size + 1])]

    def last_sum(*parts, stages=None, weigh=0):
        for bit, many in stages or rest:
            stage = 2 + (plan + halving).index((bit, many))
            rows, columns = parts[0][0].shape[1], sum(part[0].shape[2] for part in parts)
            left = parts[0][0].shape[0] // many
            outs = call(
                functools.partial(last_kernel, [len(part) for part in parts], stage),
                [((left, rows, columns), BF)] * many,
                where, *[v for part in parts for v in part],
                flops=weigh,
            )
            parts = [[outs[0]] + [swap_batch(v, flip << bit) for flip, v in enumerate(outs[1:], 1)]]
        return outs[0], parts[0]

    def close_sum(values, weigh=0):
        return call(functools.partial(close_kernel, scale), [(values[0].shape[1:], F32)], *values, flops=weigh)[0]

    def late(values, *before):
        return [values[0]] + [after(v, *before) for v in values[1:]]

    down = [down_keep, swap_batch(down_send, 1)]
    grad_up, sum_bias_up = call(
        slope_kernel,
        [((tokens, ff), BF), ((1, ff), F32)],
        slope, grad_two, w_down,
        scratch=[
            pltpu.VMEM((tokens, width), BF),
        ],
        flops=10**11 // 3, moved=10 * 2**20, limit=8,
    )
    down[1] = after(down[1], sum_bias_up)
    sent, down, down_low = open_sum(down, width // 2)
    grad_one, grad_own, grad_other, sums_one, up_send, up_keep = call(
        up_kernel,
        [
            ((tokens, width), F32),
            ((half, tokens), BF),
            ((half, tokens), BF),
            ((8, width), F32),
            ((groups, up_rows, ff + width), BF),
            ((groups, up_rows, ff + width), BF),
        ],
        where, hidden, n_one, r_one, after(grad_up, sent), grad_two, w_up, w_out, params, context_own, context_other,
        scratch=[
            pltpu.VMEM((width, tokens), BF),
            pltpu.VMEM((2, groups * up_rows, tokens), BF),
            pltpu.VMEM((tokens, width), F32),
            pltpu.VMEM((width, tokens), BF),
        ],
        limit=13,
        flops=2 * 10**11 // 3, moved=30 * 2**20,
    )
    up = [up_keep, swap_batch(up_send, 1)]
    early = size == heads and len(halving) == 2
    if early:
        flat = lambda v: v.reshape(low_groups, -1, v.shape[3])
        down_cut, down_rows = down[0].shape[3], down[0].shape[2]
        sent, down = last_sum(
            [flat(v) for v in late(down, grad_one)], [flat(v) for v in down_low], stages=halving[:1], weigh=WEIGH
        )
    else:
        sent, down, down_low = turn_sum(late(down, grad_one), down_low, weigh=WEIGH)
    sent, up, up_low = open_sum(late(up, sent), (ff + width) // 2)
    end = half // HEAD_DIM - 2
    weights = (own_mine, w_mine, own_theirs, w_theirs)
    qa_send, qa_keep, grads, sums = attend_back(
        where, turned, mask, kept_own, kept_other, (after(grad_own, sent), grad_other), groups, end
    )
    qa_got = swap_batch(qa_send, 1)
    if early:
        sent, down = last_sum(late(down, sums), stages=halving[1:])
    else:
        sent, down = last_sum(late(down, sums), down_low)
    sent, up, up_low = turn_sum(late(up, sent), up_low)
    qb_send, qb_keep = attend_end(
        where, turned, after(grads, sent), groups, 2, sums, sums_one, sums_two, sum_bias_up
    )
    cut_a, cut_b = 3 * end * HEAD_DIM // 2, 2 * LANES
    sent, qa, qa_low = open_sum([qa_keep, after(qa_got, qb_keep)], cut_a, True)
    input_grad = call(
        input_kernel,
        [((tokens, width), BF)],
        where, after(grads, sent), *weights, grad_one,
        flops=WEIGH, moved=10 * 2**20, limit=10,
    )[0]
    if early:
        down[1] = after(down[1], input_grad)
        qa[0] = after(qa[0], down[1])
    sent, up = last_sum(late(up, input_grad), up_low, stages=halving[:1])
    qb_got = swap_batch(after(qb_send, sent), 1)
    sent, qa, qa_low = turn_sum(late(qa, sent), qa_low, True, weigh=WEIGH)
    sent, qb, qb_low = open_sum([qb_keep, after(qb_got, sent)], cut_b, True)
    sent, up = last_sum(late(up, sent), stages=halving[1:])
    sent, qb, qb_low = turn_sum(late(qb, sent), qb_low, True, weigh=WEIGH)
    if early:
        by_low, by_head = (down_rows, down_cut), (down_rows, down[0].shape[2] - down_cut)
        outs = call(
            functools.partial(part_kernel, down_cut), [(by_low, BF)] * 2 + [(by_head, BF)] * 2,
            where, *[v.reshape(1, 2, down_rows, -1) for v in [after(down[0], sent), *down[1:]]],
        )
        down = [outs[0], swap_batch(outs[1], 1 << low[0]), outs[2], swap_head(outs[3])]
        sent = outs[1]
    sent, qkv = last_sum(late(qa, sent), qa_low, qb, qb_low)
    sum_up = close_sum(late(up, sent))
    own, pieces = up_rows // heads, ff // (heads * width)
    wide = (end * HEAD_DIM, 2 * HEAD_DIM)
    shapes = [((up_rows, 3, half), F32)] + [((own,), F32)] * 8 + [((pieces * up_rows,), F32)]
    if early:
        down = [down[0], after(down[1], sum_up), down[2], after(down[3], sum_up)]
        shapes.append(((down_rows, down_cut + down[2].shape[1]), F32))
        sum_qkv, *small, spread, sum_down = call(
            functools.partial(close_both_kernel, scale, *wide), shapes, *down, *qkv
        )
    else:
        sum_down = close_sum(late(down, sum_up))
        sum_qkv, *small, spread = call(functools.partial(close_last_kernel, scale, *wide), shapes, *qkv)
    return (
        out, input_grad, sum_qkv, small[0], small[1], sum_up[:, ff:], small[4], small[2], small[3],
        sum_up[:, :ff], spread, sum_down, small[7], small[5], small[6],
    )


def solution(mesh):
    rows = P(BOTH, None)
    placed = (rows, rows, P("batch"), P("batch"), P(None, None, "head"), P("head"), P("head")) + (P(),) * 10
    flat = P(BOTH)
    return jax.shard_map(
        on_device,
        mesh=mesh,
        in_specs=placed,
        out_specs=(
            rows, rows, P("batch", None, "head"), flat, flat, rows, flat, flat, flat, rows, flat, rows, flat,
            flat, flat,
        ),
        check_vma=False,
    )
```

```python
import functools

import jax
import jax.numpy as jnp
from jax import lax
from jax.experimental import pallas as pl
from jax.experimental.pallas import tpu as pltpu
from jax.sharding import PartitionSpec as P

HEAD_DIM = 64
LANES = 128
BF = jnp.bfloat16
F32 = jnp.float32
BOTH = ("batch", "head")
VMEM = pl.BlockSpec(memory_space=pltpu.VMEM)
ANY = pl.BlockSpec(memory_space=pltpu.HBM)
SMEM = pl.BlockSpec(memory_space=pltpu.SMEM)


def nn(left, right):
    return lax.dot_general(left, right, (((1,), (0,)), ((), ())), preferred_element_type=F32)


def nt(left, right):
    return lax.dot_general(left, right, (((1,), (1,)), ((), ())), preferred_element_type=F32)


class Near:
    def __init__(self, value):
        self.value = value


class Far:
    def __init__(self, value):
        self.value = value


def call(kernel, outs, *operands, scratch=(), flops=0, moved=0, limit=16):
    specs = [
        ANY if isinstance(a, Far) else VMEM if isinstance(a, Near) or a.dtype != jnp.int32 else SMEM for a in operands
    ]
    operands = [a.value if isinstance(a, (Far, Near)) else a for a in operands]
    return pl.pallas_call(
        kernel,
        in_specs=specs,
        out_specs=[VMEM] * len(outs),
        out_shape=[jax.ShapeDtypeStruct(s, t) for s, t in outs],
        scratch_shapes=list(scratch),
        cost_estimate=pl.CostEstimate(flops=flops, bytes_accessed=moved, transcendentals=0),
        compiler_params=pltpu.CompilerParams(vmem_limit_bytes=limit * 2**20),
    )(*operands)


def tn(left, right):
    return lax.dot_general(left, right, (((0,), (0,)), ((), ())), preferred_element_type=F32)


def head_lines(width, part, number):
    return pl.ds(pl.multiple_of(part * width + number * HEAD_DIM, HEAD_DIM), HEAD_DIM)


def in_turn(count, first_ref, second_ref, begin, finish):
    begin(first_ref, 0)

    @pl.loop(0, count // 2)
    def _(i):
        begin(second_ref, 2 * i + 1)
        finish(first_ref, 2 * i)
        begin(first_ref, jnp.minimum(2 * i + 2, count - 1))
        finish(second_ref, 2 * i + 1)


def attend_kernel(given, turned_rows, where_ref, x_ref, bias_ref, mine_ref, theirs_ref, *refs):
    if given:
        mask_ref, qkv_ref, stats_ref, context_ref, first_ref, second_ref = refs
    else:
        (ids_ref, length_ref, w_out_ref, mask_ref, summed_ref, turned_ref, qkv_ref, stats_ref, context_ref,
         first_ref, second_ref) = refs
        turn_rows(x_ref[...].T, turned_ref, turned_rows)
        spans = mask_ref.shape[0] // LANES
        mine_ids = jnp.concatenate([ids_ref[pl.ds(where_ref[1] * spans + i, 1), :] for i in range(spans)], 1)
        columns = jnp.broadcast_to(mine_ids, (LANES, mine_ids.shape[1])).T
        position = lax.broadcasted_iota(jnp.int32, columns.shape, 0)
        live = position < length_ref[where_ref[1]]
        for at in range(0, mask_ref.shape[1], LANES):
            allowed = (columns == mine_ids[:, at : at + LANES]) & live
            mask_ref[:, at : at + LANES] = jnp.where(allowed, 0.0, -1e30)
    width, tokens = context_ref.shape
    depth = mine_ref.shape[1]
    mine = pl.ds(pl.multiple_of(where_ref[0] * depth, LANES), depth)
    theirs = pl.ds(pl.multiple_of((1 - where_ref[0]) * depth, LANES), depth)
    for part in range(3):
        projected = nn(x_ref[:, mine], mine_ref[part]) + nn(x_ref[:, theirs], theirs_ref[part])
        if part == 0:
            projected = (projected + bias_ref[0:1, :width].astype(F32)) * 0.125
        if part == 2:
            projected = projected + bias_ref[0:1, width:].astype(F32)
        qkv_ref[part * width : (part + 1) * width, :] = projected.astype(BF).T

    def begin(ref, i):
        ref[...] = tn(qkv_ref[head_lines(width, 1, i), :], qkv_ref[head_lines(width, 0, i), :])

    def finish(ref, i):
        held = []
        for at in range(0, tokens, LANES):
            columns = slice(at, at + LANES)
            scores = ref[:, columns] + mask_ref[:, columns]
            largest = jnp.max(scores, 0, keepdims=True)
            weights = jnp.exp(scores - largest)
            stats_ref[i, 0:1, columns] = largest
            stats_ref[i, 1:2, columns] = 1.0 / jnp.sum(weights, 0, keepdims=True)
            held.append(weights.astype(BF))
        context = nn(qkv_ref[head_lines(width, 2, i), :], jnp.concatenate(held, 1))
        context_ref[head_lines(width, 0, i), :] = (context * stats_ref[i, 1:2, :]).astype(BF)

    in_turn(width // HEAD_DIM, first_ref, second_ref, begin, finish)
    if not given:
        lines = pl.ds(pl.multiple_of(where_ref[1] * width, LANES), width)
        attended = tn(context_ref[...], w_out_ref[lines, :])
        summed_ref[...] = x_ref[...].astype(F32) + attended


def attend(where, x, bias, mine, theirs, *rest, turned_rows=0):
    tokens, width = x.shape[0], mine.shape[2]
    given = len(rest) == 1
    return call(
        functools.partial(attend_kernel, given, turned_rows),
        ([] if given else [((tokens, tokens), F32), (x.shape, F32), ((2, x.shape[1] // 2, tokens), BF)])
        + [((3 * width, tokens), BF), ((width // HEAD_DIM, 8, tokens), F32), ((width, tokens), BF)],
        where, x, bias, mine, theirs, *(rest if given else [Near(rest[0]), *rest[1:]]),
        scratch=[pltpu.VMEM((tokens, tokens), F32), pltpu.VMEM((tokens, tokens), F32)],
        flops=10**11 // 3,
        moved=8 * 2**20,
        limit=8 if given else 12,
    )


def lines_kernel(*refs):
    out_ref = refs[-1]
    width, line = out_ref.shape[1], 0
    for ref in refs[:-1]:
        for at in range(0, ref.shape[0], width):
            out_ref[line : line + 1, :] = ref[pl.ds(at, width)].astype(F32).reshape(1, width)
            line += 1


def pair_kernel(first_ref, second_ref, out_ref):
    half = first_ref.shape[0]
    out_ref[:, :half] = first_ref[...].astype(F32).reshape(1, half)
    out_ref[:, half:] = second_ref[...].astype(F32).reshape(1, half)


def gather_kernel(where_ref, first_ref, second_ref, third_ref, out_ref):
    rows = first_ref.shape[1]
    low = jnp.bitwise_and(where_ref[2], 1)
    out_ref[:, pl.ds(pl.multiple_of(low * rows, rows), rows), :] = first_ref[...]
    out_ref[:, pl.ds(pl.multiple_of((1 - low) * rows, rows), rows), :] = third_ref[...]
    out_ref[:, 2 * rows :, :] = second_ref[...]


def normed(summed):
    centre = summed - jnp.mean(summed, -1, keepdims=True)
    scale_inv = lax.rsqrt(jnp.mean(centre * centre, -1, keepdims=True) + 1e-05)
    return centre * scale_inv, scale_inv


def norm_back(grad, n, scale_inv, gain):
    scaled = grad * gain
    first = jnp.mean(scaled, -1, keepdims=True)
    second = jnp.mean(scaled * n, -1, keepdims=True)
    return scale_inv * (scaled - first - n * second)


def turn_rows(lines, turned_ref, rows):
    tokens = lines.shape[1]
    blocks = lines.reshape(-1, 2, rows, tokens)
    turned_ref[0] = blocks[:, 0].reshape(-1, tokens)
    turned_ref[1] = blocks[:, 1].reshape(-1, tokens)


BIAS_OUT, GAIN_ONE, SHIFT_ONE, BIAS_DOWN, GAIN_TWO, SHIFT_TWO, BIAS_UP = range(7)


CHUNK = 512
WEIGH = 10**12 // 20
LINES = 16


def blocks(count):
    return [slice(at, at + LINES) for at in range(0, count, LINES)]


def fold(value):
    return jnp.sum(value.reshape(-1, 8, value.shape[-1]), 0)


def total(folded):
    return jnp.sum(folded, 0, keepdims=True)


def ffn_kernel(
    where_ref, summed_ref, other_ref, w_out_ref, params_ref, w_up_ref, w_down_ref, cot_ref,
    out_ref, hidden_ref, n_one_ref, r_one_ref, active_ref, slope_ref, grad_two_ref, sums_ref,
    first_ref, second_ref, branch_ref, bias_ref,
):
    half = other_ref.shape[0]
    tokens, width = summed_ref.shape
    head = where_ref[1]
    count = w_up_ref.shape[1] // CHUNK
    span = lambda i: pl.ds(pl.multiple_of(i * CHUNK, CHUNK), CHUNK)

    params = params_ref[...].astype(F32)
    row = lambda i: params[i : i + 1]
    for i in range(bias_ref.shape[1] // width):
        bias_ref[:, i * width : (i + 1) * width] = row(BIAS_UP + i)
    other_at = pl.multiple_of((1 - head) * half, LANES)
    branch_ref[...] = tn(other_ref[...], w_out_ref[pl.ds(other_at, half), :])

    for at in blocks(tokens):
        n, r = normed(summed_ref[at, :] + branch_ref[at, :] + row(BIAS_OUT))
        n_one_ref[at, :] = n
        r_one_ref[at, :] = jnp.broadcast_to(r, (LINES, LANES))
        hidden_ref[at, :] = (n * row(GAIN_ONE) + row(SHIFT_ONE)).astype(BF)

    def upward(ref, at):
        ref[...] = nn(hidden_ref[...], w_up_ref[:, at])

    def gelu(ref, at):
        bias = bias_ref[:, at]
        for start in range(0, tokens, LINES):
            lines = slice(start, start + LINES)
            v = ref[lines, :] + bias
            phi = 0.5 + 0.5 * lax.erf(v * 0.7071067811865476)
            active_ref[lines, at] = (v * phi).astype(BF)
            density = jnp.exp(-0.5 * v * v) * 0.3989422804014327
            slope_ref[lines, at] = (phi + v * density).astype(BF)

    def downward(at):
        branch_ref[...] += nn(active_ref[:, at], w_down_ref[at, :])

    branch_ref[...] = jnp.zeros_like(branch_ref)
    upward(first_ref, span(0))

    @pl.loop(0, count // 2)
    def _(i):
        upward(second_ref, span(2 * i + 1))
        gelu(first_ref, span(2 * i))
        downward(span(2 * i))
        upward(first_ref, span(jnp.minimum(2 * i + 2, count - 1)))
        gelu(second_ref, span(2 * i + 1))
        downward(span(2 * i + 1))

    sums = [0.0, 0.0, 0.0]
    for at in blocks(tokens):
        n, r = normed(hidden_ref[at, :].astype(F32) + branch_ref[at, :] + row(BIAS_DOWN))
        out_ref[at, :] = (n * row(GAIN_TWO) + row(SHIFT_TWO)).astype(BF)
        cot = cot_ref[at, :].astype(F32)
        grad = norm_back(cot, n, r, row(GAIN_TWO))
        grad_two_ref[at, :] = grad
        terms = (cot * n, cot, grad.astype(BF).astype(F32))
        sums = [earlier + fold(term) for earlier, term in zip(sums, terms)]
    for i, folded in enumerate(sums):
        sums_ref[i : i + 1] = total(folded)


def down_kernel(where_ref, active_ref, grad_two_ref, send_ref, keep_ref):
    core = where_ref[0]
    groups, rows = send_ref.shape[0], send_ref.shape[1]
    grad_branch = grad_two_ref[...].astype(BF)
    for i in range(groups):
        block = nn(active_ref[:, i * 2 * rows : (i + 1) * 2 * rows].T, grad_branch).astype(BF)
        low, high = block[:rows], block[rows:]
        keep_ref[i] = jnp.where(core == 0, low, high)
        send_ref[i] = jnp.where(core == 0, high, low)


def slope_kernel(
    slope_ref, grad_two_ref, w_down_ref, grad_up_ref, bias_up_ref, branch_ref
):
    count = w_down_ref.shape[0] // CHUNK
    span = lambda i: pl.ds(pl.multiple_of(i * CHUNK, CHUNK), CHUNK)

    branch_ref[...] = grad_two_ref[...].astype(BF)

    @pl.loop(0, count)
    def _(i):
        grad_active = nt(branch_ref[...], w_down_ref[span(i), :])
        grad_up = (grad_active * slope_ref[:, span(i)].astype(F32)).astype(BF)
        grad_up_ref[:, span(i)] = grad_up
        bias_up_ref[:, span(i)] = jnp.sum(grad_up.astype(F32), 0, keepdims=True)


def up_kernel(
    where_ref, hidden_ref, n_one_ref, r_one_ref, grad_up_ref, grad_two_ref, w_up_ref, w_out_ref, params_ref,
    own_ref, other_ref,
    grad_one_ref, grad_own_ref, grad_other_ref, sums_ref, send_ref, keep_ref,
    both_ref, turned_ref, grad_hidden_ref, grad_context_ref,
):
    half = grad_own_ref.shape[0]
    head, core = where_ref[1], where_ref[0]
    params = params_ref[...].astype(F32)
    row = lambda i: params[i : i + 1]
    groups, rows = send_ref.shape[0], send_ref.shape[1]
    tokens = hidden_ref.shape[0]
    turn_rows(hidden_ref[...].T, turned_ref, rows)

    @pl.loop(0, w_up_ref.shape[1] // CHUNK)
    def _(i):
        at = pl.ds(pl.multiple_of(i * CHUNK, CHUNK), CHUNK)
        grad_up = grad_up_ref[:, at]
        send_ref[:, :, at] = nn(turned_ref[1 - core], grad_up).astype(BF).reshape(groups, rows, CHUNK)
        keep_ref[:, :, at] = nn(turned_ref[core], grad_up).astype(BF).reshape(groups, rows, CHUNK)

    grad_hidden_ref[...] = nt(grad_up_ref[...], w_up_ref[...])
    sums = [0.0, 0.0, 0.0]
    for at in blocks(tokens):
        grad_hidden = grad_hidden_ref[at, :] + grad_two_ref[at, :]
        n_one = n_one_ref[at, :]
        grad_one = norm_back(grad_hidden, n_one, r_one_ref[at, :1], row(GAIN_ONE))
        grad_one_ref[at, :] = grad_one
        terms = (grad_hidden * n_one, grad_hidden, grad_one.astype(BF).astype(F32))
        sums = [earlier + fold(term) for earlier, term in zip(sums, terms)]
    for i, folded in enumerate(sums):
        sums_ref[i : i + 1] = total(folded)
    grad_attended = grad_one_ref[...].astype(BF)
    grad_context_ref[...] = nt(w_out_ref[...], grad_attended).astype(BF)
    own_at = pl.multiple_of(head * half, LANES)
    other_at = pl.multiple_of((1 - head) * half, LANES)
    both_ref[pl.ds(own_at, half), :] = own_ref[...]
    both_ref[pl.ds(other_at, half), :] = other_ref[...]
    turn_rows(both_ref[...], turned_ref, rows)
    ff = w_up_ref.shape[1]
    send_ref[:, :, ff:] = nn(turned_ref[1 - core], grad_attended).astype(BF).reshape(groups, rows, -1)
    keep_ref[:, :, ff:] = nn(turned_ref[core], grad_attended).astype(BF).reshape(groups, rows, -1)
    grad_own_ref[...] = grad_context_ref[pl.ds(own_at, half), :]
    grad_other_ref[...] = grad_context_ref[pl.ds(other_at, half), :]


def back_kernel(
    where_ref, turned_ref, mask_ref, qkv_own_ref, qkv_other_ref, stats_own_ref, stats_other_ref, context_own_ref,
    context_other_ref, grad_own_ref, grad_other_ref,
    send_ref, keep_ref, grads_ref, sums_ref,
    first_ref, second_ref,
):
    core = where_ref[0]
    width, tokens = context_own_ref.shape
    count = width // HEAD_DIM
    halves = (
        (qkv_own_ref, stats_own_ref, context_own_ref, grad_own_ref),
        (qkv_other_ref, stats_other_ref, context_other_ref, grad_other_ref),
    )

    def scaled(half, i):
        return (halves[half][3][head_lines(width, 0, i), :].astype(F32) * halves[half][1][i, 1:2, :]).astype(BF)

    def begin(ref, half, i):
        q, k, v = [halves[half][0][head_lines(width, part, i), :] for part in range(3)]
        ref[0] = tn(k, q)
        ref[1] = tn(v, scaled(half, i))

    def finish(ref, half, i):
        q, k, v = [halves[half][0][head_lines(width, part, i), :] for part in range(3)]
        grad = scaled(half, i)
        context = halves[half][2][head_lines(width, 0, i), :]
        inner = jnp.sum(grad.astype(F32) * context.astype(F32), 0, keepdims=True)
        held, moved = [], []
        for at in range(0, tokens, LANES):
            span = slice(at, at + LANES)
            weights = jnp.exp(ref[0, :, span] + mask_ref[:, span] - halves[half][1][i, 0:1, span])
            held.append(weights.astype(BF))
            moved.append((weights * (ref[1, :, span] - inner[:, span])).astype(BF))
        weights, grad_scores = jnp.concatenate(held, 1), jnp.concatenate(moved, 1)
        grads_ref[half, head_lines(width, 0, i), :] = nn(k, grad_scores).astype(BF) * 0.125
        grads_ref[half, head_lines(width, 1, i), :] = nt(q, grad_scores).astype(BF)
        grads_ref[half, head_lines(width, 2, i), :] = nt(grad, weights).astype(BF)

    begin(first_ref, 0, 0)

    @pl.loop(0, count)
    def _(i):
        begin(second_ref, 1, i)
        finish(first_ref, 0, i)
        begin(first_ref, 0, jnp.minimum(i + 1, count - 1))
        finish(second_ref, 1, i)

    weigh_heads(core, turned_ref, grads_ref, send_ref, keep_ref, 0, send_ref.shape[3])
    ones = jnp.ones((LANES, tokens), BF)
    for half in range(2):
        sums_ref[half] = nt(grads_ref[half], ones)


def weigh_heads(core, turned_ref, grads_ref, send_ref, keep_ref, start, columns):
    groups, rows = send_ref.shape[1:3]
    width, wide = grads_ref.shape[1] // 3, columns // 3
    for half in range(2):
        for out_ref, lines in ((send_ref, 1 - core), (keep_ref, core)):
            for part in range(3):
                at = part * width + start
                found = nt(turned_ref[lines], grads_ref[half, at : at + wide, :]).astype(BF)
                out_ref[half, :, :, part * wide : (part + 1) * wide] = found.reshape(groups, rows, wide)


def end_kernel(
    where_ref, turned_ref, grads_ref, sums_ref, sums_one_ref, sums_two_ref, bias_up_ref,
    send_ref, keep_ref,
    table_ref, flipped_ref, ext_ref,
):
    core, head = where_ref[0], where_ref[1]
    groups, rows, columns = send_ref.shape[1:]
    columns -= LANES
    width = grads_ref.shape[1] // 3
    weigh_heads(core, turned_ref, grads_ref, send_ref, keep_ref, width - columns // 3, columns)
    table_ref[...] = jnp.zeros_like(table_ref)
    table_ref[2:5] = sums_one_ref[0:3]
    table_ref[5:8] = sums_two_ref[0:3]
    flipped_ref[...] = table_ref[...].T
    lane = lax.broadcasted_iota(jnp.int32, (1, LANES), 1)
    for half, at in ((0, head), (1, 1 - head)):
        lines = pl.ds(pl.multiple_of(at * width, LANES), width)
        query, value = sums_ref[half, :width], sums_ref[half, 2 * width :]
        flipped_ref[lines] = jnp.where(lane == 0, query, jnp.where(lane == 1, value, flipped_ref[lines]))
    own = rows // 2
    table = flipped_ref[...].reshape(groups, 2, 2, own, LANES)
    ff = bias_up_ref.shape[1]
    spread = jnp.broadcast_to(bias_up_ref[...], (LANES, ff)).T.reshape(groups, 2, 2, ff // (4 * groups * rows), rows, LANES)
    lane = lax.broadcasted_iota(jnp.int32, (groups, rows, LANES), 2)
    for to_core in range(2):
        for to_head in range(2):
            block = jnp.concatenate([table[:, to_core, to_head], jnp.zeros((groups, rows - own, LANES), F32)], 1)
            for piece in range(spread.shape[3]):
                block = jnp.where(lane == 8 + piece, spread[:, to_core, to_head, piece], block)
            ext_ref[to_core, to_head] = block.astype(BF)
    for half, at in ((0, head), (1, 1 - head)):
        send_ref[half, :, :, columns:] = ext_ref[1 - core, at]
        keep_ref[half, :, :, columns:] = ext_ref[core, at]


def attend_back(where, turned, mask, own, other, grads, groups, count):
    width, tokens = own[2].shape
    rows = turned.shape[1] // groups
    kept = [v for pair in zip(own, other) for v in pair]
    block = ((2, groups, rows, 3 * count * HEAD_DIM), BF)
    return call(
        back_kernel,
        [block, block, ((2, 3 * width, tokens), BF), ((2, 3 * width, LANES), F32)],
        where, turned, mask, *kept, *grads,
        scratch=[pltpu.VMEM((2, tokens, tokens), F32), pltpu.VMEM((2, tokens, tokens), F32)],
        flops=2 * 10**11 // 3,
        moved=10 * 2**20,
        limit=14,
    )


def attend_end(where, turned, grads, groups, count, *sums):
    depth = 2 * turned.shape[1]
    rows = turned.shape[1] // groups
    block = ((2, groups, rows, 3 * count * HEAD_DIM + LANES), BF)
    return call(
        end_kernel,
        [block, block],
        where, turned, grads, *sums,
        scratch=[
            pltpu.VMEM((LANES, depth), F32), pltpu.VMEM((depth, LANES), F32),
            pltpu.VMEM((2, 2, groups, rows, LANES), BF),
        ],
        flops=2 * 10**11 // 3,
        moved=10 * 2**20,
        limit=8,
    )


def input_kernel(
    where_ref, grads_ref, mine_own_ref, mine_other_ref, theirs_own_ref, theirs_other_ref, grad_one_ref, out_ref
):
    depth, width = mine_own_ref.shape[1:]
    core = where_ref[0]
    plain = [grads_ref[half].T for half in range(2)]
    for at, weights_refs in ((core, (mine_own_ref, mine_other_ref)), (1 - core, (theirs_own_ref, theirs_other_ref))):
        lanes = pl.ds(pl.multiple_of(at * depth, LANES), depth)
        terms = [
            nt(plain[half][:, part * width : (part + 1) * width], weights_refs[half][part])
            for half in range(2)
            for part in range(3)
        ]
        out_ref[:, lanes] = (grad_one_ref[:, lanes] + sum(terms)).astype(BF)


def each(count, body):
    if count == 1:
        body(0)
    else:
        pl.loop(0, count)(body)


def open_kernel(cut, split, where_ref, *refs):
    count = split or 2
    terms, outs = refs[:count], refs[count:]
    head_send, head_own, low_own, *low_sends = outs
    low, head = where_ref[2], where_ref[1]
    size = len(low_sends) + 1

    def block(i, bits, half, columns):
        if split:
            return terms[0][half, i, bits, :, columns] + terms[1][half, i, bits, :, columns]
        return terms[0][i, bits, half, :, columns] + terms[1][i, bits, half, :, columns]

    def body(i):
        for bits in range(size):
            head_own[i, bits] = block(i, bits, 0 if split else head, slice(0, cut))
            head_send[i, bits] = block(i, bits, 1 if split else 1 - head, slice(0, cut))
        for flip, out in enumerate([low_own, *low_sends]):
            for half in range(2):
                if split != 4:
                    out[i, half] = block(i, low ^ flip, half, slice(cut, None))
                    continue
                wide = terms[0].shape[4] - cut
                out[i, half, :, :wide] = block(i, low ^ flip, half, slice(cut, None))
                out[i, half, :, wide:] = terms[2][half, i, low ^ flip] + terms[3][half, i, low ^ flip]

    each(head_own.shape[0], body)


def turn_kernel(split, size, where_ref, *refs):
    first, second, outs = refs[:2], refs[2 : 2 + size], refs[2 + size :]
    first_outs, (second_own, second_send) = outs[:size], outs[size:]
    low, head = where_ref[2], where_ref[1]
    own, other = (0, 1) if split else (head, 1 - head)

    def add(values, *at):
        return functools.reduce(jnp.add, [v[at] for v in values])

    def body(i):
        for flip, out in enumerate(first_outs):
            out[i] = add(first, i, low ^ flip)
        second_own[i] = add(second, i, own)
        second_send[i] = add(second, i, other)

    each(second_own.shape[0], body)


def last_kernel(counts, stage, where_ref, *refs):
    parts, at = [], 0
    for count in counts:
        parts.append(refs[at : at + count])
        at += count
    outs = refs[at:]
    index = where_ref[stage]
    size = len(outs)

    def body(i):
        for flip, out in enumerate(outs):
            start = 0
            for part in parts:
                columns = slice(start, start + part[0].shape[2])
                start = columns.stop
                values = [v[i * size + (index ^ flip)].astype(F32) for v in part]
                out[i, :, columns] = functools.reduce(jnp.add, values).astype(BF)

    each(outs[0].shape[0], body)


def part_kernel(cut, where_ref, *refs):
    terms, (first_own, first_send, second_own, second_send) = refs[:-4], refs[-4:]
    low, head = where_ref[2], where_ref[1]
    for out, index, columns in (
        (first_own, low, slice(0, cut)), (first_send, 1 - low, slice(0, cut)),
        (second_own, head, slice(cut, None)), (second_send, 1 - head, slice(cut, None)),
    ):
        out[...] = functools.reduce(jnp.add, [v[0, index, :, columns] for v in terms])


def close_parts_kernel(scale, *refs):
    out = refs[-1]
    cut = refs[0].shape[1]
    for columns, pair in ((slice(0, cut), refs[0:2]), (slice(cut, None), refs[2:4])):
        out[:, columns] = (pair[0][...].astype(F32) + pair[1][...].astype(F32)) * scale


def close_last_kernel(scale, wide_a, wide_b, *refs):
    terms, out_ref, small_refs, spread_ref = refs[:-10], refs[-10], refs[-9:-1], refs[-1]
    summed = functools.reduce(jnp.add, [v[0].astype(F32) for v in terms]) * scale
    rows, start = summed.shape[0], 3 * wide_a
    for part in range(3):
        out_ref[:, part, :wide_a] = summed[:, part * wide_a : (part + 1) * wide_a]
        out_ref[:, part, wide_a:] = summed[:, start + part * wide_b : start + (part + 1) * wide_b]
    lines = summed[:, 3 * (wide_a + wide_b) :].T
    for i, ref in enumerate(small_refs):
        ref[...] = lines[i, : ref.shape[0]]
    pieces = spread_ref.shape[0] // rows
    spread_ref[...] = jnp.concatenate([lines[8 + i : 9 + i, :rows] for i in range(pieces)], 1)[0]


def close_both_kernel(scale, wide_a, wide_b, *refs):
    close_parts_kernel(scale, *refs[:4], refs[-1])
    close_last_kernel(scale, wide_a, wide_b, *refs[4:-1])


def close_kernel(scale, *refs):
    refs[-1][...] = functools.reduce(jnp.add, [v[0].astype(F32) for v in refs[:-1]]) * scale


def pause_kernel(token_ref, out_ref):
    out_ref[...] = token_ref[...]


def pause(*others):
    token = after(jnp.zeros((8, LANES), F32), *others)
    return call(pause_kernel, [((8, LANES), F32)], token, flops=10**13, limit=2)[0]


def after(value, *others):
    return lax.optimization_barrier((value, *others))[0]


def pick(value, index, axis):
    return lax.dynamic_index_in_dim(value, index, axis, keepdims=False)


def on_device(
    inputs, cotangent, segment_ids, lengths, w_qkv, bias_query, bias_value, w_out, bias_out, gain_one,
    shift_one, w_up, bias_up, w_down, bias_down, gain_two, shift_two,
):
    width = w_out.shape[0]
    half = w_qkv.shape[2]
    ff = w_up.shape[1]
    tokens = inputs.shape[0]
    batch = lax.axis_size("batch")
    heads = lax.axis_size("head")
    place, head = lax.axis_index("batch"), lax.axis_index("head")
    core = place % 2
    scale = 1.0 / (lengths.shape[0] * batch)

    plan, bit, bits = [], 1, batch.bit_length() - 1
    if (bits - 1) % 2:
        plan.append((1, 2))
        bit = 2
    while bit < bits:
        plan.append((bit, 4))
        bit += 2
    halving = [(at, 2) for at in range(plan[0][0] + plan[0][1] // 2, bits)]
    where = jnp.stack([core, head] + [(place >> at) % many for at, many in plan + halving]).astype(jnp.int32)

    def swap_batch(value, flip):
        return lax.ppermute(value, "batch", [(i, i ^ flip) for i in range(batch)])

    def swap_head(value):
        return lax.ppermute(value, "head", [(0, 1), (1, 0)])

    depth = width // 2

    def columns(source, at):
        part = lax.dynamic_slice_in_dim(source, at * depth, depth, 0)
        return part.transpose(1, 0, 2)

    third = depth // 3

    def piece(at):
        return lax.dynamic_slice_in_dim(w_qkv, core * depth + at * third, third, 0).transpose(1, 0, 2)

    early_piece = piece((place >> 1) % 2)
    w_first = swap_head(early_piece)
    late_piece = piece(after(jnp.int32(2), early_piece))
    w_second = swap_head(late_piece)
    pair = (after(bias_query, late_piece), bias_value)
    small_own = call(pair_kernel, [((1, width), F32)], *pair, limit=2)[0]
    small_other = swap_head(small_own)
    own_mine = columns(after(w_qkv, late_piece), core)
    w_third = swap_batch(w_first, 2)
    ids = segment_ids.reshape(-1, LANES)
    prepared = (inputs, where, columns(after(w_qkv, own_mine), 1 - core), small_own, ids)
    inputs, where, own_theirs, small_own, ids = lax.optimization_barrier(prepared)

    mask, summed, turned, *kept_own = attend(
        where, inputs, small_own, own_mine, own_theirs, ids, lengths, w_out, turned_rows=width // batch
    )
    context_own = kept_own[2]
    vectors = [bias_out, gain_one, shift_one, bias_down, gain_two, shift_two, bias_up]
    params = call(
        lines_kernel, [((BIAS_UP + ff // width, width), F32)], after(vectors[0], context_own), *vectors[1:], limit=2
    )[0]
    w_first, w_second, w_third = [after(v, context_own, small_other) for v in (w_first, w_second, w_third)]
    w_mine = call(gather_kernel, [(own_mine.shape, BF)], where, w_first, w_second, w_third, limit=6)[0]
    w_theirs = swap_batch(w_mine, 1)
    kept_other = attend(where, inputs, small_other, w_mine, w_theirs, mask)
    context_other = kept_other[2]

    groups = batch // 2
    ffn_rows, up_rows = ff // batch, width // batch
    out, hidden, n_one, r_one, active, slope, grad_two, sums_two = call(
        ffn_kernel,
        [
            ((tokens, width), BF),
            ((tokens, width), BF),
            ((tokens, width), F32),
            ((tokens, LANES), F32),
            ((tokens, ff), BF),
            ((tokens, ff), BF),
            ((tokens, width), F32),
            ((8, width), F32),
        ],
        where, summed, context_other, w_out, params, w_up, w_down, cotangent,
        scratch=[
            pltpu.VMEM((tokens, CHUNK), F32), pltpu.VMEM((tokens, CHUNK), F32), pltpu.VMEM((tokens, width), F32),
            pltpu.VMEM((1, ff), F32),
        ],
        flops=2 * 10**11 // 3, moved=30 * 2**20, limit=14,
    )
    down_send, down_keep = call(
        down_kernel,
        [((groups, ffn_rows, width), BF), ((groups, ffn_rows, width), BF)],
        where, active, grad_two,
        flops=6 * 10**10 // 3, moved=10 * 2**20, limit=12,
    )
    low, rest = plan[0], plan[1:]
    size = low[1]
    low_groups = groups // size

    def open_sum(values, cut, split=False, weigh=0):
        rows, columns = values[0].shape[-2] // (1 if split else heads), values[0].shape[-1]
        lead = (heads, low_groups, size) if split else (low_groups, size, heads)
        more = sum(v.shape[-1] for v in values[2::2])
        values = [v.reshape(*lead, rows, v.shape[-1]) for v in values]
        columns += more
        by_head, by_low = (low_groups, size, rows, cut), (low_groups, heads, rows, columns - cut)
        head_send, head_own, low_own, *low_sends = call(
            functools.partial(open_kernel, cut, len(values) if split else 0), [(by_head, BF)] * 2 + [(by_low, BF)] * size, where, *values,
            flops=weigh,
        )
        got = [swap_batch(v, flip << low[0]) for flip, v in enumerate(low_sends, 1)]
        return head_send, [head_own, swap_head(head_send)], [low_own, *got]

    def turn_sum(first, second, split=False, weigh=0):
        rows = first[0].shape[2]
        cut, more = first[0].shape[3], second[0].shape[3]
        outs = call(
            functools.partial(turn_kernel, split, size),
            [((low_groups, rows, cut), BF)] * size + [((low_groups, rows, more), BF)] * 2,
            where, *first, *second,
            flops=weigh,
        )
        got = [swap_batch(v, flip << low[0]) for flip, v in enumerate(outs[1:size], 1)]
        return outs[0], [outs[0], *got], [outs[size], swap_head(outs[size + 1])]

    def last_sum(*parts, stages=None, weigh=0):
        for bit, many in stages or rest:
            stage = 2 + (plan + halving).index((bit, many))
            rows, columns = parts[0][0].shape[1], sum(part[0].shape[2] for part in parts)
            left = parts[0][0].shape[0] // many
            outs = call(
                functools.partial(last_kernel, [len(part) for part in parts], stage),
                [((left, rows, columns), BF)] * many,
                where, *[v for part in parts for v in part],
                flops=weigh,
            )
            parts = [[outs[0]] + [swap_batch(v, flip << bit) for flip, v in enumerate(outs[1:], 1)]]
        return outs[0], parts[0]

    def close_sum(values, weigh=0):
        return call(functools.partial(close_kernel, scale), [(values[0].shape[1:], F32)], *values, flops=weigh)[0]

    def late(values, *before):
        return [values[0]] + [after(v, *before) for v in values[1:]]

    down = [down_keep, swap_batch(down_send, 1)]
    grad_up, sum_bias_up = call(
        slope_kernel,
        [((tokens, ff), BF), ((1, ff), F32)],
        slope, grad_two, w_down,
        scratch=[
            pltpu.VMEM((tokens, width), BF),
        ],
        flops=10**11 // 3, moved=10 * 2**20, limit=8,
    )
    down[1] = after(down[1], sum_bias_up)
    sent, down, down_low = open_sum(down, width // 2)
    grad_one, grad_own, grad_other, sums_one, up_send, up_keep = call(
        up_kernel,
        [
            ((tokens, width), F32),
            ((half, tokens), BF),
            ((half, tokens), BF),
            ((8, width), F32),
            ((groups, up_rows, ff + width), BF),
            ((groups, up_rows, ff + width), BF),
        ],
        where, hidden, n_one, r_one, after(grad_up, sent), grad_two, w_up, w_out, params, context_own, context_other,
        scratch=[
            pltpu.VMEM((width, tokens), BF),
            pltpu.VMEM((2, groups * up_rows, tokens), BF),
            pltpu.VMEM((tokens, width), F32),
            pltpu.VMEM((width, tokens), BF),
        ],
        limit=13,
        flops=2 * 10**11 // 3, moved=30 * 2**20,
    )
    up = [up_keep, swap_batch(up_send, 1)]
    early = size == heads and len(halving) == 2
    if early:
        flat = lambda v: v.reshape(low_groups, -1, v.shape[3])
        down_cut, down_rows = down[0].shape[3], down[0].shape[2]
        sent, down = last_sum(
            [flat(v) for v in late(down, grad_one)], [flat(v) for v in down_low], stages=halving[:1], weigh=WEIGH
        )
    else:
        sent, down, down_low = turn_sum(late(down, grad_one), down_low, weigh=WEIGH)
    sent, up, up_low = open_sum(late(up, sent), (ff + width) // 2)
    end = half // HEAD_DIM - 2
    weights = (own_mine, w_mine, own_theirs, w_theirs)
    qa_send, qa_keep, grads, sums = attend_back(
        where, turned, mask, kept_own, kept_other, (after(grad_own, sent), grad_other), groups, end
    )
    qa_got = swap_batch(qa_send, 1)
    if early:
        sent, down = last_sum(late(down, sums), stages=halving[1:])
    else:
        sent, down = last_sum(late(down, sums), down_low)
    sent, up, up_low = turn_sum(late(up, sent), up_low)
    qb_send, qb_keep = attend_end(
        where, turned, after(grads, sent), groups, 2, sums, sums_one, sums_two, sum_bias_up
    )
    cut_a, cut_b = 3 * end * HEAD_DIM // 2, 2 * LANES
    sent, qa, qa_low = open_sum([qa_keep, after(qa_got, qb_keep)], cut_a, True)
    input_grad = call(
        input_kernel,
        [((tokens, width), BF)],
        where, after(grads, sent), *weights, grad_one,
        flops=WEIGH, moved=10 * 2**20, limit=10,
    )[0]
    if early:
        down[1] = after(down[1], input_grad)
        up[0] = after(up[0], down[1])
    sent, up = last_sum(late(up, input_grad), up_low, stages=halving[:1])
    qb_got = swap_batch(after(qb_send, sent), 1)
    sent, qa, qa_low = turn_sum(late(qa, sent), qa_low, True, weigh=WEIGH)
    sent, qb, qb_low = open_sum([qb_keep, after(qb_got, sent)], cut_b, True)
    sent, up = last_sum(late(up, sent), stages=halving[1:])
    sent, qb, qb_low = turn_sum(late(qb, sent), qb_low, True, weigh=WEIGH)
    if early:
        by_low, by_head = (down_rows, down_cut), (down_rows, down[0].shape[2] - down_cut)
        outs = call(
            functools.partial(part_kernel, down_cut), [(by_low, BF)] * 2 + [(by_head, BF)] * 2,
            where, *[v.reshape(1, 2, down_rows, -1) for v in [after(down[0], sent), *down[1:]]],
        )
        down = [outs[0], swap_batch(outs[1], 1 << low[0]), outs[2], swap_head(outs[3])]
        sent = outs[1]
    sent, qkv = last_sum(late(qa, sent), qa_low, qb, qb_low)
    sum_up = close_sum(late(up, sent))
    own, pieces = up_rows // heads, ff // (heads * width)
    wide = (end * HEAD_DIM, 2 * HEAD_DIM)
    shapes = [((up_rows, 3, half), F32)] + [((own,), F32)] * 8 + [((pieces * up_rows,), F32)]
    if early:
        down = [down[0], after(down[1], sum_up), down[2], after(down[3], sum_up)]
        shapes.append(((down_rows, down_cut + down[2].shape[1]), F32))
        sum_qkv, *small, spread, sum_down = call(
            functools.partial(close_both_kernel, scale, *wide), shapes, *down, *qkv
        )
    else:
        sum_down = close_sum(late(down, sum_up))
        sum_qkv, *small, spread = call(functools.partial(close_last_kernel, scale, *wide), shapes, *qkv)
    return (
        out, input_grad, sum_qkv, small[0], small[1], sum_up[:, ff:], small[4], small[2], small[3],
        sum_up[:, :ff], spread, sum_down, small[7], small[5], small[6],
    )


def solution(mesh):
    rows = P(BOTH, None)
    placed = (rows, rows, P("batch"), P("batch"), P(None, None, "head"), P("head"), P("head")) + (P(),) * 10
    flat = P(BOTH)
    return jax.shard_map(
        on_device,
        mesh=mesh,
        in_specs=placed,
        out_specs=(
            rows, rows, P("batch", None, "head"), flat, flat, rows, flat, flat, flat, rows, flat, rows, flat,
            flat, flat,
        ),
        check_vma=False,
    )
```
